32 devices in a mesh: pairs: 8 (over z, x), seq: 4 (over y, core).
Axes of the slice: x: 2, y: 2, z: 4, core: 2. Of those that a mesh axis runs over, the one named last changes fastest.
Arguments:
- enc_input: bfloat16 [32, 512, 768], P('pairs', 'seq'), may hold values from -6 to 6
- dec_input: bfloat16 [32, 768], P(('pairs', 'seq')), may hold values from -6 to 6
- lengths: int32 [32], P('pairs'), may hold values from 129 to 512, as said below
- attend_gain: float32 [768], replicated, may hold values from 0.5 to 1.5
- query_weight: bfloat16 [768, 768], replicated, may hold values from -0.0390625 to 0.0390625
- key_weight: bfloat16 [768, 768], replicated, may hold values from -0.21875 to 0.21875
- value_weight: bfloat16 [768, 768], replicated, may hold values from -0.21875 to 0.21875
- output_weight: bfloat16 [768, 768], replicated, may hold values from -1.25 to 1.25
- bias_table: float32 [32, 12], replicated, may hold values from -4 to 4
- expand_gain: float32 [768], replicated, may hold values from 0.5 to 1.5
- expand_weight: bfloat16 [768, 3072], replicated, may hold values from -0.21875 to 0.21875
- reduce_weight: bfloat16 [3072, 768], replicated, may hold values from -0.109375 to 0.109375
- final_gain: float32 [768], replicated, may hold values from 0.5 to 1.5
- self_gain: float32 [768], replicated, may hold values from 0.5 to 1.5
- self_value: bfloat16 [768, 768], replicated, may hold values from -0.21875 to 0.21875
- self_output: bfloat16 [768, 768], replicated, may hold values from -0.21875 to 0.21875
- cross_gain: float32 [768], replicated, may hold values from 0.5 to 1.5
- cross_query: bfloat16 [768, 768], replicated, may hold values from -0.0390625 to 0.0390625
- cross_key: bfloat16 [768, 768], replicated, may hold values from -0.21875 to 0.21875
- cross_value: bfloat16 [768, 768], replicated, may hold values from -0.21875 to 0.21875
- cross_output: bfloat16 [768, 768], replicated, may hold values from -1.25 to 1.25
- feed_gain: float32 [768], replicated, may hold values from 0.5 to 1.5
- feed_expand: bfloat16 [768, 3072], replicated, may hold values from -0.21875 to 0.21875
- feed_reduce: bfloat16 [3072, 768], replicated, may hold values from -0.109375 to 0.109375
- enc_cotangent: bfloat16 [32, 512, 768], P('pairs', 'seq'), may hold values from -6 to 6
- dec_cotangent: bfloat16 [32, 768], P(('pairs', 'seq')), may hold values from -6 to 6
Outputs:
- encoded: bfloat16 [32, 512, 768], P('pairs', 'seq')
- decoded: bfloat16 [32, 768], P(('pairs', 'seq'))
- enc_input_grad: bfloat16 [32, 512, 768], P('pairs', 'seq')
- dec_input_grad: bfloat16 [32, 768], P(('pairs', 'seq'))
- attend_gain_grad: float32 [768], replicated
- query_weight_grad: float32 [768, 768], P('pairs', 'seq')
- key_weight_grad: float32 [768, 768], P('pairs', 'seq')
- value_weight_grad: float32 [768, 768], P('pairs', 'seq')
- output_weight_grad: float32 [768, 768], P('pairs', 'seq')
- bias_table_grad: float32 [32, 12], replicated
- expand_gain_grad: float32 [768], replicated
- expand_weight_grad: float32 [768, 3072], P('pairs', 'seq')
- reduce_weight_grad: float32 [3072, 768], P('pairs', 'seq')
- final_gain_grad: float32 [768], replicated
- self_gain_grad: float32 [768], replicated
- self_value_grad: float32 [768, 768], P('pairs', 'seq')
- self_output_grad: float32 [768, 768], P('pairs', 'seq')
- cross_gain_grad: float32 [768], replicated
- cross_query_grad: float32 [768, 768], P('pairs', 'seq')
- cross_key_grad: float32 [768, 768], P('pairs', 'seq')
- cross_value_grad: float32 [768, 768], P('pairs', 'seq')
- cross_output_grad: float32 [768, 768], P('pairs', 'seq')
- feed_gain_grad: float32 [768], replicated
- feed_expand_grad: float32 [768, 3072], P('pairs', 'seq')
- feed_reduce_grad: float32 [3072, 768], P('pairs', 'seq')
The draws below stay inside these ranges and needn't reach their ends.
Inputs may be any that keep to these rules, and one draw needn't show every extreme that they name: A pair whose length exceeds 512 // 2 has bucket 512, else bucket 512 // 2 and lengths over 128. In each aligned block of 4 pairs one pair has length 512.
All inputs are finite; a program needn't handle non-finite values.
Results may differ from the reference program's by a relative error of at most 0.023.
Values may be sent and summed in bfloat16 or wider, within the bound.
A program may use at most 256 MiB of HBM per device.

```python
import math
import jax
import jax.numpy as jnp
from jax import lax

D = 768
H = 12
HD = 64
FF = 3072
NB = 32
SEQ = 512
PAIRS_DEV = 4
PAIRS = 32


def draw_lengths(key, part):
    key = jax.random.fold_in(key, 11)
    key_big, key_len, key_full = jax.random.split(key, 3)
    larger = jax.random.randint(key_big, (PAIRS,), 0, 2)
    ceiling = jnp.where(larger == 1, SEQ, SEQ // 2)
    bottom = jnp.where(larger == 1, SEQ // 2 + 1, SEQ // 4 + 1)
    spread = jax.random.randint(key_len, (PAIRS,), 0, 1 << 20)
    length = bottom + spread % (ceiling - bottom + 1)
    chosen = jax.random.randint(key_full, (PAIRS // PAIRS_DEV,), 0, PAIRS_DEV)
    slots = jnp.arange(PAIRS, dtype=jnp.int32)
    filled = slots % PAIRS_DEV == jnp.repeat(chosen, PAIRS_DEV)
    return jnp.where(filled, SEQ, length).astype(jnp.int32)


def block_levels(own_key, extent, pieces, least, top_value):
    level = 1.0
    for axis_at, blocks in pieces:
        draws = jax.random.uniform(jax.random.fold_in(jax.random.fold_in(own_key, 6), axis_at), (blocks,), jnp.float32, least / len(pieces), top_value / len(pieces))
        level = level * jnp.repeat(jnp.exp(draws), extent[axis_at] // blocks).reshape((-1,) + (1,) * (len(extent) - 1 - axis_at))
    return level


def gaussian(stream_key, dims, deviation, limit, pieces=(), held_as=jnp.bfloat16):
    level = block_levels(stream_key, dims, pieces, -0.22, 0.18) if pieces else 1.0
    entries = jax.random.normal(stream_key, dims, jnp.float32) * deviation * level
    return jnp.minimum(jnp.maximum(entries, -limit), limit).astype(held_as)


def setup_inputs(seed: int = 0) -> dict:
    seeds = jax.random.split(jax.random.key(seed), 27)
    return {
        "enc_input": gaussian(seeds[0], (PAIRS, SEQ, D), 1.0, 6.0, ((0, 8), (1, 4))),
        "dec_input": gaussian(seeds[1], (PAIRS, D), 1.0, 6.0, ((0, 32),)),
        "lengths": draw_lengths(jax.random.fold_in(seeds[26], 71), 0),
        "attend_gain": jnp.clip(1.0 + 0.1 * jax.random.normal(seeds[3], (D,), jnp.float32), 0.5, 1.5),
        "query_weight": gaussian(seeds[4], (D, D), (32 * D) ** -0.5, 0.0390625),
        "key_weight": gaussian(seeds[5], (D, D), D ** -0.5, 0.21875),
        "value_weight": gaussian(seeds[6], (D, D), D ** -0.5, 0.21875),
        "output_weight": gaussian(seeds[7], (D, D), (D // 32) ** -0.5, 1.25),
        "bias_table": gaussian(seeds[8], (NB, H), 1.0, 4.0, (), jnp.float32),
        "expand_gain": jnp.clip(1.0 + 0.1 * jax.random.normal(seeds[9], (D,), jnp.float32), 0.5, 1.5),
        "expand_weight": gaussian(seeds[10], (D, FF), D ** -0.5, 0.21875),
        "reduce_weight": gaussian(seeds[11], (FF, D), FF ** -0.5, 0.109375),
        "final_gain": jnp.clip(1.0 + 0.1 * jax.random.normal(seeds[12], (D,), jnp.float32), 0.5, 1.5),
        "self_gain": jnp.clip(1.0 + 0.1 * jax.random.normal(seeds[13], (D,), jnp.float32), 0.5, 1.5),
        "self_value": gaussian(seeds[14], (D, D), D ** -0.5, 0.21875),
        "self_output": gaussian(seeds[15], (D, D), D ** -0.5, 0.21875),
        "cross_gain": jnp.clip(1.0 + 0.1 * jax.random.normal(seeds[16], (D,), jnp.float32), 0.5, 1.5),
        "cross_query": gaussian(seeds[17], (D, D), (32 * D) ** -0.5, 0.0390625),
        "cross_key": gaussian(seeds[18], (D, D), D ** -0.5, 0.21875),
        "cross_value": gaussian(seeds[19], (D, D), D ** -0.5, 0.21875),
        "cross_output": gaussian(seeds[20], (D, D), (D // 32) ** -0.5, 1.25),
        "feed_gain": jnp.clip(1.0 + 0.1 * jax.random.normal(seeds[21], (D,), jnp.float32), 0.5, 1.5),
        "feed_expand": gaussian(seeds[22], (D, FF), D ** -0.5, 0.21875),
        "feed_reduce": gaussian(seeds[23], (FF, D), FF ** -0.5, 0.109375),
        "enc_cotangent": gaussian(seeds[24], (PAIRS, SEQ, D), 1.0, 6.0, ((0, 8), (1, 4))),
        "dec_cotangent": gaussian(seeds[25], (PAIRS, D), 1.0, 6.0, ((0, 32),)),
    }


EPSILON = 1e-06
EDGES = (12, 16, 23, 32, 46, 64, 91)
HIGHEST = lax.Precision.HIGHEST

@jax.custom_vjp
def low(v):
    return lax.optimization_barrier(v.astype(jnp.bfloat16)).astype(jnp.float32)

@jax.custom_vjp
def low_back(v):
    return v

def low_keep(v):
    return (low(v), None)

def low_pass(kept, grad):
    return (grad,)

def back_keep(v):
    return (v, None)

def back_low(kept, grad):
    return (low(grad),)
low.defvjp(low_keep, low_pass)
low_back.defvjp(back_keep, back_low)

def rel_bucket(query_pos, key_pos):
    offset = key_pos[None, :] - query_pos[:, None]
    distance = jnp.abs(offset)
    far_bucket = jnp.full_like(distance, 8)
    for threshold in EDGES:
        far_bucket = far_bucket + (distance >= threshold).astype(jnp.int32)
    bucket_id = jnp.where(distance < 8, distance, far_bucket)
    return bucket_id + 16 * (offset > 0).astype(jnp.int32)

def rms_norm(values, gains):
    return values * lax.rsqrt(lax.optimization_barrier(jnp.mean(values * values, axis=-1, keepdims=True)) + EPSILON) * gains

def smooth(values):
    return 0.5 * values * (1.0 + jnp.tanh(0.7978845608 * (values + 0.044715 * values * values * values)))

def masked_softmax(scores, visible):
    masked = jnp.where(visible, scores, -1e+30)
    row_max = lax.optimization_barrier(jnp.max(masked, axis=-1, keepdims=True))
    raised = jnp.exp(masked - row_max)
    return raised / lax.optimization_barrier(jnp.sum(raised, axis=-1, keepdims=True))

def project(inputs, matrix):
    return jnp.matmul(inputs, matrix, precision=HIGHEST)

def forward(weights, enc_value, dec_value, lengths):
    attend_gain, query_weight, key_weight, value_weight, output_weight, bias_table, expand_gain, expand_weight, reduce_weight, final_gain, self_gain, self_value, self_output, cross_gain, cross_query, cross_key, cross_value, cross_output, feed_gain, feed_expand, feed_reduce = weights
    positions = jnp.arange(SEQ, dtype=jnp.int32)
    onehot = (rel_bucket(positions, positions)[:, :, None] == jnp.arange(NB, dtype=jnp.int32)[None, None, :]).astype(jnp.float32)
    position_bias = jnp.einsum('tub,bh->htu', onehot, bias_table, precision=HIGHEST)
    group = math.gcd(PAIRS, 8)

    def one_group(tokens, dec_rows, group_lengths):
        live = positions[None, :] < group_lengths[:, None]
        normed = low(rms_norm(tokens, attend_gain))
        query = low_back(low(project(normed, query_weight))).reshape(group, SEQ, H, HD)
        key = low_back(low(project(normed, key_weight))).reshape(group, SEQ, H, HD)
        value = low_back(low(project(normed, value_weight))).reshape(group, SEQ, H, HD)
        scores = low_back(jnp.einsum('gthd,guhd->ghtu', query, key, precision=HIGHEST) + position_bias[None])
        probs = masked_softmax(scores, live[:, None, None, :])
        context = low_back(low(jnp.einsum('ghtu,guhd->gthd', low(probs), value, precision=HIGHEST))).reshape(group, SEQ, D)
        hidden = tokens + low_back(project(context, output_weight))
        upper = low_back(project(low(rms_norm(hidden, expand_gain)), expand_weight))
        enc_block = live.astype(jnp.float32)[:, :, None] * (hidden + low_back(project(low(smooth(upper)), reduce_weight)))
        enc_normed = low_back(low(rms_norm(enc_block, final_gain)))
        self_normed = low(rms_norm(dec_rows, self_gain))
        self_values = low_back(low(project(self_normed, self_value)))
        after = dec_rows + low_back(project(self_values, self_output))
        cross_normed = low(rms_norm(after, cross_gain))
        cross_q = low_back(low(project(cross_normed, cross_query))).reshape(group, H, HD)
        cross_k = low_back(low(project(enc_normed, cross_key))).reshape(group, SEQ, H, HD)
        cross_v = low_back(low(project(enc_normed, cross_value))).reshape(group, SEQ, H, HD)
        cross_scores = low_back(jnp.einsum('ghd,guhd->ghu', cross_q, cross_k, precision=HIGHEST))
        cross_probs = masked_softmax(cross_scores, live[:, None, :])
        cross_context = low_back(low(jnp.einsum('ghu,guhd->ghd', low(cross_probs), cross_v, precision=HIGHEST))).reshape(group, D)
        middle = after + low_back(project(cross_context, cross_output))
        dec_upper = low_back(project(low(rms_norm(middle, feed_gain)), feed_expand))
        dec_block = middle + low_back(project(low(smooth(dec_upper)), feed_reduce))
        return (enc_block, dec_block)
    checked = jax.checkpoint(one_group)

    def scan_step(carry, slab):
        return (carry, checked(slab[0], slab[1], slab[2]))
    slabs = (enc_value.reshape(-1, group, SEQ, D), dec_value.reshape(-1, group, D), lengths.reshape(-1, group))
    carry_out, stacked = lax.scan(scan_step, jnp.zeros((), jnp.float32), slabs)
    return (stacked[0].reshape(PAIRS, SEQ, D), stacked[1].reshape(PAIRS, D))

def reference(enc_input, dec_input, lengths, attend_gain, query_weight, key_weight, value_weight, output_weight, bias_table, expand_gain, expand_weight, reduce_weight, final_gain, self_gain, self_value, self_output, cross_gain, cross_query, cross_key, cross_value, cross_output, feed_gain, feed_expand, feed_reduce, enc_cotangent, dec_cotangent):
    weights = tuple((item.astype(jnp.float32) for item in (attend_gain, query_weight, key_weight, value_weight, output_weight, bias_table, expand_gain, expand_weight, reduce_weight, final_gain, self_gain, self_value, self_output, cross_gain, cross_query, cross_key, cross_value, cross_output, feed_gain, feed_expand, feed_reduce)))

    def whole(weight_set, enc_value, dec_value):
        return forward(weight_set, enc_value, dec_value, lengths)
    outputs, pullback = jax.vjp(whole, weights, enc_input.astype(jnp.float32), dec_input.astype(jnp.float32))
    grads, enc_grad, dec_grad = pullback((enc_cotangent.astype(jnp.float32), dec_cotangent.astype(jnp.float32)))
    return (outputs[0].astype(jnp.bfloat16), outputs[1].astype(jnp.bfloat16), enc_grad.astype(jnp.bfloat16), dec_grad.astype(jnp.bfloat16), grads[0], grads[1], grads[2], grads[3], grads[4], grads[5], grads[6], grads[7], grads[8], grads[9], grads[10], grads[11], grads[12], grads[13], grads[14], grads[15], grads[16], grads[17], grads[18], grads[19], grads[20])
```

```python
import functools

import jax
import jax.numpy as jnp
from jax import lax
from jax.experimental import pallas as pl
from jax.experimental.pallas import tpu as pltpu
from jax.sharding import PartitionSpec as P

EPSILON = 1e-06
EDGES = (12, 16, 23, 32, 46, 64, 91)
HIGHEST = lax.Precision.HIGHEST
MESH = pl.DeviceIdType.MESH
BF = jnp.bfloat16
F32 = jnp.float32


def rel_bucket(query_pos, key_pos):
    offset = key_pos[None, :] - query_pos[:, None]
    distance = jnp.abs(offset)
    far_bucket = jnp.full_like(distance, 8)
    for threshold in EDGES:
        far_bucket = far_bucket + (distance >= threshold).astype(jnp.int32)
    bucket_id = jnp.where(distance < 8, distance, far_bucket)
    return bucket_id + 16 * (offset > 0).astype(jnp.int32)


def rms_norm(values, gains):
    return values * lax.rsqrt(jnp.mean(values * values, axis=-1, keepdims=True) + EPSILON) * gains


def smooth(values):
    return (
        0.5
        * values
        * (1.0 + jnp.tanh(0.7978845608 * (values + 0.044715 * values * values * values)))
    )


def mm(a, b):
    return jnp.dot(a, b, preferred_element_type=F32)


def mm_t(a, b):
    return lax.dot_general(a, b, (((1,), (1,)), ((), ())), preferred_element_type=F32)


def t_mm(a, b):
    return lax.dot_general(a, b, (((0,), (0,)), ((), ())), preferred_element_type=F32)


def norm_back(values, gains, upstream):
    return jax.vjp(rms_norm, values, gains)[1](upstream)


def smooth_back(values, upstream):
    return jax.vjp(smooth, values)[1](upstream)[0]


def exchange_kernel(np_, ns, u, small, dec, enc, red, small_out, dec_out, enc_out,
                    own, r0, r1a, r1b, s1a, s1b, r2, s2, r3, sm, smr, smz,
                    loc, s0s, s0r, s1s, s1r, s2s, s2r, s3s, s3r,
                    ms, mr, mzs, mzr, ds, dr, es, er):
    units = u.shape[0]
    nz = np_ // 2
    rows = u.shape[5]
    p = lax.axis_index("pairs")
    s = lax.axis_index("seq")
    c = lax.rem(s, 2)
    y = s // 2
    x = lax.rem(p, 2)
    z = p // 2
    me = p * ns + s
    count = np_ * ns
    core_peer = (p, s + 1 - 2 * c)
    y_peer = (p, lax.rem(s + 2, 4))
    x_peer = (p + 1 - 2 * x, s)

    def place(d):
        lin = lax.rem(me + d, count)
        return (lin // ns, lax.rem(lin, ns))

    barrier = pltpu.get_barrier_semaphore()

    @pl.loop(1, count)
    def _(d):
        pl.semaphore_signal(barrier, inc=1, device_id=place(d), device_id_type=MESH)

    pl.semaphore_wait(barrier, count - 1)

    def remote(src, dst, send, recv, peer):
        return pltpu.make_async_remote_copy(
            src_ref=src, dst_ref=dst, send_sem=send, recv_sem=recv,
            device_id=peer, device_id_type=MESH)

    def core_copy(k):
        return remote(u.at[k, 1 - c], r0.at[k], s0s.at[k], s0r.at[k], core_peer)

    def own_copy(k):
        return pltpu.make_async_copy(u.at[k, c], own.at[k], loc.at[k])

    @pl.loop(0, units)
    def _(k):
        core_copy(k).start()
        own_copy(k).start()

    def dec_copy(d):
        q = place(d)
        return remote(dec.at[q[0] * ns + q[1]], dec_out.at[me], ds.at[d], dr.at[d], q)

    keep_dec = pltpu.make_async_copy(dec.at[me], dec_out.at[me], loc.at[units])
    keep_dec.start()

    @pl.loop(1, count)
    def _(d):
        dec_copy(d).start()

    def enc_copy(d):
        t = lax.rem(s + d, ns)
        return remote(enc.at[:, t], enc_out.at[:, s], es.at[d], er.at[d], (p, t))

    keep_enc = pltpu.make_async_copy(enc.at[:, s], enc_out.at[:, s], loc.at[units + 1])
    keep_enc.start()
    for d in range(1, ns):
        enc_copy(d).start()

    sm[0] = small[...]
    for i, peer in enumerate((core_peer, y_peer, x_peer)):
        copy = remote(sm.at[i], smr.at[i], ms.at[i], mr.at[i], peer)
        copy.start()
        copy.wait()
        if i < 2:
            sm[i + 1] = sm[i] + smr[i]
        else:
            smz[z] = sm[i] + smr[i]

    def z_small(d):
        return remote(smz.at[z], smz.at[z], mzs.at[d], mzr.at[d],
                      (lax.rem(z + d, nz) * 2 + x, s))

    @pl.loop(1, nz)
    def _(d):
        z_small(d).start()

    def y_first(k):
        return remote(own.at[2 * k, 1 - y], r1a.at[k], s1s.at[2 * k], s1r.at[2 * k], y_peer)

    def x_first(k):
        return remote(own.at[2 * k + 1, :, :, 1 - x], r1b.at[k], s1s.at[2 * k + 1],
                      s1r.at[2 * k + 1], x_peer)

    def x_second(k):
        return remote(s1a.at[k, :, 1 - x], r2.at[2 * k], s2s.at[2 * k], s2r.at[2 * k], x_peer)

    def y_second(k):
        return remote(s1b.at[k, 1 - y], r2.at[2 * k + 1], s2s.at[2 * k + 1],
                      s2r.at[2 * k + 1], y_peer)

    def z_last(k, d):
        t = lax.rem(z + d, nz)
        return remote(s2.at[k, t], r3.at[k, d], s3s.at[k, d], s3r.at[k, d], (t * 2 + x, s))

    def stage0(k):
        core_copy(k).wait()
        own_copy(k).wait()

        @pl.loop(0, 2)
        def _(a):
            @pl.loop(0, nz)
            def _(b):
                for e in range(2):
                    own[k, a, b, e] = (own[k, a, b, e].astype(F32)
                                       + r0[k, a, b, e].astype(F32)).astype(BF)

    @pl.loop(0, units // 2)
    def _(k):
        stage0(2 * k)
        y_first(k).start()
        stage0(2 * k + 1)
        x_first(k).start()

    @pl.loop(0, units // 2)
    def _(k):
        y_first(k).wait()

        @pl.loop(0, nz)
        def _(b):
            for e in range(2):
                s1a[k, b, e] = (own[2 * k, y, b, e].astype(F32)
                                + r1a[k, b, e].astype(F32)).astype(BF)

        x_second(k).start()
        x_first(k).wait()

        @pl.loop(0, nz)
        def _(b):
            for e in range(2):
                s1b[k, e, b] = (own[2 * k + 1, e, b, x].astype(F32)
                                + r1b[k, e, b].astype(F32)).astype(BF)

        y_second(k).start()

    @pl.loop(0, units // 2)
    def _(k):
        x_second(k).wait()

        @pl.loop(0, nz)
        def _(b):
            s2[2 * k, b] = (s1a[k, b, x].astype(F32) + r2[2 * k, b].astype(F32)).astype(BF)

        @pl.loop(1, nz)
        def _(d):
            z_last(2 * k, d).start()

        y_second(k).wait()

        @pl.loop(0, nz)
        def _(b):
            s2[2 * k + 1, b] = (s1b[k, y, b].astype(F32)
                                + r2[2 * k + 1, b].astype(F32)).astype(BF)

        @pl.loop(1, nz)
        def _(d):
            z_last(2 * k + 1, d).start()

    @pl.loop(0, units)
    def _(k):
        red[k] = s2[k, z].astype(F32)

        @pl.loop(1, nz)
        def _(d):
            z_last(k, d).wait()
            red[k] = red[k] + r3[k, d].astype(F32)

    @pl.loop(1, nz)
    def _(d):
        z_small(d).wait()

    small_out[...] = smz[0]

    @pl.loop(1, nz)
    def _(d):
        small_out[...] = small_out[...] + smz[d]

    keep_dec.wait()
    keep_enc.wait()
    for d in range(1, ns):
        enc_copy(d).wait()

    @pl.loop(1, count)
    def _(d):
        dec_copy(d).wait()


def exchange(np_, ns, u, small, dec, enc):
    units = u.shape[0]
    half = units // 2
    nz = np_ // 2
    rows, cols = u.shape[5:]
    count = np_ * ns
    dma = pltpu.SemaphoreType.DMA
    anywhere = pl.BlockSpec(memory_space=pl.ANY)
    vmem = pl.BlockSpec(memory_space=pltpu.VMEM)
    return pl.pallas_call(
        functools.partial(exchange_kernel, np_, ns),
        out_shape=(
            jax.ShapeDtypeStruct((units, rows, cols), F32),
            jax.ShapeDtypeStruct(small.shape, F32),
            jax.ShapeDtypeStruct(dec.shape, BF),
            jax.ShapeDtypeStruct(enc.shape, BF),
        ),
        in_specs=[anywhere, vmem, anywhere, anywhere],
        out_specs=(vmem, vmem, anywhere, anywhere),
        scratch_shapes=[
            pltpu.VMEM((units, 2, nz, 2, rows, cols), BF),
            pltpu.VMEM((units, 2, nz, 2, rows, cols), BF),
            pltpu.VMEM((half, nz, 2, rows, cols), BF),
            pltpu.VMEM((half, 2, nz, rows, cols), BF),
            pltpu.VMEM((half, nz, 2, rows, cols), BF),
            pltpu.VMEM((half, 2, nz, rows, cols), BF),
            pltpu.VMEM((units, nz, rows, cols), BF),
            pltpu.VMEM((units, nz, rows, cols), BF),
            pltpu.VMEM((units, nz, rows, cols), BF),
            pltpu.VMEM((3,) + small.shape, F32),
            pltpu.VMEM((3,) + small.shape, F32),
            pltpu.VMEM((nz,) + small.shape, F32),
            dma((units + 2,)),
            dma((units,)), dma((units,)), dma((units,)), dma((units,)),
            dma((units,)), dma((units,)), dma((units, nz)), dma((units, nz)),
            dma((3,)), dma((3,)), dma((nz,)), dma((nz,)),
            dma((count,)), dma((count,)), dma((ns,)), dma((ns,)),
        ],
        compiler_params=pltpu.CompilerParams(
            collective_id=0, has_side_effects=True, vmem_limit_bytes=58 * 1024 * 1024),
        name="exchange",
    )(u, small, dec, enc)


def per_device(
    enc_input, dec_input, lengths, attend_gain, query_weight, key_weight, value_weight,
    output_weight, bias_table, expand_gain, expand_weight, reduce_weight, final_gain,
    self_gain, self_value, self_output, cross_gain, cross_query, cross_key, cross_value,
    cross_output, feed_gain, feed_expand, feed_reduce, enc_cotangent, dec_cotangent,
):
    group, local_rows, width = enc_input.shape
    heads = bias_table.shape[1]
    size = width // heads
    ns = lax.axis_size("seq")
    np_ = lax.axis_size("pairs")
    place = lax.axis_index("seq")
    seq_len = local_rows * ns
    key_pos = jnp.arange(seq_len, dtype=jnp.int32)
    length = lax.dynamic_slice_in_dim(lengths, place, 1)[0]
    enc_work = lax.all_to_all(enc_input, "seq", split_axis=0, concat_axis=1, tiled=True)[0]
    cot_work = lax.all_to_all(enc_cotangent, "seq", split_axis=0, concat_axis=1, tiled=True)[0]
    visible = key_pos < length
    row_live = visible.astype(F32)[:, None]
    onehot = (
        rel_bucket(key_pos, key_pos)[:, :, None]
        == jnp.arange(bias_table.shape[0], dtype=jnp.int32)[None, None, :]
    ).astype(F32)
    position_bias = jnp.einsum("tub,bh->htu", onehot, bias_table, precision=HIGHEST)
    enc_value = enc_work.astype(F32)

    def heads_of(array):
        return array.reshape(seq_len, heads, size)

    normed = rms_norm(enc_value, attend_gain).astype(BF)
    query = mm(normed, query_weight).astype(BF)
    key = mm(normed, key_weight).astype(BF)
    value = mm(normed, value_weight).astype(BF)
    scores = jnp.einsum("thd,uhd->htu", heads_of(query), heads_of(key),
                        preferred_element_type=F32) + position_bias
    masked = jnp.where(visible, scores, -1e30)
    probs = jax.nn.softmax(masked, axis=-1)
    probs_low = probs.astype(BF)
    context = jnp.einsum("htu,uhd->thd", probs_low, heads_of(value),
                         preferred_element_type=F32).astype(BF).reshape(seq_len, width)
    hidden = enc_value + mm(context, output_weight)
    mixed = rms_norm(hidden, expand_gain).astype(BF)
    upper = mm(mixed, expand_weight)
    active = smooth(upper).astype(BF)
    enc_block = row_live * (hidden + mm(active, reduce_weight))
    enc_normed = rms_norm(enc_block, final_gain).astype(BF)

    dec_value = dec_input.astype(F32)
    self_normed = rms_norm(dec_value, self_gain).astype(BF)
    self_values = mm(self_normed, self_value).astype(BF)
    after = dec_value + mm(self_values, self_output)
    cross_normed = rms_norm(after, cross_gain).astype(BF)
    cross_q = mm(cross_normed, cross_query).astype(BF)
    own_head = (jnp.arange(width, dtype=jnp.int32)[None, :] // size
                == jnp.arange(heads, dtype=jnp.int32)[:, None])

    def spread(row):
        return jnp.where(own_head, row, jnp.zeros_like(row))

    def collect(rows):
        return jnp.sum(jnp.where(own_head, rows, 0.0), axis=0, keepdims=True)

    q_rows = mm_t(spread(cross_q), cross_key).astype(BF)
    cross_scores = jnp.where(visible[None, :], mm_t(q_rows, enc_normed), -1e30)
    cross_probs = jax.nn.softmax(cross_scores, axis=-1)
    cross_low = cross_probs.astype(BF)
    mean_rows = mm(cross_low, enc_normed).astype(BF)
    cross_context = collect(mm(mean_rows, cross_value)).astype(BF)
    middle = after + mm(cross_context, cross_output)
    feed_normed = rms_norm(middle, feed_gain).astype(BF)
    dec_upper = mm(feed_normed, feed_expand)
    dec_active = smooth(dec_upper).astype(BF)
    dec_block = middle + mm(dec_active, feed_reduce)
    dec_grad_out = dec_cotangent.astype(F32)
    dec_upper_grad = smooth_back(dec_upper, mm_t(dec_cotangent, feed_reduce)).astype(BF)
    middle_norm, grad_feed_gain = norm_back(middle, feed_gain, mm_t(dec_upper_grad, feed_expand))
    middle_grad = dec_grad_out + middle_norm
    cross_branch = middle_grad.astype(BF)
    context_grad = mm_t(cross_branch, cross_output).astype(BF)
    g_rows = mm_t(spread(context_grad), cross_value).astype(BF)
    cross_prob_grad = mm_t(g_rows, enc_normed)
    cross_score_grad = (
        cross_probs
        * (cross_prob_grad - jnp.sum(cross_probs * cross_prob_grad, axis=-1, keepdims=True))
    ).astype(BF)
    score_rows = mm(cross_score_grad, enc_normed).astype(BF)
    cross_q_grad = collect(mm(score_rows, cross_key)).astype(BF)
    rows_grad = t_mm(
        jnp.concatenate([cross_score_grad, cross_low], axis=0),
        jnp.concatenate([q_rows, g_rows], axis=0),
    ).astype(BF)
    after_norm, grad_cross_gain = norm_back(after, cross_gain, mm_t(cross_q_grad, cross_query))
    after_grad = middle_grad + after_norm
    self_branch = after_grad.astype(BF)
    self_values_grad = mm_t(self_branch, self_output).astype(BF)
    dec_norm, grad_self_gain = norm_back(dec_value, self_gain, mm_t(self_values_grad, self_value))
    dec_input_grad = (after_grad + dec_norm).astype(BF)

    block_norm, grad_final_gain = norm_back(enc_block, final_gain, rows_grad.astype(F32))
    block_grad = row_live * (cot_work.astype(F32) + block_norm)
    reduce_branch = block_grad.astype(BF)
    upper_grad = smooth_back(upper, mm_t(reduce_branch, reduce_weight)).astype(BF)
    hidden_norm, grad_expand_gain = norm_back(hidden, expand_gain, mm_t(upper_grad, expand_weight))
    hidden_grad = block_grad + hidden_norm
    attend_branch = hidden_grad.astype(BF)
    context_back = heads_of(mm_t(attend_branch, output_weight).astype(BF))
    prob_grad = jnp.einsum("thd,uhd->htu", context_back, heads_of(value),
                           preferred_element_type=F32)
    value_grad = jnp.einsum("htu,thd->uhd", probs_low, context_back,
                            preferred_element_type=F32).astype(BF).reshape(seq_len, width)
    score_grad = (probs * (prob_grad - jnp.sum(probs * prob_grad, axis=-1, keepdims=True))
                  ).astype(BF)
    grad_bias = jnp.einsum("htu,tub->bh", score_grad.astype(F32), onehot, precision=HIGHEST)
    query_grad = jnp.einsum("htu,uhd->thd", score_grad, heads_of(key),
                            preferred_element_type=F32).astype(BF).reshape(seq_len, width)
    key_grad = jnp.einsum("htu,thd->uhd", score_grad, heads_of(query),
                          preferred_element_type=F32).astype(BF).reshape(seq_len, width)
    normed_grad = (mm_t(query_grad, query_weight) + mm_t(key_grad, key_weight)
                   + mm_t(value_grad, value_weight))
    input_norm, grad_attend_gain = norm_back(enc_value, attend_gain, normed_grad)
    input_grad = (hidden_grad + input_norm).astype(BF)

    nz = np_ // 2
    r = width // np_
    rp = -(-r // 16) * 16
    cols = width // ns

    def pad(unit):
        return jnp.pad(unit, ((0, 0),) * 4 + ((0, rp - r), (0, 0)))

    def narrow_pair(first, second):
        both = jnp.stack([first, second]).astype(BF).reshape(2, nz, 2, r, 2, 2, cols)
        return pad(both.transpose(5, 4, 1, 2, 3, 0, 6).reshape(2, 2, nz, 2, r, 2 * cols))

    grad_expand = t_mm(mixed, upper_grad).astype(BF)
    grad_reduce = t_mm(active, reduce_branch).astype(BF)
    wide = grad_expand.reshape(nz, 2, r, 2, 2, 2, 2 * cols).transpose(5, 4, 3, 0, 1, 2, 6)
    tall = grad_reduce.reshape(nz, 2, 4, r, 2, 2, cols).transpose(2, 5, 4, 0, 1, 3, 6)
    units = jnp.stack([
        pad(wide[0]), pad(wide[1]),
        pad(jnp.concatenate([tall[0], tall[1]], axis=-1)),
        pad(jnp.concatenate([tall[2], tall[3]], axis=-1)),
        narrow_pair(t_mm(normed, query_grad), t_mm(normed, key_grad)),
        narrow_pair(t_mm(normed, value_grad), t_mm(context, attend_branch)),
    ])
    small = jnp.concatenate([
        grad_attend_gain, grad_expand_gain, grad_final_gain, grad_self_gain, grad_cross_gain,
        grad_feed_gain, grad_bias.reshape(-1)])
    small_rows = -(-small.size // 1024) * 8
    small = jnp.pad(small, (0, small_rows * 128 - small.size)).reshape(small_rows, 128)

    left = jnp.concatenate([
        jnp.concatenate([self_normed, self_values, cross_normed, cross_context, feed_normed])
        .reshape(5, np_, r).transpose(1, 0, 2).reshape(np_, 5 * r),
        dec_active.reshape(np_, 4 * r)], axis=1)
    mid = jnp.stack([score_rows, mean_rows]).reshape(2, ns, heads // ns, np_, r)
    mid = mid.transpose(3, 1, 0, 2, 4).reshape(np_, ns, 6 * r)
    right = jnp.concatenate([
        jnp.concatenate([self_values_grad, self_branch, cross_q_grad, cross_branch,
                         cross_q, context_grad, dec_cotangent])
        .reshape(7, ns, cols).transpose(1, 0, 2).reshape(ns, 7 * cols),
        dec_upper_grad.reshape(ns, 4 * cols)], axis=1)
    dec_all = jnp.concatenate([
        jnp.broadcast_to(left[:, None], (np_, ns, 9 * r)), mid,
        jnp.broadcast_to(right[None], (np_, ns, 11 * cols))], axis=-1)
    dec_all = dec_all.reshape(np_ * ns, -1)
    used = dec_all.shape[1]
    dec_rows = -(-used // 2048) * 16
    dec_all = jnp.pad(dec_all, ((0, 0), (0, dec_rows * 128 - used)))
    dec_all = dec_all.reshape(np_ * ns, dec_rows, 128)
    both = jnp.stack([enc_block.astype(BF), input_grad]).reshape(2, ns, local_rows, width)

    red, small_sum, dec_got, both_out = exchange(np_, ns, units, small, dec_all, both)

    got = dec_got.reshape(np_ * ns, -1)
    lefts = got[:, :9 * r].reshape(-1, 9, r)
    mids = got[:, 9 * r:15 * r].reshape(-1, 6, r)
    rights = got[:, 15 * r:15 * r + 11 * cols].reshape(-1, 11, cols)
    plain = jnp.einsum("nkr,nkc->krc", lefts[:, :4], rights[:, :4], preferred_element_type=F32)
    crossed = jnp.einsum("nkhr,nkhd->krhd", mids.reshape(-1, 2, 3, r),
                         rights[:, 4:6].reshape(-1, 2, 3, size),
                         preferred_element_type=F32).reshape(2, r, cols)
    feed_in = jnp.einsum("nr,nc->rc", lefts[:, 4], rights[:, 7:11].reshape(-1, 4 * cols),
                         preferred_element_type=F32)
    feed_out = jnp.einsum("nr,nc->rc", lefts[:, 5:9].reshape(-1, 4 * r), rights[:, 6],
                          preferred_element_type=F32)
    red = red[:, :r]
    small_flat = small_sum.reshape(-1)
    gains = [small_flat[i * width:(i + 1) * width] for i in range(6)]
    bias = small_flat[6 * width:6 * width + bias_table.size].reshape(bias_table.shape)
    grad_reduce_out = jnp.concatenate(
        [red[2][:, :cols], red[2][:, cols:], red[3][:, :cols], red[3][:, cols:]], axis=0)
    return (
        both_out[0], dec_block.astype(BF), both_out[1], dec_input_grad,
        gains[0],
        red[4][:, :cols], red[4][:, cols:], red[5][:, :cols], red[5][:, cols:],
        bias,
        gains[1],
        jnp.concatenate([red[0], red[1]], axis=1), grad_reduce_out,
        gains[2],
        gains[3], plain[0], plain[1],
        gains[4], plain[2], crossed[0], crossed[1], plain[3],
        gains[5], feed_in, feed_out,
    )


def solution(mesh):
    rows = P("pairs", "seq", None)
    single = P(("pairs", "seq"), None)
    block = P("pairs", "seq")
    return jax.shard_map(
        per_device,
        mesh=mesh,
        in_specs=(rows, single, P("pairs")) + (P(),) * 21 + (rows, single),
        out_specs=(
            rows, single, rows, single,
            P(), block, block, block, block, P(), P(), block, block, P(),
            P(), block, block, P(), block, block, block, block, P(), block, block,
        ),
        check_vma=False,
    )
```

```python
import functools

import jax
import jax.numpy as jnp
from jax import lax
from jax.experimental import pallas as pl
from jax.experimental.pallas import tpu as pltpu
from jax.sharding import PartitionSpec as P

EPSILON = 1e-06
EDGES = (12, 16, 23, 32, 46, 64, 91)
HIGHEST = lax.Precision.HIGHEST
MESH = pl.DeviceIdType.MESH
BF = jnp.bfloat16
F32 = jnp.float32


def rel_bucket(query_pos, key_pos):
    offset = key_pos[None, :] - query_pos[:, None]
    distance = jnp.abs(offset)
    far_bucket = jnp.full_like(distance, 8)
    for threshold in EDGES:
        far_bucket = far_bucket + (distance >= threshold).astype(jnp.int32)
    bucket_id = jnp.where(distance < 8, distance, far_bucket)
    return bucket_id + 16 * (offset > 0).astype(jnp.int32)


def mm(a, b):
    return jnp.dot(a, b, preferred_element_type=F32)
def mm_t(a, b):
    return lax.dot_general(a, b, (((1,), (1,)), ((), ())), preferred_element_type=F32)
def t_mm(a, b):
    return lax.dot_general(a, b, (((0,), (0,)), ((), ())), preferred_element_type=F32)

def rms_scale(v):
    return lax.rsqrt(jnp.mean(v * v, axis=-1, keepdims=True) + EPSILON)

def encode_kernel(length, x, ag, eg, fg, band, far, wq, wk, wv, wo, we, wr,
                  normed, q, k, v, probs, context_t, hidden, mixed, active, slope, block, rows, low,
                  wqs, wks, wvs, wos, wes, wrs, v_t, s_t, ctx, sems, psem, pbuf):
    n, width = x.shape
    heads = far.shape[0]
    ff = wes.shape[1]
    copies = [pltpu.make_async_copy(a, b, sems.at[i])
              for i, (a, b) in enumerate(((wq, wqs), (wk, wks), (wv, wvs), (wo, wos), (we, wes), (wr, wrs)))]
    for c in copies:
        c.start()

    @pl.loop(0, n // 128)
    def _(i):
        r = pl.ds(i * 128, 128)
        t = x[r].astype(F32)
        normed[r] = (t * rms_scale(t) * ag[...]).astype(BF)

    for w, out, c in ((wqs, q, copies[0]), (wks, k, copies[1]), (wvs, v, copies[2])):
        c.wait()

        @pl.loop(0, width // 256)
        def _(j):
            cols = pl.ds(j * 256, 256)
            out[:, cols] = mm(normed[...], w[:, cols]).astype(BF)

    lane = lax.broadcasted_iota(jnp.int32, (n, 128), 1)
    row = lax.broadcasted_iota(jnp.int32, (n, 128), 0)
    q_mark = jnp.where(lane == 0, 1.0, 0.0).astype(BF)
    k_mark = jnp.where((lane == 0) & (row >= length[0]), -1e30, 0.0).astype(BF)

    @pl.loop(0, heads // 2)
    def _(g):
        cols = pl.ds(g * 128, 128)
        v_t[...] = v[:, cols].T
        qq = jnp.concatenate([q[:, cols], q_mark], axis=1)
        kp = k[:, cols]
        for a in range(2):
            h = 2 * g + a
            mine = (lane < 64) if a == 0 else (lane >= 64)
            kk = jnp.concatenate([jnp.where(mine, kp, jnp.zeros_like(kp)), k_mark], axis=1)
            s_t[...] = mm_t(kk, qq)
            for j in range(n // 128):
                tile = []
                for i in range(n // 128):
                    s = s_t[i * 128:(i + 1) * 128, j * 128:(j + 1) * 128]
                    if abs(i - j) <= 1:
                        s = s + band[h, (i - j + 1) * 128:(i - j + 2) * 128, :]
                    elif i > j:
                        s = s + far[h, 1]
                    else:
                        s = s + far[h, 0]
                    tile.append(s)
                s = jnp.concatenate(tile, axis=0)
                m = jnp.max(s, axis=0, keepdims=True)
                e = jnp.exp(s - m)
                total = jnp.sum(e, axis=0, keepdims=True)
                pbuf[a, :, j * 128:(j + 1) * 128] = (e * (1.0 / total)).astype(BF)
            ctx[pl.ds(pl.multiple_of(h * 64, 64), 64), :] = mm(v_t[a * 64:(a + 1) * 64, :], pbuf[a]).astype(BF)
            cp = pltpu.make_async_copy(pbuf.at[a], probs.at[h], psem.at[a])
            cp.start()
        for a in range(2):
            pltpu.make_async_copy(pbuf.at[a], probs.at[2 * g + a], psem.at[a]).wait()

    context_t[...] = ctx[...]
    copies[3].wait()

    @pl.loop(0, n // 128)
    def _(i):
        r = pl.ds(i * 128, 128)
        hid = x[r].astype(F32) + t_mm(ctx[:, r], wos[...])
        hidden[r] = hid
        mixed[r] = (hid * rms_scale(hid) * eg[...]).astype(BF)

    copies[4].wait()

    @pl.loop(0, ff // 256)
    def _(j):
        cols = pl.ds(j * 256, 256)
        u = mm(mixed[...], wes[:, cols])
        u2 = u * u
        t = jnp.tanh(u * (0.7978845608 + (0.7978845608 * 0.044715) * u2))
        half = 0.5 + 0.5 * t
        active[:, cols] = (u * half).astype(BF)
        slope[:, cols] = (half + half * (1.0 - t) * u * (0.7978845608 + (3 * 0.7978845608 * 0.044715) * u2)).astype(BF)

    copies[5].wait()

    @pl.loop(0, width // 256)
    def _(j):
        cols = pl.ds(j * 256, 256)
        block[:, cols] = mm(active[...], wrs[:, cols])

    @pl.loop(0, n // 128)
    def _(i):
        r = pl.ds(i * 128, 128)
        alive = (lax.broadcasted_iota(jnp.int32, (128, 1), 0) + i * 128 < length[0]).astype(F32)
        b = alive * (hidden[r] + block[r])
        block[r] = b
        low[r] = b.astype(BF)
        rows[r] = (b * rms_scale(b) * fg[...]).astype(BF)


def encode(length, x, ag, eg, fg, band, far, wq, wk, wv, wo, we, wr):
    n, width = x.shape
    ff = we.shape[1]
    heads = far.shape[0]
    sm = pl.BlockSpec(memory_space=pltpu.SMEM)
    vm = pl.BlockSpec(memory_space=pltpu.VMEM)
    hb = pl.BlockSpec(memory_space=pl.ANY)
    S = jax.ShapeDtypeStruct
    full = S((n, width), BF)
    return pl.pallas_call(
        encode_kernel,
        out_shape=(full, full, full, full, S((heads, n, n), BF), S((width, n), BF), S((n, width), F32), full,
                   S((n, ff), BF), S((n, ff), BF), S((n, width), F32), full, full),
        in_specs=[sm, vm, vm, vm, vm, vm, sm] + [hb] * 6,
        out_specs=(vm,) * 4 + (hb,) + (vm,) * 8,
        scratch_shapes=[pltpu.VMEM(w.shape, BF) for w in (wq, wk, wv, wo, we, wr)] + [
            pltpu.VMEM((128, n), BF), pltpu.VMEM((n, n), F32), pltpu.VMEM((width, n), BF),
            pltpu.SemaphoreType.DMA((6,)), pltpu.SemaphoreType.DMA((2,)), pltpu.VMEM((2, n, n), BF)],
        compiler_params=pltpu.CompilerParams(vmem_limit_bytes=60 * 1024 * 1024),
        name="encode",
    )(length, x, ag.reshape(1, -1), eg.reshape(1, -1), fg.reshape(1, -1), band, far, wq, wk, wv, wo, we, wr)


def gelu_parts(u):
    u2 = u * u
    t = jnp.tanh(u * (0.7978845608 + (0.7978845608 * 0.044715) * u2))
    half = 0.5 + 0.5 * t
    return u * half, half + half * (1.0 - t) * u * (0.7978845608 + (3 * 0.7978845608 * 0.044715) * u2)

def norm_down(v, r, g, dy):
    vr = v * r
    gd = g * dy
    return r * (gd - vr * jnp.mean(vr * gd, axis=-1, keepdims=True)), vr * dy

def decode_kernel(length, rows, dec_in, dec_cot, sg, cg, fg, *rest):
    hbm = rest[:8]
    (out, in_grad, gains, left, right, wide, mids, rows_grad) = rest[8:16]
    bufs = rest[16:24]
    sems = rest[24]
    sv, so, cq, ck, cv, co, fe, fr = bufs
    copies = [pltpu.make_async_copy(a, b, sems.at[i]) for i, (a, b) in enumerate(zip(hbm, bufs))]
    for c in copies:
        c.start()
    n, width = rows.shape
    heads = mids.shape[1]
    size = width // heads
    x = dec_in[...].astype(F32)
    cot = dec_cot[...]
    own = (lax.broadcasted_iota(jnp.int32, (heads, width), 1) // size
           == lax.broadcasted_iota(jnp.int32, (heads, width), 0))

    def spread(r):
        return jnp.where(own, r.astype(F32), 0.0).astype(BF)

    def collect(r):
        return jnp.sum(jnp.where(own, r, 0.0), axis=0, keepdims=True)

    x_r = rms_scale(x)
    self_normed = (x * x_r * sg[...]).astype(BF)
    copies[0].wait()
    self_values = mm(self_normed, sv[...]).astype(BF)
    copies[1].wait()
    after = x + mm(self_values, so[...])
    after_r = rms_scale(after)
    cross_normed = (after * after_r * cg[...]).astype(BF)
    copies[2].wait()
    cross_q = mm(cross_normed, cq[...]).astype(BF)
    copies[3].wait()
    q_rows = mm_t(spread(cross_q), ck[...]).astype(BF)
    s = mm_t(q_rows, rows[...])
    s = jnp.where(lax.broadcasted_iota(jnp.int32, s.shape, 1) < length[0], s, -1e30)
    e = jnp.exp(s - jnp.max(s, axis=-1, keepdims=True))
    probs = e / jnp.sum(e, axis=-1, keepdims=True)
    low = probs.astype(BF)
    mean_rows = mm(low, rows[...]).astype(BF)
    copies[4].wait()
    cross_context = collect(mm(mean_rows, cv[...])).astype(BF)
    copies[5].wait()
    middle = after + mm(cross_context, co[...])
    middle_r = rms_scale(middle)
    feed_normed = (middle * middle_r * fg[...]).astype(BF)
    copies[6].wait()
    active, slope = gelu_parts(mm(feed_normed, fe[...]))
    active = active.astype(BF)
    copies[7].wait()
    out[...] = (middle + mm(active, fr[...])).astype(BF)
    upper_grad = (slope * mm_t(cot, fr[...])).astype(BF)
    middle_down, feed_gain = norm_down(middle, middle_r, fg[...], mm_t(upper_grad, fe[...]))
    middle_grad = cot.astype(F32) + middle_down
    cross_branch = middle_grad.astype(BF)
    context_grad = mm_t(cross_branch, co[...]).astype(BF)
    g_rows = mm_t(spread(context_grad), cv[...]).astype(BF)
    prob_grad = mm_t(g_rows, rows[...])
    score_grad = (probs * (prob_grad - jnp.sum(probs * prob_grad, axis=-1, keepdims=True))).astype(BF)
    score_rows = mm(score_grad, rows[...]).astype(BF)
    pad = jnp.zeros((16 - heads % 16, n), BF)
    padw = jnp.zeros((16 - heads % 16, width), BF)
    rows_grad[...] = t_mm(jnp.concatenate([score_grad, pad, low, pad], axis=0),
                          jnp.concatenate([q_rows, padw, g_rows, padw], axis=0)).astype(BF)
    cross_q_grad = collect(mm(score_rows, ck[...])).astype(BF)
    after_down, cross_gain = norm_down(after, after_r, cg[...], mm_t(cross_q_grad, cq[...]))
    after_grad = middle_grad + after_down
    self_branch = after_grad.astype(BF)
    self_values_grad = mm_t(self_branch, so[...]).astype(BF)
    x_down, self_gain = norm_down(x, x_r, sg[...], mm_t(self_values_grad, sv[...]))
    in_grad[...] = (after_grad + x_down).astype(BF)
    gains[0:1, :] = self_gain
    gains[1:2, :] = cross_gain
    gains[2:3, :] = feed_gain
    for i, r in enumerate((self_normed, self_values, cross_normed, cross_context, feed_normed)):
        left[i:i + 1, :] = r.astype(F32)
    for i, r in enumerate((self_values_grad, self_branch, cross_q_grad, cross_branch, cross_q, context_grad, cot)):
        right[i:i + 1, :] = r.astype(F32)
    wide[0:1, :] = active.astype(F32)
    wide[1:2, :] = upper_grad.astype(F32)
    mids[0] = score_rows.astype(F32)
    mids[1] = mean_rows.astype(F32)

def decode(length, rows, dec_in, dec_cot, sg, cg, fg, heads, *weights):
    n, width = rows.shape
    ff = weights[6].shape[1]
    sm = pl.BlockSpec(memory_space=pltpu.SMEM)
    vm = pl.BlockSpec(memory_space=pltpu.VMEM)
    hb = pl.BlockSpec(memory_space=pl.ANY)
    S = jax.ShapeDtypeStruct
    return pl.pallas_call(
        decode_kernel,
        out_shape=(S((1, width), BF), S((1, width), BF), S((3, width), F32), S((5, width), F32), S((7, width), F32),
                   S((2, ff), F32), S((2, heads, width), F32), S((n, width), BF)),
        in_specs=[sm] + [vm] * 6 + [hb] * 8,
        out_specs=(vm,) * 8,
        scratch_shapes=[pltpu.VMEM(w.shape, BF) for w in weights] + [pltpu.SemaphoreType.DMA((8,))],
        compiler_params=pltpu.CompilerParams(vmem_limit_bytes=60 * 1024 * 1024),
        name="decode",
    )(length, rows, dec_in, dec_cot, sg.reshape(1, -1), cg.reshape(1, -1), fg.reshape(1, -1), *weights)


def feed_back_kernel(length, rows_grad, block, cot, fg, hidden, eg, mixed, active, slope, wr, we,
                     wide, tall, hidden_grad, branch, gains, wrs, wes, bg, rb, rb_t, ug, mixed_t, dmixed, sems):
    n, width = block.shape
    ff = active.shape[1]
    groups, lanes = tall.shape[3], tall.shape[5]
    cols_dev = width // 4
    copies = [pltpu.make_async_copy(a, b, sems.at[i]) for i, (a, b) in enumerate(((wr, wrs), (we, wes)))]
    for c in copies:
        c.start()
    gains[...] = jnp.zeros_like(gains)

    @pl.loop(0, n // 128)
    def _(i):
        r = pl.ds(i * 128, 128)
        alive = (lax.broadcasted_iota(jnp.int32, (128, 1), 0) + i * 128 < length[0]).astype(F32)
        v = block[r]
        down, gain = norm_down(v, rms_scale(v), fg[...], rows_grad[r].astype(F32))
        b = alive * (cot[r].astype(F32) + down)
        bg[r] = b
        rb[r] = b.astype(BF)
        rb_t[:, pl.ds(pl.multiple_of(i * 128, 128), 128)] = b.T.astype(BF)
        mixed_t[:, pl.ds(pl.multiple_of(i * 128, 128), 128)] = mixed[r].T
        gains[0:1, :] += jnp.sum(gain, axis=0, keepdims=True)

    copies[0].wait()

    @pl.loop(0, ff // 256)
    def _(j):
        cols = pl.ds(pl.multiple_of(j * 256, 256), 256)
        ug[:, cols] = (slope[:, cols].astype(F32) * mm_t(rb[...], wrs[cols, :])).astype(BF)

    copies[1].wait()

    @pl.loop(0, width // 256)
    def _(j):
        cols = pl.ds(pl.multiple_of(j * 256, 256), 256)
        dmixed[:, cols] = mm_t(ug[...], wes[cols, :])

    @pl.loop(0, n // 128)
    def _(i):
        r = pl.ds(i * 128, 128)
        v = hidden[r]
        down, gain = norm_down(v, rms_scale(v), eg[...], dmixed[r])
        h = bg[r] + down
        hidden_grad[r] = h
        branch[r] = h.astype(BF)
        gains[1:2, :] += jnp.sum(gain, axis=0, keepdims=True)

    @pl.loop(0, 4)
    def _(j):
        for half in range(2):
            cols = pl.ds(pl.multiple_of(j * (ff // 4) + half * (ff // 8), 128), ff // 8)
            wide[half, lax.rem(j, 2), j // 2] = mm(mixed_t[...], ug[:, cols]).astype(BF)

    chunk = ff // 8
    per_group = lanes // chunk

    @pl.loop(0, 8)
    def _(i):
        cols = pl.ds(pl.multiple_of(i * chunk, 128), chunk)
        g = mm(rb_t[...], active[:, cols]).astype(BF)
        for j in range(4):
            for half in range(2):
                r = j * cols_dev + half * (cols_dev // 2)
                part = g[r:r + cols_dev // 2]
                if per_group == 1:
                    tall[half, j % 2, j // 2, i] = part
                else:
                    tall[half, j % 2, j // 2, 0, :, cols] = part


def feed_back(groups, length, rows_grad, block, cot, fg, hidden, eg, mixed, active, slope, wr, we):
    n, width = block.shape
    ff = active.shape[1]
    sm = pl.BlockSpec(memory_space=pltpu.SMEM)
    vm = pl.BlockSpec(memory_space=pltpu.VMEM)
    hb = pl.BlockSpec(memory_space=pl.ANY)
    S = jax.ShapeDtypeStruct
    V = pltpu.VMEM
    return pl.pallas_call(
        feed_back_kernel,
        out_shape=(S((2, 2, 2, width, ff // 8), BF),
                   S((2, 2, 2, groups, width // 8, ff // groups), BF), S((n, width), F32), S((n, width), BF), S((2, width), F32)),
        in_specs=[sm] + [vm] * 9 + [hb] * 2,
        out_specs=(vm,) * 5,
        scratch_shapes=[V(wr.shape, BF), V(we.shape, BF), V((n, width), F32), V((n, width), BF), V((width, n), BF),
                        V((n, ff), BF), V((width, n), BF), V((n, width), F32), pltpu.SemaphoreType.DMA((2,))],
        compiler_params=pltpu.CompilerParams(vmem_limit_bytes=60 * 1024 * 1024),
        name="feed_back",
    )(length, rows_grad, block, cot, fg.reshape(1, -1), hidden, eg.reshape(1, -1), mixed, active, slope, wr, we)


def attend_back_kernel(x, ag, q, k, v, probs, context_t, branch, hidden_grad, normed, wq, wk, wv, wo,
                       units, in_grad, gain_out, band, far,
                       wqs, wks, wvs, wos, d_out, dp, ds, dq_t, dq, dk, dv, k_t, normed_t, ng, pbuf, psem, sems):
    n, width = x.shape
    heads = probs.shape[0]
    copies = [pltpu.make_async_copy(a, b, sems.at[i])
              for i, (a, b) in enumerate(((wo, wos), (wq, wqs), (wk, wks), (wv, wvs)))]
    for c in copies:
        c.start()

    def fetch(h, slot):
        return pltpu.make_async_copy(probs.at[h], pbuf.at[slot], psem.at[slot])

    fetch(0, 0).start()
    fetch(1, 1).start()
    far[...] = jnp.zeros_like(far)
    copies[0].wait()

    @pl.loop(0, width // 256)
    def _(j):
        cols = pl.ds(pl.multiple_of(j * 256, 256), 256)
        d_out[:, cols] = mm_t(branch[...], wos[cols, :]).astype(BF)

    lane = lax.broadcasted_iota(jnp.int32, (n, 128), 1)

    @pl.loop(0, heads // 2)
    def _(g):
        cols = pl.ds(pl.multiple_of(g * 128, 128), 128)
        k_t[...] = k[:, cols].T
        dop = d_out[:, cols]
        qp = q[:, cols]
        vp = v[:, cols]
        zero = jnp.zeros_like(qp)
        dk_sum = None
        for a in range(2):
            h = 2 * g + a
            mine = (lane < 64) if a == 0 else (lane >= 64)
            dp[...] = mm_t(jnp.where(mine, vp, zero), dop)
            fetch(h, a).wait()
            for j in range(n // 128):
                p = pbuf[a, :, j * 128:(j + 1) * 128].astype(F32)
                pd = p * dp[:, j * 128:(j + 1) * 128]
                total = jnp.sum(pd, axis=0, keepdims=True)
                s = pd - p * total
                ds[:, j * 128:(j + 1) * 128] = s.astype(BF)
                for i in range(n // 128):
                    t = s[i * 128:(i + 1) * 128]
                    if abs(i - j) <= 1:
                        if j == 0 or (i == j + 1 and j == 0) or (j == 1 and i == 0):
                            band[h, (i - j + 1) * 128:(i - j + 2) * 128, :] = t
                        else:
                            band[h, (i - j + 1) * 128:(i - j + 2) * 128, :] += t
                    else:
                        w = 1 if i > j else 0
                        far[w, pl.ds(h, 1), :] += jnp.sum(t, axis=0, keepdims=True)
            dvp = mm(pbuf[a], jnp.where(mine, dop, zero))
            dkp = mm(ds[...], jnp.where(mine, qp, zero))
            dq_t[pl.ds(pl.multiple_of(h * 64, 64), 64), :] = mm(k_t[a * 64:(a + 1) * 64, :], ds[...]).astype(BF)
            if a == 0:
                dk_sum, dv_sum = dkp, dvp
            else:
                dk[:, cols] = (dk_sum + dkp).astype(BF)
                dv[:, cols] = (dv_sum + dvp).astype(BF)

            @pl.when(h + 2 < heads)
            def _():
                fetch(h + 2, a).start()

    @pl.loop(0, n // 128)
    def _(i):
        r = pl.ds(pl.multiple_of(i * 128, 128), 128)
        dq[r] = dq_t[:, r].T
        normed_t[:, r] = normed[r].T

    for c in copies[1:]:
        c.wait()

    @pl.loop(0, width // 256)
    def _(j):
        cols = pl.ds(pl.multiple_of(j * 256, 256), 256)
        ng[:, cols] = mm_t(dq[...], wqs[cols, :]) + mm_t(dk[...], wks[cols, :]) + mm_t(dv[...], wvs[cols, :])

    gain_out[...] = jnp.zeros_like(gain_out)

    @pl.loop(0, n // 128)
    def _(i):
        r = pl.ds(i * 128, 128)
        t = x[r].astype(F32)
        down, gain = norm_down(t, rms_scale(t), ag[...], ng[r])
        in_grad[r] = (hidden_grad[r] + down).astype(BF)
        gain_out[...] += jnp.sum(gain, axis=0, keepdims=True)

    part = width // 4
    zero = jnp.zeros((n, part), BF)
    for j in range(4):
        c = slice(j * part, (j + 1) * part)
        g = mm(normed_t[...], jnp.concatenate([dq[:, c], dk[:, c]], axis=1))
        units[0, j % 2, j // 2] = g.astype(BF)
        g = (mm(normed_t[...], jnp.concatenate([dv[:, c], zero], axis=1))
             + mm(context_t[...], jnp.concatenate([zero, branch[:, c]], axis=1)))
        units[1, j % 2, j // 2] = g.astype(BF)


def attend_back(x, ag, q, k, v, probs, context_t, branch, hidden_grad, normed, wq, wk, wv, wo):
    n, width = x.shape
    heads = probs.shape[0]
    vm = pl.BlockSpec(memory_space=pltpu.VMEM)
    hb = pl.BlockSpec(memory_space=pl.ANY)
    S = jax.ShapeDtypeStruct
    V = pltpu.VMEM
    nar = V((n, width), BF)
    return pl.pallas_call(
        attend_back_kernel,
        out_shape=(S((2, 2, 2, width, width // 2), BF), S((n, width), BF), S((1, width), F32),
                   S((heads, 384, 128), F32), S((2, heads, 128), F32)),
        in_specs=[vm] * 5 + [hb] + [vm] * 4 + [hb] * 4,
        out_specs=(vm,) * 5,
        scratch_shapes=[V(w.shape, BF) for w in (wq, wk, wv, wo)] + [
            nar, V((n, n), F32), V((n, n), BF), V((width, n), BF), nar, nar, nar, V((128, n), BF),
            V((width, n), BF), V((n, width), F32), V((2, n, n), BF), pltpu.SemaphoreType.DMA((2,)), pltpu.SemaphoreType.DMA((4,))],
        compiler_params=pltpu.CompilerParams(vmem_limit_bytes=60 * 1024 * 1024),
        name="attend_back",
    )(x, ag.reshape(1, -1), q, k, v, probs, context_t, branch, hidden_grad, normed, wq, wk, wv, wo)


def exchange_kernel(np_, ns, wide, tall, attn, small, dec, enc, red, small_out, dec_out, enc_out,
                    own, r0, r1a, r1b, s1a, s1b, r2, s2, r3, sm, smr, smz,
                    loc, s0s, s0r, s1s, s1r, s2s, s2r, s3s, s3r,
                    ms, mr, mzs, mzr, ds, dr, es, er):
    units = 6
    nz = np_ // 2
    p = lax.axis_index("pairs")
    s = lax.axis_index("seq")
    c = lax.rem(s, 2)
    y = s // 2
    x = lax.rem(p, 2)
    z = p // 2
    me = p * ns + s
    count = np_ * ns
    core_peer = (p, s + 1 - 2 * c)
    y_peer = (p, lax.rem(s + 2, 4))
    x_peer = (p + 1 - 2 * x, s)

    def place(d):
        lin = lax.rem(me + d, count)
        return (lin // ns, lax.rem(lin, ns))

    barrier = pltpu.get_barrier_semaphore()

    @pl.loop(1, count)
    def _(d):
        pl.semaphore_signal(barrier, inc=1, device_id=place(d), device_id_type=MESH)

    pl.semaphore_wait(barrier, count - 1)

    def remote(src, dst, send, recv, peer):
        return pltpu.make_async_remote_copy(
            src_ref=src, dst_ref=dst, send_sem=send, recv_sem=recv,
            device_id=peer, device_id_type=MESH)

    def unit(k, core):
        return (wide, tall, attn)[k // 2].at[k % 2, core]

    def core_copy(k):
        return remote(unit(k, 1 - c), r0.at[k], s0s.at[k], s0r.at[k], core_peer)

    def own_copy(k):
        return pltpu.make_async_copy(unit(k, c), own.at[k], loc.at[k])

    for k in range(units):
        core_copy(k).start()
        own_copy(k).start()

    def dec_copy(d):
        q = place(d)
        return remote(dec.at[q[0] * ns + q[1]], dec_out.at[me], ds.at[d], dr.at[d], q)

    keep_dec = pltpu.make_async_copy(dec.at[me], dec_out.at[me], loc.at[units])
    keep_dec.start()

    @pl.loop(1, count)
    def _(d):
        dec_copy(d).start()

    def enc_copy(d):
        t = lax.rem(s + d, ns)
        return remote(enc.at[:, t], enc_out.at[:, s], es.at[d], er.at[d], (p, t))

    keep_enc = pltpu.make_async_copy(enc.at[:, s], enc_out.at[:, s], loc.at[units + 1])
    keep_enc.start()
    for d in range(1, ns):
        enc_copy(d).start()

    sm[0] = small[...]
    for i, peer in enumerate((core_peer, y_peer, x_peer)):
        copy = remote(sm.at[i], smr.at[i], ms.at[i], mr.at[i], peer)
        copy.start()
        copy.wait()
        if i < 2:
            sm[i + 1] = sm[i] + smr[i]
        else:
            smz[z] = sm[i] + smr[i]

    def z_small(d):
        return remote(smz.at[z], smz.at[z], mzs.at[d], mzr.at[d],
                      (lax.rem(z + d, nz) * 2 + x, s))

    @pl.loop(1, nz)
    def _(d):
        z_small(d).start()

    def y_first(k):
        return remote(own.at[2 * k, 1 - y], r1a.at[k], s1s.at[2 * k], s1r.at[2 * k], y_peer)

    def x_first(k):
        return remote(own.at[2 * k + 1, :, :, 1 - x], r1b.at[k], s1s.at[2 * k + 1],
                      s1r.at[2 * k + 1], x_peer)

    def x_second(k):
        return remote(s1a.at[k, :, 1 - x], r2.at[2 * k], s2s.at[2 * k], s2r.at[2 * k], x_peer)

    def y_second(k):
        return remote(s1b.at[k, 1 - y], r2.at[2 * k + 1], s2s.at[2 * k + 1],
                      s2r.at[2 * k + 1], y_peer)

    def z_last(k, d):
        t = lax.rem(z + d, nz)
        return remote(s2.at[k, t], r3.at[k, d], s3s.at[k, d], s3r.at[k, d], (t * 2 + x, s))

    def stage0(k):
        core_copy(k).wait()
        own_copy(k).wait()

        @pl.loop(0, 2)
        def _(a):
            @pl.loop(0, nz)
            def _(b):
                for e in range(2):
                    own[k, a, b, e] = (own[k, a, b, e].astype(F32)
                                       + r0[k, a, b, e].astype(F32)).astype(BF)

    for k in range(units // 2):
        stage0(2 * k)
        y_first(k).start()
        stage0(2 * k + 1)
        x_first(k).start()

    @pl.loop(0, units // 2)
    def _(k):
        y_first(k).wait()

        @pl.loop(0, nz)
        def _(b):
            for e in range(2):
                s1a[k, b, e] = (own[2 * k, y, b, e].astype(F32)
                                + r1a[k, b, e].astype(F32)).astype(BF)

        x_second(k).start()
        x_first(k).wait()

        @pl.loop(0, nz)
        def _(b):
            for e in range(2):
                s1b[k, e, b] = (own[2 * k + 1, e, b, x].astype(F32)
                                + r1b[k, e, b].astype(F32)).astype(BF)

        y_second(k).start()

    @pl.loop(0, units // 2)
    def _(k):
        x_second(k).wait()

        @pl.loop(0, nz)
        def _(b):
            s2[2 * k, b] = (s1a[k, b, x].astype(F32) + r2[2 * k, b].astype(F32)).astype(BF)

        @pl.loop(1, nz)
        def _(d):
            z_last(2 * k, d).start()

        y_second(k).wait()

        @pl.loop(0, nz)
        def _(b):
            s2[2 * k + 1, b] = (s1b[k, y, b].astype(F32)
                                + r2[2 * k + 1, b].astype(F32)).astype(BF)

        @pl.loop(1, nz)
        def _(d):
            z_last(2 * k + 1, d).start()

    @pl.loop(0, units)
    def _(k):
        red[k] = s2[k, z].astype(F32)

        @pl.loop(1, nz)
        def _(d):
            z_last(k, d).wait()
            red[k] = red[k] + r3[k, d].astype(F32)

    @pl.loop(1, nz)
    def _(d):
        z_small(d).wait()

    small_out[...] = smz[0]

    @pl.loop(1, nz)
    def _(d):
        small_out[...] = small_out[...] + smz[d]

    keep_dec.wait()
    keep_enc.wait()
    for d in range(1, ns):
        enc_copy(d).wait()

    @pl.loop(1, count)
    def _(d):
        dec_copy(d).wait()


def exchange(np_, ns, wide, tall, attn, small, dec, enc):
    units = 6
    half = units // 2
    nz = np_ // 2
    rows, cols = wide.shape[5:]
    count = np_ * ns
    dma = pltpu.SemaphoreType.DMA
    anywhere = pl.BlockSpec(memory_space=pl.ANY)
    vmem = pl.BlockSpec(memory_space=pltpu.VMEM)
    return pl.pallas_call(
        functools.partial(exchange_kernel, np_, ns),
        out_shape=(
            jax.ShapeDtypeStruct((units, rows, cols), F32),
            jax.ShapeDtypeStruct(small.shape, F32),
            jax.ShapeDtypeStruct(dec.shape, BF),
            jax.ShapeDtypeStruct(enc.shape, BF),
        ),
        in_specs=[anywhere, anywhere, anywhere, vmem, anywhere, anywhere],
        out_specs=(vmem, vmem, anywhere, anywhere),
        scratch_shapes=[
            pltpu.VMEM((units, 2, nz, 2, rows, cols), BF),
            pltpu.VMEM((units, 2, nz, 2, rows, cols), BF),
            pltpu.VMEM((half, nz, 2, rows, cols), BF),
            pltpu.VMEM((half, 2, nz, rows, cols), BF),
            pltpu.VMEM((half, nz, 2, rows, cols), BF),
            pltpu.VMEM((half, 2, nz, rows, cols), BF),
            pltpu.VMEM((units, nz, rows, cols), BF),
            pltpu.VMEM((units, nz, rows, cols), BF),
            pltpu.VMEM((units, nz, rows, cols), BF),
            pltpu.VMEM((3,) + small.shape, F32),
            pltpu.VMEM((3,) + small.shape, F32),
            pltpu.VMEM((nz,) + small.shape, F32),
            dma((units + 2,)),
            dma((units,)), dma((units,)), dma((units,)), dma((units,)),
            dma((units,)), dma((units,)), dma((units, nz)), dma((units, nz)),
            dma((3,)), dma((3,)), dma((nz,)), dma((nz,)),
            dma((count,)), dma((count,)), dma((ns,)), dma((ns,)),
        ],
        compiler_params=pltpu.CompilerParams(
            collective_id=0, has_side_effects=True, vmem_limit_bytes=58 * 1024 * 1024),
        name="exchange",
    )(wide, tall, attn, small, dec, enc)


def per_device(
    enc_input, dec_input, lengths, attend_gain, query_weight, key_weight, value_weight,
    output_weight, bias_table, expand_gain, expand_weight, reduce_weight, final_gain,
    self_gain, self_value, self_output, cross_gain, cross_query, cross_key, cross_value,
    cross_output, feed_gain, feed_expand, feed_reduce, enc_cotangent, dec_cotangent,
):
    group, local_rows, width = enc_input.shape
    buckets, heads = bias_table.shape
    size = width // heads
    ff = expand_weight.shape[1]
    ns = lax.axis_size("seq")
    np_ = lax.axis_size("pairs")
    place = lax.axis_index("seq")
    seq_len = local_rows * ns
    length = lax.dynamic_slice_in_dim(lengths, place, 1)
    x = lax.all_to_all(enc_input, "seq", split_axis=0, concat_axis=1, tiled=True)[0]
    cot = lax.all_to_all(enc_cotangent, "seq", split_axis=0, concat_axis=1, tiled=True)[0]

    band_bucket = rel_bucket(jnp.arange(128), jnp.arange(384) - 128).T
    onehot = (jnp.arange(buckets, dtype=jnp.int32)[:, None, None] == band_bucket).astype(F32)
    band = jnp.einsum("but,bh->hut", onehot, bias_table, precision=HIGHEST)
    far = jnp.stack([bias_table[15], bias_table[31]], axis=1)

    (normed, query, key, value, probs, context_t, hidden, mixed, active, slope, block, enc_rows,
     encoded) = encode(length, x, attend_gain, expand_gain, final_gain, band, far, query_weight,
                       key_weight, value_weight, output_weight, expand_weight, reduce_weight)
    dec_block, dec_input_grad, dec_gains, left, right, wide_rows, mids, rows_grad = decode(
        length, enc_rows, dec_input, dec_cotangent, self_gain, cross_gain, feed_gain, heads,
        self_value, self_output, cross_query, cross_key, cross_value, cross_output, feed_expand,
        feed_reduce)
    nz = np_ // 2
    r = width // np_
    aligned = r % 16 == 0 and (ff // np_) % 128 == 0
    wide, tall, hidden_grad, branch, feed_gains = feed_back(
        np_ if aligned else 1, length, rows_grad, block, cot, final_gain, hidden, expand_gain,
        mixed, active, slope, reduce_weight, expand_weight)
    attn, input_grad, attend_gain_sum, band_grad, far_grad = attend_back(
        x, attend_gain, query, key, value, probs, context_t, branch, hidden_grad, normed,
        query_weight, key_weight, value_weight, output_weight)
    far_sum = jnp.sum(far_grad, axis=-1)
    grad_bias = jnp.einsum("but,hut->bh", onehot, band_grad, precision=HIGHEST)
    grad_bias = grad_bias.at[15].add(far_sum[0]).at[31].add(far_sum[1])

    rp = -(-r // 16) * 16
    lanes = ff // 8
    side = width // 8 // r

    def pad(unit):
        return jnp.pad(unit, ((0, 0),) * 5 + ((0, rp - r), (0, 0)))

    if aligned:
        tall = tall.reshape(2, 2, 2, nz, 2, r, lanes)
    else:
        tall = tall.reshape(2, 2, 2, r, side, nz, 2, ff // np_).transpose(0, 1, 2, 5, 6, 3, 4, 7)
        tall = pad(tall.reshape(2, 2, 2, nz, 2, r, lanes))
    wide = pad(wide.reshape(2, 2, 2, nz, 2, r, lanes))
    attn = pad(attn.reshape(2, 2, 2, nz, 2, r, lanes))
    cols = width // ns
    small = jnp.concatenate([
        dec_gains, feed_gains, attend_gain_sum,
        jnp.pad(grad_bias.reshape(1, -1), ((0, 1), (0, width - grad_bias.size)))])

    left_cut = jnp.concatenate([
        left.reshape(5, np_, r).transpose(1, 0, 2).reshape(np_, 5 * r),
        wide_rows[0].reshape(np_, 4 * r),
    ], axis=1)
    mid_cut = mids.reshape(2, ns, heads // ns, np_, r).transpose(3, 1, 0, 2, 4)
    mid_cut = mid_cut.reshape(np_, ns, 6 * r)
    right_cut = jnp.concatenate([
        right.reshape(7, ns, cols).transpose(1, 0, 2).reshape(ns, 7 * cols),
        wide_rows[1].reshape(ns, 4 * cols)], axis=1)
    dec_all = jnp.concatenate([
        jnp.broadcast_to(left_cut[:, None], (np_, ns, 9 * r)), mid_cut,
        jnp.broadcast_to(right_cut[None], (np_, ns, 11 * cols))], axis=-1)
    dec_all = dec_all.astype(BF).reshape(np_ * ns, -1)
    used = dec_all.shape[1]
    dec_rows = -(-used // 2048) * 16
    dec_all = jnp.pad(dec_all, ((0, 0), (0, dec_rows * 128 - used)))
    dec_all = dec_all.reshape(np_ * ns, dec_rows, 128)
    both = jnp.stack([encoded, input_grad]).reshape(2, ns, local_rows, width)

    red, small_sum, dec_got, both_out = exchange(np_, ns, wide, tall, attn, small, dec_all, both)

    got = dec_got.reshape(np_ * ns, -1)
    lefts = got[:, :9 * r].reshape(-1, 9, r)
    mid_got = got[:, 9 * r:15 * r].reshape(-1, 2, 3, r)
    rights = got[:, 15 * r:15 * r + 11 * cols].reshape(-1, 11, cols)
    plain = jnp.einsum("nkr,nkc->krc", lefts[:, :4], rights[:, :4], preferred_element_type=F32)
    crossed = jnp.einsum("nkhr,nkhd->krhd", mid_got, rights[:, 4:6].reshape(-1, 2, 3, size),
                         preferred_element_type=F32).reshape(2, r, cols)
    feed_in = jnp.einsum("nr,nc->rc", lefts[:, 4], rights[:, 7:11].reshape(-1, 4 * cols),
                         preferred_element_type=F32)
    feed_out = jnp.einsum("nr,nc->rc", lefts[:, 5:9].reshape(-1, 4 * r), rights[:, 6],
                          preferred_element_type=F32)
    red = red[:, :r]
    grad_reduce = red[2:4].reshape(2, r, side, ff // np_).reshape(cols, ff // np_).T
    bias = small_sum[6, :bias_table.size].reshape(bias_table.shape)
    return (
        both_out[0], dec_block, both_out[1], dec_input_grad,
        small_sum[5],
        red[4][:, :cols], red[4][:, cols:], red[5][:, :cols], red[5][:, cols:],
        bias,
        small_sum[4],
        jnp.concatenate([red[0], red[1]], axis=1), grad_reduce,
        small_sum[3],
        small_sum[0], plain[0], plain[1],
        small_sum[1], plain[2], crossed[0], crossed[1], plain[3],
        small_sum[2], feed_in, feed_out,
    )


def solution(mesh):
    rows = P("pairs", "seq", None)
    single = P(("pairs", "seq"), None)
    block = P("pairs", "seq")
    return jax.shard_map(
        per_device,
        mesh=mesh,
        in_specs=(rows, single, P("pairs")) + (P(),) * 21 + (rows, single),
        out_specs=(
            rows, single, rows, single,
            P(), block, block, block, block, P(), P(), block, block, P(),
            P(), block, block, P(), block, block, block, block, P(), block, block,
        ),
        check_vma=False,
    )
```

```python
import functools

import jax
import jax.numpy as jnp
from jax import lax
from jax.experimental import pallas as pl
from jax.experimental.pallas import tpu as pltpu
from jax.sharding import PartitionSpec as P

EPSILON = 1e-06
EDGES = (12, 16, 23, 32, 46, 64, 91)
HIGHEST = lax.Precision.HIGHEST
MESH = pl.DeviceIdType.MESH
BF = jnp.bfloat16
F32 = jnp.float32


def rel_bucket(query_pos, key_pos):
    offset = key_pos[None, :] - query_pos[:, None]
    distance = jnp.abs(offset)
    far_bucket = jnp.full_like(distance, 8)
    for threshold in EDGES:
        far_bucket = far_bucket + (distance >= threshold).astype(jnp.int32)
    bucket_id = jnp.where(distance < 8, distance, far_bucket)
    return bucket_id + 16 * (offset > 0).astype(jnp.int32)


def mm(a, b):
    return jnp.dot(a, b, preferred_element_type=F32)
def mm_t(a, b):
    return lax.dot_general(a, b, (((1,), (1,)), ((), ())), preferred_element_type=F32)
def t_mm(a, b):
    return lax.dot_general(a, b, (((0,), (0,)), ((), ())), preferred_element_type=F32)

def rms_scale(v):
    return lax.rsqrt(jnp.mean(v * v, axis=-1, keepdims=True) + EPSILON)

def encode_kernel(length, x, ag, eg, fg, band, far, wq, wk, wv, wo, we, wr,
                  normed, q, k, v, probs, context_t, hidden, mixed, active, slope, block, rows, low,
                  wqs, wks, wvs, wos, wes, wrs, v_t, s_t, ctx, sems, psem, pbuf):
    n, width = x.shape
    heads = far.shape[0]
    ff = wes.shape[1]
    copies = [pltpu.make_async_copy(a, b, sems.at[i])
              for i, (a, b) in enumerate(((wq, wqs), (wk, wks), (wv, wvs), (wo, wos), (we, wes), (wr, wrs)))]
    for c in copies:
        c.start()

    @pl.loop(0, n // 128)
    def _(i):
        r = pl.ds(i * 128, 128)
        t = x[r].astype(F32)
        normed[r] = (t * rms_scale(t) * ag[...]).astype(BF)

    for w, out, c in ((wqs, q, copies[0]), (wks, k, copies[1]), (wvs, v, copies[2])):
        c.wait()

        @pl.loop(0, width // 256)
        def _(j):
            cols = pl.ds(j * 256, 256)
            out[:, cols] = mm(normed[...], w[:, cols]).astype(BF)

    lane = lax.broadcasted_iota(jnp.int32, (n, 128), 1)
    row = lax.broadcasted_iota(jnp.int32, (n, 128), 0)
    q_mark = jnp.where(lane == 0, 1.0, 0.0).astype(BF)
    k_mark = jnp.where((lane == 0) & (row >= length[0]), -1e30, 0.0).astype(BF)

    @pl.loop(0, heads // 2)
    def _(g):
        cols = pl.ds(g * 128, 128)
        v_t[...] = v[:, cols].T
        qq = jnp.concatenate([q[:, cols], q_mark], axis=1)
        kp = k[:, cols]
        for a in range(2):
            h = 2 * g + a
            mine = (lane < 64) if a == 0 else (lane >= 64)
            kk = jnp.concatenate([jnp.where(mine, kp, jnp.zeros_like(kp)), k_mark], axis=1)
            s_t[...] = mm_t(kk, qq)
            for j in range(n // 128):
                tile = []
                for i in range(n // 128):
                    s = s_t[i * 128:(i + 1) * 128, j * 128:(j + 1) * 128]
                    if abs(i - j) <= 1:
                        s = s + band[h, (i - j + 1) * 128:(i - j + 2) * 128, :]
                    elif i > j:
                        s = s + far[h, 1]
                    else:
                        s = s + far[h, 0]
                    tile.append(s)
                s = jnp.concatenate(tile, axis=0)
                m = jnp.max(s, axis=0, keepdims=True)
                e = jnp.exp(s - m)
                total = jnp.sum(e, axis=0, keepdims=True)
                pbuf[a, :, j * 128:(j + 1) * 128] = (e * (1.0 / total)).astype(BF)
            ctx[pl.ds(pl.multiple_of(h * 64, 64), 64), :] = mm(v_t[a * 64:(a + 1) * 64, :], pbuf[a]).astype(BF)
            cp = pltpu.make_async_copy(pbuf.at[a], probs.at[h], psem.at[a])
            cp.start()
        for a in range(2):
            pltpu.make_async_copy(pbuf.at[a], probs.at[2 * g + a], psem.at[a]).wait()

    context_t[...] = ctx[...]
    copies[3].wait()

    @pl.loop(0, n // 128)
    def _(i):
        r = pl.ds(i * 128, 128)
        hid = x[r].astype(F32) + t_mm(ctx[:, r], wos[...])
        hidden[r] = hid
        mixed[r] = (hid * rms_scale(hid) * eg[...]).astype(BF)

    copies[4].wait()

    @pl.loop(0, ff // 256)
    def _(j):
        cols = pl.ds(j * 256, 256)
        u = mm(mixed[...], wes[:, cols])
        u2 = u * u
        t = jnp.tanh(u * (0.7978845608 + (0.7978845608 * 0.044715) * u2))
        half = 0.5 + 0.5 * t
        active[:, cols] = (u * half).astype(BF)
        slope[:, cols] = (half + half * (1.0 - t) * u * (0.7978845608 + (3 * 0.7978845608 * 0.044715) * u2)).astype(BF)

    copies[5].wait()

    @pl.loop(0, width // 256)
    def _(j):
        cols = pl.ds(j * 256, 256)
        block[:, cols] = mm(active[...], wrs[:, cols])

    @pl.loop(0, n // 128)
    def _(i):
        r = pl.ds(i * 128, 128)
        alive = (lax.broadcasted_iota(jnp.int32, (128, 1), 0) + i * 128 < length[0]).astype(F32)
        b = alive * (hidden[r] + block[r])
        block[r] = b
        low[r] = b.astype(BF)
        rows[r] = (b * rms_scale(b) * fg[...]).astype(BF)


def encode(length, x, ag, eg, fg, band, far, wq, wk, wv, wo, we, wr):
    n, width = x.shape
    ff = we.shape[1]
    heads = far.shape[0]
    sm = pl.BlockSpec(memory_space=pltpu.SMEM)
    vm = pl.BlockSpec(memory_space=pltpu.VMEM)
    hb = pl.BlockSpec(memory_space=pl.ANY)
    S = jax.ShapeDtypeStruct
    full = S((n, width), BF)
    return pl.pallas_call(
        encode_kernel,
        out_shape=(full, full, full, full, S((heads, n, n), BF), S((width, n), BF), S((n, width), F32), full,
                   S((n, ff), BF), S((n, ff), BF), S((n, width), F32), full, full),
        in_specs=[sm, vm, vm, vm, vm, vm, sm] + [hb] * 6,
        out_specs=(vm,) * 4 + (hb,) + (vm,) * 8,
        scratch_shapes=[pltpu.VMEM(w.shape, BF) for w in (wq, wk, wv, wo, we, wr)] + [
            pltpu.VMEM((128, n), BF), pltpu.VMEM((n, n), F32), pltpu.VMEM((width, n), BF),
            pltpu.SemaphoreType.DMA((6,)), pltpu.SemaphoreType.DMA((2,)), pltpu.VMEM((2, n, n), BF)],
        compiler_params=pltpu.CompilerParams(vmem_limit_bytes=60 * 1024 * 1024),
        name="encode",
    )(length, x, ag.reshape(1, -1), eg.reshape(1, -1), fg.reshape(1, -1), band, far, wq, wk, wv, wo, we, wr)


def gelu_parts(u):
    u2 = u * u
    t = jnp.tanh(u * (0.7978845608 + (0.7978845608 * 0.044715) * u2))
    half = 0.5 + 0.5 * t
    return u * half, half + half * (1.0 - t) * u * (0.7978845608 + (3 * 0.7978845608 * 0.044715) * u2)

def norm_down(v, r, g, dy):
    vr = v * r
    gd = g * dy
    return r * (gd - vr * jnp.mean(vr * gd, axis=-1, keepdims=True)), vr * dy

def decode_kernel(length, rows, dec_in, dec_cot, sg, cg, fg, *rest):
    hbm = rest[:8]
    (out, in_grad, gains, left, right, wide, mids, rows_grad) = rest[8:16]
    bufs = rest[16:24]
    sems = rest[24]
    sv, so, cq, ck, cv, co, fe, fr = bufs
    copies = [pltpu.make_async_copy(a, b, sems.at[i]) for i, (a, b) in enumerate(zip(hbm, bufs))]
    for c in copies:
        c.start()
    n, width = rows.shape
    heads = mids.shape[1]
    size = width // heads
    x = dec_in[...].astype(F32)
    cot = dec_cot[...]
    own = (lax.broadcasted_iota(jnp.int32, (heads, width), 1) // size
           == lax.broadcasted_iota(jnp.int32, (heads, width), 0))

    def spread(r):
        return jnp.where(own, r.astype(F32), 0.0).astype(BF)

    def collect(r):
        return jnp.sum(jnp.where(own, r, 0.0), axis=0, keepdims=True)

    x_r = rms_scale(x)
    self_normed = (x * x_r * sg[...]).astype(BF)
    copies[0].wait()
    self_values = mm(self_normed, sv[...]).astype(BF)
    copies[1].wait()
    after = x + mm(self_values, so[...])
    after_r = rms_scale(after)
    cross_normed = (after * after_r * cg[...]).astype(BF)
    copies[2].wait()
    cross_q = mm(cross_normed, cq[...]).astype(BF)
    copies[3].wait()
    q_rows = mm_t(spread(cross_q), ck[...]).astype(BF)
    s = mm_t(q_rows, rows[...])
    s = jnp.where(lax.broadcasted_iota(jnp.int32, s.shape, 1) < length[0], s, -1e30)
    e = jnp.exp(s - jnp.max(s, axis=-1, keepdims=True))
    probs = e / jnp.sum(e, axis=-1, keepdims=True)
    low = probs.astype(BF)
    mean_rows = mm(low, rows[...]).astype(BF)
    copies[4].wait()
    cross_context = collect(mm(mean_rows, cv[...])).astype(BF)
    copies[5].wait()
    middle = after + mm(cross_context, co[...])
    middle_r = rms_scale(middle)
    feed_normed = (middle * middle_r * fg[...]).astype(BF)
    copies[6].wait()
    active, slope = gelu_parts(mm(feed_normed, fe[...]))
    active = active.astype(BF)
    copies[7].wait()
    out[...] = (middle + mm(active, fr[...])).astype(BF)
    upper_grad = (slope * mm_t(cot, fr[...])).astype(BF)
    middle_down, feed_gain = norm_down(middle, middle_r, fg[...], mm_t(upper_grad, fe[...]))
    middle_grad = cot.astype(F32) + middle_down
    cross_branch = middle_grad.astype(BF)
    context_grad = mm_t(cross_branch, co[...]).astype(BF)
    g_rows = mm_t(spread(context_grad), cv[...]).astype(BF)
    prob_grad = mm_t(g_rows, rows[...])
    score_grad = (probs * (prob_grad - jnp.sum(probs * prob_grad, axis=-1, keepdims=True))).astype(BF)
    score_rows = mm(score_grad, rows[...]).astype(BF)
    pad = jnp.zeros((16 - heads % 16, n), BF)
    padw = jnp.zeros((16 - heads % 16, width), BF)
    rows_grad[...] = t_mm(jnp.concatenate([score_grad, pad, low, pad], axis=0),
                          jnp.concatenate([q_rows, padw, g_rows, padw], axis=0)).astype(BF)
    cross_q_grad = collect(mm(score_rows, ck[...])).astype(BF)
    after_down, cross_gain = norm_down(after, after_r, cg[...], mm_t(cross_q_grad, cq[...]))
    after_grad = middle_grad + after_down
    self_branch = after_grad.astype(BF)
    self_values_grad = mm_t(self_branch, so[...]).astype(BF)
    x_down, self_gain = norm_down(x, x_r, sg[...], mm_t(self_values_grad, sv[...]))
    in_grad[...] = (after_grad + x_down).astype(BF)
    gains[0:1, :] = self_gain
    gains[1:2, :] = cross_gain
    gains[2:3, :] = feed_gain
    for i, r in enumerate((self_normed, self_values, cross_normed, cross_context, feed_normed)):
        left[i:i + 1, :] = r.astype(F32)
    for i, r in enumerate((self_values_grad, self_branch, cross_q_grad, cross_branch, cross_q, context_grad, cot)):
        right[i:i + 1, :] = r.astype(F32)
    wide[0:1, :] = active.astype(F32)
    wide[1:2, :] = upper_grad.astype(F32)
    mids[0] = score_rows.astype(F32)
    mids[1] = mean_rows.astype(F32)

def decode(length, rows, dec_in, dec_cot, sg, cg, fg, heads, *weights):
    n, width = rows.shape
    ff = weights[6].shape[1]
    sm = pl.BlockSpec(memory_space=pltpu.SMEM)
    vm = pl.BlockSpec(memory_space=pltpu.VMEM)
    hb = pl.BlockSpec(memory_space=pl.ANY)
    S = jax.ShapeDtypeStruct
    return pl.pallas_call(
        decode_kernel,
        out_shape=(S((1, width), BF), S((1, width), BF), S((3, width), F32), S((5, width), F32), S((7, width), F32),
                   S((2, ff), F32), S((2, heads, width), F32), S((n, width), BF)),
        in_specs=[sm] + [vm] * 6 + [hb] * 8,
        out_specs=(vm,) * 8,
        scratch_shapes=[pltpu.VMEM(w.shape, BF) for w in weights] + [pltpu.SemaphoreType.DMA((8,))],
        compiler_params=pltpu.CompilerParams(vmem_limit_bytes=60 * 1024 * 1024),
        name="decode",
    )(length, rows, dec_in, dec_cot, sg.reshape(1, -1), cg.reshape(1, -1), fg.reshape(1, -1), *weights)


def feed_back_kernel(length, rows_grad, block, cot, fg, hidden, eg, mixed, active, slope, wr, we,
                     wide, tall, hidden_grad, branch, gains, wrs, wes, bg, rb, rb_t, ug, mixed_t, dmixed, sems):
    n, width = block.shape
    ff = active.shape[1]
    groups, lanes = tall.shape[3], tall.shape[5]
    cols_dev = width // 4
    copies = [pltpu.make_async_copy(a, b, sems.at[i]) for i, (a, b) in enumerate(((wr, wrs), (we, wes)))]
    for c in copies:
        c.start()
    gains[...] = jnp.zeros_like(gains)

    @pl.loop(0, n // 128)
    def _(i):
        r = pl.ds(i * 128, 128)
        alive = (lax.broadcasted_iota(jnp.int32, (128, 1), 0) + i * 128 < length[0]).astype(F32)
        v = block[r]
        down, gain = norm_down(v, rms_scale(v), fg[...], rows_grad[r].astype(F32))
        b = alive * (cot[r].astype(F32) + down)
        bg[r] = b
        rb[r] = b.astype(BF)
        rb_t[:, pl.ds(pl.multiple_of(i * 128, 128), 128)] = b.T.astype(BF)
        mixed_t[:, pl.ds(pl.multiple_of(i * 128, 128), 128)] = mixed[r].T
        gains[0:1, :] += jnp.sum(gain, axis=0, keepdims=True)

    copies[0].wait()

    @pl.loop(0, ff // 256)
    def _(j):
        cols = pl.ds(pl.multiple_of(j * 256, 256), 256)
        ug[:, cols] = (slope[:, cols].astype(F32) * mm_t(rb[...], wrs[cols, :])).astype(BF)

    copies[1].wait()

    @pl.loop(0, width // 256)
    def _(j):
        cols = pl.ds(pl.multiple_of(j * 256, 256), 256)
        dmixed[:, cols] = mm_t(ug[...], wes[cols, :])

    @pl.loop(0, n // 128)
    def _(i):
        r = pl.ds(i * 128, 128)
        v = hidden[r]
        down, gain = norm_down(v, rms_scale(v), eg[...], dmixed[r])
        h = bg[r] + down
        hidden_grad[r] = h
        branch[r] = h.astype(BF)
        gains[1:2, :] += jnp.sum(gain, axis=0, keepdims=True)

    @pl.loop(0, 4)
    def _(j):
        for half in range(2):
            cols = pl.ds(pl.multiple_of(j * (ff // 4) + half * (ff // 8), 128), ff // 8)
            wide[half, lax.rem(j, 2), j // 2] = mm(mixed_t[...], ug[:, cols]).astype(BF)

    chunk = ff // 8
    per_group = lanes // chunk

    @pl.loop(0, 8)
    def _(i):
        cols = pl.ds(pl.multiple_of(i * chunk, 128), chunk)
        g = mm(rb_t[...], active[:, cols]).astype(BF)
        for j in range(4):
            for half in range(2):
                r = j * cols_dev + half * (cols_dev // 2)
                part = g[r:r + cols_dev // 2]
                if per_group == 1:
                    tall[half, j % 2, j // 2, i] = part
                else:
                    tall[half, j % 2, j // 2, 0, :, cols] = part


def feed_back(groups, length, rows_grad, block, cot, fg, hidden, eg, mixed, active, slope, wr, we):
    n, width = block.shape
    ff = active.shape[1]
    sm = pl.BlockSpec(memory_space=pltpu.SMEM)
    vm = pl.BlockSpec(memory_space=pltpu.VMEM)
    hb = pl.BlockSpec(memory_space=pl.ANY)
    S = jax.ShapeDtypeStruct
    V = pltpu.VMEM
    return pl.pallas_call(
        feed_back_kernel,
        out_shape=(S((2, 2, 2, width, ff // 8), BF),
                   S((2, 2, 2, groups, width // 8, ff // groups), BF), S((n, width), F32), S((n, width), BF), S((2, width), F32)),
        in_specs=[sm] + [vm] * 9 + [hb] * 2,
        out_specs=(vm,) * 5,
        scratch_shapes=[V(wr.shape, BF), V(we.shape, BF), V((n, width), F32), V((n, width), BF), V((width, n), BF),
                        V((n, ff), BF), V((width, n), BF), V((n, width), F32), pltpu.SemaphoreType.DMA((2,))],
        compiler_params=pltpu.CompilerParams(vmem_limit_bytes=60 * 1024 * 1024),
        name="feed_back",
    )(length, rows_grad, block, cot, fg.reshape(1, -1), hidden, eg.reshape(1, -1), mixed, active, slope, wr, we)


def backward_kernel(np_, ns, x, ag, q, k, v, context_t, branch, hidden_grad, normed, gains_dec, gains_feed,
                    probs, wo, wq, wk, wv, wide, tall, dec, encoded,
                    red, small_out, dec_out, enc_out, grad_out,
                    wos, wqs, wks, wvs, d_out, dp, ds, dq_t, dq, dk, dv, k_t, normed_t, ng, in_grad,
                    pbuf, band, diag, own, au, r0, r1y, r1x, r1a, r2, r3, sm, smr, smz,
                    psem, wsem, loc, c_s, c_r, a_s, a_r, b_s, b_r, ac_s, ac_r, ax_s, ax_r, z_s, z_r,
                    m_s, m_r, mz_s, mz_r, d_s, d_r, e_s, e_r, g_s, g_r):
    n, width = x.shape
    heads = probs.shape[0]
    nz = np_ // 2
    rows, lanes = r0.shape[4:]
    count = np_ * ns
    p = lax.axis_index("pairs")
    s = lax.axis_index("seq")
    c = lax.rem(s, 2)
    y = s // 2
    xx = lax.rem(p, 2)
    z = p // 2
    me = p * ns + s
    core_peer = (p, s + 1 - 2 * c)
    y_peer = (p, lax.rem(s + 2, 4))
    x_peer = (p + 1 - 2 * xx, s)

    def place(d):
        lin = lax.rem(me + d, count)
        return (lin // ns, lax.rem(lin, ns))

    barrier = pltpu.get_barrier_semaphore()

    @pl.loop(1, count)
    def _(d):
        pl.semaphore_signal(barrier, inc=1, device_id=place(d), device_id_type=MESH)

    def remote(src, dst, send, recv, peer):
        return pltpu.make_async_remote_copy(
            src_ref=src, dst_ref=dst, send_sem=send, recv_sem=recv,
            device_id=peer, device_id_type=MESH)

    weights = [pltpu.make_async_copy(a, b, wsem.at[i])
               for i, (a, b) in enumerate(((wo, wos), (wq, wqs), (wk, wks), (wv, wvs)))]

    def fetch(h, slot):
        return pltpu.make_async_copy(probs.at[h], pbuf.at[slot], psem.at[slot])

    def unit(i, core):
        return (wide, tall)[i // 2].at[i % 2, core]

    def core_copy(i):
        return remote(unit(i, 1 - c), r0.at[i], c_s.at[i], c_r.at[i], core_peer)

    def own_copy(i):
        return pltpu.make_async_copy(unit(i, c), own.at[i], loc.at[i])

    def first(i):
        if i % 2 == 0:
            return remote(own.at[i, 1 - y], r1y.at[i // 2], a_s.at[i], a_r.at[i], y_peer)
        return remote(own.at[i, :, :, 1 - xx], r1x.at[i // 2], a_s.at[i], a_r.at[i], x_peer)

    def second(i):
        if i % 2 == 0:
            return remote(own.at[i, y, :, 1 - xx], r2.at[i], b_s.at[i], b_r.at[i], x_peer)
        return remote(own.at[i, 1 - y, :, xx], r2.at[i], b_s.at[i], b_r.at[i], y_peer)

    def final(i):
        return own.at[i, y] if i < 4 else au.at[i - 4, c, y]

    def last(i, d):
        t = lax.rem(z + d, nz)
        return remote(final(i).at[t, xx], r3.at[i, d], z_s.at[i, d], z_r.at[i, d], (t * 2 + xx, s))

    def attn_core(w, half):
        return remote(au.at[w, 1 - c, half], r0.at[4 + w, half], ac_s.at[w, half], ac_r.at[w, half], core_peer)

    def attn_x(w, half):
        return remote(au.at[w, c, half, :, 1 - xx], r1a.at[w, half], ax_s.at[w, half], ax_r.at[w, half], x_peer)

    def attn_y(w):
        return remote(au.at[w, c, 1 - y, :, xx], r2.at[4 + w], b_s.at[4 + w], b_r.at[4 + w], y_peer)

    def dec_copy(d):
        to = place(d)
        return remote(dec.at[to[0] * ns + to[1]], dec_out.at[me], d_s.at[d], d_r.at[d], to)

    def enc_copy(d):
        t = lax.rem(s + d, ns)
        return remote(encoded.at[t], enc_out.at[s], e_s.at[d], e_r.at[d], (p, t))

    def grad_copy(d):
        t = lax.rem(s + d, ns)
        return remote(in_grad.at[t], grad_out.at[s], g_s.at[d], g_r.at[d], (p, t))

    keep_dec = pltpu.make_async_copy(dec.at[me], dec_out.at[me], loc.at[4])
    keep_enc = pltpu.make_async_copy(encoded.at[s], enc_out.at[s], loc.at[5])
    keep_grad = pltpu.make_async_copy(in_grad.at[s], grad_out.at[s], loc.at[6])

    def step_a(i):
        core_copy(i).wait()
        own_copy(i).wait()

        @pl.loop(0, nz)
        def _(b):
            for a in range(2):
                for e in range(2):
                    own[i, a, b, e] = own[i, a, b, e] + r0[i, a, b, e]

        first(i).start()

    def step_b(i):
        first(i).wait()

        @pl.loop(0, nz)
        def _(b):
            for e in range(2):
                if i % 2 == 0:
                    own[i, y, b, e] = own[i, y, b, e] + r1y[i // 2, b, e]
                else:
                    own[i, e, b, xx] = own[i, e, b, xx] + r1x[i // 2, e, b]

        second(i).start()

    def step_c(i):
        if i < 4:
            second(i).wait()
        else:
            attn_y(i - 4).wait()

        @pl.loop(0, nz)
        def _(b):
            f = final(i)
            f[b, xx] = f[b, xx] + r2[i, b]

        @pl.loop(1, nz)
        def _(d):
            last(i, d).start()

    def step_d(i):
        red[i] = final(i)[z, xx].astype(F32)

        @pl.loop(1, nz)
        def _(d):
            last(i, d).wait()
            red[i] = red[i] + r3[i, d].astype(F32)

    def attn_a(w, half):
        attn_core(w, half).wait()

        @pl.loop(0, nz)
        def _(b):
            for e in range(2):
                au[w, c, half, b, e] = au[w, c, half, b, e] + r0[4 + w, half, b, e]

        attn_x(w, half).start()

    def attn_b(w, half):
        attn_x(w, half).wait()

        @pl.loop(0, nz)
        def _(b):
            au[w, c, half, b, xx] = au[w, c, half, b, xx] + r1a[w, half, b]

    for copy in weights:
        copy.start()
    first_half, last_half = 1 - y, y
    fetch(first_half * (heads // 2), 0).start()
    fetch(first_half * (heads // 2) + 1, 1).start()
    for i in range(4):
        own_copy(i).start()
    keep_dec.start()
    keep_enc.start()
    diag[...] = jnp.zeros_like(diag)
    weights[0].wait()

    @pl.loop(0, width // 384)
    def _(j):
        cols = pl.ds(pl.multiple_of(j * 384, 128), 384)
        d_out[:, cols] = mm_t(branch[...], wos[cols, :]).astype(BF)

    pl.semaphore_wait(barrier, count - 1)
    for i in range(4):
        core_copy(i).start()
    for d in range(1, ns):
        enc_copy(d).start()

    @pl.loop(1, count)
    def _(d):
        dec_copy(d).start()

    @pl.loop(0, n // 128)
    def _(i):
        r = pl.ds(pl.multiple_of(i * 128, 128), 128)
        normed_t[:, r] = normed[r].T

    lane = lax.broadcasted_iota(jnp.int32, (n, 128), 1)
    lane_s = lax.broadcasted_iota(jnp.int32, (128, 128), 1)
    row_s = lax.broadcasted_iota(jnp.int32, (128, 128), 0)

    def pair(half, g):
        cols = pl.ds(pl.multiple_of(half * (width // 2) + g * 128, 128), 128)
        k_t[...] = k[:, cols].T
        dop = d_out[:, cols]
        qp = q[:, cols]
        vp = v[:, cols]
        zero = jnp.zeros_like(qp)
        for a in range(2):
            h = half * (heads // 2) + 2 * g + a
            mine = (lane < 64) if a == 0 else (lane >= 64)
            dp[...] = mm_t(jnp.where(mine, vp, zero), dop)
            fetch(h, a).wait()
            for j in range(n // 128):
                pj = pbuf[a, :, j * 128:(j + 1) * 128].astype(F32)
                pd = pj * dp[:, j * 128:(j + 1) * 128]
                total = jnp.sum(pd, axis=0, keepdims=True)
                sg = pd - pj * total
                ds[:, j * 128:(j + 1) * 128] = sg.astype(BF)
                for i in range(n // 128):
                    t = sg[i * 128:(i + 1) * 128]
                    if abs(i - j) <= 1:
                        b = (i - j + 1) * 128
                        if j == 0 or (j == 1 and i == 0):
                            band[b:b + 128, :] = t
                        else:
                            band[b:b + 128, :] += t
                    else:
                        f = 5 if i > j else 4
                        diag[h, f:f + 1, :] += jnp.sum(t, axis=0, keepdims=True)
            dvp = mm(pbuf[a], jnp.where(mine, dop, zero))
            dkp = mm(ds[...], jnp.where(mine, qp, zero))
            dq_t[pl.ds(pl.multiple_of(h * 64, 64), 64), :] = mm(k_t[a * 64:(a + 1) * 64, :], ds[...]).astype(BF)
            if a == 0:
                dk_sum, dv_sum = dkp, dvp
            else:
                dk[:, cols] = (dk_sum + dkp).astype(BF)
                dv[:, cols] = (dv_sum + dvp).astype(BF)
            for b in range(3):
                t = band[b * 128:(b + 1) * 128, :]
                for bit in range(7):
                    t = jnp.where((row_s >> bit) % 2 == 1, pltpu.roll(t, 128 - (1 << bit), 1), t)
                straight = jnp.sum(jnp.where(lane_s + row_s < 128, t, 0.0), axis=0, keepdims=True)
                whole = jnp.sum(t, axis=0, keepdims=True)
                diag[h, b:b + 1, :] += straight
                diag[h, b + 1:b + 2, :] += whole - straight

    part = width // 4

    def units_of(half):
        cols = pl.ds(pl.multiple_of(half * (width // 2), 128), width // 2)
        lower = pl.ds(pl.multiple_of(half * (width // 2), 128), width // 2)
        dq_h = dq_t[lower, :].T
        dq[:, cols] = dq_h
        dk_h = dk[:, cols]
        dv_h = dv[:, cols]
        br_h = branch[:, cols]
        zero = jnp.zeros((n, part), BF)
        for cc in range(2):
            e = slice(cc * part, (cc + 1) * part)
            g = mm(normed_t[...], jnp.concatenate([dq_h[:, e], dk_h[:, e]], axis=1))
            au[0, cc, half] = g.astype(BF).reshape(nz, 2, rows, lanes)
            g = (mm(normed_t[...], jnp.concatenate([dv_h[:, e], zero], axis=1))
                 + mm(context_t[...], jnp.concatenate([zero, br_h[:, e]], axis=1)))
            au[1, cc, half] = g.astype(BF).reshape(nz, 2, rows, lanes)
        for w in range(2):
            attn_core(w, half).start()

    quarter = heads // 4

    @pl.loop(0, quarter)
    def _(g):
        pair(first_half, g)
        nxt = jnp.where(g == quarter - 1, last_half * (heads // 2), first_half * (heads // 2) + 2 * (g + 1))
        fetch(nxt, 0).start()
        fetch(nxt + 1, 1).start()

        @pl.when(g == 0)
        def _():
            step_a(0)
            step_a(1)

        @pl.when(g == 1)
        def _():
            step_a(2)
            step_a(3)

    units_of(first_half)

    @pl.loop(0, quarter)
    def _(g):
        pair(last_half, g)

        @pl.when(g < quarter - 1)
        def _():
            nxt = last_half * (heads // 2) + 2 * (g + 1)
            fetch(nxt, 0).start()
            fetch(nxt + 1, 1).start()

        @pl.when(g == 0)
        def _():
            attn_a(0, first_half)
            attn_a(1, first_half)

        @pl.when(g == 1)
        def _():
            step_b(0)
            step_b(1)

    units_of(last_half)
    for copy in weights[1:]:
        copy.wait()

    @pl.loop(0, 2)
    def _(i):
        r = pl.ds(pl.multiple_of(i * (n // 2), 128), n // 2)
        ng[r] = mm_t(dq[r], wqs[...]) + mm_t(dk[r], wks[...]) + mm_t(dv[r], wvs[...])

    attn_a(0, last_half)
    attn_a(1, last_half)
    sm[...] = jnp.zeros_like(sm)
    slot_rows = n // ns
    gain_sum = jnp.zeros((1, width), F32)
    for i in range(ns):
        r = slice(i * slot_rows, (i + 1) * slot_rows)
        t = x[r].astype(F32)
        down, gain = norm_down(t, rms_scale(t), ag[...], ng[r])
        in_grad[i] = (hidden_grad[r] + down).astype(BF)
        gain_sum = gain_sum + jnp.sum(gain, axis=0, keepdims=True)
    keep_grad.start()
    for d in range(1, ns):
        grad_copy(d).start()

    col = lax.broadcasted_iota(jnp.int32, (128, width), 1)
    offset = (col // 128 - 1) * 128 - lax.rem(col, 128)
    offset = jnp.where(col >= width - 128, 256, jnp.where(col >= width - 256, -256, offset))
    dist = jnp.abs(offset)
    bucket = jnp.full_like(dist, 8)
    for edge in EDGES:
        bucket = bucket + (dist >= edge).astype(jnp.int32)
    bucket = jnp.where(dist < 8, dist, bucket) + jnp.where(offset > 0, 16, 0)
    pick = jnp.where(bucket == lax.broadcasted_iota(jnp.int32, (128, width), 0), 1.0, 0.0)
    bias = jnp.zeros((16, 128), F32)
    for i in range(width // 128):
        bias = bias + lax.dot_general(diag[:, i, :], pick[:, i * 128:(i + 1) * 128], (((1,), (1,)), ((), ())),
                                      precision=HIGHEST, preferred_element_type=F32)
    sm[0, 40:56, :] = bias
    gains = [gains_dec[i:i + 1, :] for i in range(3)] + [gains_feed[i:i + 1, :] for i in range(2)] + [gain_sum]
    for i, gain in enumerate(gains):
        for j in range(width // 128):
            sm[0, i * 6 + j:i * 6 + j + 1, :] = gain[:, j * 128:(j + 1) * 128]

    def small_copy(i):
        return remote(sm.at[i], smr.at[i], m_s.at[i], m_r.at[i], (core_peer, y_peer, x_peer)[i])

    def z_small(d):
        return remote(smz.at[z], smz.at[z], mz_s.at[d], mz_r.at[d], (lax.rem(z + d, nz) * 2 + xx, s))

    small_copy(0).start()
    step_b(2)
    step_b(3)
    small_copy(0).wait()
    sm[1] = sm[0] + smr[0]
    small_copy(1).start()
    attn_b(0, first_half)
    attn_y(0).start()
    attn_b(1, first_half)
    attn_y(1).start()
    step_c(0)
    step_c(1)
    small_copy(1).wait()
    sm[2] = sm[1] + smr[1]
    small_copy(2).start()
    step_c(2)
    step_c(3)
    attn_b(0, last_half)
    small_copy(2).wait()
    smz[z] = sm[2] + smr[2]

    @pl.loop(1, nz)
    def _(d):
        z_small(d).start()

    step_c(4)
    attn_b(1, last_half)
    step_c(5)
    for i in range(6):
        step_d(i)

    @pl.loop(1, nz)
    def _(d):
        z_small(d).wait()

    small_out[...] = smz[0]

    @pl.loop(1, nz)
    def _(d):
        small_out[...] = small_out[...] + smz[d]

    keep_dec.wait()
    keep_enc.wait()
    keep_grad.wait()
    for d in range(1, ns):
        enc_copy(d).wait()
        grad_copy(d).wait()

    @pl.loop(1, count)
    def _(d):
        dec_copy(d).wait()


def backward(np_, ns, x, ag, q, k, v, context_t, branch, hidden_grad, normed, gains_dec, gains_feed,
             probs, wo, wq, wk, wv, wide, tall, dec, encoded):
    n, width = x.shape
    heads = probs.shape[0]
    nz = np_ // 2
    rows, lanes = wide.shape[5:]
    count = np_ * ns
    padded = normed.shape[1]
    vm = pl.BlockSpec(memory_space=pltpu.VMEM)
    hb = pl.BlockSpec(memory_space=pl.ANY)
    S = jax.ShapeDtypeStruct
    V = pltpu.VMEM
    dma = pltpu.SemaphoreType.DMA
    nar = V((n, width), BF)
    square = V((width, width), BF)
    slots = (ns, n // ns, width)
    small = (64, 128)
    return pl.pallas_call(
        functools.partial(backward_kernel, np_, ns),
        out_shape=(S((6, rows, lanes), F32), S(small, F32), S(dec.shape, BF), S(slots, BF), S(slots, BF)),
        in_specs=[vm] * 11 + [hb] * 9,
        out_specs=(vm, vm, hb, hb, hb),
        scratch_shapes=[
            square, square, square, square, nar, V((n, n), F32), V((n, n), BF), V((width, n), BF), nar, nar, nar,
            V((128, n), BF), V((padded, n), BF), V((n, width), F32), V(slots, BF),
            V((2, n, n), BF), V((384, 128), F32), V((16, 8, 128), F32),
            V((4, 2, nz, 2, rows, lanes), BF), V((2, 2, 2, nz, 2, rows, lanes), BF), V((6, 2, nz, 2, rows, lanes), BF),
            V((2, nz, 2, rows, lanes), BF), V((2, 2, nz, rows, lanes), BF), V((2, 2, nz, rows, lanes), BF),
            V((6, nz, rows, lanes), BF), V((6, nz, rows, lanes), BF),
            V((3,) + small, F32), V((3,) + small, F32), V((nz,) + small, F32),
            dma((2,)), dma((4,)), dma((7,)), dma((4,)), dma((4,)), dma((4,)), dma((4,)), dma((6,)), dma((6,)),
            dma((2, 2)), dma((2, 2)), dma((2, 2)), dma((2, 2)), dma((6, nz)), dma((6, nz)),
            dma((3,)), dma((3,)), dma((nz,)), dma((nz,)), dma((count,)), dma((count,)),
            dma((ns,)), dma((ns,)), dma((ns,)), dma((ns,)),
        ],
        compiler_params=pltpu.CompilerParams(
            collective_id=0, has_side_effects=True, vmem_limit_bytes=62 * 1024 * 1024),
        name="backward",
    )(x, ag.reshape(1, -1), q, k, v, context_t, branch, hidden_grad, normed, gains_dec, gains_feed,
      probs, wo, wq, wk, wv, wide, tall, dec, encoded.reshape(slots))


def per_device(
    enc_input, dec_input, lengths, attend_gain, query_weight, key_weight, value_weight,
    output_weight, bias_table, expand_gain, expand_weight, reduce_weight, final_gain,
    self_gain, self_value, self_output, cross_gain, cross_query, cross_key, cross_value,
    cross_output, feed_gain, feed_expand, feed_reduce, enc_cotangent, dec_cotangent,
):
    group, local_rows, width = enc_input.shape
    buckets, heads = bias_table.shape
    size = width // heads
    ff = expand_weight.shape[1]
    ns = lax.axis_size("seq")
    np_ = lax.axis_size("pairs")
    place = lax.axis_index("seq")
    seq_len = local_rows * ns
    length = lax.dynamic_slice_in_dim(lengths, place, 1)
    x = lax.all_to_all(enc_input, "seq", split_axis=0, concat_axis=1, tiled=True)[0]
    cot = lax.all_to_all(enc_cotangent, "seq", split_axis=0, concat_axis=1, tiled=True)[0]

    band_bucket = rel_bucket(jnp.arange(128), jnp.arange(384) - 128).T
    onehot = (jnp.arange(buckets, dtype=jnp.int32)[:, None, None] == band_bucket).astype(F32)
    band = jnp.einsum("but,bh->hut", onehot, bias_table, precision=HIGHEST)
    far = jnp.stack([bias_table[15], bias_table[31]], axis=1)

    (normed, query, key, value, probs, context_t, hidden, mixed, active, slope, block, enc_rows,
     encoded) = encode(length, x, attend_gain, expand_gain, final_gain, band, far, query_weight,
                       key_weight, value_weight, output_weight, expand_weight, reduce_weight)
    dec_block, dec_input_grad, dec_gains, left, right, wide_rows, mids, rows_grad = decode(
        length, enc_rows, dec_input, dec_cotangent, self_gain, cross_gain, feed_gain, heads,
        self_value, self_output, cross_query, cross_key, cross_value, cross_output, feed_expand,
        feed_reduce)
    nz = np_ // 2
    r = width // np_
    aligned = r % 16 == 0 and (ff // np_) % 128 == 0
    wide, tall, hidden_grad, branch, feed_gains = feed_back(
        np_ if aligned else 1, length, rows_grad, block, cot, final_gain, hidden, expand_gain,
        mixed, active, slope, reduce_weight, expand_weight)
    rp = -(-r // 16) * 16
    lanes = ff // 8
    side = width // 8 // r

    def pad(unit):
        return jnp.pad(unit, ((0, 0),) * 5 + ((0, rp - r), (0, 0)))

    if aligned:
        tall = tall.reshape(2, 2, 2, nz, 2, r, lanes)
    else:
        tall = tall.reshape(2, 2, 2, r, side, nz, 2, ff // np_).transpose(0, 1, 2, 5, 6, 3, 4, 7)
        tall = pad(tall.reshape(2, 2, 2, nz, 2, r, lanes))
    wide = pad(wide.reshape(2, 2, 2, nz, 2, r, lanes))
    cols = width // ns

    left_cut = jnp.concatenate([
        left.reshape(5, np_, r).transpose(1, 0, 2).reshape(np_, 5 * r),
        wide_rows[0].reshape(np_, 4 * r),
    ], axis=1)
    mid_cut = mids.reshape(2, ns, heads // ns, np_, r).transpose(3, 1, 0, 2, 4)
    mid_cut = mid_cut.reshape(np_, ns, 6 * r)
    right_cut = jnp.concatenate([
        right.reshape(7, ns, cols).transpose(1, 0, 2).reshape(ns, 7 * cols),
        wide_rows[1].reshape(ns, 4 * cols)], axis=1)
    dec_all = jnp.concatenate([
        jnp.broadcast_to(left_cut[:, None], (np_, ns, 9 * r)), mid_cut,
        jnp.broadcast_to(right_cut[None], (np_, ns, 11 * cols))], axis=-1)
    dec_all = dec_all.astype(BF).reshape(np_ * ns, -1)
    used = dec_all.shape[1]
    dec_rows = -(-used // 2048) * 16
    dec_all = jnp.pad(dec_all, ((0, 0), (0, dec_rows * 128 - used)))
    dec_all = dec_all.reshape(np_ * ns, dec_rows, 128)

    if rp != r:
        gap = ((0, 0), (0, 0), (0, rp - r))
        normed = jnp.pad(normed.reshape(seq_len, np_, r), gap).reshape(seq_len, np_ * rp)
        gap = ((0, 0), (0, rp - r), (0, 0))
        context_t = jnp.pad(context_t.reshape(np_, r, seq_len), gap).reshape(np_ * rp, seq_len)
    red, small_sum, dec_got, enc_out, grad_out = backward(
        np_, ns, x, attend_gain, query, key, value, context_t, branch, hidden_grad, normed,
        dec_gains, feed_gains, probs, output_weight, query_weight, key_weight, value_weight,
        wide, tall, dec_all, encoded)

    got = dec_got.reshape(np_ * ns, -1)
    lefts = got[:, :9 * r].reshape(-1, 9, r)
    mid_got = got[:, 9 * r:15 * r].reshape(-1, 2, 3, r)
    rights = got[:, 15 * r:15 * r + 11 * cols].reshape(-1, 11, cols)
    plain = jnp.einsum("nkr,nkc->krc", lefts[:, :4], rights[:, :4], preferred_element_type=F32)
    crossed = jnp.einsum("nkhr,nkhd->krhd", mid_got, rights[:, 4:6].reshape(-1, 2, 3, size),
                         preferred_element_type=F32).reshape(2, r, cols)
    feed_in = jnp.einsum("nr,nc->rc", lefts[:, 4], rights[:, 7:11].reshape(-1, 4 * cols),
                         preferred_element_type=F32)
    feed_out = jnp.einsum("nr,nc->rc", lefts[:, 5:9].reshape(-1, 4 * r), rights[:, 6],
                          preferred_element_type=F32)
    red = red[:, :r]
    grad_reduce = red[2:4].reshape(2, r, side, ff // np_).reshape(cols, ff // np_).T
    gains = small_sum[:36].reshape(6, width)
    bias = small_sum[40:40 + heads, :buckets].T
    return (
        enc_out, dec_block, grad_out, dec_input_grad,
        gains[5],
        red[4][:, :cols], red[4][:, cols:], red[5][:, :cols], red[5][:, cols:],
        bias,
        gains[4],
        jnp.concatenate([red[0], red[1]], axis=1), grad_reduce,
        gains[3],
        gains[0], plain[0], plain[1],
        gains[1], plain[2], crossed[0], crossed[1], plain[3],
        gains[2], feed_in, feed_out,
    )


def solution(mesh):
    rows = P("pairs", "seq", None)
    single = P(("pairs", "seq"), None)
    block = P("pairs", "seq")
    return jax.shard_map(
        per_device,
        mesh=mesh,
        in_specs=(rows, single, P("pairs")) + (P(),) * 21 + (rows, single),
        out_specs=(
            rows, single, rows, single,
            P(), block, block, block, block, P(), P(), block, block, P(),
            P(), block, block, P(), block, block, block, block, P(), block, block,
        ),
        check_vma=False,
    )
```

```python
import functools

import jax
import jax.numpy as jnp
from jax import lax
from jax.experimental import pallas as pl
from jax.experimental.pallas import tpu as pltpu
from jax.sharding import PartitionSpec as P

EPSILON = 1e-06
EDGES = (12, 16, 23, 32, 46, 64, 91)
HIGHEST = lax.Precision.HIGHEST
MESH = pl.DeviceIdType.MESH
BF = jnp.bfloat16
F32 = jnp.float32


def rel_bucket(query_pos, key_pos):
    offset = key_pos[None, :] - query_pos[:, None]
    distance = jnp.abs(offset)
    far_bucket = jnp.full_like(distance, 8)
    for threshold in EDGES:
        far_bucket = far_bucket + (distance >= threshold).astype(jnp.int32)
    bucket_id = jnp.where(distance < 8, distance, far_bucket)
    return bucket_id + 16 * (offset > 0).astype(jnp.int32)


def mm(a, b):
    return jnp.dot(a, b, preferred_element_type=F32)
def mm_t(a, b):
    return lax.dot_general(a, b, (((1,), (1,)), ((), ())), preferred_element_type=F32)
def t_mm(a, b):
    return lax.dot_general(a, b, (((0,), (0,)), ((), ())), preferred_element_type=F32)

def rms_scale(v):
    return lax.rsqrt(jnp.mean(v * v, axis=-1, keepdims=True) + EPSILON)

def encode_kernel(length, x, ag, eg, fg, band, far, wq, wk, wv, wo, we, wr,
                  normed_t, q, k, v, probs, context_t, hidden, mixed_t, active, slope, block, rows, low,
                  wqs, wks, wvs, wos, wes, wrs, normed, nt, qs, ks, vs, ctx, hid, mixed, mt, act, slo, blk, rws, lws,
                  v_t, s_t, pbuf, sems, psem, osem):
    n, width = x.shape
    heads = far.shape[0]
    ff = wes.shape[1]
    copies = [pltpu.make_async_copy(a, b, sems.at[i])
              for i, (a, b) in enumerate(((wq, wqs), (wk, wks), (wv, wvs), (wo, wos), (we, wes), (wr, wrs)))]
    for c in copies:
        c.start()
    saved = {}

    def save(name, src, dst):
        saved[name] = pltpu.make_async_copy(src, dst, osem.at[len(saved)])
        saved[name].start()

    for i in range(n // 128):
        r = slice(i * 128, (i + 1) * 128)
        t = x[r].astype(F32)
        t = t * rms_scale(t) * ag[...]
        normed[r] = t.astype(BF)
        nt[:, r] = t.T.astype(BF)
    save("normed", nt, normed_t)

    for name, w, out, dst, c in (("q", wqs, qs, q, copies[0]), ("k", wks, ks, k, copies[1]), ("v", wvs, vs, v, copies[2])):
        c.wait()
        for i in range(2):
            r = slice(i * (n // 2), (i + 1) * (n // 2))
            out[r] = mm(normed[r], w[...]).astype(BF)
        save(name, out, dst)

    lane = lax.broadcasted_iota(jnp.int32, (n, 128), 1)
    row = lax.broadcasted_iota(jnp.int32, (n, 128), 0)
    q_mark = jnp.where(lane == 0, 1.0, 0.0).astype(BF)
    k_mark = jnp.where((lane == 0) & (row >= length[0]), -1e30, 0.0).astype(BF)

    def keep(h, a):
        return pltpu.make_async_copy(pbuf.at[a], probs.at[h], psem.at[a])

    @pl.loop(0, heads // 2)
    def _(g):
        cols = pl.ds(pl.multiple_of(g * 128, 128), 128)
        v_t[...] = vs[:, cols].T
        qq = jnp.concatenate([qs[:, cols], q_mark], axis=1)
        kp = ks[:, cols]
        for a in range(2):
            h = 2 * g + a
            mine = (lane < 64) if a == 0 else (lane >= 64)
            kk = jnp.concatenate([jnp.where(mine, kp, jnp.zeros_like(kp)), k_mark], axis=1)
            s_t[a] = mm_t(kk, qq)

            @pl.when(g > 0)
            def _():
                keep(h - 2, a).wait()

            for j in range(n // 128):
                tile = []
                for i in range(n // 128):
                    s = s_t[a, i * 128:(i + 1) * 128, j * 128:(j + 1) * 128]
                    if abs(i - j) <= 1:
                        s = s + band[h, (i - j + 1) * 128:(i - j + 2) * 128, :]
                    elif i > j:
                        s = s + far[h, 1]
                    else:
                        s = s + far[h, 0]
                    tile.append(s)
                s = jnp.concatenate(tile, axis=0)
                m = jnp.max(s, axis=0, keepdims=True)
                e = jnp.exp(s - m)
                total = jnp.sum(e, axis=0, keepdims=True)
                pbuf[a, :, j * 128:(j + 1) * 128] = (e * (1.0 / total)).astype(BF)
            ctx[pl.ds(pl.multiple_of(h * 64, 64), 64), :] = mm(v_t[a * 64:(a + 1) * 64, :], pbuf[a]).astype(BF)
            keep(h, a).start()

    save("context", ctx, context_t)
    copies[3].wait()
    for i in range(2):
        r = slice(i * (n // 2), (i + 1) * (n // 2))
        h = x[r].astype(F32) + mm(ctx[:, r].T, wos[...])
        hid[r] = h
        t = h * rms_scale(h) * eg[...]
        mixed[r] = t.astype(BF)
        mt[:, r] = t.T.astype(BF)
    save("hidden", hid, hidden)
    save("mixed", mt, mixed_t)
    copies[4].wait()

    @pl.loop(0, ff // 512)
    def _(j):
        cols = pl.ds(pl.multiple_of(j * 512, 512), 512)
        u = mm(mixed[...], wes[:, cols])
        u2 = u * u
        t = jnp.tanh(u * (0.7978845608 + (0.7978845608 * 0.044715) * u2))
        half = 0.5 + 0.5 * t
        act[:, cols] = (u * half).astype(BF)
        slo[:, cols] = (half + half * (1.0 - t) * u * (0.7978845608 + (3 * 0.7978845608 * 0.044715) * u2)).astype(BF)

    save("active", act, active)
    save("slope", slo, slope)
    copies[5].wait()
    for i in range(2):
        r = slice(i * (n // 2), (i + 1) * (n // 2))
        alive = (lax.broadcasted_iota(jnp.int32, (n // 2, 1), 0) + i * (n // 2) < length[0]).astype(F32)
        b = alive * (hid[r] + mm(act[r], wrs[...]))
        blk[r] = b
        lws[r] = b.astype(BF)
        rws[r] = (b * rms_scale(b) * fg[...]).astype(BF)
    save("block", blk, block)
    save("rows", rws, rows)
    save("low", lws, low)
    for a in range(2):
        keep(heads - 2 + a, a).wait()
    for c in saved.values():
        c.wait()


def encode(length, x, ag, eg, fg, band, far, wq, wk, wv, wo, we, wr):
    n, width = x.shape
    ff = we.shape[1]
    heads = far.shape[0]
    sm = pl.BlockSpec(memory_space=pltpu.SMEM)
    vm = pl.BlockSpec(memory_space=pltpu.VMEM)
    hb = pl.BlockSpec(memory_space=pl.ANY)
    S = jax.ShapeDtypeStruct
    V = pltpu.VMEM
    full, tall, floats, broad = ((n, width), BF), ((width, n), BF), ((n, width), F32), ((n, ff), BF)
    return pl.pallas_call(
        encode_kernel,
        out_shape=tuple(S(*t) for t in (tall, full, full, full, ((heads, n, n), BF), tall, floats, tall,
                                        broad, broad, floats, full, full)),
        in_specs=[sm, vm, vm, vm, vm, vm, sm] + [hb] * 6,
        out_specs=(hb,) * 13,
        scratch_shapes=[V(w.shape, BF) for w in (wq, wk, wv, wo, we, wr)] + [V(*t) for t in (
            full, tall, full, full, full, tall, floats, full, tall, broad, broad, floats, full, full,
            ((128, n), BF), ((2, n, n), F32), ((2, n, n), BF))] + [
            pltpu.SemaphoreType.DMA((6,)), pltpu.SemaphoreType.DMA((2,)), pltpu.SemaphoreType.DMA((12,))],
        compiler_params=pltpu.CompilerParams(vmem_limit_bytes=60 * 1024 * 1024),
        name="encode",
    )(length, x, ag.reshape(1, -1), eg.reshape(1, -1), fg.reshape(1, -1), band, far, wq, wk, wv, wo, we, wr)


def gelu_parts(u):
    u2 = u * u
    t = jnp.tanh(u * (0.7978845608 + (0.7978845608 * 0.044715) * u2))
    half = 0.5 + 0.5 * t
    return u * half, half + half * (1.0 - t) * u * (0.7978845608 + (3 * 0.7978845608 * 0.044715) * u2)

def norm_down(v, r, g, dy):
    vr = v * r
    gd = g * dy
    return r * (gd - vr * jnp.mean(vr * gd, axis=-1, keepdims=True)), vr * dy

def decode_kernel(length, rows, dec_in, dec_cot, sg, cg, fg, *rest):
    hbm = rest[:8]
    (out, in_grad, gains, left, right, wide, mids, rows_grad) = rest[8:16]
    bufs = rest[16:24]
    sems = rest[24]
    sv, so, cq, ck, cv, co, fe, fr = bufs
    copies = [pltpu.make_async_copy(a, b, sems.at[i]) for i, (a, b) in enumerate(zip(hbm, bufs))]
    for c in copies:
        c.start()
    n, width = rows.shape
    heads = mids.shape[1]
    size = width // heads
    x = dec_in[...].astype(F32)
    cot = dec_cot[...]
    own = (lax.broadcasted_iota(jnp.int32, (heads, width), 1) // size
           == lax.broadcasted_iota(jnp.int32, (heads, width), 0))

    def spread(r):
        return jnp.where(own, r.astype(F32), 0.0).astype(BF)

    def collect(r):
        return jnp.sum(jnp.where(own, r, 0.0), axis=0, keepdims=True)

    x_r = rms_scale(x)
    self_normed = (x * x_r * sg[...]).astype(BF)
    copies[0].wait()
    self_values = mm(self_normed, sv[...]).astype(BF)
    copies[1].wait()
    after = x + mm(self_values, so[...])
    after_r = rms_scale(after)
    cross_normed = (after * after_r * cg[...]).astype(BF)
    copies[2].wait()
    cross_q = mm(cross_normed, cq[...]).astype(BF)
    copies[3].wait()
    q_rows = mm_t(spread(cross_q), ck[...]).astype(BF)
    s = mm_t(q_rows, rows[...])
    s = jnp.where(lax.broadcasted_iota(jnp.int32, s.shape, 1) < length[0], s, -1e30)
    e = jnp.exp(s - jnp.max(s, axis=-1, keepdims=True))
    probs = e / jnp.sum(e, axis=-1, keepdims=True)
    low = probs.astype(BF)
    mean_rows = mm(low, rows[...]).astype(BF)
    copies[4].wait()
    cross_context = collect(mm(mean_rows, cv[...])).astype(BF)
    copies[5].wait()
    middle = after + mm(cross_context, co[...])
    middle_r = rms_scale(middle)
    feed_normed = (middle * middle_r * fg[...]).astype(BF)
    copies[6].wait()
    active, slope = gelu_parts(mm(feed_normed, fe[...]))
    active = active.astype(BF)
    copies[7].wait()
    out[...] = (middle + mm(active, fr[...])).astype(BF)
    upper_grad = (slope * mm_t(cot, fr[...])).astype(BF)
    middle_down, feed_gain = norm_down(middle, middle_r, fg[...], mm_t(upper_grad, fe[...]))
    middle_grad = cot.astype(F32) + middle_down
    cross_branch = middle_grad.astype(BF)
    context_grad = mm_t(cross_branch, co[...]).astype(BF)
    g_rows = mm_t(spread(context_grad), cv[...]).astype(BF)
    prob_grad = mm_t(g_rows, rows[...])
    score_grad = (probs * (prob_grad - jnp.sum(probs * prob_grad, axis=-1, keepdims=True))).astype(BF)
    score_rows = mm(score_grad, rows[...]).astype(BF)
    pad = jnp.zeros((16 - heads % 16, n), BF)
    padw = jnp.zeros((16 - heads % 16, width), BF)
    rows_grad[...] = t_mm(jnp.concatenate([score_grad, pad, low, pad], axis=0),
                          jnp.concatenate([q_rows, padw, g_rows, padw], axis=0)).astype(BF)
    cross_q_grad = collect(mm(score_rows, ck[...])).astype(BF)
    after_down, cross_gain = norm_down(after, after_r, cg[...], mm_t(cross_q_grad, cq[...]))
    after_grad = middle_grad + after_down
    self_branch = after_grad.astype(BF)
    self_values_grad = mm_t(self_branch, so[...]).astype(BF)
    x_down, self_gain = norm_down(x, x_r, sg[...], mm_t(self_values_grad, sv[...]))
    in_grad[...] = (after_grad + x_down).astype(BF)
    gains[0:1, :] = self_gain
    gains[1:2, :] = cross_gain
    gains[2:3, :] = feed_gain
    for i, r in enumerate((self_normed, self_values, cross_normed, cross_context, feed_normed)):
        left[i:i + 1, :] = r.astype(F32)
    for i, r in enumerate((self_values_grad, self_branch, cross_q_grad, cross_branch, cross_q, context_grad, cot)):
        right[i:i + 1, :] = r.astype(F32)
    wide[0:1, :] = active.astype(F32)
    wide[1:2, :] = upper_grad.astype(F32)
    mids[0] = score_rows.astype(F32)
    mids[1] = mean_rows.astype(F32)

def decode(length, rows, dec_in, dec_cot, sg, cg, fg, heads, *weights):
    n, width = rows.shape
    ff = weights[6].shape[1]
    sm = pl.BlockSpec(memory_space=pltpu.SMEM)
    vm = pl.BlockSpec(memory_space=pltpu.VMEM)
    hb = pl.BlockSpec(memory_space=pl.ANY)
    S = jax.ShapeDtypeStruct
    return pl.pallas_call(
        decode_kernel,
        out_shape=(S((1, width), BF), S((1, width), BF), S((3, width), F32), S((5, width), F32), S((7, width), F32),
                   S((2, ff), F32), S((2, heads, width), F32), S((n, width), BF)),
        in_specs=[sm] + [vm] * 6 + [hb] * 8,
        out_specs=(vm,) * 8,
        scratch_shapes=[pltpu.VMEM(w.shape, BF) for w in weights] + [pltpu.SemaphoreType.DMA((8,))],
        compiler_params=pltpu.CompilerParams(vmem_limit_bytes=60 * 1024 * 1024),
        name="decode",
    )(length, rows, dec_in, dec_cot, sg.reshape(1, -1), cg.reshape(1, -1), fg.reshape(1, -1), *weights)


def feed_back_kernel(length, rows_grad, block, cot, fg, hidden, eg, mixed, active, slope, wr, we,
                     wide, tall, hidden_grad, branch, gains, wrs, wes, bg, rb, rb_t, ug, mixed_t, dmixed, sems):
    n, width = block.shape
    ff = active.shape[1]
    groups, lanes = tall.shape[3], tall.shape[5]
    cols_dev = width // 4
    copies = [pltpu.make_async_copy(a, b, sems.at[i]) for i, (a, b) in enumerate(((wr, wrs), (we, wes)))]
    for c in copies:
        c.start()
    gains[...] = jnp.zeros_like(gains)

    @pl.loop(0, n // 128)
    def _(i):
        r = pl.ds(i * 128, 128)
        alive = (lax.broadcasted_iota(jnp.int32, (128, 1), 0) + i * 128 < length[0]).astype(F32)
        v = block[r]
        down, gain = norm_down(v, rms_scale(v), fg[...], rows_grad[r].astype(F32))
        b = alive * (cot[r].astype(F32) + down)
        bg[r] = b
        rb[r] = b.astype(BF)
        rb_t[:, pl.ds(pl.multiple_of(i * 128, 128), 128)] = b.T.astype(BF)
        mixed_t[:, pl.ds(pl.multiple_of(i * 128, 128), 128)] = mixed[r].T
        gains[0:1, :] += jnp.sum(gain, axis=0, keepdims=True)

    copies[0].wait()

    @pl.loop(0, ff // 256)
    def _(j):
        cols = pl.ds(pl.multiple_of(j * 256, 256), 256)
        ug[:, cols] = (slope[:, cols].astype(F32) * mm_t(rb[...], wrs[cols, :])).astype(BF)

    copies[1].wait()

    @pl.loop(0, width // 256)
    def _(j):
        cols = pl.ds(pl.multiple_of(j * 256, 256), 256)
        dmixed[:, cols] = mm_t(ug[...], wes[cols, :])

    @pl.loop(0, n // 128)
    def _(i):
        r = pl.ds(i * 128, 128)
        v = hidden[r]
        down, gain = norm_down(v, rms_scale(v), eg[...], dmixed[r])
        h = bg[r] + down
        hidden_grad[r] = h
        branch[r] = h.astype(BF)
        gains[1:2, :] += jnp.sum(gain, axis=0, keepdims=True)

    @pl.loop(0, 4)
    def _(j):
        for half in range(2):
            cols = pl.ds(pl.multiple_of(j * (ff // 4) + half * (ff // 8), 128), ff // 8)
            wide[half, lax.rem(j, 2), j // 2] = mm(mixed_t[...], ug[:, cols]).astype(BF)

    chunk = ff // 8
    per_group = lanes // chunk

    @pl.loop(0, 8)
    def _(i):
        cols = pl.ds(pl.multiple_of(i * chunk, 128), chunk)
        g = mm(rb_t[...], active[:, cols]).astype(BF)
        for j in range(4):
            for half in range(2):
                r = j * cols_dev + half * (cols_dev // 2)
                part = g[r:r + cols_dev // 2]
                if per_group == 1:
                    tall[half, j % 2, j // 2, i] = part
                else:
                    tall[half, j % 2, j // 2, 0, :, cols] = part


def feed_back(groups, length, rows_grad, block, cot, fg, hidden, eg, mixed, active, slope, wr, we):
    n, width = block.shape
    ff = active.shape[1]
    sm = pl.BlockSpec(memory_space=pltpu.SMEM)
    vm = pl.BlockSpec(memory_space=pltpu.VMEM)
    hb = pl.BlockSpec(memory_space=pl.ANY)
    S = jax.ShapeDtypeStruct
    V = pltpu.VMEM
    return pl.pallas_call(
        feed_back_kernel,
        out_shape=(S((2, 2, 2, width, ff // 8), BF),
                   S((2, 2, 2, groups, width // 8, ff // groups), BF), S((n, width), F32), S((n, width), BF), S((2, width), F32)),
        in_specs=[sm] + [vm] * 9 + [hb] * 2,
        out_specs=(vm,) * 5,
        scratch_shapes=[V(wr.shape, BF), V(we.shape, BF), V((n, width), F32), V((n, width), BF), V((width, n), BF),
                        V((n, ff), BF), V((width, n), BF), V((n, width), F32), pltpu.SemaphoreType.DMA((2,))],
        compiler_params=pltpu.CompilerParams(vmem_limit_bytes=60 * 1024 * 1024),
        name="feed_back",
    )(length, rows_grad, block, cot, fg.reshape(1, -1), hidden, eg.reshape(1, -1), mixed, active, slope, wr, we)


def backward_kernel(np_, ns, x, ag, q, k, v, context_t, branch, hidden_grad, normed, gains_dec, gains_feed,
                    probs, wo, wq, wk, wv, wide, tall, dec, encoded,
                    red, small_out, dec_out, enc_out, grad_out,
                    wos, wqs, wks, wvs, d_out, dp, ds, dq_t, dq, dk, dv, k_t, normed_t, ng, in_grad,
                    pbuf, band, diag, own, au, r0, r1y, r1x, r1a, r2, r3, sm, smr, smz,
                    psem, wsem, loc, c_s, c_r, a_s, a_r, b_s, b_r, ac_s, ac_r, ax_s, ax_r, z_s, z_r,
                    m_s, m_r, mz_s, mz_r, d_s, d_r, e_s, e_r, g_s, g_r):
    n, width = x.shape
    heads = probs.shape[0]
    nz = np_ // 2
    rows, lanes = r0.shape[4:]
    count = np_ * ns
    p = lax.axis_index("pairs")
    s = lax.axis_index("seq")
    c = lax.rem(s, 2)
    y = s // 2
    xx = lax.rem(p, 2)
    z = p // 2
    me = p * ns + s
    core_peer = (p, s + 1 - 2 * c)
    y_peer = (p, lax.rem(s + 2, 4))
    x_peer = (p + 1 - 2 * xx, s)

    def place(d):
        lin = lax.rem(me + d, count)
        return (lin // ns, lax.rem(lin, ns))

    barrier = pltpu.get_barrier_semaphore()

    @pl.loop(1, count)
    def _(d):
        pl.semaphore_signal(barrier, inc=1, device_id=place(d), device_id_type=MESH)

    def remote(src, dst, send, recv, peer):
        return pltpu.make_async_remote_copy(
            src_ref=src, dst_ref=dst, send_sem=send, recv_sem=recv,
            device_id=peer, device_id_type=MESH)

    weights = [pltpu.make_async_copy(a, b, wsem.at[i])
               for i, (a, b) in enumerate(((wo, wos), (wq, wqs), (wk, wks), (wv, wvs)))]

    def fetch(h, slot):
        return pltpu.make_async_copy(probs.at[h], pbuf.at[slot], psem.at[slot])

    def unit(i, core):
        return (wide, tall)[i // 2].at[i % 2, core]

    def core_copy(i):
        return remote(unit(i, 1 - c), r0.at[i], c_s.at[i], c_r.at[i], core_peer)

    def own_copy(i):
        return pltpu.make_async_copy(unit(i, c), own.at[i], loc.at[i])

    def first(i):
        if i % 2 == 0:
            return remote(own.at[i, 1 - y], r1y.at[i // 2], a_s.at[i], a_r.at[i], y_peer)
        return remote(own.at[i, :, :, 1 - xx], r1x.at[i // 2], a_s.at[i], a_r.at[i], x_peer)

    def second(i):
        if i % 2 == 0:
            return remote(own.at[i, y, :, 1 - xx], r2.at[i], b_s.at[i], b_r.at[i], x_peer)
        return remote(own.at[i, 1 - y, :, xx], r2.at[i], b_s.at[i], b_r.at[i], y_peer)

    def final(i):
        return own.at[i, y] if i < 4 else au.at[i - 4, c, y]

    def last(i, d):
        t = lax.rem(z + d, nz)
        return remote(final(i).at[t, xx], r3.at[i, d], z_s.at[i, d], z_r.at[i, d], (t * 2 + xx, s))

    def attn_core(w, half):
        return remote(au.at[w, 1 - c, half], r0.at[4 + w, half], ac_s.at[w, half], ac_r.at[w, half], core_peer)

    def attn_x(w, half):
        return remote(au.at[w, c, half, :, 1 - xx], r1a.at[w, half], ax_s.at[w, half], ax_r.at[w, half], x_peer)

    def attn_y(w):
        return remote(au.at[w, c, 1 - y, :, xx], r2.at[4 + w], b_s.at[4 + w], b_r.at[4 + w], y_peer)

    def dec_copy(d):
        to = place(d)
        return remote(dec.at[to[0] * ns + to[1]], dec_out.at[me], d_s.at[d], d_r.at[d], to)

    def enc_copy(d):
        t = lax.rem(s + d, ns)
        return remote(encoded.at[t], enc_out.at[s], e_s.at[d], e_r.at[d], (p, t))

    def grad_copy(d):
        t = lax.rem(s + d, ns)
        return remote(in_grad.at[t], grad_out.at[s], g_s.at[d], g_r.at[d], (p, t))

    keep_dec = pltpu.make_async_copy(dec.at[me], dec_out.at[me], loc.at[4])
    keep_enc = pltpu.make_async_copy(encoded.at[s], enc_out.at[s], loc.at[5])
    keep_grad = pltpu.make_async_copy(in_grad.at[s], grad_out.at[s], loc.at[6])

    def step_a(i):
        core_copy(i).wait()
        own_copy(i).wait()

        @pl.loop(0, nz)
        def _(b):
            for a in range(2):
                for e in range(2):
                    own[i, a, b, e] = own[i, a, b, e] + r0[i, a, b, e]

        first(i).start()

    def step_b(i):
        first(i).wait()

        @pl.loop(0, nz)
        def _(b):
            for e in range(2):
                if i % 2 == 0:
                    own[i, y, b, e] = own[i, y, b, e] + r1y[i // 2, b, e]
                else:
                    own[i, e, b, xx] = own[i, e, b, xx] + r1x[i // 2, e, b]

        second(i).start()

    def step_c(i):
        if i < 4:
            second(i).wait()
        else:
            attn_y(i - 4).wait()

        @pl.loop(0, nz)
        def _(b):
            f = final(i)
            f[b, xx] = f[b, xx] + r2[i, b]

        @pl.loop(1, nz)
        def _(d):
            last(i, d).start()

    def step_d(i):
        red[i] = final(i)[z, xx].astype(F32)

        @pl.loop(1, nz)
        def _(d):
            last(i, d).wait()
            red[i] = red[i] + r3[i, d].astype(F32)

    def attn_a(w, half):
        attn_core(w, half).wait()

        @pl.loop(0, nz)
        def _(b):
            for e in range(2):
                au[w, c, half, b, e] = au[w, c, half, b, e] + r0[4 + w, half, b, e]

        attn_x(w, half).start()

    def attn_b(w, half):
        attn_x(w, half).wait()

        @pl.loop(0, nz)
        def _(b):
            au[w, c, half, b, xx] = au[w, c, half, b, xx] + r1a[w, half, b]

    for copy in weights:
        copy.start()
    first_half, last_half = 1 - y, y
    fetch(first_half * (heads // 2), 0).start()
    fetch(first_half * (heads // 2) + 1, 1).start()
    for i in range(4):
        own_copy(i).start()
    keep_dec.start()
    keep_enc.start()
    diag[...] = jnp.zeros_like(diag)
    weights[0].wait()

    @pl.loop(0, width // 384)
    def _(j):
        cols = pl.ds(pl.multiple_of(j * 384, 128), 384)
        d_out[:, cols] = mm_t(branch[...], wos[cols, :]).astype(BF)

    pl.semaphore_wait(barrier, count - 1)
    for i in range(4):
        core_copy(i).start()
    for d in range(1, ns):
        enc_copy(d).start()

    @pl.loop(1, count)
    def _(d):
        dec_copy(d).start()

    @pl.loop(0, n // 128)
    def _(i):
        r = pl.ds(pl.multiple_of(i * 128, 128), 128)
        normed_t[:, r] = normed[r].T

    lane = lax.broadcasted_iota(jnp.int32, (n, 128), 1)
    lane_s = lax.broadcasted_iota(jnp.int32, (128, 128), 1)
    row_s = lax.broadcasted_iota(jnp.int32, (128, 128), 0)

    def pair(half, g):
        cols = pl.ds(pl.multiple_of(half * (width // 2) + g * 128, 128), 128)
        k_t[...] = k[:, cols].T
        dop = d_out[:, cols]
        qp = q[:, cols]
        vp = v[:, cols]
        zero = jnp.zeros_like(qp)
        for a in range(2):
            h = half * (heads // 2) + 2 * g + a
            mine = (lane < 64) if a == 0 else (lane >= 64)
            dp[...] = mm_t(jnp.where(mine, vp, zero), dop)
            fetch(h, a).wait()
            for j in range(n // 128):
                pj = pbuf[a, :, j * 128:(j + 1) * 128].astype(F32)
                pd = pj * dp[:, j * 128:(j + 1) * 128]
                total = jnp.sum(pd, axis=0, keepdims=True)
                sg = pd - pj * total
                ds[:, j * 128:(j + 1) * 128] = sg.astype(BF)
                for i in range(n // 128):
                    t = sg[i * 128:(i + 1) * 128]
                    if abs(i - j) <= 1:
                        b = (i - j + 1) * 128
                        if j == 0 or (j == 1 and i == 0):
                            band[b:b + 128, :] = t
                        else:
                            band[b:b + 128, :] += t
                    else:
                        f = 5 if i > j else 4
                        diag[h, f:f + 1, :] += jnp.sum(t, axis=0, keepdims=True)
            dvp = mm(pbuf[a], jnp.where(mine, dop, zero))
            dkp = mm(ds[...], jnp.where(mine, qp, zero))
            dq_t[pl.ds(pl.multiple_of(h * 64, 64), 64), :] = mm(k_t[a * 64:(a + 1) * 64, :], ds[...]).astype(BF)
            if a == 0:
                dk_sum, dv_sum = dkp, dvp
            else:
                dk[:, cols] = (dk_sum + dkp).astype(BF)
                dv[:, cols] = (dv_sum + dvp).astype(BF)
            for b in range(3):
                t = band[b * 128:(b + 1) * 128, :]
                for bit in range(7):
                    t = jnp.where((row_s >> bit) % 2 == 1, pltpu.roll(t, 128 - (1 << bit), 1), t)
                straight = jnp.sum(jnp.where(lane_s + row_s < 128, t, 0.0), axis=0, keepdims=True)
                whole = jnp.sum(t, axis=0, keepdims=True)
                diag[h, b:b + 1, :] += straight
                diag[h, b + 1:b + 2, :] += whole - straight

    part = width // 4

    def units_of(half):
        cols = pl.ds(pl.multiple_of(half * (width // 2), 128), width // 2)
        lower = pl.ds(pl.multiple_of(half * (width // 2), 128), width // 2)
        dq_h = dq_t[lower, :].T
        dq[:, cols] = dq_h
        dk_h = dk[:, cols]
        dv_h = dv[:, cols]
        br_h = branch[:, cols]
        zero = jnp.zeros((n, part), BF)
        for cc in range(2):
            e = slice(cc * part, (cc + 1) * part)
            g = mm(normed_t[...], jnp.concatenate([dq_h[:, e], dk_h[:, e]], axis=1))
            au[0, cc, half] = g.astype(BF).reshape(nz, 2, rows, lanes)
            g = (mm(normed_t[...], jnp.concatenate([dv_h[:, e], zero], axis=1))
                 + mm(context_t[...], jnp.concatenate([zero, br_h[:, e]], axis=1)))
            au[1, cc, half] = g.astype(BF).reshape(nz, 2, rows, lanes)
        for w in range(2):
            attn_core(w, half).start()

    quarter = heads // 4

    @pl.loop(0, quarter)
    def _(g):
        pair(first_half, g)
        nxt = jnp.where(g == quarter - 1, last_half * (heads // 2), first_half * (heads // 2) + 2 * (g + 1))
        fetch(nxt, 0).start()
        fetch(nxt + 1, 1).start()

        @pl.when(g == 0)
        def _():
            step_a(0)
            step_a(1)

        @pl.when(g == 1)
        def _():
            step_a(2)
            step_a(3)

    units_of(first_half)

    @pl.loop(0, quarter)
    def _(g):
        pair(last_half, g)

        @pl.when(g < quarter - 1)
        def _():
            nxt = last_half * (heads // 2) + 2 * (g + 1)
            fetch(nxt, 0).start()
            fetch(nxt + 1, 1).start()

        @pl.when(g == 0)
        def _():
            attn_a(0, first_half)
            attn_a(1, first_half)

        @pl.when(g == 1)
        def _():
            step_b(0)
            step_b(1)

    units_of(last_half)
    for copy in weights[1:]:
        copy.wait()

    @pl.loop(0, 2)
    def _(i):
        r = pl.ds(pl.multiple_of(i * (n // 2), 128), n // 2)
        ng[r] = mm_t(dq[r], wqs[...]) + mm_t(dk[r], wks[...]) + mm_t(dv[r], wvs[...])

    attn_a(0, last_half)
    attn_a(1, last_half)
    sm[...] = jnp.zeros_like(sm)
    slot_rows = n // ns
    gain_sum = jnp.zeros((1, width), F32)
    for i in range(ns):
        r = slice(i * slot_rows, (i + 1) * slot_rows)
        t = x[r].astype(F32)
        down, gain = norm_down(t, rms_scale(t), ag[...], ng[r])
        in_grad[i] = (hidden_grad[r] + down).astype(BF)
        gain_sum = gain_sum + jnp.sum(gain, axis=0, keepdims=True)
    keep_grad.start()
    for d in range(1, ns):
        grad_copy(d).start()

    col = lax.broadcasted_iota(jnp.int32, (128, width), 1)
    offset = (col // 128 - 1) * 128 - lax.rem(col, 128)
    offset = jnp.where(col >= width - 128, 256, jnp.where(col >= width - 256, -256, offset))
    dist = jnp.abs(offset)
    bucket = jnp.full_like(dist, 8)
    for edge in EDGES:
        bucket = bucket + (dist >= edge).astype(jnp.int32)
    bucket = jnp.where(dist < 8, dist, bucket) + jnp.where(offset > 0, 16, 0)
    pick = jnp.where(bucket == lax.broadcasted_iota(jnp.int32, (128, width), 0), 1.0, 0.0)
    bias = jnp.zeros((16, 128), F32)
    for i in range(width // 128):
        bias = bias + lax.dot_general(diag[:, i, :], pick[:, i * 128:(i + 1) * 128], (((1,), (1,)), ((), ())),
                                      precision=HIGHEST, preferred_element_type=F32)
    sm[0, 40:56, :] = bias
    gains = [gains_dec[i:i + 1, :] for i in range(3)] + [gains_feed[i:i + 1, :] for i in range(2)] + [gain_sum]
    for i, gain in enumerate(gains):
        for j in range(width // 128):
            sm[0, i * 6 + j:i * 6 + j + 1, :] = gain[:, j * 128:(j + 1) * 128]

    def small_copy(i):
        return remote(sm.at[i], smr.at[i], m_s.at[i], m_r.at[i], (core_peer, y_peer, x_peer)[i])

    def z_small(d):
        return remote(smz.at[z], smz.at[z], mz_s.at[d], mz_r.at[d], (lax.rem(z + d, nz) * 2 + xx, s))

    small_copy(0).start()
    step_b(2)
    step_b(3)
    small_copy(0).wait()
    sm[1] = sm[0] + smr[0]
    small_copy(1).start()
    attn_b(0, first_half)
    attn_y(0).start()
    attn_b(1, first_half)
    attn_y(1).start()
    step_c(0)
    step_c(1)
    small_copy(1).wait()
    sm[2] = sm[1] + smr[1]
    small_copy(2).start()
    step_c(2)
    step_c(3)
    attn_b(0, last_half)
    small_copy(2).wait()
    smz[z] = sm[2] + smr[2]

    @pl.loop(1, nz)
    def _(d):
        z_small(d).start()

    step_c(4)
    attn_b(1, last_half)
    step_c(5)
    for i in range(6):
        step_d(i)

    @pl.loop(1, nz)
    def _(d):
        z_small(d).wait()

    small_out[...] = smz[0]

    @pl.loop(1, nz)
    def _(d):
        small_out[...] = small_out[...] + smz[d]

    keep_dec.wait()
    keep_enc.wait()
    keep_grad.wait()
    for d in range(1, ns):
        enc_copy(d).wait()
        grad_copy(d).wait()

    @pl.loop(1, count)
    def _(d):
        dec_copy(d).wait()


def backward(np_, ns, x, ag, q, k, v, context_t, branch, hidden_grad, normed, gains_dec, gains_feed,
             probs, wo, wq, wk, wv, wide, tall, dec, encoded):
    n, width = x.shape
    heads = probs.shape[0]
    nz = np_ // 2
    rows, lanes = wide.shape[5:]
    count = np_ * ns
    padded = normed.shape[1]
    vm = pl.BlockSpec(memory_space=pltpu.VMEM)
    hb = pl.BlockSpec(memory_space=pl.ANY)
    S = jax.ShapeDtypeStruct
    V = pltpu.VMEM
    dma = pltpu.SemaphoreType.DMA
    nar = V((n, width), BF)
    square = V((width, width), BF)
    slots = (ns, n // ns, width)
    small = (64, 128)
    return pl.pallas_call(
        functools.partial(backward_kernel, np_, ns),
        out_shape=(S((6, rows, lanes), F32), S(small, F32), S(dec.shape, BF), S(slots, BF), S(slots, BF)),
        in_specs=[vm] * 11 + [hb] * 9,
        out_specs=(vm, vm, hb, hb, hb),
        scratch_shapes=[
            square, square, square, square, nar, V((n, n), F32), V((n, n), BF), V((width, n), BF), nar, nar, nar,
            V((128, n), BF), V((padded, n), BF), V((n, width), F32), V(slots, BF),
            V((2, n, n), BF), V((384, 128), F32), V((16, 8, 128), F32),
            V((4, 2, nz, 2, rows, lanes), BF), V((2, 2, 2, nz, 2, rows, lanes), BF), V((6, 2, nz, 2, rows, lanes), BF),
            V((2, nz, 2, rows, lanes), BF), V((2, 2, nz, rows, lanes), BF), V((2, 2, nz, rows, lanes), BF),
            V((6, nz, rows, lanes), BF), V((6, nz, rows, lanes), BF),
            V((3,) + small, F32), V((3,) + small, F32), V((nz,) + small, F32),
            dma((2,)), dma((4,)), dma((7,)), dma((4,)), dma((4,)), dma((4,)), dma((4,)), dma((6,)), dma((6,)),
            dma((2, 2)), dma((2, 2)), dma((2, 2)), dma((2, 2)), dma((6, nz)), dma((6, nz)),
            dma((3,)), dma((3,)), dma((nz,)), dma((nz,)), dma((count,)), dma((count,)),
            dma((ns,)), dma((ns,)), dma((ns,)), dma((ns,)),
        ],
        compiler_params=pltpu.CompilerParams(
            collective_id=0, has_side_effects=True, vmem_limit_bytes=62 * 1024 * 1024),
        name="backward",
    )(x, ag.reshape(1, -1), q, k, v, context_t, branch, hidden_grad, normed, gains_dec, gains_feed,
      probs, wo, wq, wk, wv, wide, tall, dec, encoded.reshape(slots))


def fused_kernel(np_, ns, length, fg, eg, ag, gains_dec,
                 rows_grad, block, cot, wr, active, wide_w, hidden, slope, mixed_t_in, wo, wq, wk, wv, q_in, k_in,
                 v_in, x_in, normed_t_in, context_t_in, probs, dec, encoded,
                 red, small_out, dec_out, enc_out, grad_out,
                 acts, grads, w1, wes, bg, hid, dm, rg, ct, rb, rb_t, mixed_t, normed_t, context_t,
                 dp, ds, pbuf, k_t, band, diag, fu, r0, r1y, r1x, r1a, r2, r3, sm, smr, smz,
                 psem, isem, loc, c_s, c_r, a_s, a_r, b_s, b_r, ac_s, ac_r, ax_s, ax_r, z_s, z_r,
                 m_s, m_r, mz_s, mz_r, d_s, d_r, e_s, e_r, g_s, g_r):
    n, width = hid.shape
    ff = acts.shape[1]
    heads = probs.shape[0]
    nz = np_ // 2
    rows, lanes = r0.shape[4:]
    count = np_ * ns
    p = lax.axis_index("pairs")
    s = lax.axis_index("seq")
    c = lax.rem(s, 2)
    y = s // 2
    xx = lax.rem(p, 2)
    z = p // 2
    me = p * ns + s
    core_peer = (p, s + 1 - 2 * c)
    y_peer = (p, lax.rem(s + 2, 4))
    x_peer = (p + 1 - 2 * xx, s)

    def place(d):
        lin = lax.rem(me + d, count)
        return (lin // ns, lax.rem(lin, ns))

    barrier = pltpu.get_barrier_semaphore()

    @pl.loop(1, count)
    def _(d):
        pl.semaphore_signal(barrier, inc=1, device_id=place(d), device_id_type=MESH)

    def remote(src, dst, send, recv, peer):
        return pltpu.make_async_remote_copy(
            src_ref=src, dst_ref=dst, send_sem=send, recv_sem=recv,
            device_id=peer, device_id_type=MESH)

    def load(i, src, dst):
        return pltpu.make_async_copy(src, dst, isem.at[i])

    def part_of(ref, i):
        return ref.at[:, pl.ds(i * width, width)]

    loads = [load(i, a, b) for i, (a, b) in enumerate((
        (rows_grad, rg), (block, bg), (cot, ct), (active, acts), (wr, w1), (slope, grads), (mixed_t_in, mixed_t),
        (wide_w, wes), (hidden, hid), (normed_t_in, normed_t), (context_t_in, context_t)))]
    weights = [load(11 + i, a, w1.at[pl.ds(i * width, width)]) for i, a in enumerate((wo, wq, wk, wv))]
    heads_in = [load(15 + i, a, part_of(grads, i)) for i, a in enumerate((q_in, k_in, v_in, x_in))]
    d_out, dq, dk, dv = (part_of(acts, i) for i in range(4))
    q, k, v, x = (part_of(grads, i) for i in range(4))
    branch, dq_t, ng, in_grad, hidden_grad = ct, rb_t, dm, rg, bg
    wos, wqs, wks, wvs = (w1.at[pl.ds(i * width, width)] for i in range(4))

    def fetch(h, slot):
        return pltpu.make_async_copy(probs.at[h], pbuf.at[slot], psem.at[slot])

    own = fu.at[c]

    def au(w, core, half):
        return fu.at[1 - c, 2 * w + core, half]

    def core_copy(i):
        return remote(fu.at[1 - c, i], r0.at[i], c_s.at[i], c_r.at[i], core_peer)

    def first(i):
        if i % 2 == 0:
            return remote(own.at[i, 1 - y], r1y.at[i // 2], a_s.at[i], a_r.at[i], y_peer)
        return remote(own.at[i, :, :, 1 - xx], r1x.at[i // 2], a_s.at[i], a_r.at[i], x_peer)

    def second(i):
        if i % 2 == 0:
            return remote(own.at[i, y, :, 1 - xx], r2.at[i], b_s.at[i], b_r.at[i], x_peer)
        return remote(own.at[i, 1 - y, :, xx], r2.at[i], b_s.at[i], b_r.at[i], y_peer)

    def final(i):
        return own.at[i, y] if i < 4 else au(i - 4, c, y)

    def last(i, d):
        t = lax.rem(z + d, nz)
        return remote(final(i).at[t, xx], r3.at[i, d], z_s.at[i, d], z_r.at[i, d], (t * 2 + xx, s))

    def attn_core(w, half):
        return remote(au(w, 1 - c, half), r0.at[4 + w, half], ac_s.at[w, half], ac_r.at[w, half], core_peer)

    def attn_x(w, half):
        return remote(au(w, c, half).at[:, 1 - xx], r1a.at[w, half], ax_s.at[w, half], ax_r.at[w, half], x_peer)

    def attn_y(w):
        return remote(au(w, c, 1 - y).at[:, xx], r2.at[4 + w], b_s.at[4 + w], b_r.at[4 + w], y_peer)

    def dec_copy(d):
        to = place(d)
        return remote(dec.at[to[0] * ns + to[1]], dec_out.at[me], d_s.at[d], d_r.at[d], to)

    def enc_copy(d):
        t = lax.rem(s + d, ns)
        return remote(encoded.at[t], enc_out.at[s], e_s.at[d], e_r.at[d], (p, t))

    def grad_copy(d):
        t = lax.rem(s + d, ns)
        return remote(in_grad.at[t], grad_out.at[s], g_s.at[d], g_r.at[d], (p, t))

    keep_dec = pltpu.make_async_copy(dec.at[me], dec_out.at[me], loc.at[4])
    keep_enc = pltpu.make_async_copy(encoded.at[s], enc_out.at[s], loc.at[5])
    keep_grad = pltpu.make_async_copy(in_grad.at[s], grad_out.at[s], loc.at[6])

    def step_a(i):
        core_copy(i).wait()

        @pl.loop(0, nz)
        def _(b):
            for a in range(2):
                for e in range(2):
                    own[i, a, b, e] = own[i, a, b, e] + r0[i, a, b, e]

        first(i).start()

    def step_b(i):
        first(i).wait()

        @pl.loop(0, nz)
        def _(b):
            for e in range(2):
                if i % 2 == 0:
                    own[i, y, b, e] = own[i, y, b, e] + r1y[i // 2, b, e]
                else:
                    own[i, e, b, xx] = own[i, e, b, xx] + r1x[i // 2, e, b]

        second(i).start()

    def step_c(i):
        if i < 4:
            second(i).wait()
        else:
            attn_y(i - 4).wait()

        @pl.loop(0, nz)
        def _(b):
            f = final(i)
            f[b, xx] = f[b, xx] + r2[i, b]

        @pl.loop(1, nz)
        def _(d):
            last(i, d).start()

    def step_d(i):
        red[i] = final(i)[z, xx].astype(F32)

        @pl.loop(1, nz)
        def _(d):
            last(i, d).wait()
            red[i] = red[i] + r3[i, d].astype(F32)

    def attn_a(w, half):
        attn_core(w, half).wait()

        @pl.loop(0, nz)
        def _(b):
            for e in range(2):
                u = au(w, c, half)
                u[b, e] = u[b, e] + r0[4 + w, half, b, e]

        attn_x(w, half).start()

    def attn_b(w, half):
        attn_x(w, half).wait()

        @pl.loop(0, nz)
        def _(b):
            u = au(w, c, half)
            u[b, xx] = u[b, xx] + r1a[w, half, b]

    for copy in loads:
        copy.start()
    first_half, last_half = 1 - y, y
    fetch(first_half * (heads // 2), 0).start()
    fetch(first_half * (heads // 2) + 1, 1).start()
    keep_dec.start()
    keep_enc.start()
    diag[...] = jnp.zeros_like(diag)
    slot_rows = n // ns
    sm[...] = jnp.zeros_like(sm)

    def put_gain(i, gain):
        for j in range(width // 128):
            sm[0, i * 6 + j:i * 6 + j + 1, :] = gain[:, j * 128:(j + 1) * 128]

    for i in range(3):
        put_gain(i, gains_dec[i:i + 1, :])
    for i in range(3):
        loads[i].wait()
    final_gain = jnp.zeros((1, width), F32)
    for i in range(ns):
        r = slice(i * slot_rows, (i + 1) * slot_rows)
        alive = (lax.broadcasted_iota(jnp.int32, (slot_rows, 1), 0) + i * slot_rows < length[0]).astype(F32)
        b = bg[r]
        down, gain = norm_down(b, rms_scale(b), fg[...], rg[i].astype(F32))
        b = alive * (ct[r].astype(F32) + down)
        bg[r] = b
        low = b.astype(BF)
        rb[r] = low
        rb_t[:, r] = low.T
        final_gain = final_gain + jnp.sum(gain, axis=0, keepdims=True)
    put_gain(3, final_gain)
    pl.semaphore_wait(barrier, count - 1)
    for d in range(1, ns):
        enc_copy(d).start()

    @pl.loop(1, count)
    def _(d):
        dec_copy(d).start()

    part = width // 4
    loads[3].wait()

    @pl.loop(0, nz)
    def _(b):
        cols = pl.ds(pl.multiple_of(b * 2 * lanes, 128), 2 * lanes)
        g = mm(rb_t[...], acts[:, cols]).astype(BF)
        for j in range(4):
            for half in range(2):
                lo = j * part + half * rows
                for e in range(2):
                    fu[j % 2, 2 + half, j // 2, b, e] = g[lo:lo + rows, e * lanes:(e + 1) * lanes]

    core_copy(2).start()
    core_copy(3).start()
    loads[4].wait()
    loads[5].wait()

    @pl.loop(0, ff // width)
    def _(j):
        cols = pl.ds(pl.multiple_of(j * width, 128), width)
        grads[:, cols] = (grads[:, cols].astype(F32) * mm_t(rb[...], w1[cols, :])).astype(BF)

    for copy in weights:
        copy.start()
    step_a(2)
    step_a(3)
    loads[6].wait()

    @pl.loop(0, 4)
    def _(j):
        cols = pl.ds(pl.multiple_of(j * 2 * lanes, 128), 2 * lanes)
        g = mm(mixed_t[...], grads[:, cols]).astype(BF)
        for half in range(2):
            fu[lax.rem(j, 2), half, j // 2] = g[:, half * lanes:(half + 1) * lanes].reshape(nz, 2, rows, lanes)

    core_copy(0).start()
    core_copy(1).start()
    loads[7].wait()
    dm[...] = mm_t(grads[...], wes[...])
    for copy in heads_in:
        copy.start()
    step_a(0)
    step_a(1)
    loads[8].wait()
    expand_gain = jnp.zeros((1, width), F32)
    for i in range(ns):
        r = slice(i * slot_rows, (i + 1) * slot_rows)
        t = hid[r]
        down, gain = norm_down(t, rms_scale(t), eg[...], dm[r])
        t = bg[r] + down
        bg[r] = t
        branch[r] = t.astype(BF)
        expand_gain = expand_gain + jnp.sum(gain, axis=0, keepdims=True)
    put_gain(4, expand_gain)
    weights[0].wait()

    @pl.loop(0, width // 384)
    def _(j):
        cols = pl.ds(pl.multiple_of(j * 384, 128), 384)
        d_out[:, cols] = mm_t(branch[...], w1[cols, :]).astype(BF)

    for copy in heads_in:
        copy.wait()
    for copy in loads[9:]:
        copy.wait()

    lane = lax.broadcasted_iota(jnp.int32, (n, 128), 1)
    lane_s = lax.broadcasted_iota(jnp.int32, (128, 128), 1)
    row_s = lax.broadcasted_iota(jnp.int32, (128, 128), 0)

    def pair(half, g):
        cols = pl.ds(pl.multiple_of(half * (width // 2) + g * 128, 128), 128)
        k_t[...] = k[:, cols].T
        dop = d_out[:, cols]
        qp = q[:, cols]
        vp = v[:, cols]
        zero = jnp.zeros_like(qp)
        for a in range(2):
            h = half * (heads // 2) + 2 * g + a
            mine = (lane < 64) if a == 0 else (lane >= 64)
            dp[...] = mm_t(jnp.where(mine, vp, zero), dop)
            fetch(h, a).wait()
            for j in range(n // 128):
                pj = pbuf[a, :, j * 128:(j + 1) * 128].astype(F32)
                pd = pj * dp[:, j * 128:(j + 1) * 128]
                total = jnp.sum(pd, axis=0, keepdims=True)
                sg = pd - pj * total
                ds[:, j * 128:(j + 1) * 128] = sg.astype(BF)
                for i in range(n // 128):
                    t = sg[i * 128:(i + 1) * 128]
                    if abs(i - j) <= 1:
                        b = (i - j + 1) * 128
                        if j == 0 or (j == 1 and i == 0):
                            band[b:b + 128, :] = t
                        else:
                            band[b:b + 128, :] += t
                    else:
                        f = 5 if i > j else 4
                        diag[h, f:f + 1, :] += jnp.sum(t, axis=0, keepdims=True)
            dvp = mm(pbuf[a], jnp.where(mine, dop, zero))
            dkp = mm(ds[...], jnp.where(mine, qp, zero))
            dq_t[pl.ds(pl.multiple_of(h * 64, 64), 64), :] = mm(k_t[a * 64:(a + 1) * 64, :], ds[...]).astype(BF)
            if a == 0:
                dk_sum, dv_sum = dkp, dvp
            else:
                dk[:, cols] = (dk_sum + dkp).astype(BF)
                dv[:, cols] = (dv_sum + dvp).astype(BF)
            for b in range(3):
                t = band[b * 128:(b + 1) * 128, :]
                for bit in range(7):
                    t = jnp.where((row_s >> bit) % 2 == 1, pltpu.roll(t, 128 - (1 << bit), 1), t)
                straight = jnp.sum(jnp.where(lane_s + row_s < 128, t, 0.0), axis=0, keepdims=True)
                whole = jnp.sum(t, axis=0, keepdims=True)
                diag[h, b:b + 1, :] += straight
                diag[h, b + 1:b + 2, :] += whole - straight

    def units_of(half):
        cols = pl.ds(pl.multiple_of(half * (width // 2), 128), width // 2)
        lower = pl.ds(pl.multiple_of(half * (width // 2), 128), width // 2)
        dq_h = dq_t[lower, :].T
        dq[:, cols] = dq_h
        dk_h = dk[:, cols]
        dv_h = dv[:, cols]
        br_h = branch[:, cols]
        zero = jnp.zeros((n, part), BF)
        for cc in range(2):
            e = slice(cc * part, (cc + 1) * part)
            g = mm(normed_t[...], jnp.concatenate([dq_h[:, e], dk_h[:, e]], axis=1))
            au(0, cc, half)[...] = g.astype(BF).reshape(nz, 2, rows, lanes)
            g = (mm(normed_t[...], jnp.concatenate([dv_h[:, e], zero], axis=1))
                 + mm(context_t[...], jnp.concatenate([zero, br_h[:, e]], axis=1)))
            au(1, cc, half)[...] = g.astype(BF).reshape(nz, 2, rows, lanes)
        for w in range(2):
            attn_core(w, half).start()

    quarter = heads // 4

    @pl.loop(0, quarter)
    def _(g):
        pair(first_half, g)
        nxt = jnp.where(g == quarter - 1, last_half * (heads // 2), first_half * (heads // 2) + 2 * (g + 1))
        fetch(nxt, 0).start()
        fetch(nxt + 1, 1).start()

        @pl.when(g == 1)
        def _():
            step_b(3)

    units_of(first_half)

    @pl.loop(0, quarter)
    def _(g):
        pair(last_half, g)

        @pl.when(g < quarter - 1)
        def _():
            nxt = last_half * (heads // 2) + 2 * (g + 1)
            fetch(nxt, 0).start()
            fetch(nxt + 1, 1).start()

        @pl.when(g == 0)
        def _():
            attn_a(0, first_half)
            attn_a(1, first_half)

        @pl.when(g == 1)
        def _():
            step_b(2)
            step_c(3)

    units_of(last_half)
    for copy in weights[1:]:
        copy.wait()

    @pl.loop(0, 2)
    def _(i):
        r = pl.ds(pl.multiple_of(i * (n // 2), 128), n // 2)
        ng[r] = mm_t(dq[r], wqs[...]) + mm_t(dk[r], wks[...]) + mm_t(dv[r], wvs[...])

    attn_a(0, last_half)
    attn_a(1, last_half)
    gain_sum = jnp.zeros((1, width), F32)
    for i in range(ns):
        r = slice(i * slot_rows, (i + 1) * slot_rows)
        t = x[r].astype(F32)
        down, gain = norm_down(t, rms_scale(t), ag[...], ng[r])
        in_grad[i] = (hidden_grad[r] + down).astype(BF)
        gain_sum = gain_sum + jnp.sum(gain, axis=0, keepdims=True)
    keep_grad.start()
    for d in range(1, ns):
        grad_copy(d).start()

    col = lax.broadcasted_iota(jnp.int32, (128, width), 1)
    offset = (col // 128 - 1) * 128 - lax.rem(col, 128)
    offset = jnp.where(col >= width - 128, 256, jnp.where(col >= width - 256, -256, offset))
    dist = jnp.abs(offset)
    bucket = jnp.full_like(dist, 8)
    for edge in EDGES:
        bucket = bucket + (dist >= edge).astype(jnp.int32)
    bucket = jnp.where(dist < 8, dist, bucket) + jnp.where(offset > 0, 16, 0)
    pick = jnp.where(bucket == lax.broadcasted_iota(jnp.int32, (128, width), 0), 1.0, 0.0)
    bias = jnp.zeros((16, 128), F32)
    for i in range(width // 128):
        bias = bias + lax.dot_general(diag[:, i, :], pick[:, i * 128:(i + 1) * 128], (((1,), (1,)), ((), ())),
                                      precision=HIGHEST, preferred_element_type=F32)
    sm[0, 40:56, :] = bias
    put_gain(5, gain_sum)

    def small_copy(i):
        return remote(sm.at[i], smr.at[i], m_s.at[i], m_r.at[i], (core_peer, y_peer, x_peer)[i])

    def z_small(d):
        return remote(smz.at[z], smz.at[z], mz_s.at[d], mz_r.at[d], (lax.rem(z + d, nz) * 2 + xx, s))

    small_copy(0).start()
    step_b(1)
    step_b(0)
    small_copy(0).wait()
    sm[1] = sm[0] + smr[0]
    small_copy(1).start()
    attn_b(0, first_half)
    attn_y(0).start()
    attn_b(1, first_half)
    attn_y(1).start()
    step_c(2)
    small_copy(1).wait()
    sm[2] = sm[1] + smr[1]
    small_copy(2).start()
    step_c(1)
    step_c(0)
    attn_b(0, last_half)
    small_copy(2).wait()
    smz[z] = sm[2] + smr[2]

    @pl.loop(1, nz)
    def _(d):
        z_small(d).start()

    step_c(4)
    attn_b(1, last_half)
    step_c(5)
    for i in range(6):
        step_d(i)

    @pl.loop(1, nz)
    def _(d):
        z_small(d).wait()

    small_out[...] = smz[0]

    @pl.loop(1, nz)
    def _(d):
        small_out[...] = small_out[...] + smz[d]

    keep_dec.wait()
    keep_enc.wait()
    keep_grad.wait()
    for d in range(1, ns):
        enc_copy(d).wait()
        grad_copy(d).wait()

    @pl.loop(1, count)
    def _(d):
        dec_copy(d).wait()


def fused(np_, ns, length, fg, eg, ag, gains_dec, rows_grad, block, cot, wr, active, we, hidden, slope, mixed_t,
          wo, wq, wk, wv, q, k, v, x, normed_t, context_t, probs, dec, encoded):
    n, width = hidden.shape
    ff = active.shape[1]
    heads = probs.shape[0]
    nz = np_ // 2
    rows, lanes = width // np_, ff // np_
    count = np_ * ns
    smem = pl.BlockSpec(memory_space=pltpu.SMEM)
    vm = pl.BlockSpec(memory_space=pltpu.VMEM)
    hb = pl.BlockSpec(memory_space=pl.ANY)
    S = jax.ShapeDtypeStruct
    V = pltpu.VMEM
    dma = pltpu.SemaphoreType.DMA
    nar, tall = V((n, width), BF), V((width, n), BF)
    floats = V((n, width), F32)
    slots = (ns, n // ns, width)
    small = (64, 128)
    return pl.pallas_call(
        functools.partial(fused_kernel, np_, ns),
        out_shape=(S((6, rows, lanes), F32), S(small, F32), S(dec.shape, BF), S(slots, BF), S(slots, BF)),
        in_specs=[smem] + [vm] * 4 + [hb] * 22,
        out_specs=(vm, vm, hb, hb, hb),
        scratch_shapes=[
            V((n, ff), BF), V((n, ff), BF), V((ff, width), BF), V((width, ff), BF), floats, floats, floats,
            V(slots, BF), nar, nar, tall, tall, tall, tall,
            V((n, n), F32), V((n, n), BF), V((2, n, n), BF), V((128, n), BF), V((384, 128), F32), V((16, 8, 128), F32),
            V((2, 4, 2, nz, 2, rows, lanes), BF), V((6, 2, nz, 2, rows, lanes), BF),
            V((2, nz, 2, rows, lanes), BF), V((2, 2, nz, rows, lanes), BF), V((2, 2, nz, rows, lanes), BF),
            V((6, nz, rows, lanes), BF), V((6, nz, rows, lanes), BF),
            V((3,) + small, F32), V((3,) + small, F32), V((nz,) + small, F32),
            dma((2,)), dma((19,)), dma((7,)), dma((4,)), dma((4,)), dma((4,)), dma((4,)), dma((6,)), dma((6,)),
            dma((2, 2)), dma((2, 2)), dma((2, 2)), dma((2, 2)), dma((6, nz)), dma((6, nz)),
            dma((3,)), dma((3,)), dma((nz,)), dma((nz,)), dma((count,)), dma((count,)),
            dma((ns,)), dma((ns,)), dma((ns,)), dma((ns,)),
        ],
        compiler_params=pltpu.CompilerParams(
            collective_id=0, has_side_effects=True, vmem_limit_bytes=62 * 1024 * 1024),
        name="fused_backward",
    )(length, fg.reshape(1, -1), eg.reshape(1, -1), ag.reshape(1, -1), gains_dec, rows_grad.reshape(slots), block, cot, wr,
      active, we, hidden, slope, mixed_t, wo, wq, wk, wv, q, k, v, x, normed_t, context_t, probs, dec,
      encoded.reshape(slots))


def two_kernels(
    np_, ns, r, rp, lanes, side, length, final_gain, expand_gain, attend_gain, dec_gains,
    rows_grad, block, cot, reduce_weight, active, expand_weight, hidden, slope, mixed_t,
    output_weight, query_weight, key_weight, value_weight, query, key, value, x, normed_t,
    context_t, probs, dec_all, encoded,
):
    seq_len, ff = active.shape
    nz = np_ // 2
    wide, tall, hidden_grad, branch, feed_gains = feed_back(
        1, length, rows_grad, block, cot, final_gain, hidden, expand_gain, mixed_t.T, active,
        slope, reduce_weight, expand_weight)

    def pad(unit):
        return jnp.pad(unit, ((0, 0),) * 5 + ((0, rp - r), (0, 0)))

    tall = tall.reshape(2, 2, 2, r, side, nz, 2, ff // np_).transpose(0, 1, 2, 5, 6, 3, 4, 7)
    tall = pad(tall.reshape(2, 2, 2, nz, 2, r, lanes))
    wide = pad(wide.reshape(2, 2, 2, nz, 2, r, lanes))
    gap = ((0, 0), (0, rp - r), (0, 0))
    normed_t = jnp.pad(normed_t.reshape(np_, r, seq_len), gap).reshape(np_ * rp, seq_len)
    context_t = jnp.pad(context_t.reshape(np_, r, seq_len), gap).reshape(np_ * rp, seq_len)
    return backward(
        np_, ns, x, attend_gain, query, key, value, context_t, branch, hidden_grad, normed_t.T,
        dec_gains, feed_gains, probs, output_weight, query_weight, key_weight, value_weight,
        wide, tall, dec_all, encoded)


def per_device(
    enc_input, dec_input, lengths, attend_gain, query_weight, key_weight, value_weight,
    output_weight, bias_table, expand_gain, expand_weight, reduce_weight, final_gain,
    self_gain, self_value, self_output, cross_gain, cross_query, cross_key, cross_value,
    cross_output, feed_gain, feed_expand, feed_reduce, enc_cotangent, dec_cotangent,
):
    group, local_rows, width = enc_input.shape
    buckets, heads = bias_table.shape
    size = width // heads
    ff = expand_weight.shape[1]
    ns = lax.axis_size("seq")
    np_ = lax.axis_size("pairs")
    place = lax.axis_index("seq")
    seq_len = local_rows * ns
    length = lax.dynamic_slice_in_dim(lengths, place, 1)
    x = lax.all_to_all(enc_input, "seq", split_axis=0, concat_axis=1, tiled=True)[0]
    cot = lax.all_to_all(enc_cotangent, "seq", split_axis=0, concat_axis=1, tiled=True)[0]

    band_bucket = rel_bucket(jnp.arange(128), jnp.arange(384) - 128).T
    onehot = (jnp.arange(buckets, dtype=jnp.int32)[:, None, None] == band_bucket).astype(F32)
    band = jnp.einsum("but,bh->hut", onehot, bias_table, precision=HIGHEST)
    far = jnp.stack([bias_table[15], bias_table[31]], axis=1)

    (normed_t, query, key, value, probs, context_t, hidden, mixed_t, active, slope, block, enc_rows,
     encoded) = encode(length, x, attend_gain, expand_gain, final_gain, band, far, query_weight,
                       key_weight, value_weight, output_weight, expand_weight, reduce_weight)
    dec_block, dec_input_grad, dec_gains, left, right, wide_rows, mids, rows_grad = decode(
        length, enc_rows, dec_input, dec_cotangent, self_gain, cross_gain, feed_gain, heads,
        self_value, self_output, cross_query, cross_key, cross_value, cross_output, feed_expand,
        feed_reduce)
    r = width // np_
    aligned = r % 16 == 0 and (ff // np_) % 128 == 0 and ff == 4 * width
    rp = -(-r // 16) * 16
    lanes = ff // 8
    side = width // 8 // r
    cols = width // ns

    left_cut = jnp.concatenate([
        left.reshape(5, np_, r).transpose(1, 0, 2).reshape(np_, 5 * r),
        wide_rows[0].reshape(np_, 4 * r),
    ], axis=1)
    mid_cut = mids.reshape(2, ns, heads // ns, np_, r).transpose(3, 1, 0, 2, 4)
    mid_cut = mid_cut.reshape(np_, ns, 6 * r)
    right_cut = jnp.concatenate([
        right.reshape(7, ns, cols).transpose(1, 0, 2).reshape(ns, 7 * cols),
        wide_rows[1].reshape(ns, 4 * cols)], axis=1)
    dec_all = jnp.concatenate([
        jnp.broadcast_to(left_cut[:, None], (np_, ns, 9 * r)), mid_cut,
        jnp.broadcast_to(right_cut[None], (np_, ns, 11 * cols))], axis=-1)
    dec_all = dec_all.astype(BF).reshape(np_ * ns, -1)
    used = dec_all.shape[1]
    dec_rows = -(-used // 2048) * 16
    dec_all = jnp.pad(dec_all, ((0, 0), (0, dec_rows * 128 - used)))
    dec_all = dec_all.reshape(np_ * ns, dec_rows, 128)

    if aligned:
        red, small_sum, dec_got, enc_out, grad_out = fused(
            np_, ns, length, final_gain, expand_gain, attend_gain, dec_gains, rows_grad, block, cot,
            reduce_weight, active, expand_weight, hidden, slope, mixed_t, output_weight,
            query_weight, key_weight, value_weight, query, key, value, x, normed_t, context_t,
            probs, dec_all, encoded)
    else:
        red, small_sum, dec_got, enc_out, grad_out = two_kernels(
            np_, ns, r, rp, lanes, side, length, final_gain, expand_gain, attend_gain, dec_gains,
            rows_grad, block, cot, reduce_weight, active, expand_weight, hidden, slope, mixed_t,
            output_weight, query_weight, key_weight, value_weight, query, key, value, x, normed_t,
            context_t, probs, dec_all, encoded)

    got = dec_got.reshape(np_ * ns, -1)
    lefts = got[:, :9 * r].reshape(-1, 9, r)
    mid_got = got[:, 9 * r:15 * r].reshape(-1, 2, 3, r)
    rights = got[:, 15 * r:15 * r + 11 * cols].reshape(-1, 11, cols)
    plain = jnp.einsum("nkr,nkc->krc", lefts[:, :4], rights[:, :4], preferred_element_type=F32)
    crossed = jnp.einsum("nkhr,nkhd->krhd", mid_got, rights[:, 4:6].reshape(-1, 2, 3, size),
                         preferred_element_type=F32).reshape(2, r, cols)
    feed_in = jnp.einsum("nr,nc->rc", lefts[:, 4], rights[:, 7:11].reshape(-1, 4 * cols),
                         preferred_element_type=F32)
    feed_out = jnp.einsum("nr,nc->rc", lefts[:, 5:9].reshape(-1, 4 * r), rights[:, 6],
                          preferred_element_type=F32)
    red = red[:, :r]
    grad_reduce = red[2:4].reshape(2, r, side, ff // np_).reshape(cols, ff // np_).T
    gains = small_sum[:36].reshape(6, width)
    bias = small_sum[40:40 + heads, :buckets].T
    return (
        enc_out, dec_block, grad_out, dec_input_grad,
        gains[5],
        red[4][:, :cols], red[4][:, cols:], red[5][:, :cols], red[5][:, cols:],
        bias,
        gains[4],
        jnp.concatenate([red[0], red[1]], axis=1), grad_reduce,
        gains[3],
        gains[0], plain[0], plain[1],
        gains[1], plain[2], crossed[0], crossed[1], plain[3],
        gains[2], feed_in, feed_out,
    )


def solution(mesh):
    rows = P("pairs", "seq", None)
    single = P(("pairs", "seq"), None)
    block = P("pairs", "seq")
    return jax.shard_map(
        per_device,
        mesh=mesh,
        in_specs=(rows, single, P("pairs")) + (P(),) * 21 + (rows, single),
        out_specs=(
            rows, single, rows, single,
            P(), block, block, block, block, P(), P(), block, block, P(),
            P(), block, block, P(), block, block, block, block, P(), block, block,
        ),
        check_vma=False,
    )
```

```python
import functools
import itertools

import jax
import jax.numpy as jnp
from jax import lax
from jax.experimental import pallas as pl
from jax.experimental.pallas import tpu as pltpu
from jax.sharding import PartitionSpec as P

EPSILON = 1e-06
EDGES = (12, 16, 23, 32, 46, 64, 91)
HIGHEST = lax.Precision.HIGHEST
MESH = pl.DeviceIdType.MESH
BF = jnp.bfloat16
F32 = jnp.float32


def rel_bucket(query_pos, key_pos):
    offset = key_pos[None, :] - query_pos[:, None]
    distance = jnp.abs(offset)
    far_bucket = jnp.full_like(distance, 8)
    for threshold in EDGES:
        far_bucket = far_bucket + (distance >= threshold).astype(jnp.int32)
    bucket_id = jnp.where(distance < 8, distance, far_bucket)
    return bucket_id + 16 * (offset > 0).astype(jnp.int32)


def mm(a, b):
    return jnp.dot(a, b, preferred_element_type=F32)
def mm_t(a, b):
    return lax.dot_general(a, b, (((1,), (1,)), ((), ())), preferred_element_type=F32)
def t_mm(a, b):
    return lax.dot_general(a, b, (((0,), (0,)), ((), ())), preferred_element_type=F32)

def rms_scale(v):
    return lax.rsqrt(jnp.mean(v * v, axis=-1, keepdims=True) + EPSILON)

def encode_kernel(length, x, ag, eg, fg, band, far, wq, wk, wv, wo, we, wr,
                  normed_t, q, k, v, probs, context_t, hidden, mixed_t, active, slope, block, rows, low,
                  wqs, wks, wvs, wos, wes, wrs, normed, nt, qs, ks, vs, ctx, hid, mixed, mt, act, slo, blk, rws, lws,
                  v_t, s_t, pbuf, sems, psem, osem):
    n, width = x.shape
    heads = far.shape[0]
    ff = wes.shape[1]
    copies = [pltpu.make_async_copy(a, b, sems.at[i])
              for i, (a, b) in enumerate(((wq, wqs), (wk, wks), (wv, wvs), (wo, wos), (we, wes), (wr, wrs)))]
    for c in copies:
        c.start()
    saved = {}

    def save(name, src, dst):
        saved[name] = pltpu.make_async_copy(src, dst, osem.at[len(saved)])
        saved[name].start()

    for i in range(n // 128):
        r = slice(i * 128, (i + 1) * 128)
        t = x[r].astype(F32)
        t = t * rms_scale(t) * ag[...]
        normed[r] = t.astype(BF)
        nt[:, r] = t.T.astype(BF)
    save("normed", nt, normed_t)

    for name, w, out, dst, c in (("q", wqs, qs, q, copies[0]), ("k", wks, ks, k, copies[1]), ("v", wvs, vs, v, copies[2])):
        c.wait()
        for i in range(2):
            r = slice(i * (n // 2), (i + 1) * (n // 2))
            out[r] = mm(normed[r], w[...]).astype(BF)
        save(name, out, dst)

    lane = lax.broadcasted_iota(jnp.int32, (n, 128), 1)
    row = lax.broadcasted_iota(jnp.int32, (n, 128), 0)
    q_mark = jnp.where(lane == 0, 1.0, 0.0).astype(BF)
    k_mark = jnp.where((lane == 0) & (row >= length[0]), -1e30, 0.0).astype(BF)

    def keep(h, a):
        return pltpu.make_async_copy(pbuf.at[a], probs.at[h], psem.at[a])

    @pl.loop(0, heads // 2)
    def _(g):
        cols = pl.ds(pl.multiple_of(g * 128, 128), 128)
        v_t[...] = vs[:, cols].T
        qq = jnp.concatenate([qs[:, cols], q_mark], axis=1)
        kp = ks[:, cols]
        for a in range(2):
            h = 2 * g + a
            mine = (lane < 64) if a == 0 else (lane >= 64)
            kk = jnp.concatenate([jnp.where(mine, kp, jnp.zeros_like(kp)), k_mark], axis=1)
            s_t[a] = mm_t(kk, qq)

            @pl.when(g > 0)
            def _():
                keep(h - 2, a).wait()

            for j in range(n // 128):
                tile = []
                for i in range(n // 128):
                    s = s_t[a, i * 128:(i + 1) * 128, j * 128:(j + 1) * 128]
                    if abs(i - j) <= 1:
                        s = s + band[h, (i - j + 1) * 128:(i - j + 2) * 128, :]
                    elif i > j:
                        s = s + far[h, 1]
                    else:
                        s = s + far[h, 0]
                    tile.append(s)
                s = jnp.concatenate(tile, axis=0)
                m = jnp.max(s, axis=0, keepdims=True)
                e = jnp.exp(s - m)
                total = jnp.sum(e, axis=0, keepdims=True)
                pbuf[a, :, j * 128:(j + 1) * 128] = (e * (1.0 / total)).astype(BF)
            ctx[pl.ds(pl.multiple_of(h * 64, 64), 64), :] = mm(v_t[a * 64:(a + 1) * 64, :], pbuf[a]).astype(BF)
            keep(h, a).start()

    save("context", ctx, context_t)
    copies[3].wait()
    for i in range(2):
        r = slice(i * (n // 2), (i + 1) * (n // 2))
        h = x[r].astype(F32) + mm(ctx[:, r].T, wos[...])
        hid[r] = h
        t = h * rms_scale(h) * eg[...]
        mixed[r] = t.astype(BF)
        mt[:, r] = t.T.astype(BF)
    save("hidden", hid, hidden)
    save("mixed", mt, mixed_t)
    copies[4].wait()

    @pl.loop(0, ff // 512)
    def _(j):
        cols = pl.ds(pl.multiple_of(j * 512, 512), 512)
        u = mm(mixed[...], wes[:, cols])
        u2 = u * u
        t = jnp.tanh(u * (0.7978845608 + (0.7978845608 * 0.044715) * u2))
        half = 0.5 + 0.5 * t
        act[:, cols] = (u * half).astype(BF)
        slo[:, cols] = (half + half * (1.0 - t) * u * (0.7978845608 + (3 * 0.7978845608 * 0.044715) * u2)).astype(BF)

    save("active", act, active)
    save("slope", slo, slope)
    copies[5].wait()
    for i in range(2):
        r = slice(i * (n // 2), (i + 1) * (n // 2))
        alive = (lax.broadcasted_iota(jnp.int32, (n // 2, 1), 0) + i * (n // 2) < length[0]).astype(F32)
        b = alive * (hid[r] + mm(act[r], wrs[...]))
        blk[r] = b
        lws[r] = b.astype(BF)
        rws[r] = (b * rms_scale(b) * fg[...]).astype(BF)
    save("block", blk, block)
    save("rows", rws, rows)
    save("low", lws, low)
    for a in range(2):
        keep(heads - 2 + a, a).wait()
    for c in saved.values():
        c.wait()


def encode(length, x, ag, eg, fg, band, far, wq, wk, wv, wo, we, wr):
    n, width = x.shape
    ff = we.shape[1]
    heads = far.shape[0]
    sm = pl.BlockSpec(memory_space=pltpu.SMEM)
    vm = pl.BlockSpec(memory_space=pltpu.VMEM)
    hb = pl.BlockSpec(memory_space=pl.ANY)
    S = jax.ShapeDtypeStruct
    V = pltpu.VMEM
    full, tall, floats, broad = ((n, width), BF), ((width, n), BF), ((n, width), F32), ((n, ff), BF)
    return pl.pallas_call(
        encode_kernel,
        out_shape=tuple(S(*t) for t in (tall, full, full, full, ((heads, n, n), BF), tall, floats, tall,
                                        broad, broad, floats, full, full)),
        in_specs=[sm, vm, vm, vm, vm, vm, sm] + [hb] * 6,
        out_specs=(hb,) * 13,
        scratch_shapes=[V(w.shape, BF) for w in (wq, wk, wv, wo, we, wr)] + [V(*t) for t in (
            full, tall, full, full, full, tall, floats, full, tall, broad, broad, floats, full, full,
            ((128, n), BF), ((2, n, n), F32), ((2, n, n), BF))] + [
            pltpu.SemaphoreType.DMA((6,)), pltpu.SemaphoreType.DMA((2,)), pltpu.SemaphoreType.DMA((12,))],
        compiler_params=pltpu.CompilerParams(vmem_limit_bytes=60 * 1024 * 1024),
        name="encode",
    )(length, x, ag.reshape(1, -1), eg.reshape(1, -1), fg.reshape(1, -1), band, far, wq, wk, wv, wo, we, wr)


def gelu_parts(u):
    u2 = u * u
    t = jnp.tanh(u * (0.7978845608 + (0.7978845608 * 0.044715) * u2))
    half = 0.5 + 0.5 * t
    return u * half, half + half * (1.0 - t) * u * (0.7978845608 + (3 * 0.7978845608 * 0.044715) * u2)

def norm_down(v, r, g, dy):
    vr = v * r
    gd = g * dy
    return r * (gd - vr * jnp.mean(vr * gd, axis=-1, keepdims=True)), vr * dy

def decode_kernel(length, rows, dec_in, dec_cot, sg, cg, fg, *rest):
    hbm = rest[:8]
    (out, in_grad, gains, left, right, wide, mids, rows_grad) = rest[8:16]
    bufs = rest[16:24]
    sems = rest[24]
    sv, so, cq, ck, cv, co, fe, fr = bufs
    copies = [pltpu.make_async_copy(a, b, sems.at[i]) for i, (a, b) in enumerate(zip(hbm, bufs))]
    for c in copies:
        c.start()
    n, width = rows.shape
    heads = mids.shape[1]
    size = width // heads
    x = dec_in[...].astype(F32)
    cot = dec_cot[...]
    own = (lax.broadcasted_iota(jnp.int32, (heads, width), 1) // size
           == lax.broadcasted_iota(jnp.int32, (heads, width), 0))

    def spread(r):
        return jnp.where(own, r.astype(F32), 0.0).astype(BF)

    def collect(r):
        return jnp.sum(jnp.where(own, r, 0.0), axis=0, keepdims=True)

    x_r = rms_scale(x)
    self_normed = (x * x_r * sg[...]).astype(BF)
    copies[0].wait()
    self_values = mm(self_normed, sv[...]).astype(BF)
    copies[1].wait()
    after = x + mm(self_values, so[...])
    after_r = rms_scale(after)
    cross_normed = (after * after_r * cg[...]).astype(BF)
    copies[2].wait()
    cross_q = mm(cross_normed, cq[...]).astype(BF)
    copies[3].wait()
    q_rows = mm_t(spread(cross_q), ck[...]).astype(BF)
    s = mm_t(q_rows, rows[...])
    s = jnp.where(lax.broadcasted_iota(jnp.int32, s.shape, 1) < length[0], s, -1e30)
    e = jnp.exp(s - jnp.max(s, axis=-1, keepdims=True))
    probs = e / jnp.sum(e, axis=-1, keepdims=True)
    low = probs.astype(BF)
    mean_rows = mm(low, rows[...]).astype(BF)
    copies[4].wait()
    cross_context = collect(mm(mean_rows, cv[...])).astype(BF)
    copies[5].wait()
    middle = after + mm(cross_context, co[...])
    middle_r = rms_scale(middle)
    feed_normed = (middle * middle_r * fg[...]).astype(BF)
    copies[6].wait()
    active, slope = gelu_parts(mm(feed_normed, fe[...]))
    active = active.astype(BF)
    copies[7].wait()
    out[...] = (middle + mm(active, fr[...])).astype(BF)
    upper_grad = (slope * mm_t(cot, fr[...])).astype(BF)
    middle_down, feed_gain = norm_down(middle, middle_r, fg[...], mm_t(upper_grad, fe[...]))
    middle_grad = cot.astype(F32) + middle_down
    cross_branch = middle_grad.astype(BF)
    context_grad = mm_t(cross_branch, co[...]).astype(BF)
    g_rows = mm_t(spread(context_grad), cv[...]).astype(BF)
    prob_grad = mm_t(g_rows, rows[...])
    score_grad = (probs * (prob_grad - jnp.sum(probs * prob_grad, axis=-1, keepdims=True))).astype(BF)
    score_rows = mm(score_grad, rows[...]).astype(BF)
    pad = jnp.zeros((16 - heads % 16, n), BF)
    padw = jnp.zeros((16 - heads % 16, width), BF)
    rows_grad[...] = t_mm(jnp.concatenate([score_grad, pad, low, pad], axis=0),
                          jnp.concatenate([q_rows, padw, g_rows, padw], axis=0)).astype(BF)
    cross_q_grad = collect(mm(score_rows, ck[...])).astype(BF)
    after_down, cross_gain = norm_down(after, after_r, cg[...], mm_t(cross_q_grad, cq[...]))
    after_grad = middle_grad + after_down
    self_branch = after_grad.astype(BF)
    self_values_grad = mm_t(self_branch, so[...]).astype(BF)
    x_down, self_gain = norm_down(x, x_r, sg[...], mm_t(self_values_grad, sv[...]))
    in_grad[...] = (after_grad + x_down).astype(BF)
    gains[0:1, :] = self_gain
    gains[1:2, :] = cross_gain
    gains[2:3, :] = feed_gain
    for i, r in enumerate((self_normed, self_values, cross_normed, cross_context, feed_normed)):
        left[i:i + 1, :] = r.astype(F32)
    for i, r in enumerate((self_values_grad, self_branch, cross_q_grad, cross_branch, cross_q, context_grad, cot)):
        right[i:i + 1, :] = r.astype(F32)
    wide[0:1, :] = active.astype(F32)
    wide[1:2, :] = upper_grad.astype(F32)
    mids[0] = score_rows.astype(F32)
    mids[1] = mean_rows.astype(F32)

def decode(length, rows, dec_in, dec_cot, sg, cg, fg, heads, *weights):
    n, width = rows.shape
    ff = weights[6].shape[1]
    sm = pl.BlockSpec(memory_space=pltpu.SMEM)
    vm = pl.BlockSpec(memory_space=pltpu.VMEM)
    hb = pl.BlockSpec(memory_space=pl.ANY)
    S = jax.ShapeDtypeStruct
    return pl.pallas_call(
        decode_kernel,
        out_shape=(S((1, width), BF), S((1, width), BF), S((3, width), F32), S((5, width), F32), S((7, width), F32),
                   S((2, ff), F32), S((2, heads, width), F32), S((n, width), BF)),
        in_specs=[sm] + [vm] * 6 + [hb] * 8,
        out_specs=(vm,) * 8,
        scratch_shapes=[pltpu.VMEM(w.shape, BF) for w in weights] + [pltpu.SemaphoreType.DMA((8,))],
        compiler_params=pltpu.CompilerParams(vmem_limit_bytes=60 * 1024 * 1024),
        name="decode",
    )(length, rows, dec_in, dec_cot, sg.reshape(1, -1), cg.reshape(1, -1), fg.reshape(1, -1), *weights)


def feed_back_kernel(length, rows_grad, block, cot, fg, hidden, eg, mixed, active, slope, wr, we,
                     wide, tall, hidden_grad, branch, gains, wrs, wes, bg, rb, rb_t, ug, mixed_t, dmixed, sems):
    n, width = block.shape
    ff = active.shape[1]
    groups, lanes = tall.shape[3], tall.shape[5]
    cols_dev = width // 4
    copies = [pltpu.make_async_copy(a, b, sems.at[i]) for i, (a, b) in enumerate(((wr, wrs), (we, wes)))]
    for c in copies:
        c.start()
    gains[...] = jnp.zeros_like(gains)

    @pl.loop(0, n // 128)
    def _(i):
        r = pl.ds(i * 128, 128)
        alive = (lax.broadcasted_iota(jnp.int32, (128, 1), 0) + i * 128 < length[0]).astype(F32)
        v = block[r]
        down, gain = norm_down(v, rms_scale(v), fg[...], rows_grad[r].astype(F32))
        b = alive * (cot[r].astype(F32) + down)
        bg[r] = b
        rb[r] = b.astype(BF)
        rb_t[:, pl.ds(pl.multiple_of(i * 128, 128), 128)] = b.T.astype(BF)
        mixed_t[:, pl.ds(pl.multiple_of(i * 128, 128), 128)] = mixed[r].T
        gains[0:1, :] += jnp.sum(gain, axis=0, keepdims=True)

    copies[0].wait()

    @pl.loop(0, ff // 256)
    def _(j):
        cols = pl.ds(pl.multiple_of(j * 256, 256), 256)
        ug[:, cols] = (slope[:, cols].astype(F32) * mm_t(rb[...], wrs[cols, :])).astype(BF)

    copies[1].wait()

    @pl.loop(0, width // 256)
    def _(j):
        cols = pl.ds(pl.multiple_of(j * 256, 256), 256)
        dmixed[:, cols] = mm_t(ug[...], wes[cols, :])

    @pl.loop(0, n // 128)
    def _(i):
        r = pl.ds(i * 128, 128)
        v = hidden[r]
        down, gain = norm_down(v, rms_scale(v), eg[...], dmixed[r])
        h = bg[r] + down
        hidden_grad[r] = h
        branch[r] = h.astype(BF)
        gains[1:2, :] += jnp.sum(gain, axis=0, keepdims=True)

    @pl.loop(0, 4)
    def _(j):
        for half in range(2):
            cols = pl.ds(pl.multiple_of(j * (ff // 4) + half * (ff // 8), 128), ff // 8)
            wide[half, lax.rem(j, 2), j // 2] = mm(mixed_t[...], ug[:, cols]).astype(BF)

    chunk = ff // 8
    per_group = lanes // chunk

    @pl.loop(0, 8)
    def _(i):
        cols = pl.ds(pl.multiple_of(i * chunk, 128), chunk)
        g = mm(rb_t[...], active[:, cols]).astype(BF)
        for j in range(4):
            for half in range(2):
                r = j * cols_dev + half * (cols_dev // 2)
                part = g[r:r + cols_dev // 2]
                if per_group == 1:
                    tall[half, j % 2, j // 2, i] = part
                else:
                    tall[half, j % 2, j // 2, 0, :, cols] = part


def feed_back(groups, length, rows_grad, block, cot, fg, hidden, eg, mixed, active, slope, wr, we):
    n, width = block.shape
    ff = active.shape[1]
    sm = pl.BlockSpec(memory_space=pltpu.SMEM)
    vm = pl.BlockSpec(memory_space=pltpu.VMEM)
    hb = pl.BlockSpec(memory_space=pl.ANY)
    S = jax.ShapeDtypeStruct
    V = pltpu.VMEM
    return pl.pallas_call(
        feed_back_kernel,
        out_shape=(S((2, 2, 2, width, ff // 8), BF),
                   S((2, 2, 2, groups, width // 8, ff // groups), BF), S((n, width), F32), S((n, width), BF), S((2, width), F32)),
        in_specs=[sm] + [vm] * 9 + [hb] * 2,
        out_specs=(vm,) * 5,
        scratch_shapes=[V(wr.shape, BF), V(we.shape, BF), V((n, width), F32), V((n, width), BF), V((width, n), BF),
                        V((n, ff), BF), V((width, n), BF), V((n, width), F32), pltpu.SemaphoreType.DMA((2,))],
        compiler_params=pltpu.CompilerParams(vmem_limit_bytes=60 * 1024 * 1024),
        name="feed_back",
    )(length, rows_grad, block, cot, fg.reshape(1, -1), hidden, eg.reshape(1, -1), mixed, active, slope, wr, we)


def backward_kernel(np_, ns, x, ag, q, k, v, context_t, branch, hidden_grad, normed, gains_dec, gains_feed,
                    probs, wo, wq, wk, wv, wide, tall, dec, encoded,
                    red, small_out, dec_out, enc_out, grad_out,
                    wos, wqs, wks, wvs, d_out, dp, ds, dq_t, dq, dk, dv, k_t, normed_t, ng, in_grad,
                    pbuf, band, diag, own, au, r0, r1y, r1x, r1a, r2, r3, sm, smr, smz,
                    psem, wsem, loc, c_s, c_r, a_s, a_r, b_s, b_r, ac_s, ac_r, ax_s, ax_r, z_s, z_r,
                    m_s, m_r, mz_s, mz_r, d_s, d_r, e_s, e_r, g_s, g_r):
    n, width = x.shape
    heads = probs.shape[0]
    nz = np_ // 2
    rows, lanes = r0.shape[4:]
    count = np_ * ns
    p = lax.axis_index("pairs")
    s = lax.axis_index("seq")
    c = lax.rem(s, 2)
    y = s // 2
    xx = lax.rem(p, 2)
    z = p // 2
    me = p * ns + s
    core_peer = (p, s + 1 - 2 * c)
    y_peer = (p, lax.rem(s + 2, 4))
    x_peer = (p + 1 - 2 * xx, s)

    def place(d):
        lin = lax.rem(me + d, count)
        return (lin // ns, lax.rem(lin, ns))

    barrier = pltpu.get_barrier_semaphore()

    @pl.loop(1, count)
    def _(d):
        pl.semaphore_signal(barrier, inc=1, device_id=place(d), device_id_type=MESH)

    def remote(src, dst, send, recv, peer):
        return pltpu.make_async_remote_copy(
            src_ref=src, dst_ref=dst, send_sem=send, recv_sem=recv,
            device_id=peer, device_id_type=MESH)

    weights = [pltpu.make_async_copy(a, b, wsem.at[i])
               for i, (a, b) in enumerate(((wo, wos), (wq, wqs), (wk, wks), (wv, wvs)))]

    def fetch(h, slot):
        return pltpu.make_async_copy(probs.at[h], pbuf.at[slot], psem.at[slot])

    def unit(i, core):
        return (wide, tall)[i // 2].at[i % 2, core]

    def core_copy(i):
        return remote(unit(i, 1 - c), r0.at[i], c_s.at[i], c_r.at[i], core_peer)

    def own_copy(i):
        return pltpu.make_async_copy(unit(i, c), own.at[i], loc.at[i])

    def first(i):
        if i % 2 == 0:
            return remote(own.at[i, 1 - y], r1y.at[i // 2], a_s.at[i], a_r.at[i], y_peer)
        return remote(own.at[i, :, :, 1 - xx], r1x.at[i // 2], a_s.at[i], a_r.at[i], x_peer)

    def second(i):
        if i % 2 == 0:
            return remote(own.at[i, y, :, 1 - xx], r2.at[i], b_s.at[i], b_r.at[i], x_peer)
        return remote(own.at[i, 1 - y, :, xx], r2.at[i], b_s.at[i], b_r.at[i], y_peer)

    def final(i):
        return own.at[i, y] if i < 4 else au.at[i - 4, c, y]

    def last(i, d):
        t = lax.rem(z + d, nz)
        return remote(final(i).at[t, xx], r3.at[i, d], z_s.at[i, d], z_r.at[i, d], (t * 2 + xx, s))

    def attn_core(w, half):
        return remote(au.at[w, 1 - c, half], r0.at[4 + w, half], ac_s.at[w, half], ac_r.at[w, half], core_peer)

    def attn_x(w, half):
        return remote(au.at[w, c, half, :, 1 - xx], r1a.at[w, half], ax_s.at[w, half], ax_r.at[w, half], x_peer)

    def attn_y(w):
        return remote(au.at[w, c, 1 - y, :, xx], r2.at[4 + w], b_s.at[4 + w], b_r.at[4 + w], y_peer)

    def dec_copy(d):
        to = place(d)
        return remote(dec.at[to[0] * ns + to[1]], dec_out.at[me], d_s.at[d], d_r.at[d], to)

    def enc_copy(d):
        t = lax.rem(s + d, ns)
        return remote(encoded.at[t], enc_out.at[s], e_s.at[d], e_r.at[d], (p, t))

    def grad_copy(d):
        t = lax.rem(s + d, ns)
        return remote(in_grad.at[t], grad_out.at[s], g_s.at[d], g_r.at[d], (p, t))

    keep_dec = pltpu.make_async_copy(dec.at[me], dec_out.at[me], loc.at[4])
    keep_enc = pltpu.make_async_copy(encoded.at[s], enc_out.at[s], loc.at[5])
    keep_grad = pltpu.make_async_copy(in_grad.at[s], grad_out.at[s], loc.at[6])

    def step_a(i):
        core_copy(i).wait()
        own_copy(i).wait()

        @pl.loop(0, nz)
        def _(b):
            for a in range(2):
                for e in range(2):
                    own[i, a, b, e] = own[i, a, b, e] + r0[i, a, b, e]

        first(i).start()

    def step_b(i):
        first(i).wait()

        @pl.loop(0, nz)
        def _(b):
            for e in range(2):
                if i % 2 == 0:
                    own[i, y, b, e] = own[i, y, b, e] + r1y[i // 2, b, e]
                else:
                    own[i, e, b, xx] = own[i, e, b, xx] + r1x[i // 2, e, b]

        second(i).start()

    def step_c(i):
        if i < 4:
            second(i).wait()
        else:
            attn_y(i - 4).wait()

        @pl.loop(0, nz)
        def _(b):
            f = final(i)
            f[b, xx] = f[b, xx] + r2[i, b]

        @pl.loop(1, nz)
        def _(d):
            last(i, d).start()

    def step_d(i):
        red[i] = final(i)[z, xx].astype(F32)

        @pl.loop(1, nz)
        def _(d):
            last(i, d).wait()
            red[i] = red[i] + r3[i, d].astype(F32)

    def attn_a(w, half):
        attn_core(w, half).wait()

        @pl.loop(0, nz)
        def _(b):
            for e in range(2):
                au[w, c, half, b, e] = au[w, c, half, b, e] + r0[4 + w, half, b, e]

        attn_x(w, half).start()

    def attn_b(w, half):
        attn_x(w, half).wait()

        @pl.loop(0, nz)
        def _(b):
            au[w, c, half, b, xx] = au[w, c, half, b, xx] + r1a[w, half, b]

    for copy in weights:
        copy.start()
    first_half, last_half = 1 - y, y
    fetch(first_half * (heads // 2), 0).start()
    fetch(first_half * (heads // 2) + 1, 1).start()
    for i in range(4):
        own_copy(i).start()
    keep_dec.start()
    keep_enc.start()
    diag[...] = jnp.zeros_like(diag)
    weights[0].wait()

    @pl.loop(0, width // 384)
    def _(j):
        cols = pl.ds(pl.multiple_of(j * 384, 128), 384)
        d_out[:, cols] = mm_t(branch[...], wos[cols, :]).astype(BF)

    pl.semaphore_wait(barrier, count - 1)
    for i in range(4):
        core_copy(i).start()
    for d in range(1, ns):
        enc_copy(d).start()

    @pl.loop(1, count)
    def _(d):
        dec_copy(d).start()

    @pl.loop(0, n // 128)
    def _(i):
        r = pl.ds(pl.multiple_of(i * 128, 128), 128)
        normed_t[:, r] = normed[r].T

    lane = lax.broadcasted_iota(jnp.int32, (n, 128), 1)
    lane_s = lax.broadcasted_iota(jnp.int32, (128, 128), 1)
    row_s = lax.broadcasted_iota(jnp.int32, (128, 128), 0)

    def pair(half, g):
        cols = pl.ds(pl.multiple_of(half * (width // 2) + g * 128, 128), 128)
        k_t[...] = k[:, cols].T
        dop = d_out[:, cols]
        qp = q[:, cols]
        vp = v[:, cols]
        zero = jnp.zeros_like(qp)
        for a in range(2):
            h = half * (heads // 2) + 2 * g + a
            mine = (lane < 64) if a == 0 else (lane >= 64)
            dp[...] = mm_t(jnp.where(mine, vp, zero), dop)
            fetch(h, a).wait()
            for j in range(n // 128):
                pj = pbuf[a, :, j * 128:(j + 1) * 128].astype(F32)
                pd = pj * dp[:, j * 128:(j + 1) * 128]
                total = jnp.sum(pd, axis=0, keepdims=True)
                sg = pd - pj * total
                ds[:, j * 128:(j + 1) * 128] = sg.astype(BF)
                for i in range(n // 128):
                    t = sg[i * 128:(i + 1) * 128]
                    if abs(i - j) <= 1:
                        b = (i - j + 1) * 128
                        if j == 0 or (j == 1 and i == 0):
                            band[b:b + 128, :] = t
                        else:
                            band[b:b + 128, :] += t
                    else:
                        f = 5 if i > j else 4
                        diag[h, f:f + 1, :] += jnp.sum(t, axis=0, keepdims=True)
            dvp = mm(pbuf[a], jnp.where(mine, dop, zero))
            dkp = mm(ds[...], jnp.where(mine, qp, zero))
            dq_t[pl.ds(pl.multiple_of(h * 64, 64), 64), :] = mm(k_t[a * 64:(a + 1) * 64, :], ds[...]).astype(BF)
            if a == 0:
                dk_sum, dv_sum = dkp, dvp
            else:
                dk[:, cols] = (dk_sum + dkp).astype(BF)
                dv[:, cols] = (dv_sum + dvp).astype(BF)
            for b in range(3):
                t = band[b * 128:(b + 1) * 128, :]
                for bit in range(7):
                    t = jnp.where((row_s >> bit) % 2 == 1, pltpu.roll(t, 128 - (1 << bit), 1), t)
                straight = jnp.sum(jnp.where(lane_s + row_s < 128, t, 0.0), axis=0, keepdims=True)
                whole = jnp.sum(t, axis=0, keepdims=True)
                diag[h, b:b + 1, :] += straight
                diag[h, b + 1:b + 2, :] += whole - straight

    part = width // 4

    def units_of(half):
        cols = pl.ds(pl.multiple_of(half * (width // 2), 128), width // 2)
        lower = pl.ds(pl.multiple_of(half * (width // 2), 128), width // 2)
        dq_h = dq_t[lower, :].T
        dq[:, cols] = dq_h
        dk_h = dk[:, cols]
        dv_h = dv[:, cols]
        br_h = branch[:, cols]
        zero = jnp.zeros((n, part), BF)
        for cc in range(2):
            e = slice(cc * part, (cc + 1) * part)
            g = mm(normed_t[...], jnp.concatenate([dq_h[:, e], dk_h[:, e]], axis=1))
            au[0, cc, half] = g.astype(BF).reshape(nz, 2, rows, lanes)
            g = (mm(normed_t[...], jnp.concatenate([dv_h[:, e], zero], axis=1))
                 + mm(context_t[...], jnp.concatenate([zero, br_h[:, e]], axis=1)))
            au[1, cc, half] = g.astype(BF).reshape(nz, 2, rows, lanes)
        for w in range(2):
            attn_core(w, half).start()

    quarter = heads // 4

    @pl.loop(0, quarter)
    def _(g):
        pair(first_half, g)
        nxt = jnp.where(g == quarter - 1, last_half * (heads // 2), first_half * (heads // 2) + 2 * (g + 1))
        fetch(nxt, 0).start()
        fetch(nxt + 1, 1).start()

        @pl.when(g == 0)
        def _():
            step_a(0)
            step_a(1)

        @pl.when(g == 1)
        def _():
            step_a(2)
            step_a(3)

    units_of(first_half)

    @pl.loop(0, quarter)
    def _(g):
        pair(last_half, g)

        @pl.when(g < quarter - 1)
        def _():
            nxt = last_half * (heads // 2) + 2 * (g + 1)
            fetch(nxt, 0).start()
            fetch(nxt + 1, 1).start()

        @pl.when(g == 0)
        def _():
            attn_a(0, first_half)
            attn_a(1, first_half)

        @pl.when(g == 1)
        def _():
            step_b(0)
            step_b(1)

    units_of(last_half)
    for copy in weights[1:]:
        copy.wait()

    @pl.loop(0, 2)
    def _(i):
        r = pl.ds(pl.multiple_of(i * (n // 2), 128), n // 2)
        ng[r] = mm_t(dq[r], wqs[...]) + mm_t(dk[r], wks[...]) + mm_t(dv[r], wvs[...])

    attn_a(0, last_half)
    attn_a(1, last_half)
    sm[...] = jnp.zeros_like(sm)
    slot_rows = n // ns
    gain_sum = jnp.zeros((1, width), F32)
    for i in range(ns):
        r = slice(i * slot_rows, (i + 1) * slot_rows)
        t = x[r].astype(F32)
        down, gain = norm_down(t, rms_scale(t), ag[...], ng[r])
        in_grad[i] = (hidden_grad[r] + down).astype(BF)
        gain_sum = gain_sum + jnp.sum(gain, axis=0, keepdims=True)
    keep_grad.start()
    for d in range(1, ns):
        grad_copy(d).start()

    col = lax.broadcasted_iota(jnp.int32, (128, width), 1)
    offset = (col // 128 - 1) * 128 - lax.rem(col, 128)
    offset = jnp.where(col >= width - 128, 256, jnp.where(col >= width - 256, -256, offset))
    dist = jnp.abs(offset)
    bucket = jnp.full_like(dist, 8)
    for edge in EDGES:
        bucket = bucket + (dist >= edge).astype(jnp.int32)
    bucket = jnp.where(dist < 8, dist, bucket) + jnp.where(offset > 0, 16, 0)
    pick = jnp.where(bucket == lax.broadcasted_iota(jnp.int32, (128, width), 0), 1.0, 0.0)
    bias = jnp.zeros((16, 128), F32)
    for i in range(width // 128):
        bias = bias + lax.dot_general(diag[:, i, :], pick[:, i * 128:(i + 1) * 128], (((1,), (1,)), ((), ())),
                                      precision=HIGHEST, preferred_element_type=F32)
    sm[0, 40:56, :] = bias
    gains = [gains_dec[i:i + 1, :] for i in range(3)] + [gains_feed[i:i + 1, :] for i in range(2)] + [gain_sum]
    for i, gain in enumerate(gains):
        for j in range(width // 128):
            sm[0, i * 6 + j:i * 6 + j + 1, :] = gain[:, j * 128:(j + 1) * 128]

    def small_copy(i):
        return remote(sm.at[i], smr.at[i], m_s.at[i], m_r.at[i], (core_peer, y_peer, x_peer)[i])

    def z_small(d):
        return remote(smz.at[z], smz.at[z], mz_s.at[d], mz_r.at[d], (lax.rem(z + d, nz) * 2 + xx, s))

    small_copy(0).start()
    step_b(2)
    step_b(3)
    small_copy(0).wait()
    sm[1] = sm[0] + smr[0]
    small_copy(1).start()
    attn_b(0, first_half)
    attn_y(0).start()
    attn_b(1, first_half)
    attn_y(1).start()
    step_c(0)
    step_c(1)
    small_copy(1).wait()
    sm[2] = sm[1] + smr[1]
    small_copy(2).start()
    step_c(2)
    step_c(3)
    attn_b(0, last_half)
    small_copy(2).wait()
    smz[z] = sm[2] + smr[2]

    @pl.loop(1, nz)
    def _(d):
        z_small(d).start()

    step_c(4)
    attn_b(1, last_half)
    step_c(5)
    for i in range(6):
        step_d(i)

    @pl.loop(1, nz)
    def _(d):
        z_small(d).wait()

    small_out[...] = smz[0]

    @pl.loop(1, nz)
    def _(d):
        small_out[...] = small_out[...] + smz[d]

    keep_dec.wait()
    keep_enc.wait()
    keep_grad.wait()
    for d in range(1, ns):
        enc_copy(d).wait()
        grad_copy(d).wait()

    @pl.loop(1, count)
    def _(d):
        dec_copy(d).wait()


def backward(np_, ns, x, ag, q, k, v, context_t, branch, hidden_grad, normed, gains_dec, gains_feed,
             probs, wo, wq, wk, wv, wide, tall, dec, encoded):
    n, width = x.shape
    heads = probs.shape[0]
    nz = np_ // 2
    rows, lanes = wide.shape[5:]
    count = np_ * ns
    padded = normed.shape[1]
    vm = pl.BlockSpec(memory_space=pltpu.VMEM)
    hb = pl.BlockSpec(memory_space=pl.ANY)
    S = jax.ShapeDtypeStruct
    V = pltpu.VMEM
    dma = pltpu.SemaphoreType.DMA
    nar = V((n, width), BF)
    square = V((width, width), BF)
    slots = (ns, n // ns, width)
    small = (64, 128)
    return pl.pallas_call(
        functools.partial(backward_kernel, np_, ns),
        out_shape=(S((6, rows, lanes), F32), S(small, F32), S(dec.shape, BF), S(slots, BF), S(slots, BF)),
        in_specs=[vm] * 11 + [hb] * 9,
        out_specs=(vm, vm, hb, hb, hb),
        scratch_shapes=[
            square, square, square, square, nar, V((n, n), F32), V((n, n), BF), V((width, n), BF), nar, nar, nar,
            V((128, n), BF), V((padded, n), BF), V((n, width), F32), V(slots, BF),
            V((2, n, n), BF), V((384, 128), F32), V((16, 8, 128), F32),
            V((4, 2, nz, 2, rows, lanes), BF), V((2, 2, 2, nz, 2, rows, lanes), BF), V((6, 2, nz, 2, rows, lanes), BF),
            V((2, nz, 2, rows, lanes), BF), V((2, 2, nz, rows, lanes), BF), V((2, 2, nz, rows, lanes), BF),
            V((6, nz, rows, lanes), BF), V((6, nz, rows, lanes), BF),
            V((3,) + small, F32), V((3,) + small, F32), V((nz,) + small, F32),
            dma((2,)), dma((4,)), dma((7,)), dma((4,)), dma((4,)), dma((4,)), dma((4,)), dma((6,)), dma((6,)),
            dma((2, 2)), dma((2, 2)), dma((2, 2)), dma((2, 2)), dma((6, nz)), dma((6, nz)),
            dma((3,)), dma((3,)), dma((nz,)), dma((nz,)), dma((count,)), dma((count,)),
            dma((ns,)), dma((ns,)), dma((ns,)), dma((ns,)),
        ],
        compiler_params=pltpu.CompilerParams(
            collective_id=0, has_side_effects=True, vmem_limit_bytes=62 * 1024 * 1024),
        name="backward",
    )(x, ag.reshape(1, -1), q, k, v, context_t, branch, hidden_grad, normed, gains_dec, gains_feed,
      probs, wo, wq, wk, wv, wide, tall, dec, encoded.reshape(slots))


PARTS = 2
ORDERS = {
    "t00": "xfny",
    "t10": "fnyx",
    "t01": "nyfx",
    "t11": "yxfn",
    "w00": "nyfx",
    "w10": "yxfn",
    "w01": "xyfn",
    "w11": "ynxf",
    "a0": "xyfn",
    "a1": "xnyf",
}
SCHEDULE = {
    "wide": (
        ("t00", 0), ("t10", 0), ("t01", 0), ("t11", 0),
    ),
    "rows": (
        ("w00", 0),
    ),
    "dout": (
        ("w10", 0), ("w01", 0),
    ),
    "p00": (
        ("w11", 0), ("t00", 1),
    ),
    "p01": (
        ("t11", 1),
    ),
    "q0": (
        ("t01", 1), ("t10", 1), ("w01", 1), ("w10", 1),
    ),
    "p10": (
        ("t11", 2), ("h00", 0),
    ),
    "p11": (
        ("h01", 0), ("w00", 1), ("w10", 2), ("w11", 1),
    ),
    "p12": (
        ("t01", 2),
    ),
    "v1": (
        ("t00", 2), ("t10", 2), ("w01", 2), ("h00", 1),
    ),
    "ng1": (
        ("h10", 0), ("t11", 3),
    ),
    "end": (
        ("w00", 2), ("h11", 0), ("t10", 3), ("w10", 3), ("w11", 2), ("h01", 1),
        ("t00", 3), ("t01", 3), ("t11", 4), ("w01", 3), ("h10", 1), ("w10", 4),
        ("w00", 3), ("h01", 2), ("w01", 4), ("h11", 1), ("t00", 4), ("t10", 4),
        ("w11", 3), ("t01", 4), ("w00", 4), ("h10", 2), ("h11", 2), ("w11", 4),
        ("h10", 3), ("h11", 3),
    ),
}
HOPS = (1, 3, 5)


def ff_pieces():
    names = [kind + str(unit) + str(i) for kind in "tw" for i in range(PARTS) for unit in range(2)]
    return names + ["h" + str(half) + str(w) for half in range(2) for w in range(2)]


def fused_kernel(np_, ns, length, fg, eg, ag, gains_dec,
                 rows_grad, block, cot, wr, active, wide_w, hidden, slope, mixed_t_in, wo, wq, wk, wv, q_in, k_in,
                 v_in, x_in, normed_t_in, context_t_in, probs, dec, encoded,
                 red, small_out, dec_out, enc_out, grad_out,
                 acts, grads, w1, wes, bg, hid, dm, rg, ct, rb, rb_t, mixed_t, normed_t, context_t,
                 dp, ds, pbuf, k_t, band, diag, fu, r0, r0a, r1, r2, r3, r4, a1, a2, a3, over0, over1,
                 sm, smr, smz,
                 psem, isem, loc, f_s, f_r, t_s, t_r, o_s, o_r,
                 m_s, m_r, mz_s, mz_r, d_s, d_r, e_s, e_r, g_s, g_r):
    n, width = hid.shape
    ff = acts.shape[1]
    heads = probs.shape[0]
    nz = np_ // 2
    pieces = ff_pieces()
    rows, lanes = fu.shape[6:]
    step_rows = rows // PARTS
    count = np_ * ns
    p = lax.axis_index("pairs")
    s = lax.axis_index("seq")
    c = lax.rem(s, 2)
    y = s // 2
    xx = lax.rem(p, 2)
    z = p // 2
    me = p * ns + s
    core_peer = (p, s + 1 - 2 * c)
    y_peer = (p, lax.rem(s + 2, 4))
    x_peer = (p + 1 - 2 * xx, s)
    first_half, last_half = 1 - y, y
    own_at = {"x": xx, "y": y, "n": lax.rem(z, 2), "f": z // 2}
    peers = {"x": x_peer, "y": y_peer, "n": ((z + 1 - 2 * own_at["n"]) * 2 + xx, s),
             "f": (lax.rem(z + 2, 4) * 2 + xx, s)}

    def place(d):
        lin = lax.rem(me + d, count)
        return (lin // ns, lax.rem(lin, ns))

    barrier = pltpu.get_barrier_semaphore()

    @pl.loop(1, count)
    def _(d):
        pl.semaphore_signal(barrier, inc=1, device_id=place(d), device_id_type=MESH)

    def remote(src, dst, send, recv, peer):
        return pltpu.make_async_remote_copy(
            src_ref=src, dst_ref=dst, send_sem=send, recv_sem=recv,
            device_id=peer, device_id_type=MESH)

    def load(i, src, dst):
        return pltpu.make_async_copy(src, dst, isem.at[i])

    def part_of(ref, i):
        return ref.at[:, pl.ds(i * width, width)]

    loads = [load(i, a, b) for i, (a, b) in enumerate((
        (rows_grad, rg), (block, bg), (cot, ct), (active, acts), (wr, w1), (slope, grads), (mixed_t_in, mixed_t),
        (wide_w, wes), (hidden, hid), (normed_t_in, normed_t), (context_t_in, context_t)))]
    weights = [load(11 + i, a, w1.at[pl.ds(i * width, width)]) for i, a in enumerate((wo, wq, wk, wv))]
    heads_in = [load(15 + i, a, part_of(grads, i)) for i, a in enumerate((q_in, k_in, v_in, x_in))]
    d_out, dq, dk, dv = (part_of(acts, i) for i in range(4))
    q, k, v, x = (part_of(grads, i) for i in range(4))
    branch, dq_t, ng, in_grad, hidden_grad = ct, rb_t, dm, rg, bg
    wos, wqs, wks, wvs = (w1.at[pl.ds(i * width, width)] for i in range(4))

    def fetch(h, slot):
        return pltpu.make_async_copy(probs.at[h], pbuf.at[slot], psem.at[slot])

    def view(ref, dims, fixed):
        return ref.at[tuple(fixed.get(dim, slice(None)) for dim in dims)]

    def accumulate(dst, src, depth):
        for at in itertools.product(range(2), repeat=depth):
            dst[at] = dst[at] + src[at]

    def au(w, core, half):
        return fu.at[1 - c, 2 * w + core, half]

    def region(name, core):
        if name[0] == "h":
            return au(int(name[2]), core, first_half if name[1] == "0" else last_half), "fnx"
        unit = (2 if name[0] == "t" else 0) + int(name[1])
        return fu.at[core, unit, :, :, :, :, pl.ds(int(name[2]) * step_rows, step_rows)], "yfnx"

    def order_of(name):
        if name[0] != "h":
            return ORDERS[name]
        order = ORDERS["a" + name[2]]
        return order[:order.index("y")] if name[1] == "0" else order.replace("y", "")

    def core_copy(name):
        i = pieces.index(name)
        src, _ = region(name, 1 - c)
        dst = r0a.at[i - len(pieces) + 4] if name[0] == "h" else r0.at[i]
        return remote(src, dst, f_s.at[i], f_r.at[i], core_peer)

    def landing(name, j):
        i = pieces.index(name)
        if name[0] == "h":
            return (a1, a2, a3)[j].at[i - len(pieces) + 4]
        return (r1, r2, r3, r4)[j].at[i]

    def remaining(name, j):
        ref, dims = region(name, c)
        return ref, dims, {letter: own_at[letter] for letter in order_of(name)[:j]}

    def stage_copy(name, j):
        ref, dims, fixed = remaining(name, j)
        letter = order_of(name)[j]
        i = pieces.index(name)
        src = view(ref, dims, {**fixed, letter: 1 - own_at[letter]})
        return remote(src, landing(name, j), t_s.at[i, j], t_r.at[i, j], peers[letter])

    def hand_over(w):
        name = "h0" + str(w)
        ref, dims, fixed = remaining(name, len(order_of(name)))
        return remote(view(ref, dims, fixed), (over0, over1)[w], o_s.at[w], o_r.at[w], y_peer)

    def total_of(name):
        unit = 4 + int(name[2]) if name[0] == "h" else (2 if name[0] == "t" else 0) + int(name[1])
        if name[0] == "h":
            return red.at[unit]
        return red.at[unit, pl.ds(int(name[2]) * step_rows, step_rows)]

    def step(name, j):
        order = order_of(name)
        ref, dims, fixed = remaining(name, j)
        mine = view(ref, dims, fixed)
        depth = len(dims) - j
        closing = j == len(order) and name[:2] != "h0"
        joins = name[:2] == "h1" and ORDERS["a" + name[2]].index("y") == j
        if j == 0:
            core_copy(name).wait()
            landed = r0a.at[pieces.index(name) - len(pieces) + 4] if name[0] == "h" else r0.at[pieces.index(name)]
        else:
            stage_copy(name, j - 1).wait()
            landed = landing(name, j - 1)
        if joins:
            hand_over(int(name[2])).wait()
            extra = (over0, over1)[int(name[2])]
        if closing:
            total = mine[...].astype(F32) + landed[...].astype(F32)
            if joins:
                total = total + extra[...].astype(F32)
            total_of(name)[...] = total
            return
        accumulate(mine, landed, depth)
        if joins:
            accumulate(mine, extra, depth)
        if j < len(order):
            stage_copy(name, j).start()
        else:
            hand_over(int(name[2])).start()

    def run_slot(slot):
        for name, j in SCHEDULE.get(slot, ()):
            step(name, j)

    def dec_copy(d):
        to = place(d)
        return remote(dec.at[to[0] * ns + to[1]], dec_out.at[me], d_s.at[d], d_r.at[d], to)

    def enc_copy(d):
        t = lax.rem(s + d, ns)
        return remote(encoded.at[t], enc_out.at[s], e_s.at[d], e_r.at[d], (p, t))

    def grad_copy(d):
        t = lax.rem(s + d, ns)
        return remote(in_grad.at[t], grad_out.at[s], g_s.at[d], g_r.at[d], (p, t))

    keep_dec = pltpu.make_async_copy(dec.at[me], dec_out.at[me], loc.at[4])
    keep_enc = pltpu.make_async_copy(encoded.at[s], enc_out.at[s], loc.at[5])
    keep_grad = pltpu.make_async_copy(in_grad.at[s], grad_out.at[s], loc.at[6])

    for copy in loads:
        copy.start()
    fetch(first_half * (heads // 2), 0).start()
    fetch(first_half * (heads // 2) + 1, 1).start()
    keep_dec.start()
    keep_enc.start()
    diag[...] = jnp.zeros_like(diag)
    slot_rows = n // ns
    sm[...] = jnp.zeros_like(sm)

    def put_gain(i, gain):
        for j in range(width // 128):
            sm[0, i * 6 + j:i * 6 + j + 1, :] = gain[:, j * 128:(j + 1) * 128]

    for i in range(3):
        put_gain(i, gains_dec[i:i + 1, :])
    for i in range(3):
        loads[i].wait()
    final_gain = jnp.zeros((1, width), F32)
    for i in range(ns):
        r = slice(i * slot_rows, (i + 1) * slot_rows)
        alive = (lax.broadcasted_iota(jnp.int32, (slot_rows, 1), 0) + i * slot_rows < length[0]).astype(F32)
        b = bg[r]
        down, gain = norm_down(b, rms_scale(b), fg[...], rg[i].astype(F32))
        b = alive * (ct[r].astype(F32) + down)
        bg[r] = b
        low = b.astype(BF)
        rb[r] = low
        rb_t[:, r] = low.T
        final_gain = final_gain + jnp.sum(gain, axis=0, keepdims=True)
    put_gain(3, final_gain)
    pl.semaphore_wait(barrier, count - 1)
    for d in range(1, ns):
        enc_copy(d).start()

    @pl.loop(1, count)
    def _(d):
        dec_copy(d).start()

    part = width // 4
    loads[3].wait()

    @pl.loop(0, nz)
    def _(b):
        cols = pl.ds(pl.multiple_of(b * 2 * lanes, 128), 2 * lanes)
        g = mm(rb_t[...], acts[:, cols]).astype(BF)
        for j in range(4):
            for half in range(2):
                lo = j * part + half * rows
                for e in range(2):
                    fu[j % 2, 2 + half, j // 2, b // 2, lax.rem(b, 2), e] = g[lo:lo + rows, e * lanes:(e + 1) * lanes]

    for name in pieces:
        if name[0] == "t":
            core_copy(name).start()
    loads[4].wait()
    loads[5].wait()

    for j in range(ff // width):
        cols = slice(j * width, (j + 1) * width)
        grads[:, cols] = (grads[:, cols].astype(F32) * mm_t(rb[...], w1[cols, :])).astype(BF)
        run_slot("ug" + str(j))

    for copy in weights:
        copy.start()
    loads[6].wait()

    @pl.loop(0, 4)
    def _(j):
        cols = pl.ds(pl.multiple_of(j * 2 * lanes, 128), 2 * lanes)
        g = mm(mixed_t[...], grads[:, cols]).astype(BF)
        for half in range(2):
            fu[lax.rem(j, 2), half, j // 2] = g[:, half * lanes:(half + 1) * lanes].reshape(2, 2, 2, rows, lanes)

    for name in pieces:
        if name[0] == "w":
            core_copy(name).start()
    run_slot("wide")
    loads[7].wait()
    dm[...] = mm_t(grads[...], wes[...])
    for copy in heads_in:
        copy.start()
    run_slot("dm")
    loads[8].wait()
    expand_gain = jnp.zeros((1, width), F32)
    for i in range(ns):
        r = slice(i * slot_rows, (i + 1) * slot_rows)
        t = hid[r]
        down, gain = norm_down(t, rms_scale(t), eg[...], dm[r])
        t = bg[r] + down
        bg[r] = t
        branch[r] = t.astype(BF)
        expand_gain = expand_gain + jnp.sum(gain, axis=0, keepdims=True)
    put_gain(4, expand_gain)
    run_slot("rows")
    weights[0].wait()

    @pl.loop(0, width // 384)
    def _(j):
        cols = pl.ds(pl.multiple_of(j * 384, 128), 384)
        d_out[:, cols] = mm_t(branch[...], w1[cols, :]).astype(BF)

    for copy in heads_in:
        copy.wait()
    for copy in loads[9:]:
        copy.wait()

    run_slot("dout")

    lane = lax.broadcasted_iota(jnp.int32, (n, 128), 1)
    lane_s = lax.broadcasted_iota(jnp.int32, (128, 128), 1)
    row_s = lax.broadcasted_iota(jnp.int32, (128, 128), 0)

    def pair(half, g):
        cols = pl.ds(pl.multiple_of(half * (width // 2) + g * 128, 128), 128)
        k_t[...] = k[:, cols].T
        dop = d_out[:, cols]
        qp = q[:, cols]
        vp = v[:, cols]
        zero = jnp.zeros_like(qp)
        for a in range(2):
            h = half * (heads // 2) + 2 * g + a
            mine = (lane < 64) if a == 0 else (lane >= 64)
            dp[...] = mm_t(jnp.where(mine, vp, zero), dop)
            fetch(h, a).wait()
            for j in range(n // 128):
                pj = pbuf[a, :, j * 128:(j + 1) * 128].astype(F32)
                pd = pj * dp[:, j * 128:(j + 1) * 128]
                total = jnp.sum(pd, axis=0, keepdims=True)
                sg = pd - pj * total
                ds[:, j * 128:(j + 1) * 128] = sg.astype(BF)
                for i in range(n // 128):
                    t = sg[i * 128:(i + 1) * 128]
                    if abs(i - j) <= 1:
                        b = (i - j + 1) * 128
                        if j == 0 or (j == 1 and i == 0):
                            band[b:b + 128, :] = t
                        else:
                            band[b:b + 128, :] += t
                    else:
                        f = 5 if i > j else 4
                        diag[h, f:f + 1, :] += jnp.sum(t, axis=0, keepdims=True)
            dvp = mm(pbuf[a], jnp.where(mine, dop, zero))
            dkp = mm(ds[...], jnp.where(mine, qp, zero))
            dq_t[pl.ds(pl.multiple_of(h * 64, 64), 64), :] = mm(k_t[a * 64:(a + 1) * 64, :], ds[...]).astype(BF)
            if a == 0:
                dk_sum, dv_sum = dkp, dvp
            else:
                dk[:, cols] = (dk_sum + dkp).astype(BF)
                dv[:, cols] = (dv_sum + dvp).astype(BF)
            for b in range(3):
                t = band[b * 128:(b + 1) * 128, :]
                for bit in range(7):
                    t = jnp.where((row_s >> bit) % 2 == 1, pltpu.roll(t, 128 - (1 << bit), 1), t)
                straight = jnp.sum(jnp.where(lane_s + row_s < 128, t, 0.0), axis=0, keepdims=True)
                whole = jnp.sum(t, axis=0, keepdims=True)
                diag[h, b:b + 1, :] += straight
                diag[h, b + 1:b + 2, :] += whole - straight

    def units_of(half, tag):
        cols = pl.ds(pl.multiple_of(half * (width // 2), 128), width // 2)
        dq_h = dq_t[cols, :].T
        dq[:, cols] = dq_h
        dk_h = dk[:, cols]
        for cc in range(2):
            e = slice(cc * part, (cc + 1) * part)
            g = mm(normed_t[...], jnp.concatenate([dq_h[:, e], dk_h[:, e]], axis=1))
            au(0, cc, half)[...] = g.astype(BF).reshape(2, 2, 2, rows, lanes)
        core_copy("h" + tag + "0").start()
        run_slot("q" + tag)
        dv_h = dv[:, cols]
        br_h = branch[:, cols]
        zero = jnp.zeros((n, part), BF)
        for cc in range(2):
            e = slice(cc * part, (cc + 1) * part)
            g = (mm(normed_t[...], jnp.concatenate([dv_h[:, e], zero], axis=1))
                 + mm(context_t[...], jnp.concatenate([zero, br_h[:, e]], axis=1)))
            au(1, cc, half)[...] = g.astype(BF).reshape(2, 2, 2, rows, lanes)
        core_copy("h" + tag + "1").start()
        run_slot("v" + tag)

    quarter = heads // 4

    @pl.loop(0, quarter)
    def _(g):
        pair(first_half, g)
        nxt = jnp.where(g == quarter - 1, last_half * (heads // 2), first_half * (heads // 2) + 2 * (g + 1))
        fetch(nxt, 0).start()
        fetch(nxt + 1, 1).start()

        for i in range(quarter):
            if SCHEDULE.get("p0" + str(i)):
                @pl.when(g == i)
                def _():
                    run_slot("p0" + str(i))

    units_of(first_half, "0")

    @pl.loop(0, quarter)
    def _(g):
        pair(last_half, g)

        @pl.when(g < quarter - 1)
        def _():
            nxt = last_half * (heads // 2) + 2 * (g + 1)
            fetch(nxt, 0).start()
            fetch(nxt + 1, 1).start()

        for i in range(quarter):
            if SCHEDULE.get("p1" + str(i)):
                @pl.when(g == i)
                def _():
                    run_slot("p1" + str(i))

    units_of(last_half, "1")
    for copy in weights[1:]:
        copy.wait()

    for i in range(2):
        r = slice(i * (n // 2), (i + 1) * (n // 2))
        ng[r] = mm_t(dq[r], wqs[...]) + mm_t(dk[r], wks[...]) + mm_t(dv[r], wvs[...])
        run_slot("ng" + str(i))

    gain_sum = jnp.zeros((1, width), F32)
    for i in range(ns):
        r = slice(i * slot_rows, (i + 1) * slot_rows)
        t = x[r].astype(F32)
        down, gain = norm_down(t, rms_scale(t), ag[...], ng[r])
        in_grad[i] = (hidden_grad[r] + down).astype(BF)
        gain_sum = gain_sum + jnp.sum(gain, axis=0, keepdims=True)
    keep_grad.start()
    for d in range(1, ns):
        grad_copy(d).start()

    col = lax.broadcasted_iota(jnp.int32, (128, width), 1)
    offset = (col // 128 - 1) * 128 - lax.rem(col, 128)
    offset = jnp.where(col >= width - 128, 256, jnp.where(col >= width - 256, -256, offset))
    dist = jnp.abs(offset)
    bucket = jnp.full_like(dist, 8)
    for edge in EDGES:
        bucket = bucket + (dist >= edge).astype(jnp.int32)
    bucket = jnp.where(dist < 8, dist, bucket) + jnp.where(offset > 0, 16, 0)
    pick = jnp.where(bucket == lax.broadcasted_iota(jnp.int32, (128, width), 0), 1.0, 0.0)
    bias = jnp.zeros((16, 128), F32)
    for i in range(width // 128):
        bias = bias + lax.dot_general(diag[:, i, :], pick[:, i * 128:(i + 1) * 128], (((1,), (1,)), ((), ())),
                                      precision=HIGHEST, preferred_element_type=F32)
    sm[0, 40:56, :] = bias
    put_gain(5, gain_sum)

    def small_copy(i):
        return remote(sm.at[i], smr.at[i], m_s.at[i], m_r.at[i], (core_peer, y_peer, x_peer)[i])

    def z_small(d):
        return remote(smz.at[z], smz.at[z], mz_s.at[d], mz_r.at[d], (lax.rem(z + d, nz) * 2 + xx, s))

    def small_hop(i):
        small_copy(i).wait()
        if i < 2:
            sm[i + 1] = sm[i] + smr[i]
            small_copy(i + 1).start()
        else:
            smz[z] = sm[i] + smr[i]

            @pl.loop(1, nz)
            def _(d):
                z_small(d).start()

    small_copy(0).start()
    tail = SCHEDULE["end"]
    for i, (name, j) in enumerate(tail):
        step(name, j)
        if i in HOPS:
            small_hop(HOPS.index(i))

    @pl.loop(1, nz)
    def _(d):
        z_small(d).wait()

    small_out[...] = smz[0]

    @pl.loop(1, nz)
    def _(d):
        small_out[...] = small_out[...] + smz[d]

    keep_dec.wait()
    keep_enc.wait()
    keep_grad.wait()
    for d in range(1, ns):
        enc_copy(d).wait()
        grad_copy(d).wait()

    @pl.loop(1, count)
    def _(d):
        dec_copy(d).wait()


def fused(np_, ns, length, fg, eg, ag, gains_dec, rows_grad, block, cot, wr, active, we, hidden, slope, mixed_t,
          wo, wq, wk, wv, q, k, v, x, normed_t, context_t, probs, dec, encoded):
    n, width = hidden.shape
    ff = active.shape[1]
    heads = probs.shape[0]
    nz = np_ // 2
    rows, lanes = width // np_, ff // np_
    count = np_ * ns
    smem = pl.BlockSpec(memory_space=pltpu.SMEM)
    vm = pl.BlockSpec(memory_space=pltpu.VMEM)
    hb = pl.BlockSpec(memory_space=pl.ANY)
    S = jax.ShapeDtypeStruct
    V = pltpu.VMEM
    dma = pltpu.SemaphoreType.DMA
    nar, tall = V((n, width), BF), V((width, n), BF)
    floats = V((n, width), F32)
    slots = (ns, n // ns, width)
    small = (64, 128)
    ffs = 4 * PARTS
    sub = rows // PARTS

    def joint(w):
        return V((2,) * (3 - ORDERS["a" + str(w)].index("y")) + (rows, lanes), BF)

    return pl.pallas_call(
        functools.partial(fused_kernel, np_, ns),
        out_shape=(S((6, rows, lanes), F32), S(small, F32), S(dec.shape, BF), S(slots, BF), S(slots, BF)),
        in_specs=[smem] + [vm] * 4 + [hb] * 22,
        out_specs=(vm, vm, hb, hb, hb),
        scratch_shapes=[
            V((n, ff), BF), V((n, ff), BF), V((ff, width), BF), V((width, ff), BF), floats, floats, floats,
            V(slots, BF), nar, nar, tall, tall, tall, tall,
            V((n, n), F32), V((n, n), BF), V((2, n, n), BF), V((128, n), BF), V((384, 128), F32), V((16, 8, 128), F32),
            V((2, 4, 2, 2, 2, 2, rows, lanes), BF), V((ffs, 2, 2, 2, 2, sub, lanes), BF), V((4, 2, 2, 2, rows, lanes), BF),
            V((ffs, 2, 2, 2, sub, lanes), BF), V((ffs, 2, 2, sub, lanes), BF), V((ffs, 2, sub, lanes), BF),
            V((ffs, sub, lanes), BF), V((4, 2, 2, rows, lanes), BF), V((4, 2, rows, lanes), BF),
            V((4, rows, lanes), BF), joint(0), joint(1),
            V((3,) + small, F32), V((3,) + small, F32), V((nz,) + small, F32),
            dma((2,)), dma((19,)), dma((7,)), dma((ffs + 4,)), dma((ffs + 4,)), dma((ffs + 4, 4)), dma((ffs + 4, 4)),
            dma((2,)), dma((2,)),
            dma((3,)), dma((3,)), dma((nz,)), dma((nz,)), dma((count,)), dma((count,)),
            dma((ns,)), dma((ns,)), dma((ns,)), dma((ns,)),
        ],
        compiler_params=pltpu.CompilerParams(
            collective_id=0, has_side_effects=True, vmem_limit_bytes=62 * 1024 * 1024),
        name="fused_backward",
    )(length, fg.reshape(1, -1), eg.reshape(1, -1), ag.reshape(1, -1), gains_dec, rows_grad.reshape(slots), block, cot, wr,
      active, we, hidden, slope, mixed_t, wo, wq, wk, wv, q, k, v, x, normed_t, context_t, probs, dec,
      encoded.reshape(slots))


def two_kernels(
    np_, ns, r, rp, lanes, side, length, final_gain, expand_gain, attend_gain, dec_gains,
    rows_grad, block, cot, reduce_weight, active, expand_weight, hidden, slope, mixed_t,
    output_weight, query_weight, key_weight, value_weight, query, key, value, x, normed_t,
    context_t, probs, dec_all, encoded,
):
    seq_len, ff = active.shape
    nz = np_ // 2
    wide, tall, hidden_grad, branch, feed_gains = feed_back(
        1, length, rows_grad, block, cot, final_gain, hidden, expand_gain, mixed_t.T, active,
        slope, reduce_weight, expand_weight)

    def pad(unit):
        return jnp.pad(unit, ((0, 0),) * 5 + ((0, rp - r), (0, 0)))

    tall = tall.reshape(2, 2, 2, r, side, nz, 2, ff // np_).transpose(0, 1, 2, 5, 6, 3, 4, 7)
    tall = pad(tall.reshape(2, 2, 2, nz, 2, r, lanes))
    wide = pad(wide.reshape(2, 2, 2, nz, 2, r, lanes))
    gap = ((0, 0), (0, rp - r), (0, 0))
    normed_t = jnp.pad(normed_t.reshape(np_, r, seq_len), gap).reshape(np_ * rp, seq_len)
    context_t = jnp.pad(context_t.reshape(np_, r, seq_len), gap).reshape(np_ * rp, seq_len)
    return backward(
        np_, ns, x, attend_gain, query, key, value, context_t, branch, hidden_grad, normed_t.T,
        dec_gains, feed_gains, probs, output_weight, query_weight, key_weight, value_weight,
        wide, tall, dec_all, encoded)


def per_device(
    enc_input, dec_input, lengths, attend_gain, query_weight, key_weight, value_weight,
    output_weight, bias_table, expand_gain, expand_weight, reduce_weight, final_gain,
    self_gain, self_value, self_output, cross_gain, cross_query, cross_key, cross_value,
    cross_output, feed_gain, feed_expand, feed_reduce, enc_cotangent, dec_cotangent,
):
    group, local_rows, width = enc_input.shape
    buckets, heads = bias_table.shape
    size = width // heads
    ff = expand_weight.shape[1]
    ns = lax.axis_size("seq")
    np_ = lax.axis_size("pairs")
    place = lax.axis_index("seq")
    seq_len = local_rows * ns
    length = lax.dynamic_slice_in_dim(lengths, place, 1)
    x = lax.all_to_all(enc_input, "seq", split_axis=0, concat_axis=1, tiled=True)[0]
    cot = lax.all_to_all(enc_cotangent, "seq", split_axis=0, concat_axis=1, tiled=True)[0]

    band_bucket = rel_bucket(jnp.arange(128), jnp.arange(384) - 128).T
    onehot = (jnp.arange(buckets, dtype=jnp.int32)[:, None, None] == band_bucket).astype(F32)
    band = jnp.einsum("but,bh->hut", onehot, bias_table, precision=HIGHEST)
    far = jnp.stack([bias_table[15], bias_table[31]], axis=1)

    (normed_t, query, key, value, probs, context_t, hidden, mixed_t, active, slope, block, enc_rows,
     encoded) = encode(length, x, attend_gain, expand_gain, final_gain, band, far, query_weight,
                       key_weight, value_weight, output_weight, expand_weight, reduce_weight)
    dec_block, dec_input_grad, dec_gains, left, right, wide_rows, mids, rows_grad = decode(
        length, enc_rows, dec_input, dec_cotangent, self_gain, cross_gain, feed_gain, heads,
        self_value, self_output, cross_query, cross_key, cross_value, cross_output, feed_expand,
        feed_reduce)
    r = width // np_
    aligned = np_ == 8 and r % 32 == 0 and (ff // np_) % 128 == 0 and ff == 4 * width
    rp = -(-r // 16) * 16
    lanes = ff // 8
    side = width // 8 // r
    cols = width // ns

    left_cut = jnp.concatenate([
        left.reshape(5, np_, r).transpose(1, 0, 2).reshape(np_, 5 * r),
        wide_rows[0].reshape(np_, 4 * r),
    ], axis=1)
    mid_cut = mids.reshape(2, ns, heads // ns, np_, r).transpose(3, 1, 0, 2, 4)
    mid_cut = mid_cut.reshape(np_, ns, 6 * r)
    right_cut = jnp.concatenate([
        right.reshape(7, ns, cols).transpose(1, 0, 2).reshape(ns, 7 * cols),
        wide_rows[1].reshape(ns, 4 * cols)], axis=1)
    dec_all = jnp.concatenate([
        jnp.broadcast_to(left_cut[:, None], (np_, ns, 9 * r)), mid_cut,
        jnp.broadcast_to(right_cut[None], (np_, ns, 11 * cols))], axis=-1)
    dec_all = dec_all.astype(BF).reshape(np_ * ns, -1)
    used = dec_all.shape[1]
    dec_rows = -(-used // 2048) * 16
    dec_all = jnp.pad(dec_all, ((0, 0), (0, dec_rows * 128 - used)))
    dec_all = dec_all.reshape(np_ * ns, dec_rows, 128)

    if aligned:
        red, small_sum, dec_got, enc_out, grad_out = fused(
            np_, ns, length, final_gain, expand_gain, attend_gain, dec_gains, rows_grad, block, cot,
            reduce_weight, active, expand_weight, hidden, slope, mixed_t, output_weight,
            query_weight, key_weight, value_weight, query, key, value, x, normed_t, context_t,
            probs, dec_all, encoded)
    else:
        red, small_sum, dec_got, enc_out, grad_out = two_kernels(
            np_, ns, r, rp, lanes, side, length, final_gain, expand_gain, attend_gain, dec_gains,
            rows_grad, block, cot, reduce_weight, active, expand_weight, hidden, slope, mixed_t,
            output_weight, query_weight, key_weight, value_weight, query, key, value, x, normed_t,
            context_t, probs, dec_all, encoded)

    got = dec_got.reshape(np_ * ns, -1)
    lefts = got[:, :9 * r].reshape(-1, 9, r)
    mid_got = got[:, 9 * r:15 * r].reshape(-1, 2, 3, r)
    rights = got[:, 15 * r:15 * r + 11 * cols].reshape(-1, 11, cols)
    plain = jnp.einsum("nkr,nkc->krc", lefts[:, :4], rights[:, :4], preferred_element_type=F32)
    crossed = jnp.einsum("nkhr,nkhd->krhd", mid_got, rights[:, 4:6].reshape(-1, 2, 3, size),
                         preferred_element_type=F32).reshape(2, r, cols)
    feed_in = jnp.einsum("nr,nc->rc", lefts[:, 4], rights[:, 7:11].reshape(-1, 4 * cols),
                         preferred_element_type=F32)
    feed_out = jnp.einsum("nr,nc->rc", lefts[:, 5:9].reshape(-1, 4 * r), rights[:, 6],
                          preferred_element_type=F32)
    red = red[:, :r]
    grad_reduce = red[2:4].reshape(2, r, side, ff // np_).reshape(cols, ff // np_).T
    gains = small_sum[:36].reshape(6, width)
    bias = small_sum[40:40 + heads, :buckets].T
    return (
        enc_out, dec_block, grad_out, dec_input_grad,
        gains[5],
        red[4][:, :cols], red[4][:, cols:], red[5][:, :cols], red[5][:, cols:],
        bias,
        gains[4],
        jnp.concatenate([red[0], red[1]], axis=1), grad_reduce,
        gains[3],
        gains[0], plain[0], plain[1],
        gains[1], plain[2], crossed[0], crossed[1], plain[3],
        gains[2], feed_in, feed_out,
    )


def solution(mesh):
    rows = P("pairs", "seq", None)
    single = P(("pairs", "seq"), None)
    block = P("pairs", "seq")
    return jax.shard_map(
        per_device,
        mesh=mesh,
        in_specs=(rows, single, P("pairs")) + (P(),) * 21 + (rows, single),
        out_specs=(
            rows, single, rows, single,
            P(), block, block, block, block, P(), P(), block, block, P(),
            P(), block, block, P(), block, block, block, block, P(), block, block,
        ),
        check_vma=False,
    )
```

```python
import functools
import itertools

import jax
import jax.numpy as jnp
from jax import lax
from jax.experimental import pallas as pl
from jax.experimental.pallas import tpu as pltpu
from jax.sharding import PartitionSpec as P

EPSILON = 1e-06
EDGES = (12, 16, 23, 32, 46, 64, 91)
HIGHEST = lax.Precision.HIGHEST
MESH = pl.DeviceIdType.MESH
BF = jnp.bfloat16
F32 = jnp.float32


def mm(a, b):
    return jnp.dot(a, b, preferred_element_type=F32)
def mm_t(a, b):
    return lax.dot_general(a, b, (((1,), (1,)), ((), ())), preferred_element_type=F32)
def t_mm(a, b):
    return lax.dot_general(a, b, (((0,), (0,)), ((), ())), preferred_element_type=F32)

def rms_scale(v):
    return lax.rsqrt(jnp.mean(v * v, axis=-1, keepdims=True) + EPSILON)

def gelu_parts(u):
    u2 = u * u
    t = jnp.tanh(u * (0.7978845608 + (0.7978845608 * 0.044715) * u2))
    half = 0.5 + 0.5 * t
    return u * half, half + half * (1.0 - t) * u * (0.7978845608 + (3 * 0.7978845608 * 0.044715) * u2)

def norm_down(v, r, g, dy):
    vr = v * r
    gd = g * dy
    return r * (gd - vr * jnp.mean(vr * gd, axis=-1, keepdims=True)), vr * dy

def diagonal_buckets(shape, width):
    col = lax.broadcasted_iota(jnp.int32, shape, 1)
    offset = (col // 128 - 1) * 128 - lax.rem(col, 128)
    offset = jnp.where(col >= width - 128, 256, jnp.where(col >= width - 256, -256, offset))
    dist = jnp.abs(offset)
    bucket = jnp.full_like(dist, 8)
    for edge in EDGES:
        bucket = bucket + (dist >= edge).astype(jnp.int32)
    bucket = jnp.where(dist < 8, dist, bucket) + jnp.where(offset > 0, 16, 0)
    return jnp.where(bucket == lax.broadcasted_iota(jnp.int32, shape, 0), 1.0, 0.0)


def forward_kernel(np_, ns, cut, *refs):
    names = list((
        "lengths", "table", "ag", "eg", "fg", "sg", "cg", "dg", "dec_in", "dec_cot", "enc_in",
        "enc_cot", "wq", "wk", "wv", "wo", "we", "wr", "sv", "so", "cq", "ck", "cv", "co", "fe",
        "fr", "normed_t", "q", "k", "v", "probs", "context_t", "hidden", "mixed_t", "active",
        "slope", "block", "low", "x_out", "cot_out", "rows_grad", "dec_out", "dec_in_grad",
        "dec_gains",
    ))
    names += ["dec"] if cut else ["left", "right", "wide", "mids"]
    names += (
        "wqs", "wks", "wvs", "wos", "wes", "wrs", "svs", "sos", "cqs", "cks", "cvs", "cos",
        "fes", "frs", "xs", "normed", "nt", "qs", "ks", "vs", "ctx", "hid", "mixed", "mt", "act",
        "slo", "blk", "rws", "lws", "rgs", "band", "vecs", "v_t", "s_t", "pbuf",
    )
    names += ["s_left", "s_right", "s_wide", "s_mids", "s_cut", "s_both"] if cut else []
    names += (
        "sems", "psem", "osem", "x_s", "x_r", "c_s", "c_r", "loc",
    )
    R = dict(zip(names, refs, strict=True))
    G = lambda name: R[name]
    lengths, table, band, vecs = G("lengths"), G("table"), G("band"), G("vecs")
    ag, eg, fg, sg, cg, dg = (G(name)[...].reshape(1, -1) for name in ("ag", "eg", "fg", "sg", "cg", "dg"))
    xs, normed, nt, qs, ks, vs, ctx, hid, mixed, mt, act, slo, blk, rws, lws, rgs = (G(name) for name in (
        "xs", "normed", "nt", "qs", "ks", "vs", "ctx", "hid", "mixed", "mt", "act", "slo", "blk", "rws", "lws", "rgs"))
    s_t, pbuf, v_t, probs = G("s_t"), G("pbuf"), G("v_t"), G("probs")
    n, width = normed.shape
    heads = probs.shape[0]
    size = width // heads
    ff = act.shape[1]
    slot = n // ns
    p = lax.axis_index("pairs")
    s = lax.axis_index("seq")
    length = lengths[s]

    barrier = pltpu.get_barrier_semaphore()
    for d in range(1, ns):
        pl.semaphore_signal(barrier, inc=1, device_id=(p, lax.rem(s + d, ns)), device_id_type=MESH)

    def rows_copy(src, dst, send, recv, d):
        t = lax.rem(s + d, ns)
        return pltpu.make_async_remote_copy(
            src_ref=G(src).at[t], dst_ref=G(dst).at[s], send_sem=G(send).at[d], recv_sem=G(recv).at[d],
            device_id=(p, t), device_id_type=MESH)

    x_copies = [rows_copy("enc_in", "xs", "x_s", "x_r", d) for d in range(1, ns)]
    cot_copies = [rows_copy("enc_cot", "cot_out", "c_s", "c_r", d) for d in range(1, ns)]
    keep_x = pltpu.make_async_copy(G("enc_in").at[s], xs.at[s], G("loc").at[0])
    keep_cot = pltpu.make_async_copy(G("enc_cot").at[s], G("cot_out").at[s], G("loc").at[1])
    keep_x.start()
    load = {}
    for i, name in enumerate((
            "sv", "so", "cq", "ck", "fr", "wq", "wk", "wv", "wo", "we", "wr", "cv", "co", "fe")):
        load[name] = pltpu.make_async_copy(G(name), G(name + "s"), G("sems").at[i])
        load[name].start()
    pl.semaphore_wait(barrier, ns - 1)
    for copy in x_copies + cot_copies:
        copy.start()
    keep_cot.start()
    saved = []

    def save(src, dst):
        copy = pltpu.make_async_copy(src, G(dst), G("osem").at[len(saved)])
        saved.append(copy)
        copy.start()

    vec = lax.dot_general(table[...], diagonal_buckets((table.shape[0], width), width), (((0,), (0,)), ((), ())),
                          precision=HIGHEST, preferred_element_type=F32)
    for i in range(width // 128):
        vecs[:, i, :] = vec[:, i * 128:(i + 1) * 128]
    lane_s = lax.broadcasted_iota(jnp.int32, (128, 128), 1)
    row_s = lax.broadcasted_iota(jnp.int32, (128, 128), 0)

    @pl.loop(0, heads)
    def _(h):
        for b in range(3):
            t = jnp.where(lane_s + row_s < 128, vecs[h, b:b + 1, :], vecs[h, b + 1:b + 2, :])
            for bit in range(7):
                t = jnp.where((row_s >> bit) % 2 == 1, pltpu.roll(t, 1 << bit, 1), t)
            band[h, b * 128:(b + 1) * 128, :] = t

    x = G("dec_in")[...].astype(F32)
    cot = G("dec_cot")[...]
    own = (lax.broadcasted_iota(jnp.int32, (heads, width), 1) // size
           == lax.broadcasted_iota(jnp.int32, (heads, width), 0))

    def spread(r):
        return jnp.where(own, r.astype(F32), 0.0).astype(BF)

    def collect(r):
        return jnp.sum(jnp.where(own, r, 0.0), axis=0, keepdims=True)

    x_r = rms_scale(x)
    self_normed = (x * x_r * sg).astype(BF)
    load["sv"].wait()
    self_values = mm(self_normed, G("svs")[...]).astype(BF)
    load["so"].wait()
    after = x + mm(self_values, G("sos")[...])
    after_r = rms_scale(after)
    cross_normed = (after * after_r * cg).astype(BF)
    load["cq"].wait()
    cross_q = mm(cross_normed, G("cqs")[...]).astype(BF)
    load["ck"].wait()
    q_rows = mm_t(spread(cross_q), G("cks")[...]).astype(BF)
    load["fr"].wait()
    active_back = mm_t(cot, G("frs")[...])

    keep_x.wait()
    for copy in x_copies:
        copy.wait()
    save(xs, "x_out")
    for i in range(ns):
        r = slice(i * slot, (i + 1) * slot)
        t = xs[i].astype(F32)
        t = t * rms_scale(t) * ag
        normed[r] = t.astype(BF)
        nt[:, r] = t.T.astype(BF)
    save(nt, "normed_t")
    for name, out in (("q", qs), ("k", ks), ("v", vs)):
        load["w" + name].wait()
        for i in range(2):
            r = slice(i * (n // 2), (i + 1) * (n // 2))
            out[r] = mm(normed[r], G("w" + name + "s")[...]).astype(BF)
        save(out, name)

    lane = lax.broadcasted_iota(jnp.int32, (n, 128), 1)
    row = lax.broadcasted_iota(jnp.int32, (n, 128), 0)
    q_mark = jnp.where(lane == 0, 1.0, 0.0).astype(BF)
    k_mark = jnp.where((lane == 0) & (row >= length), -1e30, 0.0).astype(BF)

    def keep(h, a):
        return pltpu.make_async_copy(pbuf.at[a], probs.at[h], G("psem").at[a])

    @pl.loop(0, heads // 2)
    def _(g):
        cols = pl.ds(pl.multiple_of(g * 128, 128), 128)
        v_t[...] = vs[:, cols].T
        qq = jnp.concatenate([qs[:, cols], q_mark], axis=1)
        kp = ks[:, cols]
        for a in range(2):
            h = 2 * g + a
            mine = (lane < 64) if a == 0 else (lane >= 64)
            kk = jnp.concatenate([jnp.where(mine, kp, jnp.zeros_like(kp)), k_mark], axis=1)
            s_t[a] = mm_t(kk, qq)

            @pl.when(g > 0)
            def _():
                keep(h - 2, a).wait()

            for j in range(n // 128):
                tile = []
                for i in range(n // 128):
                    t = s_t[a, i * 128:(i + 1) * 128, j * 128:(j + 1) * 128]
                    if abs(i - j) <= 1:
                        t = t + band[h, (i - j + 1) * 128:(i - j + 2) * 128, :]
                    else:
                        f = 5 if i > j else 4
                        t = t + vecs[h, f:f + 1, :]
                    tile.append(t)
                t = jnp.concatenate(tile, axis=0)
                m = jnp.max(t, axis=0, keepdims=True)
                e = jnp.exp(t - m)
                total = jnp.sum(e, axis=0, keepdims=True)
                pbuf[a, :, j * 128:(j + 1) * 128] = (e * (1.0 / total)).astype(BF)
            ctx[pl.ds(pl.multiple_of(h * 64, 64), 64), :] = mm(v_t[a * 64:(a + 1) * 64, :], pbuf[a]).astype(BF)
            keep(h, a).start()

    save(ctx, "context_t")
    load["wo"].wait()
    for i in range(ns):
        r = slice(i * slot, (i + 1) * slot)
        t = xs[i].astype(F32) + mm(ctx[:, r].T, G("wos")[...])
        hid[r] = t
        t = t * rms_scale(t) * eg
        mixed[r] = t.astype(BF)
        mt[:, r] = t.T.astype(BF)
    save(hid, "hidden")
    save(mt, "mixed_t")
    load["we"].wait()

    @pl.loop(0, ff // 512)
    def _(j):
        cols = pl.ds(pl.multiple_of(j * 512, 512), 512)
        a, b = gelu_parts(mm(mixed[...], G("wes")[:, cols]))
        act[:, cols] = a.astype(BF)
        slo[:, cols] = b.astype(BF)

    save(act, "active")
    save(slo, "slope")
    load["wr"].wait()
    for i in range(2):
        r = slice(i * (n // 2), (i + 1) * (n // 2))
        alive = (lax.broadcasted_iota(jnp.int32, (n // 2, 1), 0) + i * (n // 2) < length).astype(F32)
        b = alive * (hid[r] + mm(act[r], G("wrs")[...]))
        blk[r] = b
        lws[r] = b.astype(BF)
        rws[r] = (b * rms_scale(b) * fg).astype(BF)
    save(blk, "block")
    save(lws, "low")

    score = mm_t(q_rows, rws[...])
    score = jnp.where(lax.broadcasted_iota(jnp.int32, score.shape, 1) < length, score, -1e30)
    e = jnp.exp(score - jnp.max(score, axis=-1, keepdims=True))
    cross_probs = e / jnp.sum(e, axis=-1, keepdims=True)
    cross_low = cross_probs.astype(BF)
    mean_rows = mm(cross_low, rws[...]).astype(BF)
    for name in ("cv", "co", "fe"):
        load[name].wait()
    cross_context = collect(mm(mean_rows, G("cvs")[...])).astype(BF)
    middle = after + mm(cross_context, G("cos")[...])
    middle_r = rms_scale(middle)
    feed_normed = (middle * middle_r * dg).astype(BF)
    dec_active, dec_slope = gelu_parts(mm(feed_normed, G("fes")[...]))
    dec_active = dec_active.astype(BF)
    upper_grad = (dec_slope * active_back).astype(BF)
    middle_down, feed_gain = norm_down(middle, middle_r, dg, mm_t(upper_grad, G("fes")[...]))
    middle_grad = cot.astype(F32) + middle_down
    cross_branch = middle_grad.astype(BF)
    context_grad = mm_t(cross_branch, G("cos")[...]).astype(BF)
    g_rows = mm_t(spread(context_grad), G("cvs")[...]).astype(BF)
    prob_grad = mm_t(g_rows, rws[...])
    score_grad = (cross_probs * (prob_grad - jnp.sum(cross_probs * prob_grad, axis=-1, keepdims=True))).astype(BF)
    pad = jnp.zeros((16 - heads % 16, n), BF)
    padw = jnp.zeros((16 - heads % 16, width), BF)
    rgs[...] = t_mm(jnp.concatenate([score_grad, pad, cross_low, pad], axis=0),
                    jnp.concatenate([q_rows, padw, g_rows, padw], axis=0)).astype(BF)
    save(rgs, "rows_grad")
    score_rows = mm(score_grad, rws[...]).astype(BF)
    cross_q_grad = collect(mm(score_rows, G("cks")[...])).astype(BF)
    after_down, cross_gain = norm_down(after, after_r, cg, mm_t(cross_q_grad, G("cqs")[...]))
    after_grad = middle_grad + after_down
    self_branch = after_grad.astype(BF)
    self_values_grad = mm_t(self_branch, G("sos")[...]).astype(BF)
    x_down, self_gain = norm_down(x, x_r, sg, mm_t(self_values_grad, G("svs")[...]))
    G("dec_in_grad")[...] = (after_grad + x_down).astype(BF)
    G("dec_out")[...] = (middle + mm(dec_active, G("frs")[...])).astype(BF)
    gains = G("dec_gains")
    gains[0:1, :] = self_gain
    gains[1:2, :] = cross_gain
    gains[2:3, :] = feed_gain
    left, right, wide, mids = (G(("s_" if cut else "") + name) for name in ("left", "right", "wide", "mids"))
    for i, r in enumerate((self_normed, self_values, cross_normed, cross_context, feed_normed)):
        left[i:i + 1, :] = r.astype(F32)
    for i, r in enumerate((self_values_grad, self_branch, cross_q_grad, cross_branch, cross_q, context_grad, cot)):
        right[i:i + 1, :] = r.astype(F32)
    wide[0:1, :] = dec_active.astype(F32)
    wide[1:2, :] = upper_grad.astype(F32)
    mids[0] = score_rows.astype(F32)
    mids[1] = mean_rows.astype(F32)
    if cut:
        dec, cuts, both = G("dec"), G("s_cut"), G("s_both")
        rows, cols, step = width // np_, width // ns, heads // ns
        both[...] = jnp.zeros_like(both)
        cuts[...] = jnp.zeros_like(cuts)
        for j in range(ns):
            for i in range(7):
                t = right[i:i + 1, j * cols:(j + 1) * cols]
                both[j, 2 * i:2 * i + 1, :] = t[:, :128]
                both[j, 2 * i + 1:2 * i + 2, 0:cols - 128] = t[:, 128:]
            for i in range(6):
                lo = j * width + i * 128
                both[j, 14 + i:15 + i, :] = wide[1:2, lo:lo + 128]
        for i in range(np_):
            cuts[0:5, 0:rows] = left[0:5, i * rows:(i + 1) * rows]
            for a in range(3):
                lo = i * (ff // np_) + a * 128
                cuts[5 + a:6 + a, :] = wide[0:1, lo:lo + 128]
            for j in range(ns):
                for w in range(2):
                    cuts[8 + w * step:8 + (w + 1) * step, 0:rows] = (
                        mids[w, j * step:(j + 1) * step, i * rows:(i + 1) * rows])
                dec[i * ns + j, 0:16, :] = cuts[...].astype(BF)
                dec[i * ns + j, 16:48, :] = both[j].astype(BF)
    for a in range(2):
        keep(heads - 2 + a, a).wait()
    keep_cot.wait()
    for copy in cot_copies:
        copy.wait()
    for copy in saved:
        copy.wait()


def forward(np_, ns, cut, lengths, table, gains, dec_in, dec_cot, enc_in, enc_cot, weights):
    group, slot, width = enc_in.shape
    n = slot * ns
    ff = weights[4].shape[1]
    heads = table.shape[1]
    smem = pl.BlockSpec(memory_space=pltpu.SMEM)
    vm = pl.BlockSpec(memory_space=pltpu.VMEM)
    hb = pl.BlockSpec(memory_space=pl.ANY)
    S = jax.ShapeDtypeStruct
    V = pltpu.VMEM
    full, tall, floats, broad = ((n, width), BF), ((width, n), BF), ((n, width), F32), ((n, ff), BF)
    slots = ((ns, slot, width), BF)
    raw = [((5, width), F32), ((7, width), F32), ((2, ff), F32), ((2, heads, width), F32)]
    outs = [tall, full, full, full, ((heads, n, n), BF), tall, floats, tall, broad, broad, floats, full, slots, slots,
            full, ((1, width), BF), ((1, width), BF), ((3, width), F32)]
    outs += [((np_ * ns, 48, 128), BF)] if cut else raw
    scratch = [slots, full, tall, full, full, full, tall, floats, full, tall, broad, broad, floats, full, full, full,
               ((heads, 384, 128), F32), ((heads, 8, 128), F32), ((128, n), BF), ((2, n, n), F32), ((2, n, n), BF)]
    scratch += raw + [((16, 128), F32), ((ns, 32, 128), F32)] if cut else []
    dma = pltpu.SemaphoreType.DMA
    return pl.pallas_call(
        functools.partial(forward_kernel, np_, ns, cut),
        out_shape=tuple(S(*t) for t in outs),
        in_specs=[smem] + [vm] * 9 + [hb] * 16,
        out_specs=(hb,) * 15 + (vm,) * (len(outs) - 15),
        scratch_shapes=[V(w.shape, BF) for w in weights] + [V(*t) for t in scratch] + [
            dma((14,)), dma((2,)), dma((16,)), dma((ns,)), dma((ns,)), dma((ns,)), dma((ns,)), dma((2,))],
        compiler_params=pltpu.CompilerParams(
            collective_id=1, has_side_effects=True, vmem_limit_bytes=62 * 1024 * 1024),
        name="forward",
    )(lengths, table, *gains, dec_in, dec_cot, enc_in, enc_cot, *weights)


def finish_kernel(heads, red, small, dec, enc, grad, *outs):
    (enc_out, grad_out, qo, ko, vo, oo, expand, reduce, bias, g0, g1, g2, g3, g4, g5,
     sv, so, cq, ck, cv, co, fe, fr, wide, sem) = outs
    copies = [pltpu.make_async_copy(enc, enc_out, sem.at[0]), pltpu.make_async_copy(grad, grad_out, sem.at[1])]
    for copy in copies:
        copy.start()
    wide[...] = dec[...].astype(F32)
    rows, cols = qo.shape
    lanes = red.shape[2]
    for i, out in ((4, (qo, ko)), (5, (vo, oo))):
        t = red[i]
        out[0][...] = t[:, :cols]
        out[1][...] = t[:, cols:]
    for i in range(2):
        expand[:, i * lanes:(i + 1) * lanes] = red[i]
        reduce[i * rows:(i + 1) * rows, :] = red[2 + i]
    bias[...] = small[40:40 + heads, 0:bias.shape[1]]
    for i, out in enumerate((g0, g1, g2, g3, g4, g5)):
        for j in range(6):
            out[pl.ds(j * 128, 128)] = small[i * 6 + j, :]

    def row(i):
        return wide[:, i, :]

    def pair(i):
        return jnp.concatenate([row(16 + 2 * i), row(17 + 2 * i)], axis=1)[:, :cols].astype(BF)

    for i, out in enumerate((sv, so, cq, co)):
        out[...] = t_mm(row(i)[:, :rows].astype(BF), pair(i))
    upper = jnp.concatenate([row(30 + i) for i in range(6)], axis=1).astype(BF)
    fe[...] = t_mm(row(4)[:, :rows].astype(BF), upper)
    active = jnp.concatenate([row(5 + i) for i in range(3)], axis=1).astype(BF)
    fr[...] = t_mm(pair(6), active)
    step = cols // 64
    for w, out in enumerate((ck, cv)):
        g = pair(4 + w)
        out[...] = jnp.concatenate(
            [t_mm(row(8 + w * step + h)[:, :rows].astype(BF), g[:, h * 64:(h + 1) * 64]) for h in range(step)], axis=1)
    for copy in copies:
        copy.wait()


def finish(heads, buckets, red, small, dec, enc, grad):
    rows, lanes = red.shape[1:]
    cols, width = lanes // 2, 2 * lanes
    vm = pl.BlockSpec(memory_space=pltpu.VMEM)
    hb = pl.BlockSpec(memory_space=pl.ANY)
    S = jax.ShapeDtypeStruct
    block, broad, tall = S((rows, cols), F32), S((rows, width), F32), S((cols, lanes), F32)
    return pl.pallas_call(
        functools.partial(finish_kernel, heads),
        out_shape=(S(enc.shape, BF), S(grad.shape, BF), block, block, block, block, broad, tall,
                   S((heads, buckets), F32)) + (S((width,), F32),) * 6 + (block,) * 6 + (broad, tall),
        in_specs=[vm, vm, vm, hb, hb],
        out_specs=(hb, hb) + (vm,) * 21,
        scratch_shapes=[pltpu.VMEM(dec.shape, F32), pltpu.SemaphoreType.DMA((2,))],
        compiler_params=pltpu.CompilerParams(vmem_limit_bytes=32 * 1024 * 1024),
        name="finish",
    )(red, small, dec, enc, grad)


PARTS = 2
ORDERS = {
    "t00": "xfny",
    "t10": "fnyx",
    "t01": "nyfx",
    "t11": "yxfn",
    "w00": "nyfx",
    "w10": "yxfn",
    "w01": "xyfn",
    "w11": "ynxf",
    "a0": "xyfn",
    "a1": "xnyf",
}
SCHEDULE = {
    "wide": (
        ("t00", 0), ("t10", 0), ("t01", 0), ("t11", 0),
    ),
    "rows": (
        ("w00", 0),
    ),
    "dout": (
        ("w10", 0), ("w01", 0),
    ),
    "p00": (
        ("w11", 0), ("t00", 1),
    ),
    "p01": (
        ("t11", 1),
    ),
    "q0": (
        ("t01", 1), ("t10", 1), ("w01", 1), ("w10", 1),
    ),
    "p10": (
        ("t11", 2), ("h00", 0),
    ),
    "p11": (
        ("h01", 0), ("w00", 1), ("w10", 2), ("w11", 1),
    ),
    "p12": (
        ("t01", 2),
    ),
    "v1": (
        ("t00", 2), ("t10", 2), ("w01", 2), ("h00", 1),
    ),
    "ng1": (
        ("h10", 0), ("t11", 3),
    ),
    "end": (
        ("w00", 2), ("h11", 0), ("t10", 3), ("w10", 3), ("w11", 2), ("h01", 1),
        ("t00", 3), ("t01", 3), ("t11", 4), ("w01", 3), ("h10", 1), ("w10", 4),
        ("w00", 3), ("h01", 2), ("w01", 4), ("h11", 1), ("t00", 4), ("t10", 4),
        ("w11", 3), ("t01", 4), ("w00", 4), ("h10", 2), ("h11", 2), ("w11", 4),
        ("h10", 3), ("h11", 3),
    ),
}
HOPS = (1, 3, 5)


def ff_pieces():
    names = [kind + str(unit) + str(i) for kind in "tw" for i in range(PARTS) for unit in range(2)]
    return names + ["h" + str(half) + str(w) for half in range(2) for w in range(2)]


def fused_kernel(np_, ns, length, fg, eg, ag, gains_dec,
                 rows_grad, block, cot, wr, active, wide_w, hidden, slope, mixed_t_in, wo, wq, wk, wv, q_in, k_in,
                 v_in, x_in, normed_t_in, context_t_in, probs, dec, encoded,
                 red, small_out, dec_out, enc_out, grad_out,
                 acts, grads, w1, wes, bg, hid, dm, rg, ct, rb, rb_t, mixed_t, normed_t, context_t,
                 dp, ds, pbuf, k_t, band, diag, fu, r0, r0a, r1, r2, r3, r4, a1, a2, a3, over0, over1,
                 sm, smr, smz,
                 psem, isem, loc, f_s, f_r, t_s, t_r, o_s, o_r,
                 m_s, m_r, mz_s, mz_r, d_s, d_r, e_s, e_r, g_s, g_r):
    n, width = hid.shape
    ff = acts.shape[1]
    fg, eg, ag = (g[...].reshape(1, -1) for g in (fg, eg, ag))
    heads = probs.shape[0]
    nz = np_ // 2
    pieces = ff_pieces()
    rows, lanes = fu.shape[6:]
    step_rows = rows // PARTS
    count = np_ * ns
    p = lax.axis_index("pairs")
    s = lax.axis_index("seq")
    c = lax.rem(s, 2)
    y = s // 2
    xx = lax.rem(p, 2)
    z = p // 2
    me = p * ns + s
    core_peer = (p, s + 1 - 2 * c)
    y_peer = (p, lax.rem(s + 2, 4))
    x_peer = (p + 1 - 2 * xx, s)
    first_half, last_half = 1 - y, y
    own_at = {"x": xx, "y": y, "n": lax.rem(z, 2), "f": z // 2}
    peers = {"x": x_peer, "y": y_peer, "n": ((z + 1 - 2 * own_at["n"]) * 2 + xx, s),
             "f": (lax.rem(z + 2, 4) * 2 + xx, s)}

    def place(d):
        lin = lax.rem(me + d, count)
        return (lin // ns, lax.rem(lin, ns))

    barrier = pltpu.get_barrier_semaphore()

    @pl.loop(1, count)
    def _(d):
        pl.semaphore_signal(barrier, inc=1, device_id=place(d), device_id_type=MESH)

    def remote(src, dst, send, recv, peer):
        return pltpu.make_async_remote_copy(
            src_ref=src, dst_ref=dst, send_sem=send, recv_sem=recv,
            device_id=peer, device_id_type=MESH)

    def load(i, src, dst):
        return pltpu.make_async_copy(src, dst, isem.at[i])

    def part_of(ref, i):
        return ref.at[:, pl.ds(i * width, width)]

    loads = [load(i, a, b) for i, (a, b) in enumerate((
        (rows_grad, rg), (block, bg), (cot, ct), (active, acts), (wr, w1), (slope, grads), (mixed_t_in, mixed_t),
        (wide_w, wes), (hidden, hid), (normed_t_in, normed_t), (context_t_in, context_t)))]
    weights = [load(11 + i, a, w1.at[pl.ds(i * width, width)]) for i, a in enumerate((wo, wq, wk, wv))]
    heads_in = [load(15 + i, a, part_of(grads, i)) for i, a in enumerate((q_in, k_in, v_in, x_in))]
    d_out, dq, dk, dv = (part_of(acts, i) for i in range(4))
    q, k, v, x = (part_of(grads, i) for i in range(4))
    branch, dq_t, ng, in_grad, hidden_grad = ct, rb_t, dm, rg, bg
    wos, wqs, wks, wvs = (w1.at[pl.ds(i * width, width)] for i in range(4))

    def fetch(h, slot):
        return pltpu.make_async_copy(probs.at[h], pbuf.at[slot], psem.at[slot])

    def view(ref, dims, fixed):
        return ref.at[tuple(fixed.get(dim, slice(None)) for dim in dims)]

    def accumulate(dst, src, depth):
        for at in itertools.product(range(2), repeat=depth):
            dst[at] = dst[at] + src[at]

    def au(w, core, half):
        return fu.at[1 - c, 2 * w + core, half]

    def region(name, core):
        if name[0] == "h":
            return au(int(name[2]), core, first_half if name[1] == "0" else last_half), "fnx"
        unit = (2 if name[0] == "t" else 0) + int(name[1])
        return fu.at[core, unit, :, :, :, :, pl.ds(int(name[2]) * step_rows, step_rows)], "yfnx"

    def order_of(name):
        if name[0] != "h":
            return ORDERS[name]
        order = ORDERS["a" + name[2]]
        return order[:order.index("y")] if name[1] == "0" else order.replace("y", "")

    def core_copy(name):
        i = pieces.index(name)
        src, _ = region(name, 1 - c)
        dst = r0a.at[i - len(pieces) + 4] if name[0] == "h" else r0.at[i]
        return remote(src, dst, f_s.at[i], f_r.at[i], core_peer)

    def landing(name, j):
        i = pieces.index(name)
        if name[0] == "h":
            return (a1, a2, a3)[j].at[i - len(pieces) + 4]
        return (r1, r2, r3, r4)[j].at[i]

    def remaining(name, j):
        ref, dims = region(name, c)
        return ref, dims, {letter: own_at[letter] for letter in order_of(name)[:j]}

    def stage_copy(name, j):
        ref, dims, fixed = remaining(name, j)
        letter = order_of(name)[j]
        i = pieces.index(name)
        src = view(ref, dims, {**fixed, letter: 1 - own_at[letter]})
        return remote(src, landing(name, j), t_s.at[i, j], t_r.at[i, j], peers[letter])

    def hand_over(w):
        name = "h0" + str(w)
        ref, dims, fixed = remaining(name, len(order_of(name)))
        return remote(view(ref, dims, fixed), (over0, over1)[w], o_s.at[w], o_r.at[w], y_peer)

    def total_of(name):
        unit = 4 + int(name[2]) if name[0] == "h" else (2 if name[0] == "t" else 0) + int(name[1])
        if name[0] == "h":
            return red.at[unit]
        return red.at[unit, pl.ds(int(name[2]) * step_rows, step_rows)]

    def step(name, j):
        order = order_of(name)
        ref, dims, fixed = remaining(name, j)
        mine = view(ref, dims, fixed)
        depth = len(dims) - j
        closing = j == len(order) and name[:2] != "h0"
        joins = name[:2] == "h1" and ORDERS["a" + name[2]].index("y") == j
        if j == 0:
            core_copy(name).wait()
            landed = r0a.at[pieces.index(name) - len(pieces) + 4] if name[0] == "h" else r0.at[pieces.index(name)]
        else:
            stage_copy(name, j - 1).wait()
            landed = landing(name, j - 1)
        if joins:
            hand_over(int(name[2])).wait()
            extra = (over0, over1)[int(name[2])]
        if closing:
            total = mine[...].astype(F32) + landed[...].astype(F32)
            if joins:
                total = total + extra[...].astype(F32)
            total_of(name)[...] = total
            return
        accumulate(mine, landed, depth)
        if joins:
            accumulate(mine, extra, depth)
        if j < len(order):
            stage_copy(name, j).start()
        else:
            hand_over(int(name[2])).start()

    def run_slot(slot):
        for name, j in SCHEDULE.get(slot, ()):
            step(name, j)

    def dec_copy(d):
        to = place(d)
        return remote(dec.at[to[0] * ns + to[1]], dec_out.at[me], d_s.at[d], d_r.at[d], to)

    def enc_copy(d):
        t = lax.rem(s + d, ns)
        return remote(encoded.at[t], enc_out.at[s], e_s.at[d], e_r.at[d], (p, t))

    def grad_copy(d):
        t = lax.rem(s + d, ns)
        return remote(in_grad.at[t], grad_out.at[s], g_s.at[d], g_r.at[d], (p, t))

    keep_dec = pltpu.make_async_copy(dec.at[me], dec_out.at[me], loc.at[4])
    keep_enc = pltpu.make_async_copy(encoded.at[s], enc_out.at[s], loc.at[5])
    keep_grad = pltpu.make_async_copy(in_grad.at[s], grad_out.at[s], loc.at[6])

    for copy in loads:
        copy.start()
    fetch(first_half * (heads // 2), 0).start()
    fetch(first_half * (heads // 2) + 1, 1).start()
    keep_dec.start()
    keep_enc.start()
    diag[...] = jnp.zeros_like(diag)
    slot_rows = n // ns
    sm[...] = jnp.zeros_like(sm)

    def put_gain(i, gain):
        for j in range(width // 128):
            sm[0, i * 6 + j:i * 6 + j + 1, :] = gain[:, j * 128:(j + 1) * 128]

    for i in range(3):
        put_gain(i, gains_dec[i:i + 1, :])
    for i in range(3):
        loads[i].wait()
    final_gain = jnp.zeros((1, width), F32)
    for i in range(ns):
        r = slice(i * slot_rows, (i + 1) * slot_rows)
        alive = (lax.broadcasted_iota(jnp.int32, (slot_rows, 1), 0) + i * slot_rows < length[s]).astype(F32)
        b = bg[r]
        down, gain = norm_down(b, rms_scale(b), fg, rg[i].astype(F32))
        b = alive * (ct[r].astype(F32) + down)
        bg[r] = b
        low = b.astype(BF)
        rb[r] = low
        rb_t[:, r] = low.T
        final_gain = final_gain + jnp.sum(gain, axis=0, keepdims=True)
    put_gain(3, final_gain)
    pl.semaphore_wait(barrier, count - 1)
    for d in range(1, ns):
        enc_copy(d).start()

    @pl.loop(1, count)
    def _(d):
        dec_copy(d).start()

    part = width // 4
    loads[3].wait()

    @pl.loop(0, nz)
    def _(b):
        cols = pl.ds(pl.multiple_of(b * 2 * lanes, 128), 2 * lanes)
        g = mm(rb_t[...], acts[:, cols]).astype(BF)
        for j in range(4):
            for half in range(2):
                lo = j * part + half * rows
                for e in range(2):
                    fu[j % 2, 2 + half, j // 2, b // 2, lax.rem(b, 2), e] = g[lo:lo + rows, e * lanes:(e + 1) * lanes]

    for name in pieces:
        if name[0] == "t":
            core_copy(name).start()
    loads[4].wait()
    loads[5].wait()

    for j in range(ff // width):
        cols = slice(j * width, (j + 1) * width)
        grads[:, cols] = (grads[:, cols].astype(F32) * mm_t(rb[...], w1[cols, :])).astype(BF)
        run_slot("ug" + str(j))

    for copy in weights:
        copy.start()
    loads[6].wait()

    @pl.loop(0, 4)
    def _(j):
        cols = pl.ds(pl.multiple_of(j * 2 * lanes, 128), 2 * lanes)
        g = mm(mixed_t[...], grads[:, cols]).astype(BF)
        for half in range(2):
            fu[lax.rem(j, 2), half, j // 2] = g[:, half * lanes:(half + 1) * lanes].reshape(2, 2, 2, rows, lanes)

    for name in pieces:
        if name[0] == "w":
            core_copy(name).start()
    run_slot("wide")
    loads[7].wait()
    dm[...] = mm_t(grads[...], wes[...])
    for copy in heads_in:
        copy.start()
    run_slot("dm")
    loads[8].wait()
    expand_gain = jnp.zeros((1, width), F32)
    for i in range(ns):
        r = slice(i * slot_rows, (i + 1) * slot_rows)
        t = hid[r]
        down, gain = norm_down(t, rms_scale(t), eg, dm[r])
        t = bg[r] + down
        bg[r] = t
        branch[r] = t.astype(BF)
        expand_gain = expand_gain + jnp.sum(gain, axis=0, keepdims=True)
    put_gain(4, expand_gain)
    run_slot("rows")
    weights[0].wait()

    @pl.loop(0, width // 384)
    def _(j):
        cols = pl.ds(pl.multiple_of(j * 384, 128), 384)
        d_out[:, cols] = mm_t(branch[...], w1[cols, :]).astype(BF)

    for copy in heads_in:
        copy.wait()
    for copy in loads[9:]:
        copy.wait()

    run_slot("dout")

    lane = lax.broadcasted_iota(jnp.int32, (n, 128), 1)
    lane_s = lax.broadcasted_iota(jnp.int32, (128, 128), 1)
    row_s = lax.broadcasted_iota(jnp.int32, (128, 128), 0)

    def pair(half, g):
        cols = pl.ds(pl.multiple_of(half * (width // 2) + g * 128, 128), 128)
        k_t[...] = k[:, cols].T
        dop = d_out[:, cols]
        qp = q[:, cols]
        vp = v[:, cols]
        zero = jnp.zeros_like(qp)
        for a in range(2):
            h = half * (heads // 2) + 2 * g + a
            mine = (lane < 64) if a == 0 else (lane >= 64)
            dp[...] = mm_t(jnp.where(mine, vp, zero), dop)
            fetch(h, a).wait()
            for j in range(n // 128):
                pj = pbuf[a, :, j * 128:(j + 1) * 128].astype(F32)
                pd = pj * dp[:, j * 128:(j + 1) * 128]
                total = jnp.sum(pd, axis=0, keepdims=True)
                sg = pd - pj * total
                ds[:, j * 128:(j + 1) * 128] = sg.astype(BF)
                for i in range(n // 128):
                    t = sg[i * 128:(i + 1) * 128]
                    if abs(i - j) <= 1:
                        b = (i - j + 1) * 128
                        if j == 0 or (j == 1 and i == 0):
                            band[b:b + 128, :] = t
                        else:
                            band[b:b + 128, :] += t
                    else:
                        f = 5 if i > j else 4
                        diag[h, f:f + 1, :] += jnp.sum(t, axis=0, keepdims=True)
            dvp = mm(pbuf[a], jnp.where(mine, dop, zero))
            dkp = mm(ds[...], jnp.where(mine, qp, zero))
            dq_t[pl.ds(pl.multiple_of(h * 64, 64), 64), :] = mm(k_t[a * 64:(a + 1) * 64, :], ds[...]).astype(BF)
            if a == 0:
                dk_sum, dv_sum = dkp, dvp
            else:
                dk[:, cols] = (dk_sum + dkp).astype(BF)
                dv[:, cols] = (dv_sum + dvp).astype(BF)
            for b in range(3):
                t = band[b * 128:(b + 1) * 128, :]
                for bit in range(7):
                    t = jnp.where((row_s >> bit) % 2 == 1, pltpu.roll(t, 128 - (1 << bit), 1), t)
                straight = jnp.sum(jnp.where(lane_s + row_s < 128, t, 0.0), axis=0, keepdims=True)
                whole = jnp.sum(t, axis=0, keepdims=True)
                diag[h, b:b + 1, :] += straight
                diag[h, b + 1:b + 2, :] += whole - straight

    def units_of(half, tag):
        cols = pl.ds(pl.multiple_of(half * (width // 2), 128), width // 2)
        dq_h = dq_t[cols, :].T
        dq[:, cols] = dq_h
        dk_h = dk[:, cols]
        for cc in range(2):
            e = slice(cc * part, (cc + 1) * part)
            g = mm(normed_t[...], jnp.concatenate([dq_h[:, e], dk_h[:, e]], axis=1))
            au(0, cc, half)[...] = g.astype(BF).reshape(2, 2, 2, rows, lanes)
        core_copy("h" + tag + "0").start()
        run_slot("q" + tag)
        dv_h = dv[:, cols]
        br_h = branch[:, cols]
        zero = jnp.zeros((n, part), BF)
        for cc in range(2):
            e = slice(cc * part, (cc + 1) * part)
            g = (mm(normed_t[...], jnp.concatenate([dv_h[:, e], zero], axis=1))
                 + mm(context_t[...], jnp.concatenate([zero, br_h[:, e]], axis=1)))
            au(1, cc, half)[...] = g.astype(BF).reshape(2, 2, 2, rows, lanes)
        core_copy("h" + tag + "1").start()
        run_slot("v" + tag)

    quarter = heads // 4

    @pl.loop(0, quarter)
    def _(g):
        pair(first_half, g)
        nxt = jnp.where(g == quarter - 1, last_half * (heads // 2), first_half * (heads // 2) + 2 * (g + 1))
        fetch(nxt, 0).start()
        fetch(nxt + 1, 1).start()

        for i in range(quarter):
            if SCHEDULE.get("p0" + str(i)):
                @pl.when(g == i)
                def _():
                    run_slot("p0" + str(i))

    units_of(first_half, "0")

    @pl.loop(0, quarter)
    def _(g):
        pair(last_half, g)

        @pl.when(g < quarter - 1)
        def _():
            nxt = last_half * (heads // 2) + 2 * (g + 1)
            fetch(nxt, 0).start()
            fetch(nxt + 1, 1).start()

        for i in range(quarter):
            if SCHEDULE.get("p1" + str(i)):
                @pl.when(g == i)
                def _():
                    run_slot("p1" + str(i))

    units_of(last_half, "1")
    for copy in weights[1:]:
        copy.wait()

    for i in range(2):
        r = slice(i * (n // 2), (i + 1) * (n // 2))
        ng[r] = mm_t(dq[r], wqs[...]) + mm_t(dk[r], wks[...]) + mm_t(dv[r], wvs[...])
        run_slot("ng" + str(i))

    gain_sum = jnp.zeros((1, width), F32)
    for i in range(ns):
        r = slice(i * slot_rows, (i + 1) * slot_rows)
        t = x[r].astype(F32)
        down, gain = norm_down(t, rms_scale(t), ag, ng[r])
        in_grad[i] = (hidden_grad[r] + down).astype(BF)
        gain_sum = gain_sum + jnp.sum(gain, axis=0, keepdims=True)
    keep_grad.start()
    for d in range(1, ns):
        grad_copy(d).start()

    pick = diagonal_buckets((128, width), width)
    bias = jnp.zeros((16, 128), F32)
    for i in range(width // 128):
        bias = bias + lax.dot_general(diag[:, i, :], pick[:, i * 128:(i + 1) * 128], (((1,), (1,)), ((), ())),
                                      precision=HIGHEST, preferred_element_type=F32)
    sm[0, 40:56, :] = bias
    put_gain(5, gain_sum)

    def small_copy(i):
        return remote(sm.at[i], smr.at[i], m_s.at[i], m_r.at[i], (core_peer, y_peer, x_peer)[i])

    def z_small(d):
        return remote(smz.at[z], smz.at[z], mz_s.at[d], mz_r.at[d], (lax.rem(z + d, nz) * 2 + xx, s))

    def small_hop(i):
        small_copy(i).wait()
        if i < 2:
            sm[i + 1] = sm[i] + smr[i]
            small_copy(i + 1).start()
        else:
            smz[z] = sm[i] + smr[i]

            @pl.loop(1, nz)
            def _(d):
                z_small(d).start()

    small_copy(0).start()
    tail = SCHEDULE["end"]
    for i, (name, j) in enumerate(tail):
        step(name, j)
        if i in HOPS:
            small_hop(HOPS.index(i))

    @pl.loop(1, nz)
    def _(d):
        z_small(d).wait()

    small_out[...] = smz[0]

    @pl.loop(1, nz)
    def _(d):
        small_out[...] = small_out[...] + smz[d]

    keep_dec.wait()
    keep_enc.wait()
    keep_grad.wait()
    for d in range(1, ns):
        enc_copy(d).wait()
        grad_copy(d).wait()

    @pl.loop(1, count)
    def _(d):
        dec_copy(d).wait()


def fused(np_, ns, length, fg, eg, ag, gains_dec, rows_grad, block, cot, wr, active, we, hidden, slope, mixed_t,
          wo, wq, wk, wv, q, k, v, x, normed_t, context_t, probs, dec, encoded):
    n, width = hidden.shape
    ff = active.shape[1]
    heads = probs.shape[0]
    nz = np_ // 2
    rows, lanes = width // np_, ff // np_
    count = np_ * ns
    smem = pl.BlockSpec(memory_space=pltpu.SMEM)
    vm = pl.BlockSpec(memory_space=pltpu.VMEM)
    hb = pl.BlockSpec(memory_space=pl.ANY)
    S = jax.ShapeDtypeStruct
    V = pltpu.VMEM
    dma = pltpu.SemaphoreType.DMA
    nar, tall = V((n, width), BF), V((width, n), BF)
    floats = V((n, width), F32)
    slots = (ns, n // ns, width)
    small = (64, 128)
    ffs = 4 * PARTS
    sub = rows // PARTS

    def joint(w):
        return V((2,) * (3 - ORDERS["a" + str(w)].index("y")) + (rows, lanes), BF)

    return pl.pallas_call(
        functools.partial(fused_kernel, np_, ns),
        out_shape=(S((6, rows, lanes), F32), S(small, F32), S(dec.shape, BF), S(slots, BF), S(slots, BF)),
        in_specs=[smem] + [vm] * 4 + [hb] * 22,
        out_specs=(vm, vm, hb, hb, hb),
        scratch_shapes=[
            V((n, ff), BF), V((n, ff), BF), V((ff, width), BF), V((width, ff), BF), floats, floats, floats,
            V(slots, BF), nar, nar, tall, tall, tall, tall,
            V((n, n), F32), V((n, n), BF), V((2, n, n), BF), V((128, n), BF), V((384, 128), F32), V((16, 8, 128), F32),
            V((2, 4, 2, 2, 2, 2, rows, lanes), BF), V((ffs, 2, 2, 2, 2, sub, lanes), BF), V((4, 2, 2, 2, rows, lanes), BF),
            V((ffs, 2, 2, 2, sub, lanes), BF), V((ffs, 2, 2, sub, lanes), BF), V((ffs, 2, sub, lanes), BF),
            V((ffs, sub, lanes), BF), V((4, 2, 2, rows, lanes), BF), V((4, 2, rows, lanes), BF),
            V((4, rows, lanes), BF), joint(0), joint(1),
            V((3,) + small, F32), V((3,) + small, F32), V((nz,) + small, F32),
            dma((2,)), dma((19,)), dma((7,)), dma((ffs + 4,)), dma((ffs + 4,)), dma((ffs + 4, 4)), dma((ffs + 4, 4)),
            dma((2,)), dma((2,)),
            dma((3,)), dma((3,)), dma((nz,)), dma((nz,)), dma((count,)), dma((count,)),
            dma((ns,)), dma((ns,)), dma((ns,)), dma((ns,)),
        ],
        compiler_params=pltpu.CompilerParams(
            collective_id=0, has_side_effects=True, vmem_limit_bytes=62 * 1024 * 1024),
        name="fused_backward",
    )(length, fg, eg, ag, gains_dec, rows_grad.reshape(slots), block, cot, wr,
      active, we, hidden, slope, mixed_t, wo, wq, wk, wv, q, k, v, x, normed_t, context_t, probs, dec,
      encoded.reshape(slots))


def feed_back_kernel(length, rows_grad, block, cot, fg, hidden, eg, mixed, active, slope, wr, we,
                     wide, tall, hidden_grad, branch, gains, wrs, wes, bg, rb, rb_t, ug, mixed_t, dmixed, sems):
    n, width = block.shape
    ff = active.shape[1]
    groups, lanes = tall.shape[3], tall.shape[5]
    cols_dev = width // 4
    copies = [pltpu.make_async_copy(a, b, sems.at[i]) for i, (a, b) in enumerate(((wr, wrs), (we, wes)))]
    for c in copies:
        c.start()
    gains[...] = jnp.zeros_like(gains)

    @pl.loop(0, n // 128)
    def _(i):
        r = pl.ds(i * 128, 128)
        alive = (lax.broadcasted_iota(jnp.int32, (128, 1), 0) + i * 128 < length[0]).astype(F32)
        v = block[r]
        down, gain = norm_down(v, rms_scale(v), fg[...], rows_grad[r].astype(F32))
        b = alive * (cot[r].astype(F32) + down)
        bg[r] = b
        rb[r] = b.astype(BF)
        rb_t[:, pl.ds(pl.multiple_of(i * 128, 128), 128)] = b.T.astype(BF)
        mixed_t[:, pl.ds(pl.multiple_of(i * 128, 128), 128)] = mixed[r].T
        gains[0:1, :] += jnp.sum(gain, axis=0, keepdims=True)

    copies[0].wait()

    @pl.loop(0, ff // 256)
    def _(j):
        cols = pl.ds(pl.multiple_of(j * 256, 256), 256)
        ug[:, cols] = (slope[:, cols].astype(F32) * mm_t(rb[...], wrs[cols, :])).astype(BF)

    copies[1].wait()

    @pl.loop(0, width // 256)
    def _(j):
        cols = pl.ds(pl.multiple_of(j * 256, 256), 256)
        dmixed[:, cols] = mm_t(ug[...], wes[cols, :])

    @pl.loop(0, n // 128)
    def _(i):
        r = pl.ds(i * 128, 128)
        v = hidden[r]
        down, gain = norm_down(v, rms_scale(v), eg[...], dmixed[r])
        h = bg[r] + down
        hidden_grad[r] = h
        branch[r] = h.astype(BF)
        gains[1:2, :] += jnp.sum(gain, axis=0, keepdims=True)

    @pl.loop(0, 4)
    def _(j):
        for half in range(2):
            cols = pl.ds(pl.multiple_of(j * (ff // 4) + half * (ff // 8), 128), ff // 8)
            wide[half, lax.rem(j, 2), j // 2] = mm(mixed_t[...], ug[:, cols]).astype(BF)

    chunk = ff // 8
    per_group = lanes // chunk

    @pl.loop(0, 8)
    def _(i):
        cols = pl.ds(pl.multiple_of(i * chunk, 128), chunk)
        g = mm(rb_t[...], active[:, cols]).astype(BF)
        for j in range(4):
            for half in range(2):
                r = j * cols_dev + half * (cols_dev // 2)
                part = g[r:r + cols_dev // 2]
                if per_group == 1:
                    tall[half, j % 2, j // 2, i] = part
                else:
                    tall[half, j % 2, j // 2, 0, :, cols] = part


def feed_back(groups, length, rows_grad, block, cot, fg, hidden, eg, mixed, active, slope, wr, we):
    n, width = block.shape
    ff = active.shape[1]
    sm = pl.BlockSpec(memory_space=pltpu.SMEM)
    vm = pl.BlockSpec(memory_space=pltpu.VMEM)
    hb = pl.BlockSpec(memory_space=pl.ANY)
    S = jax.ShapeDtypeStruct
    V = pltpu.VMEM
    return pl.pallas_call(
        feed_back_kernel,
        out_shape=(S((2, 2, 2, width, ff // 8), BF),
                   S((2, 2, 2, groups, width // 8, ff // groups), BF), S((n, width), F32), S((n, width), BF), S((2, width), F32)),
        in_specs=[sm] + [vm] * 9 + [hb] * 2,
        out_specs=(vm,) * 5,
        scratch_shapes=[V(wr.shape, BF), V(we.shape, BF), V((n, width), F32), V((n, width), BF), V((width, n), BF),
                        V((n, ff), BF), V((width, n), BF), V((n, width), F32), pltpu.SemaphoreType.DMA((2,))],
        compiler_params=pltpu.CompilerParams(vmem_limit_bytes=60 * 1024 * 1024),
        name="feed_back",
    )(length, rows_grad, block, cot, fg.reshape(1, -1), hidden, eg.reshape(1, -1), mixed, active, slope, wr, we)


def backward_kernel(np_, ns, x, ag, q, k, v, context_t, branch, hidden_grad, normed, gains_dec, gains_feed,
                    probs, wo, wq, wk, wv, wide, tall, dec, encoded,
                    red, small_out, dec_out, enc_out, grad_out,
                    wos, wqs, wks, wvs, d_out, dp, ds, dq_t, dq, dk, dv, k_t, normed_t, ng, in_grad,
                    pbuf, band, diag, own, au, r0, r1y, r1x, r1a, r2, r3, sm, smr, smz,
                    psem, wsem, loc, c_s, c_r, a_s, a_r, b_s, b_r, ac_s, ac_r, ax_s, ax_r, z_s, z_r,
                    m_s, m_r, mz_s, mz_r, d_s, d_r, e_s, e_r, g_s, g_r):
    n, width = x.shape
    heads = probs.shape[0]
    nz = np_ // 2
    rows, lanes = r0.shape[4:]
    count = np_ * ns
    p = lax.axis_index("pairs")
    s = lax.axis_index("seq")
    c = lax.rem(s, 2)
    y = s // 2
    xx = lax.rem(p, 2)
    z = p // 2
    me = p * ns + s
    core_peer = (p, s + 1 - 2 * c)
    y_peer = (p, lax.rem(s + 2, 4))
    x_peer = (p + 1 - 2 * xx, s)

    def place(d):
        lin = lax.rem(me + d, count)
        return (lin // ns, lax.rem(lin, ns))

    barrier = pltpu.get_barrier_semaphore()

    @pl.loop(1, count)
    def _(d):
        pl.semaphore_signal(barrier, inc=1, device_id=place(d), device_id_type=MESH)

    def remote(src, dst, send, recv, peer):
        return pltpu.make_async_remote_copy(
            src_ref=src, dst_ref=dst, send_sem=send, recv_sem=recv,
            device_id=peer, device_id_type=MESH)

    weights = [pltpu.make_async_copy(a, b, wsem.at[i])
               for i, (a, b) in enumerate(((wo, wos), (wq, wqs), (wk, wks), (wv, wvs)))]

    def fetch(h, slot):
        return pltpu.make_async_copy(probs.at[h], pbuf.at[slot], psem.at[slot])

    def unit(i, core):
        return (wide, tall)[i // 2].at[i % 2, core]

    def core_copy(i):
        return remote(unit(i, 1 - c), r0.at[i], c_s.at[i], c_r.at[i], core_peer)

    def own_copy(i):
        return pltpu.make_async_copy(unit(i, c), own.at[i], loc.at[i])

    def first(i):
        if i % 2 == 0:
            return remote(own.at[i, 1 - y], r1y.at[i // 2], a_s.at[i], a_r.at[i], y_peer)
        return remote(own.at[i, :, :, 1 - xx], r1x.at[i // 2], a_s.at[i], a_r.at[i], x_peer)

    def second(i):
        if i % 2 == 0:
            return remote(own.at[i, y, :, 1 - xx], r2.at[i], b_s.at[i], b_r.at[i], x_peer)
        return remote(own.at[i, 1 - y, :, xx], r2.at[i], b_s.at[i], b_r.at[i], y_peer)

    def final(i):
        return own.at[i, y] if i < 4 else au.at[i - 4, c, y]

    def last(i, d):
        t = lax.rem(z + d, nz)
        return remote(final(i).at[t, xx], r3.at[i, d], z_s.at[i, d], z_r.at[i, d], (t * 2 + xx, s))

    def attn_core(w, half):
        return remote(au.at[w, 1 - c, half], r0.at[4 + w, half], ac_s.at[w, half], ac_r.at[w, half], core_peer)

    def attn_x(w, half):
        return remote(au.at[w, c, half, :, 1 - xx], r1a.at[w, half], ax_s.at[w, half], ax_r.at[w, half], x_peer)

    def attn_y(w):
        return remote(au.at[w, c, 1 - y, :, xx], r2.at[4 + w], b_s.at[4 + w], b_r.at[4 + w], y_peer)

    def dec_copy(d):
        to = place(d)
        return remote(dec.at[to[0] * ns + to[1]], dec_out.at[me], d_s.at[d], d_r.at[d], to)

    def enc_copy(d):
        t = lax.rem(s + d, ns)
        return remote(encoded.at[t], enc_out.at[s], e_s.at[d], e_r.at[d], (p, t))

    def grad_copy(d):
        t = lax.rem(s + d, ns)
        return remote(in_grad.at[t], grad_out.at[s], g_s.at[d], g_r.at[d], (p, t))

    keep_dec = pltpu.make_async_copy(dec.at[me], dec_out.at[me], loc.at[4])
    keep_enc = pltpu.make_async_copy(encoded.at[s], enc_out.at[s], loc.at[5])
    keep_grad = pltpu.make_async_copy(in_grad.at[s], grad_out.at[s], loc.at[6])

    def step_a(i):
        core_copy(i).wait()
        own_copy(i).wait()

        @pl.loop(0, nz)
        def _(b):
            for a in range(2):
                for e in range(2):
                    own[i, a, b, e] = own[i, a, b, e] + r0[i, a, b, e]

        first(i).start()

    def step_b(i):
        first(i).wait()

        @pl.loop(0, nz)
        def _(b):
            for e in range(2):
                if i % 2 == 0:
                    own[i, y, b, e] = own[i, y, b, e] + r1y[i // 2, b, e]
                else:
                    own[i, e, b, xx] = own[i, e, b, xx] + r1x[i // 2, e, b]

        second(i).start()

    def step_c(i):
        if i < 4:
            second(i).wait()
        else:
            attn_y(i - 4).wait()

        @pl.loop(0, nz)
        def _(b):
            f = final(i)
            f[b, xx] = f[b, xx] + r2[i, b]

        @pl.loop(1, nz)
        def _(d):
            last(i, d).start()

    def step_d(i):
        red[i] = final(i)[z, xx].astype(F32)

        @pl.loop(1, nz)
        def _(d):
            last(i, d).wait()
            red[i] = red[i] + r3[i, d].astype(F32)

    def attn_a(w, half):
        attn_core(w, half).wait()

        @pl.loop(0, nz)
        def _(b):
            for e in range(2):
                au[w, c, half, b, e] = au[w, c, half, b, e] + r0[4 + w, half, b, e]

        attn_x(w, half).start()

    def attn_b(w, half):
        attn_x(w, half).wait()

        @pl.loop(0, nz)
        def _(b):
            au[w, c, half, b, xx] = au[w, c, half, b, xx] + r1a[w, half, b]

    for copy in weights:
        copy.start()
    first_half, last_half = 1 - y, y
    fetch(first_half * (heads // 2), 0).start()
    fetch(first_half * (heads // 2) + 1, 1).start()
    for i in range(4):
        own_copy(i).start()
    keep_dec.start()
    keep_enc.start()
    diag[...] = jnp.zeros_like(diag)
    weights[0].wait()

    @pl.loop(0, width // 384)
    def _(j):
        cols = pl.ds(pl.multiple_of(j * 384, 128), 384)
        d_out[:, cols] = mm_t(branch[...], wos[cols, :]).astype(BF)

    pl.semaphore_wait(barrier, count - 1)
    for i in range(4):
        core_copy(i).start()
    for d in range(1, ns):
        enc_copy(d).start()

    @pl.loop(1, count)
    def _(d):
        dec_copy(d).start()

    @pl.loop(0, n // 128)
    def _(i):
        r = pl.ds(pl.multiple_of(i * 128, 128), 128)
        normed_t[:, r] = normed[r].T

    lane = lax.broadcasted_iota(jnp.int32, (n, 128), 1)
    lane_s = lax.broadcasted_iota(jnp.int32, (128, 128), 1)
    row_s = lax.broadcasted_iota(jnp.int32, (128, 128), 0)

    def pair(half, g):
        cols = pl.ds(pl.multiple_of(half * (width // 2) + g * 128, 128), 128)
        k_t[...] = k[:, cols].T
        dop = d_out[:, cols]
        qp = q[:, cols]
        vp = v[:, cols]
        zero = jnp.zeros_like(qp)
        for a in range(2):
            h = half * (heads // 2) + 2 * g + a
            mine = (lane < 64) if a == 0 else (lane >= 64)
            dp[...] = mm_t(jnp.where(mine, vp, zero), dop)
            fetch(h, a).wait()
            for j in range(n // 128):
                pj = pbuf[a, :, j * 128:(j + 1) * 128].astype(F32)
                pd = pj * dp[:, j * 128:(j + 1) * 128]
                total = jnp.sum(pd, axis=0, keepdims=True)
                sg = pd - pj * total
                ds[:, j * 128:(j + 1) * 128] = sg.astype(BF)
                for i in range(n // 128):
                    t = sg[i * 128:(i + 1) * 128]
                    if abs(i - j) <= 1:
                        b = (i - j + 1) * 128
                        if j == 0 or (j == 1 and i == 0):
                            band[b:b + 128, :] = t
                        else:
                            band[b:b + 128, :] += t
                    else:
                        f = 5 if i > j else 4
                        diag[h, f:f + 1, :] += jnp.sum(t, axis=0, keepdims=True)
            dvp = mm(pbuf[a], jnp.where(mine, dop, zero))
            dkp = mm(ds[...], jnp.where(mine, qp, zero))
            dq_t[pl.ds(pl.multiple_of(h * 64, 64), 64), :] = mm(k_t[a * 64:(a + 1) * 64, :], ds[...]).astype(BF)
            if a == 0:
                dk_sum, dv_sum = dkp, dvp
            else:
                dk[:, cols] = (dk_sum + dkp).astype(BF)
                dv[:, cols] = (dv_sum + dvp).astype(BF)
            for b in range(3):
                t = band[b * 128:(b + 1) * 128, :]
                for bit in range(7):
                    t = jnp.where((row_s >> bit) % 2 == 1, pltpu.roll(t, 128 - (1 << bit), 1), t)
                straight = jnp.sum(jnp.where(lane_s + row_s < 128, t, 0.0), axis=0, keepdims=True)
                whole = jnp.sum(t, axis=0, keepdims=True)
                diag[h, b:b + 1, :] += straight
                diag[h, b + 1:b + 2, :] += whole - straight

    part = width // 4

    def units_of(half):
        cols = pl.ds(pl.multiple_of(half * (width // 2), 128), width // 2)
        lower = pl.ds(pl.multiple_of(half * (width // 2), 128), width // 2)
        dq_h = dq_t[lower, :].T
        dq[:, cols] = dq_h
        dk_h = dk[:, cols]
        dv_h = dv[:, cols]
        br_h = branch[:, cols]
        zero = jnp.zeros((n, part), BF)
        for cc in range(2):
            e = slice(cc * part, (cc + 1) * part)
            g = mm(normed_t[...], jnp.concatenate([dq_h[:, e], dk_h[:, e]], axis=1))
            au[0, cc, half] = g.astype(BF).reshape(nz, 2, rows, lanes)
            g = (mm(normed_t[...], jnp.concatenate([dv_h[:, e], zero], axis=1))
                 + mm(context_t[...], jnp.concatenate([zero, br_h[:, e]], axis=1)))
            au[1, cc, half] = g.astype(BF).reshape(nz, 2, rows, lanes)
        for w in range(2):
            attn_core(w, half).start()

    quarter = heads // 4

    @pl.loop(0, quarter)
    def _(g):
        pair(first_half, g)
        nxt = jnp.where(g == quarter - 1, last_half * (heads // 2), first_half * (heads // 2) + 2 * (g + 1))
        fetch(nxt, 0).start()
        fetch(nxt + 1, 1).start()

        @pl.when(g == 0)
        def _():
            step_a(0)
            step_a(1)

        @pl.when(g == 1)
        def _():
            step_a(2)
            step_a(3)

    units_of(first_half)

    @pl.loop(0, quarter)
    def _(g):
        pair(last_half, g)

        @pl.when(g < quarter - 1)
        def _():
            nxt = last_half * (heads // 2) + 2 * (g + 1)
            fetch(nxt, 0).start()
            fetch(nxt + 1, 1).start()

        @pl.when(g == 0)
        def _():
            attn_a(0, first_half)
            attn_a(1, first_half)

        @pl.when(g == 1)
        def _():
            step_b(0)
            step_b(1)

    units_of(last_half)
    for copy in weights[1:]:
        copy.wait()

    @pl.loop(0, 2)
    def _(i):
        r = pl.ds(pl.multiple_of(i * (n // 2), 128), n // 2)
        ng[r] = mm_t(dq[r], wqs[...]) + mm_t(dk[r], wks[...]) + mm_t(dv[r], wvs[...])

    attn_a(0, last_half)
    attn_a(1, last_half)
    sm[...] = jnp.zeros_like(sm)
    slot_rows = n // ns
    gain_sum = jnp.zeros((1, width), F32)
    for i in range(ns):
        r = slice(i * slot_rows, (i + 1) * slot_rows)
        t = x[r].astype(F32)
        down, gain = norm_down(t, rms_scale(t), ag[...], ng[r])
        in_grad[i] = (hidden_grad[r] + down).astype(BF)
        gain_sum = gain_sum + jnp.sum(gain, axis=0, keepdims=True)
    keep_grad.start()
    for d in range(1, ns):
        grad_copy(d).start()

    col = lax.broadcasted_iota(jnp.int32, (128, width), 1)
    offset = (col // 128 - 1) * 128 - lax.rem(col, 128)
    offset = jnp.where(col >= width - 128, 256, jnp.where(col >= width - 256, -256, offset))
    dist = jnp.abs(offset)
    bucket = jnp.full_like(dist, 8)
    for edge in EDGES:
        bucket = bucket + (dist >= edge).astype(jnp.int32)
    bucket = jnp.where(dist < 8, dist, bucket) + jnp.where(offset > 0, 16, 0)
    pick = jnp.where(bucket == lax.broadcasted_iota(jnp.int32, (128, width), 0), 1.0, 0.0)
    bias = jnp.zeros((16, 128), F32)
    for i in range(width // 128):
        bias = bias + lax.dot_general(diag[:, i, :], pick[:, i * 128:(i + 1) * 128], (((1,), (1,)), ((), ())),
                                      precision=HIGHEST, preferred_element_type=F32)
    sm[0, 40:56, :] = bias
    gains = [gains_dec[i:i + 1, :] for i in range(3)] + [gains_feed[i:i + 1, :] for i in range(2)] + [gain_sum]
    for i, gain in enumerate(gains):
        for j in range(width // 128):
            sm[0, i * 6 + j:i * 6 + j + 1, :] = gain[:, j * 128:(j + 1) * 128]

    def small_copy(i):
        return remote(sm.at[i], smr.at[i], m_s.at[i], m_r.at[i], (core_peer, y_peer, x_peer)[i])

    def z_small(d):
        return remote(smz.at[z], smz.at[z], mz_s.at[d], mz_r.at[d], (lax.rem(z + d, nz) * 2 + xx, s))

    small_copy(0).start()
    step_b(2)
    step_b(3)
    small_copy(0).wait()
    sm[1] = sm[0] + smr[0]
    small_copy(1).start()
    attn_b(0, first_half)
    attn_y(0).start()
    attn_b(1, first_half)
    attn_y(1).start()
    step_c(0)
    step_c(1)
    small_copy(1).wait()
    sm[2] = sm[1] + smr[1]
    small_copy(2).start()
    step_c(2)
    step_c(3)
    attn_b(0, last_half)
    small_copy(2).wait()
    smz[z] = sm[2] + smr[2]

    @pl.loop(1, nz)
    def _(d):
        z_small(d).start()

    step_c(4)
    attn_b(1, last_half)
    step_c(5)
    for i in range(6):
        step_d(i)

    @pl.loop(1, nz)
    def _(d):
        z_small(d).wait()

    small_out[...] = smz[0]

    @pl.loop(1, nz)
    def _(d):
        small_out[...] = small_out[...] + smz[d]

    keep_dec.wait()
    keep_enc.wait()
    keep_grad.wait()
    for d in range(1, ns):
        enc_copy(d).wait()
        grad_copy(d).wait()

    @pl.loop(1, count)
    def _(d):
        dec_copy(d).wait()


def backward(np_, ns, x, ag, q, k, v, context_t, branch, hidden_grad, normed, gains_dec, gains_feed,
             probs, wo, wq, wk, wv, wide, tall, dec, encoded):
    n, width = x.shape
    heads = probs.shape[0]
    nz = np_ // 2
    rows, lanes = wide.shape[5:]
    count = np_ * ns
    padded = normed.shape[1]
    vm = pl.BlockSpec(memory_space=pltpu.VMEM)
    hb = pl.BlockSpec(memory_space=pl.ANY)
    S = jax.ShapeDtypeStruct
    V = pltpu.VMEM
    dma = pltpu.SemaphoreType.DMA
    nar = V((n, width), BF)
    square = V((width, width), BF)
    slots = (ns, n // ns, width)
    small = (64, 128)
    return pl.pallas_call(
        functools.partial(backward_kernel, np_, ns),
        out_shape=(S((6, rows, lanes), F32), S(small, F32), S(dec.shape, BF), S(slots, BF), S(slots, BF)),
        in_specs=[vm] * 11 + [hb] * 9,
        out_specs=(vm, vm, hb, hb, hb),
        scratch_shapes=[
            square, square, square, square, nar, V((n, n), F32), V((n, n), BF), V((width, n), BF), nar, nar, nar,
            V((128, n), BF), V((padded, n), BF), V((n, width), F32), V(slots, BF),
            V((2, n, n), BF), V((384, 128), F32), V((16, 8, 128), F32),
            V((4, 2, nz, 2, rows, lanes), BF), V((2, 2, 2, nz, 2, rows, lanes), BF), V((6, 2, nz, 2, rows, lanes), BF),
            V((2, nz, 2, rows, lanes), BF), V((2, 2, nz, rows, lanes), BF), V((2, 2, nz, rows, lanes), BF),
            V((6, nz, rows, lanes), BF), V((6, nz, rows, lanes), BF),
            V((3,) + small, F32), V((3,) + small, F32), V((nz,) + small, F32),
            dma((2,)), dma((4,)), dma((7,)), dma((4,)), dma((4,)), dma((4,)), dma((4,)), dma((6,)), dma((6,)),
            dma((2, 2)), dma((2, 2)), dma((2, 2)), dma((2, 2)), dma((6, nz)), dma((6, nz)),
            dma((3,)), dma((3,)), dma((nz,)), dma((nz,)), dma((count,)), dma((count,)),
            dma((ns,)), dma((ns,)), dma((ns,)), dma((ns,)),
        ],
        compiler_params=pltpu.CompilerParams(
            collective_id=0, has_side_effects=True, vmem_limit_bytes=62 * 1024 * 1024),
        name="backward",
    )(x, ag.reshape(1, -1), q, k, v, context_t, branch, hidden_grad, normed, gains_dec, gains_feed,
      probs, wo, wq, wk, wv, wide, tall, dec, encoded.reshape(slots))


def two_kernels(
    np_, ns, r, rp, lanes, side, length, final_gain, expand_gain, attend_gain, dec_gains,
    rows_grad, block, cot, reduce_weight, active, expand_weight, hidden, slope, mixed_t,
    output_weight, query_weight, key_weight, value_weight, query, key, value, x, normed_t,
    context_t, probs, dec_all, encoded,
):
    seq_len, ff = active.shape
    nz = np_ // 2
    wide, tall, hidden_grad, branch, feed_gains = feed_back(
        1, length, rows_grad, block, cot, final_gain, hidden, expand_gain, mixed_t.T, active,
        slope, reduce_weight, expand_weight)

    def pad(unit):
        return jnp.pad(unit, ((0, 0),) * 5 + ((0, rp - r), (0, 0)))

    tall = tall.reshape(2, 2, 2, r, side, nz, 2, ff // np_).transpose(0, 1, 2, 5, 6, 3, 4, 7)
    tall = pad(tall.reshape(2, 2, 2, nz, 2, r, lanes))
    wide = pad(wide.reshape(2, 2, 2, nz, 2, r, lanes))
    gap = ((0, 0), (0, rp - r), (0, 0))
    normed_t = jnp.pad(normed_t.reshape(np_, r, seq_len), gap).reshape(np_ * rp, seq_len)
    context_t = jnp.pad(context_t.reshape(np_, r, seq_len), gap).reshape(np_ * rp, seq_len)
    return backward(
        np_, ns, x, attend_gain, query, key, value, context_t, branch, hidden_grad, normed_t.T,
        dec_gains, feed_gains, probs, output_weight, query_weight, key_weight, value_weight,
        wide, tall, dec_all, encoded)


def per_device(
    enc_input, dec_input, lengths, attend_gain, query_weight, key_weight, value_weight,
    output_weight, bias_table, expand_gain, expand_weight, reduce_weight, final_gain,
    self_gain, self_value, self_output, cross_gain, cross_query, cross_key, cross_value,
    cross_output, feed_gain, feed_expand, feed_reduce, enc_cotangent, dec_cotangent,
):
    group, local_rows, width = enc_input.shape
    buckets, heads = bias_table.shape
    size = width // heads
    ff = expand_weight.shape[1]
    ns = lax.axis_size("seq")
    np_ = lax.axis_size("pairs")
    r = width // np_
    aligned = np_ == 8 and r % 32 == 0 and (ff // np_) % 128 == 0 and ff == 4 * width
    seq_len = local_rows * ns
    weights = (query_weight, key_weight, value_weight, output_weight, expand_weight, reduce_weight,
               self_value, self_output, cross_query, cross_key, cross_value, cross_output,
               feed_expand, feed_reduce)
    (normed_t, query, key, value, probs, context_t, hidden, mixed_t, active, slope, block, encoded,
     x, cot, rows_grad, dec_block, dec_input_grad, dec_gains, *dec_rows) = forward(
        np_, ns, aligned, lengths, bias_table,
        (attend_gain, expand_gain, final_gain, self_gain, cross_gain, feed_gain),
        dec_input, dec_cotangent, enc_input, enc_cotangent, weights)
    x = x.reshape(seq_len, width)
    cot = cot.reshape(seq_len, width)
    if aligned:
        dec_all, = dec_rows
        red, small_sum, dec_got, enc_out, grad_out = fused(
            np_, ns, lengths, final_gain, expand_gain, attend_gain, dec_gains, rows_grad, block, cot,
            reduce_weight, active, expand_weight, hidden, slope, mixed_t, output_weight,
            query_weight, key_weight, value_weight, query, key, value, x, normed_t, context_t,
            probs, dec_all, encoded)
        (enc_out, grad_out, grad_query, grad_key, grad_value, grad_output, grad_expand, grad_reduce,
         bias, *rest) = finish(heads, buckets, red, small_sum, dec_got, enc_out, grad_out)
        gains = rest[:6]
        grad_sv, grad_so, grad_cq, grad_ck, grad_cv, grad_co, feed_in, feed_out = rest[6:]
        return (
            enc_out, dec_block, grad_out, dec_input_grad, gains[5], grad_query, grad_key,
            grad_value, grad_output, bias.T, gains[4], grad_expand, grad_reduce.T, gains[3],
            gains[0], grad_sv, grad_so, gains[1], grad_cq, grad_ck, grad_cv, grad_co, gains[2],
            feed_in, feed_out.T,
        )
    left, right, wide_rows, mids = dec_rows
    length = lax.dynamic_slice_in_dim(lengths, lax.axis_index("seq"), 1)
    rp = -(-r // 16) * 16
    lanes = ff // 8
    side = width // 8 // r
    cols = width // ns

    left_cut = jnp.concatenate([
        left.reshape(5, np_, r).transpose(1, 0, 2).reshape(np_, 5 * r),
        wide_rows[0].reshape(np_, 4 * r),
    ], axis=1)
    mid_cut = mids.reshape(2, ns, heads // ns, np_, r).transpose(3, 1, 0, 2, 4)
    mid_cut = mid_cut.reshape(np_, ns, 6 * r)
    right_cut = jnp.concatenate([
        right.reshape(7, ns, cols).transpose(1, 0, 2).reshape(ns, 7 * cols),
        wide_rows[1].reshape(ns, 4 * cols)], axis=1)
    dec_all = jnp.concatenate([
        jnp.broadcast_to(left_cut[:, None], (np_, ns, 9 * r)), mid_cut,
        jnp.broadcast_to(right_cut[None], (np_, ns, 11 * cols))], axis=-1)
    dec_all = dec_all.astype(BF).reshape(np_ * ns, -1)
    used = dec_all.shape[1]
    dec_rows = -(-used // 2048) * 16
    dec_all = jnp.pad(dec_all, ((0, 0), (0, dec_rows * 128 - used)))
    dec_all = dec_all.reshape(np_ * ns, dec_rows, 128)

    red, small_sum, dec_got, enc_out, grad_out = two_kernels(
        np_, ns, r, rp, lanes, side, length, final_gain, expand_gain, attend_gain, dec_gains,
        rows_grad, block, cot, reduce_weight, active, expand_weight, hidden, slope, mixed_t,
        output_weight, query_weight, key_weight, value_weight, query, key, value, x, normed_t,
        context_t, probs, dec_all, encoded)

    got = dec_got.reshape(np_ * ns, -1)
    lefts = got[:, :9 * r].reshape(-1, 9, r)
    mid_got = got[:, 9 * r:15 * r].reshape(-1, 2, 3, r)
    rights = got[:, 15 * r:15 * r + 11 * cols].reshape(-1, 11, cols)
    plain = jnp.einsum("nkr,nkc->krc", lefts[:, :4], rights[:, :4], preferred_element_type=F32)
    crossed = jnp.einsum("nkhr,nkhd->krhd", mid_got, rights[:, 4:6].reshape(-1, 2, 3, size),
                         preferred_element_type=F32).reshape(2, r, cols)
    feed_in = jnp.einsum("nr,nc->rc", lefts[:, 4], rights[:, 7:11].reshape(-1, 4 * cols),
                         preferred_element_type=F32)
    feed_out = jnp.einsum("nr,nc->rc", lefts[:, 5:9].reshape(-1, 4 * r), rights[:, 6],
                          preferred_element_type=F32)
    red = red[:, :r]
    grad_reduce = red[2:4].reshape(2, r, side, ff // np_).reshape(cols, ff // np_).T
    gains = small_sum[:36].reshape(6, width)
    bias = small_sum[40:40 + heads, :buckets].T
    return (
        enc_out, dec_block, grad_out, dec_input_grad,
        gains[5],
        red[4][:, :cols], red[4][:, cols:], red[5][:, :cols], red[5][:, cols:],
        bias,
        gains[4],
        jnp.concatenate([red[0], red[1]], axis=1), grad_reduce,
        gains[3],
        gains[0], plain[0], plain[1],
        gains[1], plain[2], crossed[0], crossed[1], plain[3],
        gains[2], feed_in, feed_out,
    )


def solution(mesh):
    rows = P("pairs", "seq", None)
    single = P(("pairs", "seq"), None)
    block = P("pairs", "seq")
    return jax.shard_map(
        per_device,
        mesh=mesh,
        in_specs=(rows, single, P("pairs")) + (P(),) * 21 + (rows, single),
        out_specs=(
            rows, single, rows, single,
            P(), block, block, block, block, P(), P(), block, block, P(),
            P(), block, block, P(), block, block, block, block, P(), block, block,
        ),
        check_vma=False,
    )
```

```python
import functools
import itertools

import jax
import jax.numpy as jnp
from jax import lax
from jax.experimental import pallas as pl
from jax.experimental.pallas import tpu as pltpu
from jax.sharding import PartitionSpec as P

EPSILON = 1e-06
EDGES = (12, 16, 23, 32, 46, 64, 91)
HIGHEST = lax.Precision.HIGHEST
MESH = pl.DeviceIdType.MESH
BF = jnp.bfloat16
F32 = jnp.float32


def mm(a, b):
    return jnp.dot(a, b, preferred_element_type=F32)
def mm_t(a, b):
    return lax.dot_general(a, b, (((1,), (1,)), ((), ())), preferred_element_type=F32)
def t_mm(a, b):
    return lax.dot_general(a, b, (((0,), (0,)), ((), ())), preferred_element_type=F32)

def rms_scale(v):
    return lax.rsqrt(jnp.mean(v * v, axis=-1, keepdims=True) + EPSILON)

def gelu_parts(u):
    u2 = u * u
    t = jnp.tanh(u * (0.7978845608 + (0.7978845608 * 0.044715) * u2))
    half = 0.5 + 0.5 * t
    return u * half, half + half * (1.0 - t) * u * (0.7978845608 + (3 * 0.7978845608 * 0.044715) * u2)

def norm_down(v, r, g, dy):
    vr = v * r
    gd = g * dy
    return r * (gd - vr * jnp.mean(vr * gd, axis=-1, keepdims=True)), vr * dy

def diagonal_buckets(shape, width):
    col = lax.broadcasted_iota(jnp.int32, shape, 1)
    offset = (col // 128 - 1) * 128 - lax.rem(col, 128)
    offset = jnp.where(col >= width - 128, 256, jnp.where(col >= width - 256, -256, offset))
    dist = jnp.abs(offset)
    bucket = jnp.full_like(dist, 8)
    for edge in EDGES:
        bucket = bucket + (dist >= edge).astype(jnp.int32)
    bucket = jnp.where(dist < 8, dist, bucket) + jnp.where(offset > 0, 16, 0)
    return jnp.where(bucket == lax.broadcasted_iota(jnp.int32, shape, 0), 1.0, 0.0)


def forward_kernel(np_, ns, cut, lengths, table, ag, eg, fg, sg, cg, dg, dec_in, dec_cot, enc_in, enc_cot,
                   wq, wk, wv, wo, we, wr, sv, so, cq, ck, cv, co, fe, fr,
                   normed_t, q, k, v, probs, context_t, hidden, mixed_t, active, slope, block, low, x_out, cot_out,
                   rows_grad, dec_out, dec_in_grad, dec_gains, *rest):
    if cut:
        dec, *rest = rest
    else:
        left, right, wide, mids, *rest = rest
    (wqs, wks, wvs, wos, wes, wrs, svs, sos, cqs, cks, cvs, cos, fes, frs, xs, normed, nt, qs, ks, vs, ctx, hid,
     mixed, mt, act, slo, blk, rws, lws, rgs, band, vecs, v_t, s_t, pbuf, *rest) = rest
    if cut:
        left, right, wide, mids, cuts, both, *rest = rest
    sems, psem, osem, x_s, x_r, c_s, c_r, loc = rest
    ag, eg, fg, sg, cg, dg = (g[...].reshape(1, -1) for g in (ag, eg, fg, sg, cg, dg))
    n, width = normed.shape
    heads = probs.shape[0]
    size = width // heads
    ff = act.shape[1]
    slot = n // ns
    p = lax.axis_index("pairs")
    s = lax.axis_index("seq")
    length = lengths[s]

    barrier = pltpu.get_barrier_semaphore()
    for d in range(1, ns):
        pl.semaphore_signal(barrier, inc=1, device_id=(p, lax.rem(s + d, ns)), device_id_type=MESH)

    def rows_copy(src, dst, send, recv, d):
        t = lax.rem(s + d, ns)
        return pltpu.make_async_remote_copy(
            src_ref=src.at[t], dst_ref=dst.at[s], send_sem=send.at[d], recv_sem=recv.at[d],
            device_id=(p, t), device_id_type=MESH)

    x_copies = [rows_copy(enc_in, xs, x_s, x_r, d) for d in range(1, ns)]
    cot_copies = [rows_copy(enc_cot, cot_out, c_s, c_r, d) for d in range(1, ns)]
    keep_x = pltpu.make_async_copy(enc_in.at[s], xs.at[s], loc.at[0])
    keep_cot = pltpu.make_async_copy(enc_cot.at[s], cot_out.at[s], loc.at[1])
    keep_x.start()
    load = []
    for src, dst in ((sv, svs), (so, sos), (cq, cqs), (ck, cks), (fr, frs), (wq, wqs), (wk, wks), (wv, wvs),
                     (wo, wos), (we, wes), (wr, wrs), (cv, cvs), (co, cos), (fe, fes)):
        load.append(pltpu.make_async_copy(src, dst, sems.at[len(load)]))
        load[-1].start()
    pl.semaphore_wait(barrier, ns - 1)
    for copy in x_copies + cot_copies:
        copy.start()
    keep_cot.start()
    saved = []

    def save(src, dst):
        copy = pltpu.make_async_copy(src, dst, osem.at[len(saved)])
        saved.append(copy)
        copy.start()

    vec = lax.dot_general(table[...], diagonal_buckets((table.shape[1], width), width), (((1,), (0,)), ((), ())),
                          precision=HIGHEST, preferred_element_type=F32)
    for i in range(width // 128):
        vecs[:, i, :] = vec[:, i * 128:(i + 1) * 128]
    lane_s = lax.broadcasted_iota(jnp.int32, (128, 128), 1)
    row_s = lax.broadcasted_iota(jnp.int32, (128, 128), 0)

    @pl.loop(0, heads)
    def _(h):
        for b in range(3):
            t = jnp.where(lane_s + row_s < 128, vecs[h, b:b + 1, :], vecs[h, b + 1:b + 2, :])
            for bit in range(7):
                t = jnp.where((row_s >> bit) % 2 == 1, pltpu.roll(t, 1 << bit, 1), t)
            band[h, b * 128:(b + 1) * 128, :] = t

    x = dec_in[...].astype(F32)
    cot = dec_cot[...]
    own = (lax.broadcasted_iota(jnp.int32, (heads, width), 1) // size
           == lax.broadcasted_iota(jnp.int32, (heads, width), 0))

    def spread(r):
        return jnp.where(own, r.astype(F32), 0.0).astype(BF)

    def collect(r):
        return jnp.sum(jnp.where(own, r, 0.0), axis=0, keepdims=True)

    x_r = rms_scale(x)
    self_normed = (x * x_r * sg).astype(BF)
    load[0].wait()
    self_values = mm(self_normed, svs[...]).astype(BF)
    load[1].wait()
    after = x + mm(self_values, sos[...])
    after_r = rms_scale(after)
    cross_normed = (after * after_r * cg).astype(BF)
    load[2].wait()
    cross_q = mm(cross_normed, cqs[...]).astype(BF)
    load[3].wait()
    q_rows = mm_t(spread(cross_q), cks[...]).astype(BF)
    load[4].wait()
    active_back = mm_t(cot, frs[...])

    keep_x.wait()
    for copy in x_copies:
        copy.wait()
    save(xs, x_out)
    for i in range(ns):
        r = slice(i * slot, (i + 1) * slot)
        t = xs[i].astype(F32)
        t = t * rms_scale(t) * ag
        normed[r] = t.astype(BF)
        nt[:, r] = t.T.astype(BF)
    save(nt, normed_t)
    for j, (w, out, dst) in enumerate(((wqs, qs, q), (wks, ks, k), (wvs, vs, v))):
        load[5 + j].wait()
        for i in range(2):
            r = slice(i * (n // 2), (i + 1) * (n // 2))
            out[r] = mm(normed[r], w[...]).astype(BF)
        save(out, dst)

    lane = lax.broadcasted_iota(jnp.int32, (n, 128), 1)
    row = lax.broadcasted_iota(jnp.int32, (n, 128), 0)
    q_mark = jnp.where(lane == 0, 1.0, 0.0).astype(BF)
    k_mark = jnp.where((lane == 0) & (row >= length), -1e30, 0.0).astype(BF)

    def keep(h, a):
        return pltpu.make_async_copy(pbuf.at[a], probs.at[h], psem.at[a])

    @pl.loop(0, heads // 2)
    def _(g):
        cols = pl.ds(pl.multiple_of(g * 128, 128), 128)
        v_t[...] = vs[:, cols].T
        qq = jnp.concatenate([qs[:, cols], q_mark], axis=1)
        kp = ks[:, cols]
        for a in range(2):
            h = 2 * g + a
            mine = (lane < 64) if a == 0 else (lane >= 64)
            kk = jnp.concatenate([jnp.where(mine, kp, jnp.zeros_like(kp)), k_mark], axis=1)
            s_t[a] = mm_t(kk, qq)

            @pl.when(g > 0)
            def _():
                keep(h - 2, a).wait()

            for j in range(n // 128):
                tile = []
                for i in range(n // 128):
                    t = s_t[a, i * 128:(i + 1) * 128, j * 128:(j + 1) * 128]
                    if abs(i - j) <= 1:
                        t = t + band[h, (i - j + 1) * 128:(i - j + 2) * 128, :]
                    else:
                        f = 5 if i > j else 4
                        t = t + vecs[h, f:f + 1, :]
                    tile.append(t)
                t = jnp.concatenate(tile, axis=0)
                m = jnp.max(t, axis=0, keepdims=True)
                e = jnp.exp(t - m)
                total = jnp.sum(e, axis=0, keepdims=True)
                pbuf[a, :, j * 128:(j + 1) * 128] = (e * (1.0 / total)).astype(BF)
            ctx[pl.ds(pl.multiple_of(h * 64, 64), 64), :] = mm(v_t[a * 64:(a + 1) * 64, :], pbuf[a]).astype(BF)
            keep(h, a).start()

    save(ctx, context_t)
    load[8].wait()
    for i in range(ns):
        r = slice(i * slot, (i + 1) * slot)
        t = xs[i].astype(F32) + mm(ctx[:, r].T, wos[...])
        hid[r] = t
        t = t * rms_scale(t) * eg
        mixed[r] = t.astype(BF)
        mt[:, r] = t.T.astype(BF)
    save(hid, hidden)
    save(mt, mixed_t)
    load[9].wait()

    @pl.loop(0, ff // 512)
    def _(j):
        cols = pl.ds(pl.multiple_of(j * 512, 512), 512)
        a, b = gelu_parts(mm(mixed[...], wes[:, cols]))
        act[:, cols] = a.astype(BF)
        slo[:, cols] = b.astype(BF)

    save(act, active)
    save(slo, slope)
    load[10].wait()
    for i in range(2):
        r = slice(i * (n // 2), (i + 1) * (n // 2))
        alive = (lax.broadcasted_iota(jnp.int32, (n // 2, 1), 0) + i * (n // 2) < length).astype(F32)
        b = alive * (hid[r] + mm(act[r], wrs[...]))
        blk[r] = b
        lws[r] = b.astype(BF)
        rws[r] = (b * rms_scale(b) * fg).astype(BF)
    save(blk, block)
    save(lws, low)

    score = mm_t(q_rows, rws[...])
    score = jnp.where(lax.broadcasted_iota(jnp.int32, score.shape, 1) < length, score, -1e30)
    e = jnp.exp(score - jnp.max(score, axis=-1, keepdims=True))
    cross_probs = e / jnp.sum(e, axis=-1, keepdims=True)
    cross_low = cross_probs.astype(BF)
    mean_rows = mm(cross_low, rws[...]).astype(BF)
    for copy in load[11:]:
        copy.wait()
    cross_context = collect(mm(mean_rows, cvs[...])).astype(BF)
    middle = after + mm(cross_context, cos[...])
    middle_r = rms_scale(middle)
    feed_normed = (middle * middle_r * dg).astype(BF)
    dec_active, dec_slope = gelu_parts(mm(feed_normed, fes[...]))
    dec_active = dec_active.astype(BF)
    upper_grad = (dec_slope * active_back).astype(BF)
    middle_down, feed_gain = norm_down(middle, middle_r, dg, mm_t(upper_grad, fes[...]))
    middle_grad = cot.astype(F32) + middle_down
    cross_branch = middle_grad.astype(BF)
    context_grad = mm_t(cross_branch, cos[...]).astype(BF)
    g_rows = mm_t(spread(context_grad), cvs[...]).astype(BF)
    prob_grad = mm_t(g_rows, rws[...])
    score_grad = (cross_probs * (prob_grad - jnp.sum(cross_probs * prob_grad, axis=-1, keepdims=True))).astype(BF)
    pad = jnp.zeros((16 - heads % 16, n), BF)
    padw = jnp.zeros((16 - heads % 16, width), BF)
    rgs[...] = t_mm(jnp.concatenate([score_grad, pad, cross_low, pad], axis=0),
                    jnp.concatenate([q_rows, padw, g_rows, padw], axis=0)).astype(BF)
    save(rgs, rows_grad)
    score_rows = mm(score_grad, rws[...]).astype(BF)
    cross_q_grad = collect(mm(score_rows, cks[...])).astype(BF)
    after_down, cross_gain = norm_down(after, after_r, cg, mm_t(cross_q_grad, cqs[...]))
    after_grad = middle_grad + after_down
    self_branch = after_grad.astype(BF)
    self_values_grad = mm_t(self_branch, sos[...]).astype(BF)
    x_down, self_gain = norm_down(x, x_r, sg, mm_t(self_values_grad, svs[...]))
    dec_in_grad[...] = (after_grad + x_down).astype(BF)
    dec_out[...] = (middle + mm(dec_active, frs[...])).astype(BF)
    gains = dec_gains
    gains[0:1, :] = self_gain
    gains[1:2, :] = cross_gain
    gains[2:3, :] = feed_gain
    for i, r in enumerate((self_normed, self_values, cross_normed, cross_context, feed_normed)):
        left[i:i + 1, :] = r.astype(F32)
    for i, r in enumerate((self_values_grad, self_branch, cross_q_grad, cross_branch, cross_q, context_grad, cot)):
        right[i:i + 1, :] = r.astype(F32)
    wide[0:1, :] = dec_active.astype(F32)
    wide[1:2, :] = upper_grad.astype(F32)
    mids[0] = score_rows.astype(F32)
    mids[1] = mean_rows.astype(F32)
    if cut:
        rows, cols, step = width // np_, width // ns, heads // ns
        both[...] = jnp.zeros_like(both)
        cuts[...] = jnp.zeros_like(cuts)
        for j in range(ns):
            for i in range(7):
                t = right[i:i + 1, j * cols:(j + 1) * cols]
                both[j, 2 * i:2 * i + 1, :] = t[:, :128]
                both[j, 2 * i + 1:2 * i + 2, 0:cols - 128] = t[:, 128:]
            for i in range(6):
                lo = j * width + i * 128
                both[j, 14 + i:15 + i, :] = wide[1:2, lo:lo + 128]
        for i in range(np_):
            cuts[0:5, 0:rows] = left[0:5, i * rows:(i + 1) * rows]
            for a in range(3):
                lo = i * (ff // np_) + a * 128
                cuts[5 + a:6 + a, :] = wide[0:1, lo:lo + 128]
            for j in range(ns):
                for w in range(2):
                    cuts[8 + w * step:8 + (w + 1) * step, 0:rows] = (
                        mids[w, j * step:(j + 1) * step, i * rows:(i + 1) * rows])
                dec[i * ns + j, 0:16, :] = cuts[...].astype(BF)
                dec[i * ns + j, 16:48, :] = both[j].astype(BF)
    for a in range(2):
        keep(heads - 2 + a, a).wait()
    keep_cot.wait()
    for copy in cot_copies:
        copy.wait()
    for copy in saved:
        copy.wait()


def forward(np_, ns, cut, lengths, table, gains, dec_in, dec_cot, enc_in, enc_cot, weights):
    group, slot, width = enc_in.shape
    n = slot * ns
    ff = weights[4].shape[1]
    heads = table.shape[0]
    smem = pl.BlockSpec(memory_space=pltpu.SMEM)
    vm = pl.BlockSpec(memory_space=pltpu.VMEM)
    hb = pl.BlockSpec(memory_space=pl.ANY)
    S = jax.ShapeDtypeStruct
    V = pltpu.VMEM
    full, tall, floats, broad = ((n, width), BF), ((width, n), BF), ((n, width), F32), ((n, ff), BF)
    slots = ((ns, slot, width), BF)
    raw = [((5, width), F32), ((7, width), F32), ((2, ff), F32), ((2, heads, width), F32)]
    outs = [tall, full, full, full, ((heads, n, n), BF), tall, floats, tall, broad, broad, floats, full, slots, slots,
            full, ((1, width), BF), ((1, width), BF), ((3, width), F32)]
    outs += [((np_ * ns, 48, 128), BF)] if cut else raw
    scratch = [slots, full, tall, full, full, full, tall, floats, full, tall, broad, broad, floats, full, full, full,
               ((heads, 384, 128), F32), ((heads, 8, 128), F32), ((128, n), BF), ((2, n, n), F32), ((2, n, n), BF)]
    scratch += raw + [((16, 128), F32), ((ns, 32, 128), F32)] if cut else []
    dma = pltpu.SemaphoreType.DMA
    return pl.pallas_call(
        functools.partial(forward_kernel, np_, ns, cut),
        out_shape=tuple(S(*t) for t in outs),
        in_specs=[smem] + [vm] * 9 + [hb] * 16,
        out_specs=(hb,) * 15 + (vm,) * (len(outs) - 15),
        scratch_shapes=[V(w.shape, BF) for w in weights] + [V(*t) for t in scratch] + [
            dma((14,)), dma((2,)), dma((16,)), dma((ns,)), dma((ns,)), dma((ns,)), dma((ns,)), dma((2,))],
        compiler_params=pltpu.CompilerParams(
            collective_id=1, has_side_effects=True, vmem_limit_bytes=62 * 1024 * 1024),
        name="forward",
    )(lengths, table, *gains, dec_in, dec_cot, enc_in, enc_cot, *weights)


def finish_kernel(heads, red, small, dec, dec_row, dec_grad, enc, grad, *outs):
    (enc_out, grad_out, row_out, row_grad_out, qo, ko, vo, oo, expand, reduce, bias, g0, g1, g2, g3, g4, g5,
     sv, so, cq, ck, cv, co, fe, fr, wide, sem) = outs
    copies = [pltpu.make_async_copy(enc, enc_out, sem.at[0]), pltpu.make_async_copy(grad, grad_out, sem.at[1])]
    for copy in copies:
        copy.start()
    row_out[...] = dec_row[...]
    row_grad_out[...] = dec_grad[...]
    wide[...] = dec[...].astype(F32)
    rows, cols = qo.shape
    lanes = red.shape[2]
    for i, out in ((4, (qo, ko)), (5, (vo, oo))):
        t = red[i]
        out[0][...] = t[:, :cols]
        out[1][...] = t[:, cols:]
    for i in range(2):
        expand[:, i * lanes:(i + 1) * lanes] = red[i]
        reduce[i * rows:(i + 1) * rows, :] = red[2 + i]
    bias[...] = small[40:40 + heads, 0:bias.shape[1]]
    for i, out in enumerate((g0, g1, g2, g3, g4, g5)):
        for j in range(6):
            out[pl.ds(j * 128, 128)] = small[i * 6 + j, :]

    def row(i):
        return wide[:, i, :]

    def pair(i):
        return jnp.concatenate([row(16 + 2 * i), row(17 + 2 * i)], axis=1)[:, :cols].astype(BF)

    for i, out in enumerate((sv, so, cq, co)):
        out[...] = t_mm(row(i)[:, :rows].astype(BF), pair(i))
    upper = jnp.concatenate([row(30 + i) for i in range(6)], axis=1).astype(BF)
    fe[...] = t_mm(row(4)[:, :rows].astype(BF), upper)
    active = jnp.concatenate([row(5 + i) for i in range(3)], axis=1).astype(BF)
    fr[...] = t_mm(pair(6), active)
    step = cols // 64
    for w, out in enumerate((ck, cv)):
        g = pair(4 + w)
        out[...] = jnp.concatenate(
            [t_mm(row(8 + w * step + h)[:, :rows].astype(BF), g[:, h * 64:(h + 1) * 64]) for h in range(step)], axis=1)
    for copy in copies:
        copy.wait()


def finish(heads, buckets, red, small, dec, dec_row, dec_grad, enc, grad):
    rows, lanes = red.shape[1:]
    cols, width = lanes // 2, 2 * lanes
    vm = pl.BlockSpec(memory_space=pltpu.VMEM)
    hb = pl.BlockSpec(memory_space=pl.ANY)
    S = jax.ShapeDtypeStruct
    block, broad, tall = S((rows, cols), F32), S((rows, width), F32), S((cols, lanes), F32)
    return pl.pallas_call(
        functools.partial(finish_kernel, heads),
        out_shape=(S(enc.shape, BF), S(grad.shape, BF), S(dec_row.shape, BF), S(dec_grad.shape, BF), block, block, block, block, broad, tall,
                   S((heads, buckets), F32)) + (S((width,), F32),) * 6 + (block,) * 6 + (broad, tall),
        in_specs=[vm] * 5 + [hb, hb],
        out_specs=(hb, hb) + (vm,) * 23,
        scratch_shapes=[pltpu.VMEM(dec.shape, F32), pltpu.SemaphoreType.DMA((2,))],
        compiler_params=pltpu.CompilerParams(vmem_limit_bytes=62 * 1024 * 1024),
        name="finish",
    )(red, small, dec, dec_row, dec_grad, enc, grad)


PARTS = 2
ORDERS = {
    "t00": "xfny",
    "t10": "fnyx",
    "t01": "nyfx",
    "t11": "yxfn",
    "w00": "nyfx",
    "w10": "yxfn",
    "w01": "xyfn",
    "w11": "ynxf",
    "a0": "xyfn",
    "a1": "xnyf",
}
SCHEDULE = {
    "wide": (
        ("t00", 0), ("t10", 0), ("t01", 0), ("t11", 0),
    ),
    "rows": (
        ("w00", 0),
    ),
    "dout": (
        ("w10", 0), ("w01", 0),
    ),
    "p00": (
        ("w11", 0), ("t00", 1),
    ),
    "p01": (
        ("t11", 1),
    ),
    "q0": (
        ("t01", 1), ("t10", 1), ("w01", 1), ("w10", 1),
    ),
    "p10": (
        ("t11", 2), ("h00", 0),
    ),
    "p11": (
        ("h01", 0), ("w00", 1), ("w10", 2), ("w11", 1),
    ),
    "p12": (
        ("t01", 2),
    ),
    "v1": (
        ("t00", 2), ("t10", 2), ("w01", 2), ("h00", 1),
    ),
    "ng1": (
        ("h10", 0), ("t11", 3),
    ),
    "end": (
        ("w00", 2), ("h11", 0), ("t10", 3), ("w10", 3), ("w11", 2), ("h01", 1),
        ("t00", 3), ("t01", 3), ("t11", 4), ("w01", 3), ("h10", 1), ("w10", 4),
        ("w00", 3), ("h01", 2), ("w01", 4), ("h11", 1), ("t00", 4), ("t10", 4),
        ("w11", 3), ("t01", 4), ("w00", 4), ("h10", 2), ("h11", 2), ("w11", 4),
        ("h10", 3), ("h11", 3),
    ),
}
HOPS = (1, 3, 5)


def ff_pieces():
    names = [kind + str(unit) + str(i) for kind in "tw" for i in range(PARTS) for unit in range(2)]
    return names + ["h" + str(half) + str(w) for half in range(2) for w in range(2)]


def fused_kernel(np_, ns, length, fg, eg, ag, gains_dec,
                 rows_grad, block, cot, wr, active, wide_w, hidden, slope, mixed_t_in, wo, wq, wk, wv, q_in, k_in,
                 v_in, x_in, normed_t_in, context_t_in, probs, dec, encoded,
                 red, small_out, dec_out, enc_out, grad_out,
                 acts, grads, w1, wes, bg, hid, dm, rg, ct, rb, rb_t, mixed_t, normed_t, context_t,
                 dp, ds, pbuf, k_t, band, diag, fu, r0, r0a, r1, r2, r3, r4, a1, a2, a3, over0, over1,
                 sm, smr, smz,
                 psem, isem, loc, f_s, f_r, t_s, t_r, o_s, o_r,
                 m_s, m_r, mz_s, mz_r, d_s, d_r, e_s, e_r, g_s, g_r):
    n, width = hid.shape
    ff = acts.shape[1]
    fg, eg, ag = (g[...].reshape(1, -1) for g in (fg, eg, ag))
    heads = probs.shape[0]
    nz = np_ // 2
    pieces = ff_pieces()
    rows, lanes = fu.shape[6:]
    step_rows = rows // PARTS
    count = np_ * ns
    p = lax.axis_index("pairs")
    s = lax.axis_index("seq")
    c = lax.rem(s, 2)
    y = s // 2
    xx = lax.rem(p, 2)
    z = p // 2
    me = p * ns + s
    core_peer = (p, s + 1 - 2 * c)
    y_peer = (p, lax.rem(s + 2, 4))
    x_peer = (p + 1 - 2 * xx, s)
    first_half, last_half = 1 - y, y
    own_at = {"x": xx, "y": y, "n": lax.rem(z, 2), "f": z // 2}
    peers = {"x": x_peer, "y": y_peer, "n": ((z + 1 - 2 * own_at["n"]) * 2 + xx, s),
             "f": (lax.rem(z + 2, 4) * 2 + xx, s)}

    def place(d):
        lin = lax.rem(me + d, count)
        return (lin // ns, lax.rem(lin, ns))

    barrier = pltpu.get_barrier_semaphore()

    @pl.loop(1, count)
    def _(d):
        pl.semaphore_signal(barrier, inc=1, device_id=place(d), device_id_type=MESH)

    def remote(src, dst, send, recv, peer):
        return pltpu.make_async_remote_copy(
            src_ref=src, dst_ref=dst, send_sem=send, recv_sem=recv,
            device_id=peer, device_id_type=MESH)

    def load(i, src, dst):
        return pltpu.make_async_copy(src, dst, isem.at[i])

    def part_of(ref, i):
        return ref.at[:, pl.ds(i * width, width)]

    loads = [load(i, a, b) for i, (a, b) in enumerate((
        (rows_grad, rg), (block, bg), (cot, ct), (active, acts), (wr, w1), (slope, grads), (mixed_t_in, mixed_t),
        (wide_w, wes), (hidden, hid), (normed_t_in, normed_t), (context_t_in, context_t)))]
    weights = [load(11 + i, a, w1.at[pl.ds(i * width, width)]) for i, a in enumerate((wo, wq, wk, wv))]
    heads_in = [load(15 + i, a, part_of(grads, i)) for i, a in enumerate((q_in, k_in, v_in, x_in))]
    d_out, dq, dk, dv = (part_of(acts, i) for i in range(4))
    q, k, v, x = (part_of(grads, i) for i in range(4))
    branch, dq_t, ng, in_grad, hidden_grad = ct, rb_t, dm, rg, bg
    wos, wqs, wks, wvs = (w1.at[pl.ds(i * width, width)] for i in range(4))

    def fetch(h, slot):
        return pltpu.make_async_copy(probs.at[h], pbuf.at[slot], psem.at[slot])

    def view(ref, dims, fixed):
        return ref.at[tuple(fixed.get(dim, slice(None)) for dim in dims)]

    def accumulate(dst, src, depth):
        for at in itertools.product(range(2), repeat=depth):
            dst[at] = dst[at] + src[at]

    def au(w, core, half):
        return fu.at[1 - c, 2 * w + core, half]

    def region(name, core):
        if name[0] == "h":
            return au(int(name[2]), core, first_half if name[1] == "0" else last_half), "fnx"
        unit = (2 if name[0] == "t" else 0) + int(name[1])
        return fu.at[core, unit, :, :, :, :, pl.ds(int(name[2]) * step_rows, step_rows)], "yfnx"

    def order_of(name):
        if name[0] != "h":
            return ORDERS[name]
        order = ORDERS["a" + name[2]]
        return order[:order.index("y")] if name[1] == "0" else order.replace("y", "")

    def core_copy(name):
        i = pieces.index(name)
        src, _ = region(name, 1 - c)
        dst = r0a.at[i - len(pieces) + 4] if name[0] == "h" else r0.at[i]
        return remote(src, dst, f_s.at[i], f_r.at[i], core_peer)

    def landing(name, j):
        i = pieces.index(name)
        if name[0] == "h":
            return (a1, a2, a3)[j].at[i - len(pieces) + 4]
        return (r1, r2, r3, r4)[j].at[i]

    def remaining(name, j):
        ref, dims = region(name, c)
        return ref, dims, {letter: own_at[letter] for letter in order_of(name)[:j]}

    def stage_copy(name, j):
        ref, dims, fixed = remaining(name, j)
        letter = order_of(name)[j]
        i = pieces.index(name)
        src = view(ref, dims, {**fixed, letter: 1 - own_at[letter]})
        return remote(src, landing(name, j), t_s.at[i, j], t_r.at[i, j], peers[letter])

    def hand_over(w):
        name = "h0" + str(w)
        ref, dims, fixed = remaining(name, len(order_of(name)))
        return remote(view(ref, dims, fixed), (over0, over1)[w], o_s.at[w], o_r.at[w], y_peer)

    def total_of(name):
        unit = 4 + int(name[2]) if name[0] == "h" else (2 if name[0] == "t" else 0) + int(name[1])
        if name[0] == "h":
            return red.at[unit]
        return red.at[unit, pl.ds(int(name[2]) * step_rows, step_rows)]

    def step(name, j):
        order = order_of(name)
        ref, dims, fixed = remaining(name, j)
        mine = view(ref, dims, fixed)
        depth = len(dims) - j
        closing = j == len(order) and name[:2] != "h0"
        joins = name[:2] == "h1" and ORDERS["a" + name[2]].index("y") == j
        if j == 0:
            core_copy(name).wait()
            landed = r0a.at[pieces.index(name) - len(pieces) + 4] if name[0] == "h" else r0.at[pieces.index(name)]
        else:
            stage_copy(name, j - 1).wait()
            landed = landing(name, j - 1)
        if joins:
            hand_over(int(name[2])).wait()
            extra = (over0, over1)[int(name[2])]
        if closing:
            total = mine[...].astype(F32) + landed[...].astype(F32)
            if joins:
                total = total + extra[...].astype(F32)
            total_of(name)[...] = total
            return
        accumulate(mine, landed, depth)
        if joins:
            accumulate(mine, extra, depth)
        if j < len(order):
            stage_copy(name, j).start()
        else:
            hand_over(int(name[2])).start()

    def run_slot(slot):
        for name, j in SCHEDULE.get(slot, ()):
            step(name, j)

    def dec_copy(d):
        to = place(d)
        return remote(dec.at[to[0] * ns + to[1]], dec_out.at[me], d_s.at[d], d_r.at[d], to)

    def enc_copy(d):
        t = lax.rem(s + d, ns)
        return remote(encoded.at[t], enc_out.at[s], e_s.at[d], e_r.at[d], (p, t))

    def grad_copy(d):
        t = lax.rem(s + d, ns)
        return remote(in_grad.at[t], grad_out.at[s], g_s.at[d], g_r.at[d], (p, t))

    keep_dec = pltpu.make_async_copy(dec.at[me], dec_out.at[me], loc.at[4])
    keep_enc = pltpu.make_async_copy(encoded.at[s], enc_out.at[s], loc.at[5])
    keep_grad = pltpu.make_async_copy(in_grad.at[s], grad_out.at[s], loc.at[6])

    for copy in loads:
        copy.start()
    fetch(first_half * (heads // 2), 0).start()
    fetch(first_half * (heads // 2) + 1, 1).start()
    keep_dec.start()
    keep_enc.start()
    diag[...] = jnp.zeros_like(diag)
    slot_rows = n // ns
    sm[...] = jnp.zeros_like(sm)

    def put_gain(i, gain):
        for j in range(width // 128):
            sm[0, i * 6 + j:i * 6 + j + 1, :] = gain[:, j * 128:(j + 1) * 128]

    for i in range(3):
        put_gain(i, gains_dec[i:i + 1, :])
    for i in range(3):
        loads[i].wait()
    final_gain = jnp.zeros((1, width), F32)
    for i in range(ns):
        r = slice(i * slot_rows, (i + 1) * slot_rows)
        alive = (lax.broadcasted_iota(jnp.int32, (slot_rows, 1), 0) + i * slot_rows < length[s]).astype(F32)
        b = bg[r]
        down, gain = norm_down(b, rms_scale(b), fg, rg[i].astype(F32))
        b = alive * (ct[r].astype(F32) + down)
        bg[r] = b
        low = b.astype(BF)
        rb[r] = low
        rb_t[:, r] = low.T
        final_gain = final_gain + jnp.sum(gain, axis=0, keepdims=True)
    put_gain(3, final_gain)
    pl.semaphore_wait(barrier, count - 1)
    for d in range(1, ns):
        enc_copy(d).start()

    @pl.loop(1, count)
    def _(d):
        dec_copy(d).start()

    part = width // 4
    loads[3].wait()

    @pl.loop(0, nz)
    def _(b):
        cols = pl.ds(pl.multiple_of(b * 2 * lanes, 128), 2 * lanes)
        g = mm(rb_t[...], acts[:, cols]).astype(BF)
        for j in range(4):
            for half in range(2):
                lo = j * part + half * rows
                for e in range(2):
                    fu[j % 2, 2 + half, j // 2, b // 2, lax.rem(b, 2), e] = g[lo:lo + rows, e * lanes:(e + 1) * lanes]

    for name in pieces:
        if name[0] == "t":
            core_copy(name).start()
    loads[4].wait()
    loads[5].wait()

    for j in range(ff // width):
        cols = slice(j * width, (j + 1) * width)
        grads[:, cols] = (grads[:, cols].astype(F32) * mm_t(rb[...], w1[cols, :])).astype(BF)
        run_slot("ug" + str(j))

    for copy in weights:
        copy.start()
    loads[6].wait()

    @pl.loop(0, 4)
    def _(j):
        cols = pl.ds(pl.multiple_of(j * 2 * lanes, 128), 2 * lanes)
        g = mm(mixed_t[...], grads[:, cols]).astype(BF)
        for half in range(2):
            fu[lax.rem(j, 2), half, j // 2] = g[:, half * lanes:(half + 1) * lanes].reshape(2, 2, 2, rows, lanes)

    for name in pieces:
        if name[0] == "w":
            core_copy(name).start()
    run_slot("wide")
    loads[7].wait()
    dm[...] = mm_t(grads[...], wes[...])
    for copy in heads_in:
        copy.start()
    run_slot("dm")
    loads[8].wait()
    expand_gain = jnp.zeros((1, width), F32)
    for i in range(ns):
        r = slice(i * slot_rows, (i + 1) * slot_rows)
        t = hid[r]
        down, gain = norm_down(t, rms_scale(t), eg, dm[r])
        t = bg[r] + down
        bg[r] = t
        branch[r] = t.astype(BF)
        expand_gain = expand_gain + jnp.sum(gain, axis=0, keepdims=True)
    put_gain(4, expand_gain)
    run_slot("rows")
    weights[0].wait()

    @pl.loop(0, width // 384)
    def _(j):
        cols = pl.ds(pl.multiple_of(j * 384, 128), 384)
        d_out[:, cols] = mm_t(branch[...], w1[cols, :]).astype(BF)

    for copy in heads_in:
        copy.wait()
    for copy in loads[9:]:
        copy.wait()

    run_slot("dout")

    lane = lax.broadcasted_iota(jnp.int32, (n, 128), 1)
    lane_s = lax.broadcasted_iota(jnp.int32, (128, 128), 1)
    row_s = lax.broadcasted_iota(jnp.int32, (128, 128), 0)

    def pair(half, g):
        cols = pl.ds(pl.multiple_of(half * (width // 2) + g * 128, 128), 128)
        k_t[...] = k[:, cols].T
        dop = d_out[:, cols]
        qp = q[:, cols]
        vp = v[:, cols]
        zero = jnp.zeros_like(qp)
        for a in range(2):
            h = half * (heads // 2) + 2 * g + a
            mine = (lane < 64) if a == 0 else (lane >= 64)
            dp[...] = mm_t(jnp.where(mine, vp, zero), dop)
            fetch(h, a).wait()
            for j in range(n // 128):
                pj = pbuf[a, :, j * 128:(j + 1) * 128].astype(F32)
                pd = pj * dp[:, j * 128:(j + 1) * 128]
                total = jnp.sum(pd, axis=0, keepdims=True)
                sg = pd - pj * total
                ds[:, j * 128:(j + 1) * 128] = sg.astype(BF)
                for i in range(n // 128):
                    t = sg[i * 128:(i + 1) * 128]
                    if abs(i - j) <= 1:
                        b = (i - j + 1) * 128
                        if j == 0 or (j == 1 and i == 0):
                            band[b:b + 128, :] = t
                        else:
                            band[b:b + 128, :] += t
                    else:
                        f = 5 if i > j else 4
                        diag[h, f:f + 1, :] += jnp.sum(t, axis=0, keepdims=True)
            dvp = mm(pbuf[a], jnp.where(mine, dop, zero))
            dkp = mm(ds[...], jnp.where(mine, qp, zero))
            dq_t[pl.ds(pl.multiple_of(h * 64, 64), 64), :] = mm(k_t[a * 64:(a + 1) * 64, :], ds[...]).astype(BF)
            if a == 0:
                dk_sum, dv_sum = dkp, dvp
            else:
                dk[:, cols] = (dk_sum + dkp).astype(BF)
                dv[:, cols] = (dv_sum + dvp).astype(BF)
            for b in range(3):
                t = band[b * 128:(b + 1) * 128, :]
                for bit in range(7):
                    t = jnp.where((row_s >> bit) % 2 == 1, pltpu.roll(t, 128 - (1 << bit), 1), t)
                straight = jnp.sum(jnp.where(lane_s + row_s < 128, t, 0.0), axis=0, keepdims=True)
                whole = jnp.sum(t, axis=0, keepdims=True)
                diag[h, b:b + 1, :] += straight
                diag[h, b + 1:b + 2, :] += whole - straight

    def units_of(half, tag):
        cols = pl.ds(pl.multiple_of(half * (width // 2), 128), width // 2)
        dq_h = dq_t[cols, :].T
        dq[:, cols] = dq_h
        dk_h = dk[:, cols]
        for cc in range(2):
            e = slice(cc * part, (cc + 1) * part)
            g = mm(normed_t[...], jnp.concatenate([dq_h[:, e], dk_h[:, e]], axis=1))
            au(0, cc, half)[...] = g.astype(BF).reshape(2, 2, 2, rows, lanes)
        core_copy("h" + tag + "0").start()
        run_slot("q" + tag)
        dv_h = dv[:, cols]
        br_h = branch[:, cols]
        zero = jnp.zeros((n, part), BF)
        for cc in range(2):
            e = slice(cc * part, (cc + 1) * part)
            g = (mm(normed_t[...], jnp.concatenate([dv_h[:, e], zero], axis=1))
                 + mm(context_t[...], jnp.concatenate([zero, br_h[:, e]], axis=1)))
            au(1, cc, half)[...] = g.astype(BF).reshape(2, 2, 2, rows, lanes)
        core_copy("h" + tag + "1").start()
        run_slot("v" + tag)

    quarter = heads // 4

    @pl.loop(0, quarter)
    def _(g):
        pair(first_half, g)
        nxt = jnp.where(g == quarter - 1, last_half * (heads // 2), first_half * (heads // 2) + 2 * (g + 1))
        fetch(nxt, 0).start()
        fetch(nxt + 1, 1).start()

        for i in range(quarter):
            if SCHEDULE.get("p0" + str(i)):
                @pl.when(g == i)
                def _():
                    run_slot("p0" + str(i))

    units_of(first_half, "0")

    @pl.loop(0, quarter)
    def _(g):
        pair(last_half, g)

        @pl.when(g < quarter - 1)
        def _():
            nxt = last_half * (heads // 2) + 2 * (g + 1)
            fetch(nxt, 0).start()
            fetch(nxt + 1, 1).start()

        for i in range(quarter):
            if SCHEDULE.get("p1" + str(i)):
                @pl.when(g == i)
                def _():
                    run_slot("p1" + str(i))

    units_of(last_half, "1")
    for copy in weights[1:]:
        copy.wait()

    for i in range(2):
        r = slice(i * (n // 2), (i + 1) * (n // 2))
        ng[r] = mm_t(dq[r], wqs[...]) + mm_t(dk[r], wks[...]) + mm_t(dv[r], wvs[...])
        run_slot("ng" + str(i))

    gain_sum = jnp.zeros((1, width), F32)
    for i in range(ns):
        r = slice(i * slot_rows, (i + 1) * slot_rows)
        t = x[r].astype(F32)
        down, gain = norm_down(t, rms_scale(t), ag, ng[r])
        in_grad[i] = (hidden_grad[r] + down).astype(BF)
        gain_sum = gain_sum + jnp.sum(gain, axis=0, keepdims=True)
    keep_grad.start()
    for d in range(1, ns):
        grad_copy(d).start()

    pick = diagonal_buckets((128, width), width)
    bias = jnp.zeros((16, 128), F32)
    for i in range(width // 128):
        bias = bias + lax.dot_general(diag[:, i, :], pick[:, i * 128:(i + 1) * 128], (((1,), (1,)), ((), ())),
                                      precision=HIGHEST, preferred_element_type=F32)
    sm[0, 40:56, :] = bias
    put_gain(5, gain_sum)

    def small_copy(i):
        return remote(sm.at[i], smr.at[i], m_s.at[i], m_r.at[i], (core_peer, y_peer, x_peer)[i])

    def z_small(d):
        return remote(smz.at[z], smz.at[z], mz_s.at[d], mz_r.at[d], (lax.rem(z + d, nz) * 2 + xx, s))

    def small_hop(i):
        small_copy(i).wait()
        if i < 2:
            sm[i + 1] = sm[i] + smr[i]
            small_copy(i + 1).start()
        else:
            smz[z] = sm[i] + smr[i]

            @pl.loop(1, nz)
            def _(d):
                z_small(d).start()

    small_copy(0).start()
    tail = SCHEDULE["end"]
    for i, (name, j) in enumerate(tail):
        step(name, j)
        if i in HOPS:
            small_hop(HOPS.index(i))

    @pl.loop(1, nz)
    def _(d):
        z_small(d).wait()

    small_out[...] = smz[0]

    @pl.loop(1, nz)
    def _(d):
        small_out[...] = small_out[...] + smz[d]

    keep_dec.wait()
    keep_enc.wait()
    keep_grad.wait()
    for d in range(1, ns):
        enc_copy(d).wait()
        grad_copy(d).wait()

    @pl.loop(1, count)
    def _(d):
        dec_copy(d).wait()


def fused(np_, ns, length, fg, eg, ag, gains_dec, rows_grad, block, cot, wr, active, we, hidden, slope, mixed_t,
          wo, wq, wk, wv, q, k, v, x, normed_t, context_t, probs, dec, encoded):
    n, width = hidden.shape
    ff = active.shape[1]
    heads = probs.shape[0]
    nz = np_ // 2
    rows, lanes = width // np_, ff // np_
    count = np_ * ns
    smem = pl.BlockSpec(memory_space=pltpu.SMEM)
    vm = pl.BlockSpec(memory_space=pltpu.VMEM)
    hb = pl.BlockSpec(memory_space=pl.ANY)
    S = jax.ShapeDtypeStruct
    V = pltpu.VMEM
    dma = pltpu.SemaphoreType.DMA
    nar, tall = V((n, width), BF), V((width, n), BF)
    floats = V((n, width), F32)
    slots = (ns, n // ns, width)
    small = (64, 128)
    ffs = 4 * PARTS
    sub = rows // PARTS

    def joint(w):
        return V((2,) * (3 - ORDERS["a" + str(w)].index("y")) + (rows, lanes), BF)

    return pl.pallas_call(
        functools.partial(fused_kernel, np_, ns),
        out_shape=(S((6, rows, lanes), F32), S(small, F32), S(dec.shape, BF), S(slots, BF), S(slots, BF)),
        in_specs=[smem] + [vm] * 4 + [hb] * 22,
        out_specs=(vm, vm, hb, hb, hb),
        scratch_shapes=[
            V((n, ff), BF), V((n, ff), BF), V((ff, width), BF), V((width, ff), BF), floats, floats, floats,
            V(slots, BF), nar, nar, tall, tall, tall, tall,
            V((n, n), F32), V((n, n), BF), V((2, n, n), BF), V((128, n), BF), V((384, 128), F32), V((16, 8, 128), F32),
            V((2, 4, 2, 2, 2, 2, rows, lanes), BF), V((ffs, 2, 2, 2, 2, sub, lanes), BF), V((4, 2, 2, 2, rows, lanes), BF),
            V((ffs, 2, 2, 2, sub, lanes), BF), V((ffs, 2, 2, sub, lanes), BF), V((ffs, 2, sub, lanes), BF),
            V((ffs, sub, lanes), BF), V((4, 2, 2, rows, lanes), BF), V((4, 2, rows, lanes), BF),
            V((4, rows, lanes), BF), joint(0), joint(1),
            V((3,) + small, F32), V((3,) + small, F32), V((nz,) + small, F32),
            dma((2,)), dma((19,)), dma((7,)), dma((ffs + 4,)), dma((ffs + 4,)), dma((ffs + 4, 4)), dma((ffs + 4, 4)),
            dma((2,)), dma((2,)),
            dma((3,)), dma((3,)), dma((nz,)), dma((nz,)), dma((count,)), dma((count,)),
            dma((ns,)), dma((ns,)), dma((ns,)), dma((ns,)),
        ],
        compiler_params=pltpu.CompilerParams(
            collective_id=0, has_side_effects=True, vmem_limit_bytes=62 * 1024 * 1024),
        name="fused_backward",
    )(length, fg, eg, ag, gains_dec, rows_grad.reshape(slots), block, cot, wr,
      active, we, hidden, slope, mixed_t, wo, wq, wk, wv, q, k, v, x, normed_t, context_t, probs, dec,
      encoded.reshape(slots))


def feed_back_kernel(length, rows_grad, block, cot, fg, hidden, eg, mixed, active, slope, wr, we,
                     wide, tall, hidden_grad, branch, gains, wrs, wes, bg, rb, rb_t, ug, mixed_t, dmixed, sems):
    n, width = block.shape
    ff = active.shape[1]
    groups, lanes = tall.shape[3], tall.shape[5]
    cols_dev = width // 4
    copies = [pltpu.make_async_copy(a, b, sems.at[i]) for i, (a, b) in enumerate(((wr, wrs), (we, wes)))]
    for c in copies:
        c.start()
    gains[...] = jnp.zeros_like(gains)

    @pl.loop(0, n // 128)
    def _(i):
        r = pl.ds(i * 128, 128)
        alive = (lax.broadcasted_iota(jnp.int32, (128, 1), 0) + i * 128 < length[0]).astype(F32)
        v = block[r]
        down, gain = norm_down(v, rms_scale(v), fg[...], rows_grad[r].astype(F32))
        b = alive * (cot[r].astype(F32) + down)
        bg[r] = b
        rb[r] = b.astype(BF)
        rb_t[:, pl.ds(pl.multiple_of(i * 128, 128), 128)] = b.T.astype(BF)
        mixed_t[:, pl.ds(pl.multiple_of(i * 128, 128), 128)] = mixed[r].T
        gains[0:1, :] += jnp.sum(gain, axis=0, keepdims=True)

    copies[0].wait()

    @pl.loop(0, ff // 256)
    def _(j):
        cols = pl.ds(pl.multiple_of(j * 256, 256), 256)
        ug[:, cols] = (slope[:, cols].astype(F32) * mm_t(rb[...], wrs[cols, :])).astype(BF)

    copies[1].wait()

    @pl.loop(0, width // 256)
    def _(j):
        cols = pl.ds(pl.multiple_of(j * 256, 256), 256)
        dmixed[:, cols] = mm_t(ug[...], wes[cols, :])

    @pl.loop(0, n // 128)
    def _(i):
        r = pl.ds(i * 128, 128)
        v = hidden[r]
        down, gain = norm_down(v, rms_scale(v), eg[...], dmixed[r])
        h = bg[r] + down
        hidden_grad[r] = h
        branch[r] = h.astype(BF)
        gains[1:2, :] += jnp.sum(gain, axis=0, keepdims=True)

    @pl.loop(0, 4)
    def _(j):
        for half in range(2):
            cols = pl.ds(pl.multiple_of(j * (ff // 4) + half * (ff // 8), 128), ff // 8)
            wide[half, lax.rem(j, 2), j // 2] = mm(mixed_t[...], ug[:, cols]).astype(BF)

    chunk = ff // 8
    per_group = lanes // chunk

    @pl.loop(0, 8)
    def _(i):
        cols = pl.ds(pl.multiple_of(i * chunk, 128), chunk)
        g = mm(rb_t[...], active[:, cols]).astype(BF)
        for j in range(4):
            for half in range(2):
                r = j * cols_dev + half * (cols_dev // 2)
                part = g[r:r + cols_dev // 2]
                if per_group == 1:
                    tall[half, j % 2, j // 2, i] = part
                else:
                    tall[half, j % 2, j // 2, 0, :, cols] = part


def feed_back(groups, length, rows_grad, block, cot, fg, hidden, eg, mixed, active, slope, wr, we):
    n, width = block.shape
    ff = active.shape[1]
    sm = pl.BlockSpec(memory_space=pltpu.SMEM)
    vm = pl.BlockSpec(memory_space=pltpu.VMEM)
    hb = pl.BlockSpec(memory_space=pl.ANY)
    S = jax.ShapeDtypeStruct
    V = pltpu.VMEM
    return pl.pallas_call(
        feed_back_kernel,
        out_shape=(S((2, 2, 2, width, ff // 8), BF),
                   S((2, 2, 2, groups, width // 8, ff // groups), BF), S((n, width), F32), S((n, width), BF), S((2, width), F32)),
        in_specs=[sm] + [vm] * 9 + [hb] * 2,
        out_specs=(vm,) * 5,
        scratch_shapes=[V(wr.shape, BF), V(we.shape, BF), V((n, width), F32), V((n, width), BF), V((width, n), BF),
                        V((n, ff), BF), V((width, n), BF), V((n, width), F32), pltpu.SemaphoreType.DMA((2,))],
        compiler_params=pltpu.CompilerParams(vmem_limit_bytes=60 * 1024 * 1024),
        name="feed_back",
    )(length, rows_grad, block, cot, fg.reshape(1, -1), hidden, eg.reshape(1, -1), mixed, active, slope, wr, we)


def backward_kernel(np_, ns, x, ag, q, k, v, context_t, branch, hidden_grad, normed, gains_dec, gains_feed,
                    probs, wo, wq, wk, wv, wide, tall, dec, encoded,
                    red, small_out, dec_out, enc_out, grad_out,
                    wos, wqs, wks, wvs, d_out, dp, ds, dq_t, dq, dk, dv, k_t, normed_t, ng, in_grad,
                    pbuf, band, diag, own, au, r0, r1y, r1x, r1a, r2, r3, sm, smr, smz,
                    psem, wsem, loc, c_s, c_r, a_s, a_r, b_s, b_r, ac_s, ac_r, ax_s, ax_r, z_s, z_r,
                    m_s, m_r, mz_s, mz_r, d_s, d_r, e_s, e_r, g_s, g_r):
    n, width = x.shape
    heads = probs.shape[0]
    nz = np_ // 2
    rows, lanes = r0.shape[4:]
    count = np_ * ns
    p = lax.axis_index("pairs")
    s = lax.axis_index("seq")
    c = lax.rem(s, 2)
    y = s // 2
    xx = lax.rem(p, 2)
    z = p // 2
    me = p * ns + s
    core_peer = (p, s + 1 - 2 * c)
    y_peer = (p, lax.rem(s + 2, 4))
    x_peer = (p + 1 - 2 * xx, s)

    def place(d):
        lin = lax.rem(me + d, count)
        return (lin // ns, lax.rem(lin, ns))

    barrier = pltpu.get_barrier_semaphore()

    @pl.loop(1, count)
    def _(d):
        pl.semaphore_signal(barrier, inc=1, device_id=place(d), device_id_type=MESH)

    def remote(src, dst, send, recv, peer):
        return pltpu.make_async_remote_copy(
            src_ref=src, dst_ref=dst, send_sem=send, recv_sem=recv,
            device_id=peer, device_id_type=MESH)

    weights = [pltpu.make_async_copy(a, b, wsem.at[i])
               for i, (a, b) in enumerate(((wo, wos), (wq, wqs), (wk, wks), (wv, wvs)))]

    def fetch(h, slot):
        return pltpu.make_async_copy(probs.at[h], pbuf.at[slot], psem.at[slot])

    def unit(i, core):
        return (wide, tall)[i // 2].at[i % 2, core]

    def core_copy(i):
        return remote(unit(i, 1 - c), r0.at[i], c_s.at[i], c_r.at[i], core_peer)

    def own_copy(i):
        return pltpu.make_async_copy(unit(i, c), own.at[i], loc.at[i])

    def first(i):
        if i % 2 == 0:
            return remote(own.at[i, 1 - y], r1y.at[i // 2], a_s.at[i], a_r.at[i], y_peer)
        return remote(own.at[i, :, :, 1 - xx], r1x.at[i // 2], a_s.at[i], a_r.at[i], x_peer)

    def second(i):
        if i % 2 == 0:
            return remote(own.at[i, y, :, 1 - xx], r2.at[i], b_s.at[i], b_r.at[i], x_peer)
        return remote(own.at[i, 1 - y, :, xx], r2.at[i], b_s.at[i], b_r.at[i], y_peer)

    def final(i):
        return own.at[i, y] if i < 4 else au.at[i - 4, c, y]

    def last(i, d):
        t = lax.rem(z + d, nz)
        return remote(final(i).at[t, xx], r3.at[i, d], z_s.at[i, d], z_r.at[i, d], (t * 2 + xx, s))

    def attn_core(w, half):
        return remote(au.at[w, 1 - c, half], r0.at[4 + w, half], ac_s.at[w, half], ac_r.at[w, half], core_peer)

    def attn_x(w, half):
        return remote(au.at[w, c, half, :, 1 - xx], r1a.at[w, half], ax_s.at[w, half], ax_r.at[w, half], x_peer)

    def attn_y(w):
        return remote(au.at[w, c, 1 - y, :, xx], r2.at[4 + w], b_s.at[4 + w], b_r.at[4 + w], y_peer)

    def dec_copy(d):
        to = place(d)
        return remote(dec.at[to[0] * ns + to[1]], dec_out.at[me], d_s.at[d], d_r.at[d], to)

    def enc_copy(d):
        t = lax.rem(s + d, ns)
        return remote(encoded.at[t], enc_out.at[s], e_s.at[d], e_r.at[d], (p, t))

    def grad_copy(d):
        t = lax.rem(s + d, ns)
        return remote(in_grad.at[t], grad_out.at[s], g_s.at[d], g_r.at[d], (p, t))

    keep_dec = pltpu.make_async_copy(dec.at[me], dec_out.at[me], loc.at[4])
    keep_enc = pltpu.make_async_copy(encoded.at[s], enc_out.at[s], loc.at[5])
    keep_grad = pltpu.make_async_copy(in_grad.at[s], grad_out.at[s], loc.at[6])

    def step_a(i):
        core_copy(i).wait()
        own_copy(i).wait()

        @pl.loop(0, nz)
        def _(b):
            for a in range(2):
                for e in range(2):
                    own[i, a, b, e] = own[i, a, b, e] + r0[i, a, b, e]

        first(i).start()

    def step_b(i):
        first(i).wait()

        @pl.loop(0, nz)
        def _(b):
            for e in range(2):
                if i % 2 == 0:
                    own[i, y, b, e] = own[i, y, b, e] + r1y[i // 2, b, e]
                else:
                    own[i, e, b, xx] = own[i, e, b, xx] + r1x[i // 2, e, b]

        second(i).start()

    def step_c(i):
        if i < 4:
            second(i).wait()
        else:
            attn_y(i - 4).wait()

        @pl.loop(0, nz)
        def _(b):
            f = final(i)
            f[b, xx] = f[b, xx] + r2[i, b]

        @pl.loop(1, nz)
        def _(d):
            last(i, d).start()

    def step_d(i):
        red[i] = final(i)[z, xx].astype(F32)

        @pl.loop(1, nz)
        def _(d):
            last(i, d).wait()
            red[i] = red[i] + r3[i, d].astype(F32)

    def attn_a(w, half):
        attn_core(w, half).wait()

        @pl.loop(0, nz)
        def _(b):
            for e in range(2):
                au[w, c, half, b, e] = au[w, c, half, b, e] + r0[4 + w, half, b, e]

        attn_x(w, half).start()

    def attn_b(w, half):
        attn_x(w, half).wait()

        @pl.loop(0, nz)
        def _(b):
            au[w, c, half, b, xx] = au[w, c, half, b, xx] + r1a[w, half, b]

    for copy in weights:
        copy.start()
    first_half, last_half = 1 - y, y
    fetch(first_half * (heads // 2), 0).start()
    fetch(first_half * (heads // 2) + 1, 1).start()
    for i in range(4):
        own_copy(i).start()
    keep_dec.start()
    keep_enc.start()
    diag[...] = jnp.zeros_like(diag)
    weights[0].wait()

    @pl.loop(0, width // 384)
    def _(j):
        cols = pl.ds(pl.multiple_of(j * 384, 128), 384)
        d_out[:, cols] = mm_t(branch[...], wos[cols, :]).astype(BF)

    pl.semaphore_wait(barrier, count - 1)
    for i in range(4):
        core_copy(i).start()
    for d in range(1, ns):
        enc_copy(d).start()

    @pl.loop(1, count)
    def _(d):
        dec_copy(d).start()

    @pl.loop(0, n // 128)
    def _(i):
        r = pl.ds(pl.multiple_of(i * 128, 128), 128)
        normed_t[:, r] = normed[r].T

    lane = lax.broadcasted_iota(jnp.int32, (n, 128), 1)
    lane_s = lax.broadcasted_iota(jnp.int32, (128, 128), 1)
    row_s = lax.broadcasted_iota(jnp.int32, (128, 128), 0)

    def pair(half, g):
        cols = pl.ds(pl.multiple_of(half * (width // 2) + g * 128, 128), 128)
        k_t[...] = k[:, cols].T
        dop = d_out[:, cols]
        qp = q[:, cols]
        vp = v[:, cols]
        zero = jnp.zeros_like(qp)
        for a in range(2):
            h = half * (heads // 2) + 2 * g + a
            mine = (lane < 64) if a == 0 else (lane >= 64)
            dp[...] = mm_t(jnp.where(mine, vp, zero), dop)
            fetch(h, a).wait()
            for j in range(n // 128):
                pj = pbuf[a, :, j * 128:(j + 1) * 128].astype(F32)
                pd = pj * dp[:, j * 128:(j + 1) * 128]
                total = jnp.sum(pd, axis=0, keepdims=True)
                sg = pd - pj * total
                ds[:, j * 128:(j + 1) * 128] = sg.astype(BF)
                for i in range(n // 128):
                    t = sg[i * 128:(i + 1) * 128]
                    if abs(i - j) <= 1:
                        b = (i - j + 1) * 128
                        if j == 0 or (j == 1 and i == 0):
                            band[b:b + 128, :] = t
                        else:
                            band[b:b + 128, :] += t
                    else:
                        f = 5 if i > j else 4
                        diag[h, f:f + 1, :] += jnp.sum(t, axis=0, keepdims=True)
            dvp = mm(pbuf[a], jnp.where(mine, dop, zero))
            dkp = mm(ds[...], jnp.where(mine, qp, zero))
            dq_t[pl.ds(pl.multiple_of(h * 64, 64), 64), :] = mm(k_t[a * 64:(a + 1) * 64, :], ds[...]).astype(BF)
            if a == 0:
                dk_sum, dv_sum = dkp, dvp
            else:
                dk[:, cols] = (dk_sum + dkp).astype(BF)
                dv[:, cols] = (dv_sum + dvp).astype(BF)
            for b in range(3):
                t = band[b * 128:(b + 1) * 128, :]
                for bit in range(7):
                    t = jnp.where((row_s >> bit) % 2 == 1, pltpu.roll(t, 128 - (1 << bit), 1), t)
                straight = jnp.sum(jnp.where(lane_s + row_s < 128, t, 0.0), axis=0, keepdims=True)
                whole = jnp.sum(t, axis=0, keepdims=True)
                diag[h, b:b + 1, :] += straight
                diag[h, b + 1:b + 2, :] += whole - straight

    part = width // 4

    def units_of(half):
        cols = pl.ds(pl.multiple_of(half * (width // 2), 128), width // 2)
        lower = pl.ds(pl.multiple_of(half * (width // 2), 128), width // 2)
        dq_h = dq_t[lower, :].T
        dq[:, cols] = dq_h
        dk_h = dk[:, cols]
        dv_h = dv[:, cols]
        br_h = branch[:, cols]
        zero = jnp.zeros((n, part), BF)
        for cc in range(2):
            e = slice(cc * part, (cc + 1) * part)
            g = mm(normed_t[...], jnp.concatenate([dq_h[:, e], dk_h[:, e]], axis=1))
            au[0, cc, half] = g.astype(BF).reshape(nz, 2, rows, lanes)
            g = (mm(normed_t[...], jnp.concatenate([dv_h[:, e], zero], axis=1))
                 + mm(context_t[...], jnp.concatenate([zero, br_h[:, e]], axis=1)))
            au[1, cc, half] = g.astype(BF).reshape(nz, 2, rows, lanes)
        for w in range(2):
            attn_core(w, half).start()

    quarter = heads // 4

    @pl.loop(0, quarter)
    def _(g):
        pair(first_half, g)
        nxt = jnp.where(g == quarter - 1, last_half * (heads // 2), first_half * (heads // 2) + 2 * (g + 1))
        fetch(nxt, 0).start()
        fetch(nxt + 1, 1).start()

        @pl.when(g == 0)
        def _():
            step_a(0)
            step_a(1)

        @pl.when(g == 1)
        def _():
            step_a(2)
            step_a(3)

    units_of(first_half)

    @pl.loop(0, quarter)
    def _(g):
        pair(last_half, g)

        @pl.when(g < quarter - 1)
        def _():
            nxt = last_half * (heads // 2) + 2 * (g + 1)
            fetch(nxt, 0).start()
            fetch(nxt + 1, 1).start()

        @pl.when(g == 0)
        def _():
            attn_a(0, first_half)
            attn_a(1, first_half)

        @pl.when(g == 1)
        def _():
            step_b(0)
            step_b(1)

    units_of(last_half)
    for copy in weights[1:]:
        copy.wait()

    @pl.loop(0, 2)
    def _(i):
        r = pl.ds(pl.multiple_of(i * (n // 2), 128), n // 2)
        ng[r] = mm_t(dq[r], wqs[...]) + mm_t(dk[r], wks[...]) + mm_t(dv[r], wvs[...])

    attn_a(0, last_half)
    attn_a(1, last_half)
    sm[...] = jnp.zeros_like(sm)
    slot_rows = n // ns
    gain_sum = jnp.zeros((1, width), F32)
    for i in range(ns):
        r = slice(i * slot_rows, (i + 1) * slot_rows)
        t = x[r].astype(F32)
        down, gain = norm_down(t, rms_scale(t), ag[...], ng[r])
        in_grad[i] = (hidden_grad[r] + down).astype(BF)
        gain_sum = gain_sum + jnp.sum(gain, axis=0, keepdims=True)
    keep_grad.start()
    for d in range(1, ns):
        grad_copy(d).start()

    col = lax.broadcasted_iota(jnp.int32, (128, width), 1)
    offset = (col // 128 - 1) * 128 - lax.rem(col, 128)
    offset = jnp.where(col >= width - 128, 256, jnp.where(col >= width - 256, -256, offset))
    dist = jnp.abs(offset)
    bucket = jnp.full_like(dist, 8)
    for edge in EDGES:
        bucket = bucket + (dist >= edge).astype(jnp.int32)
    bucket = jnp.where(dist < 8, dist, bucket) + jnp.where(offset > 0, 16, 0)
    pick = jnp.where(bucket == lax.broadcasted_iota(jnp.int32, (128, width), 0), 1.0, 0.0)
    bias = jnp.zeros((16, 128), F32)
    for i in range(width // 128):
        bias = bias + lax.dot_general(diag[:, i, :], pick[:, i * 128:(i + 1) * 128], (((1,), (1,)), ((), ())),
                                      precision=HIGHEST, preferred_element_type=F32)
    sm[0, 40:56, :] = bias
    gains = [gains_dec[i:i + 1, :] for i in range(3)] + [gains_feed[i:i + 1, :] for i in range(2)] + [gain_sum]
    for i, gain in enumerate(gains):
        for j in range(width // 128):
            sm[0, i * 6 + j:i * 6 + j + 1, :] = gain[:, j * 128:(j + 1) * 128]

    def small_copy(i):
        return remote(sm.at[i], smr.at[i], m_s.at[i], m_r.at[i], (core_peer, y_peer, x_peer)[i])

    def z_small(d):
        return remote(smz.at[z], smz.at[z], mz_s.at[d], mz_r.at[d], (lax.rem(z + d, nz) * 2 + xx, s))

    small_copy(0).start()
    step_b(2)
    step_b(3)
    small_copy(0).wait()
    sm[1] = sm[0] + smr[0]
    small_copy(1).start()
    attn_b(0, first_half)
    attn_y(0).start()
    attn_b(1, first_half)
    attn_y(1).start()
    step_c(0)
    step_c(1)
    small_copy(1).wait()
    sm[2] = sm[1] + smr[1]
    small_copy(2).start()
    step_c(2)
    step_c(3)
    attn_b(0, last_half)
    small_copy(2).wait()
    smz[z] = sm[2] + smr[2]

    @pl.loop(1, nz)
    def _(d):
        z_small(d).start()

    step_c(4)
    attn_b(1, last_half)
    step_c(5)
    for i in range(6):
        step_d(i)

    @pl.loop(1, nz)
    def _(d):
        z_small(d).wait()

    small_out[...] = smz[0]

    @pl.loop(1, nz)
    def _(d):
        small_out[...] = small_out[...] + smz[d]

    keep_dec.wait()
    keep_enc.wait()
    keep_grad.wait()
    for d in range(1, ns):
        enc_copy(d).wait()
        grad_copy(d).wait()

    @pl.loop(1, count)
    def _(d):
        dec_copy(d).wait()


def backward(np_, ns, x, ag, q, k, v, context_t, branch, hidden_grad, normed, gains_dec, gains_feed,
             probs, wo, wq, wk, wv, wide, tall, dec, encoded):
    n, width = x.shape
    heads = probs.shape[0]
    nz = np_ // 2
    rows, lanes = wide.shape[5:]
    count = np_ * ns
    padded = normed.shape[1]
    vm = pl.BlockSpec(memory_space=pltpu.VMEM)
    hb = pl.BlockSpec(memory_space=pl.ANY)
    S = jax.ShapeDtypeStruct
    V = pltpu.VMEM
    dma = pltpu.SemaphoreType.DMA
    nar = V((n, width), BF)
    square = V((width, width), BF)
    slots = (ns, n // ns, width)
    small = (64, 128)
    return pl.pallas_call(
        functools.partial(backward_kernel, np_, ns),
        out_shape=(S((6, rows, lanes), F32), S(small, F32), S(dec.shape, BF), S(slots, BF), S(slots, BF)),
        in_specs=[vm] * 11 + [hb] * 9,
        out_specs=(vm, vm, hb, hb, hb),
        scratch_shapes=[
            square, square, square, square, nar, V((n, n), F32), V((n, n), BF), V((width, n), BF), nar, nar, nar,
            V((128, n), BF), V((padded, n), BF), V((n, width), F32), V(slots, BF),
            V((2, n, n), BF), V((384, 128), F32), V((16, 8, 128), F32),
            V((4, 2, nz, 2, rows, lanes), BF), V((2, 2, 2, nz, 2, rows, lanes), BF), V((6, 2, nz, 2, rows, lanes), BF),
            V((2, nz, 2, rows, lanes), BF), V((2, 2, nz, rows, lanes), BF), V((2, 2, nz, rows, lanes), BF),
            V((6, nz, rows, lanes), BF), V((6, nz, rows, lanes), BF),
            V((3,) + small, F32), V((3,) + small, F32), V((nz,) + small, F32),
            dma((2,)), dma((4,)), dma((7,)), dma((4,)), dma((4,)), dma((4,)), dma((4,)), dma((6,)), dma((6,)),
            dma((2, 2)), dma((2, 2)), dma((2, 2)), dma((2, 2)), dma((6, nz)), dma((6, nz)),
            dma((3,)), dma((3,)), dma((nz,)), dma((nz,)), dma((count,)), dma((count,)),
            dma((ns,)), dma((ns,)), dma((ns,)), dma((ns,)),
        ],
        compiler_params=pltpu.CompilerParams(
            collective_id=0, has_side_effects=True, vmem_limit_bytes=62 * 1024 * 1024),
        name="backward",
    )(x, ag.reshape(1, -1), q, k, v, context_t, branch, hidden_grad, normed, gains_dec, gains_feed,
      probs, wo, wq, wk, wv, wide, tall, dec, encoded.reshape(slots))


def two_kernels(
    np_, ns, r, rp, lanes, side, length, final_gain, expand_gain, attend_gain, dec_gains,
    rows_grad, block, cot, reduce_weight, active, expand_weight, hidden, slope, mixed_t,
    output_weight, query_weight, key_weight, value_weight, query, key, value, x, normed_t,
    context_t, probs, dec_all, encoded,
):
    seq_len, ff = active.shape
    nz = np_ // 2
    wide, tall, hidden_grad, branch, feed_gains = feed_back(
        1, length, rows_grad, block, cot, final_gain, hidden, expand_gain, mixed_t.T, active,
        slope, reduce_weight, expand_weight)

    def pad(unit):
        return jnp.pad(unit, ((0, 0),) * 5 + ((0, rp - r), (0, 0)))

    tall = tall.reshape(2, 2, 2, r, side, nz, 2, ff // np_).transpose(0, 1, 2, 5, 6, 3, 4, 7)
    tall = pad(tall.reshape(2, 2, 2, nz, 2, r, lanes))
    wide = pad(wide.reshape(2, 2, 2, nz, 2, r, lanes))
    gap = ((0, 0), (0, rp - r), (0, 0))
    normed_t = jnp.pad(normed_t.reshape(np_, r, seq_len), gap).reshape(np_ * rp, seq_len)
    context_t = jnp.pad(context_t.reshape(np_, r, seq_len), gap).reshape(np_ * rp, seq_len)
    return backward(
        np_, ns, x, attend_gain, query, key, value, context_t, branch, hidden_grad, normed_t.T,
        dec_gains, feed_gains, probs, output_weight, query_weight, key_weight, value_weight,
        wide, tall, dec_all, encoded)


def per_device(
    enc_input, dec_input, lengths, attend_gain, query_weight, key_weight, value_weight,
    output_weight, bias_table, expand_gain, expand_weight, reduce_weight, final_gain,
    self_gain, self_value, self_output, cross_gain, cross_query, cross_key, cross_value,
    cross_output, feed_gain, feed_expand, feed_reduce, enc_cotangent, dec_cotangent,
):
    group, local_rows, width = enc_input.shape
    buckets, heads = bias_table.shape
    size = width // heads
    ff = expand_weight.shape[1]
    ns = lax.axis_size("seq")
    np_ = lax.axis_size("pairs")
    r = width // np_
    aligned = np_ == 8 and r % 32 == 0 and (ff // np_) % 128 == 0 and ff == 4 * width
    seq_len = local_rows * ns
    weights = (query_weight, key_weight, value_weight, output_weight, expand_weight, reduce_weight,
               self_value, self_output, cross_query, cross_key, cross_value, cross_output,
               feed_expand, feed_reduce)
    (normed_t, query, key, value, probs, context_t, hidden, mixed_t, active, slope, block, encoded,
     x, cot, rows_grad, dec_block, dec_input_grad, dec_gains, *dec_rows) = forward(
        np_, ns, aligned, lengths, bias_table.T,
        (attend_gain, expand_gain, final_gain, self_gain, cross_gain, feed_gain),
        dec_input, dec_cotangent, enc_input, enc_cotangent, weights)
    x = x.reshape(seq_len, width)
    cot = cot.reshape(seq_len, width)
    if aligned:
        dec_all, = dec_rows
        red, small_sum, dec_got, enc_out, grad_out = fused(
            np_, ns, lengths, final_gain, expand_gain, attend_gain, dec_gains, rows_grad, block, cot,
            reduce_weight, active, expand_weight, hidden, slope, mixed_t, output_weight,
            query_weight, key_weight, value_weight, query, key, value, x, normed_t, context_t,
            probs, dec_all, encoded)
        (enc_out, grad_out, dec_block, dec_input_grad, grad_query, grad_key, grad_value, grad_output, grad_expand, grad_reduce,
         bias, *rest) = finish(
            heads, buckets, red, small_sum, dec_got, dec_block, dec_input_grad, enc_out, grad_out)
        gains = rest[:6]
        grad_sv, grad_so, grad_cq, grad_ck, grad_cv, grad_co, feed_in, feed_out = rest[6:]
        return (
            enc_out, dec_block, grad_out, dec_input_grad, gains[5], grad_query, grad_key,
            grad_value, grad_output, bias.T, gains[4], grad_expand, grad_reduce.T, gains[3],
            gains[0], grad_sv, grad_so, gains[1], grad_cq, grad_ck, grad_cv, grad_co, gains[2],
            feed_in, feed_out.T,
        )
    left, right, wide_rows, mids = dec_rows
    length = lax.dynamic_slice_in_dim(lengths, lax.axis_index("seq"), 1)
    rp = -(-r // 16) * 16
    lanes = ff // 8
    side = width // 8 // r
    cols = width // ns

    left_cut = jnp.concatenate([
        left.reshape(5, np_, r).transpose(1, 0, 2).reshape(np_, 5 * r),
        wide_rows[0].reshape(np_, 4 * r),
    ], axis=1)
    mid_cut = mids.reshape(2, ns, heads // ns, np_, r).transpose(3, 1, 0, 2, 4)
    mid_cut = mid_cut.reshape(np_, ns, 6 * r)
    right_cut = jnp.concatenate([
        right.reshape(7, ns, cols).transpose(1, 0, 2).reshape(ns, 7 * cols),
        wide_rows[1].reshape(ns, 4 * cols)], axis=1)
    dec_all = jnp.concatenate([
        jnp.broadcast_to(left_cut[:, None], (np_, ns, 9 * r)), mid_cut,
        jnp.broadcast_to(right_cut[None], (np_, ns, 11 * cols))], axis=-1)
    dec_all = dec_all.astype(BF).reshape(np_ * ns, -1)
    used = dec_all.shape[1]
    dec_rows = -(-used // 2048) * 16
    dec_all = jnp.pad(dec_all, ((0, 0), (0, dec_rows * 128 - used)))
    dec_all = dec_all.reshape(np_ * ns, dec_rows, 128)

    red, small_sum, dec_got, enc_out, grad_out = two_kernels(
        np_, ns, r, rp, lanes, side, length, final_gain, expand_gain, attend_gain, dec_gains,
        rows_grad, block, cot, reduce_weight, active, expand_weight, hidden, slope, mixed_t,
        output_weight, query_weight, key_weight, value_weight, query, key, value, x, normed_t,
        context_t, probs, dec_all, encoded)

    got = dec_got.reshape(np_ * ns, -1)
    lefts = got[:, :9 * r].reshape(-1, 9, r)
    mid_got = got[:, 9 * r:15 * r].reshape(-1, 2, 3, r)
    rights = got[:, 15 * r:15 * r + 11 * cols].reshape(-1, 11, cols)
    plain = jnp.einsum("nkr,nkc->krc", lefts[:, :4], rights[:, :4], preferred_element_type=F32)
    crossed = jnp.einsum("nkhr,nkhd->krhd", mid_got, rights[:, 4:6].reshape(-1, 2, 3, size),
                         preferred_element_type=F32).reshape(2, r, cols)
    feed_in = jnp.einsum("nr,nc->rc", lefts[:, 4], rights[:, 7:11].reshape(-1, 4 * cols),
                         preferred_element_type=F32)
    feed_out = jnp.einsum("nr,nc->rc", lefts[:, 5:9].reshape(-1, 4 * r), rights[:, 6],
                          preferred_element_type=F32)
    red = red[:, :r]
    grad_reduce = red[2:4].reshape(2, r, side, ff // np_).reshape(cols, ff // np_).T
    gains = small_sum[:36].reshape(6, width)
    bias = small_sum[40:40 + heads, :buckets].T
    return (
        enc_out, dec_block, grad_out, dec_input_grad,
        gains[5],
        red[4][:, :cols], red[4][:, cols:], red[5][:, :cols], red[5][:, cols:],
        bias,
        gains[4],
        jnp.concatenate([red[0], red[1]], axis=1), grad_reduce,
        gains[3],
        gains[0], plain[0], plain[1],
        gains[1], plain[2], crossed[0], crossed[1], plain[3],
        gains[2], feed_in, feed_out,
    )


def solution(mesh):
    rows = P("pairs", "seq", None)
    single = P(("pairs", "seq"), None)
    block = P("pairs", "seq")
    return jax.shard_map(
        per_device,
        mesh=mesh,
        in_specs=(rows, single, P("pairs")) + (P(),) * 21 + (rows, single),
        out_specs=(
            rows, single, rows, single,
            P(), block, block, block, block, P(), P(), block, block, P(),
            P(), block, block, P(), block, block, block, block, P(), block, block,
        ),
        check_vma=False,
    )
```

```python
import functools
import itertools

import jax
import jax.numpy as jnp
from jax import lax
from jax.experimental import pallas as pl
from jax.experimental.pallas import tpu as pltpu
from jax.sharding import PartitionSpec as P

EPSILON = 1e-06
EDGES = (12, 16, 23, 32, 46, 64, 91)
HIGHEST = lax.Precision.HIGHEST
MESH = pl.DeviceIdType.MESH
BF = jnp.bfloat16
F32 = jnp.float32


def mm(a, b):
    return jnp.dot(a, b, preferred_element_type=F32)
def mm_t(a, b):
    return lax.dot_general(a, b, (((1,), (1,)), ((), ())), preferred_element_type=F32)
def t_mm(a, b):
    return lax.dot_general(a, b, (((0,), (0,)), ((), ())), preferred_element_type=F32)

def rms_scale(v):
    return lax.rsqrt(jnp.mean(v * v, axis=-1, keepdims=True) + EPSILON)

def gelu_parts(u):
    u2 = u * u
    t = jnp.tanh(u * (0.7978845608 + (0.7978845608 * 0.044715) * u2))
    half = 0.5 + 0.5 * t
    return u * half, half + half * (1.0 - t) * u * (0.7978845608 + (3 * 0.7978845608 * 0.044715) * u2)

def norm_down(v, r, g, dy):
    vr = v * r
    gd = g * dy
    return r * (gd - vr * jnp.mean(vr * gd, axis=-1, keepdims=True)), vr * dy

def diagonal_buckets(shape, width):
    col = lax.broadcasted_iota(jnp.int32, shape, 1)
    offset = (col // 128 - 1) * 128 - lax.rem(col, 128)
    offset = jnp.where(col >= width - 128, 256, jnp.where(col >= width - 256, -256, offset))
    dist = jnp.abs(offset)
    bucket = jnp.full_like(dist, 8)
    for edge in EDGES:
        bucket = bucket + (dist >= edge).astype(jnp.int32)
    bucket = jnp.where(dist < 8, dist, bucket) + jnp.where(offset > 0, 16, 0)
    return jnp.where(bucket == lax.broadcasted_iota(jnp.int32, shape, 0), 1.0, 0.0)


def forward_kernel(np_, ns, cut, lengths, table, ag, eg, fg, sg, cg, dg, dec_in, dec_cot, enc_in, enc_cot,
                   wq, wk, wv, wo, we, wr, sv, so, cq, ck, cv, co, fe, fr,
                   normed_t, q, k, v, probs, context_t, hidden, mixed_t, active, slope, block, low, x_out, cot_out,
                   rows_grad, dec_out, dec_in_grad, dec_gains, *rest):
    if cut:
        dec, *rest = rest
    else:
        left, right, wide, mids, *rest = rest
    (wqs, wks, wvs, wos, wes, wrs, svs, sos, cqs, cks, cvs, cos, fes, frs, xs, normed, nt, qs, ks, vs, ctx, hid,
     mixed, mt, act, slo, blk, rws, lws, rgs, band, vecs, v_t, s_t, pbuf, *rest) = rest
    if cut:
        left, right, wide, mids, cuts, both, *rest = rest
    sems, psem, osem, x_s, x_r, c_s, c_r, loc = rest
    ag, eg, fg, sg, cg, dg = (g[...].reshape(1, -1) for g in (ag, eg, fg, sg, cg, dg))
    n, width = normed.shape
    heads = probs.shape[0]
    size = width // heads
    ff = act.shape[1]
    slot = n // ns
    p = lax.axis_index("pairs")
    s = lax.axis_index("seq")
    length = lengths[s]

    barrier = pltpu.get_barrier_semaphore()
    for d in range(1, ns):
        pl.semaphore_signal(barrier, inc=1, device_id=(p, lax.rem(s + d, ns)), device_id_type=MESH)

    def rows_copy(src, dst, send, recv, d):
        t = lax.rem(s + d, ns)
        return pltpu.make_async_remote_copy(
            src_ref=src.at[t], dst_ref=dst.at[s], send_sem=send.at[d], recv_sem=recv.at[d],
            device_id=(p, t), device_id_type=MESH)

    x_copies = [rows_copy(enc_in, xs, x_s, x_r, d) for d in range(1, ns)]
    cot_copies = [rows_copy(enc_cot, cot_out, c_s, c_r, d) for d in range(1, ns)]
    keep_x = pltpu.make_async_copy(enc_in.at[s], xs.at[s], loc.at[0])
    keep_cot = pltpu.make_async_copy(enc_cot.at[s], cot_out.at[s], loc.at[1])
    keep_x.start()
    load = []
    for src, dst in ((sv, svs), (so, sos), (cq, cqs), (ck, cks), (fr, frs), (wq, wqs), (wk, wks), (wv, wvs),
                     (wo, wos), (we, wes), (wr, wrs), (cv, cvs), (co, cos), (fe, fes)):
        load.append(pltpu.make_async_copy(src, dst, sems.at[len(load)]))
        load[-1].start()
    pl.semaphore_wait(barrier, ns - 1)
    for copy in x_copies + cot_copies:
        copy.start()
    keep_cot.start()
    saved = []

    def save(src, dst):
        copy = pltpu.make_async_copy(src, dst, osem.at[len(saved)])
        saved.append(copy)
        copy.start()

    vec = lax.dot_general(table[...], diagonal_buckets((table.shape[1], width), width), (((1,), (0,)), ((), ())),
                          precision=HIGHEST, preferred_element_type=F32)
    for i in range(width // 128):
        vecs[:, i, :] = vec[:, i * 128:(i + 1) * 128]
    lane_s = lax.broadcasted_iota(jnp.int32, (128, 128), 1)
    row_s = lax.broadcasted_iota(jnp.int32, (128, 128), 0)

    @pl.loop(0, heads)
    def _(h):
        for b in range(3):
            t = jnp.where(lane_s + row_s < 128, vecs[h, b:b + 1, :], vecs[h, b + 1:b + 2, :])
            for bit in range(7):
                t = jnp.where((row_s >> bit) % 2 == 1, pltpu.roll(t, 1 << bit, 1), t)
            band[h, b * 128:(b + 1) * 128, :] = t

    x = dec_in[...].astype(F32)
    cot = dec_cot[...]
    own = (lax.broadcasted_iota(jnp.int32, (heads, width), 1) // size
           == lax.broadcasted_iota(jnp.int32, (heads, width), 0))

    def spread(r):
        return jnp.where(own, r.astype(F32), 0.0).astype(BF)

    def collect(r):
        return jnp.sum(jnp.where(own, r, 0.0), axis=0, keepdims=True)

    x_r = rms_scale(x)
    self_normed = (x * x_r * sg).astype(BF)
    load[0].wait()
    self_values = mm(self_normed, svs[...]).astype(BF)
    load[1].wait()
    after = x + mm(self_values, sos[...])
    after_r = rms_scale(after)
    cross_normed = (after * after_r * cg).astype(BF)
    load[2].wait()
    cross_q = mm(cross_normed, cqs[...]).astype(BF)
    load[3].wait()
    q_rows = mm_t(spread(cross_q), cks[...]).astype(BF)
    load[4].wait()
    active_back = mm_t(cot, frs[...])

    keep_x.wait()
    for copy in x_copies:
        copy.wait()
    save(xs, x_out)
    for i in range(ns):
        r = slice(i * slot, (i + 1) * slot)
        t = xs[i].astype(F32)
        t = t * rms_scale(t) * ag
        normed[r] = t.astype(BF)
        nt[:, r] = t.T.astype(BF)
    save(nt, normed_t)
    for j, (w, out, dst) in enumerate(((wqs, qs, q), (wks, ks, k), (wvs, vs, v))):
        load[5 + j].wait()
        for i in range(2):
            r = slice(i * (n // 2), (i + 1) * (n // 2))
            out[r] = mm(normed[r], w[...]).astype(BF)
        save(out, dst)

    lane = lax.broadcasted_iota(jnp.int32, (n, 128), 1)
    row = lax.broadcasted_iota(jnp.int32, (n, 128), 0)
    q_mark = jnp.where(lane == 0, 1.0, 0.0).astype(BF)
    k_mark = jnp.where((lane == 0) & (row >= length), -1e30, 0.0).astype(BF)

    def keep(h, a):
        return pltpu.make_async_copy(pbuf.at[a], probs.at[h], psem.at[a])

    @pl.loop(0, heads // 2)
    def _(g):
        cols = pl.ds(pl.multiple_of(g * 128, 128), 128)
        v_t[...] = vs[:, cols].T
        qq = jnp.concatenate([qs[:, cols], q_mark], axis=1)
        kp = ks[:, cols]
        for a in range(2):
            h = 2 * g + a
            mine = (lane < 64) if a == 0 else (lane >= 64)
            kk = jnp.concatenate([jnp.where(mine, kp, jnp.zeros_like(kp)), k_mark], axis=1)
            s_t[a] = mm_t(kk, qq)

            @pl.when(g > 0)
            def _():
                keep(h - 2, a).wait()

            for j in range(n // 128):
                tile = []
                for i in range(n // 128):
                    t = s_t[a, i * 128:(i + 1) * 128, j * 128:(j + 1) * 128]
                    if abs(i - j) <= 1:
                        t = t + band[h, (i - j + 1) * 128:(i - j + 2) * 128, :]
                    else:
                        f = 5 if i > j else 4
                        t = t + vecs[h, f:f + 1, :]
                    tile.append(t)
                t = jnp.concatenate(tile, axis=0)
                m = jnp.max(t, axis=0, keepdims=True)
                e = jnp.exp(t - m)
                total = jnp.sum(e, axis=0, keepdims=True)
                pbuf[a, :, j * 128:(j + 1) * 128] = (e * (1.0 / total)).astype(BF)
            ctx[pl.ds(pl.multiple_of(h * 64, 64), 64), :] = mm(v_t[a * 64:(a + 1) * 64, :], pbuf[a]).astype(BF)
            keep(h, a).start()

    save(ctx, context_t)
    load[8].wait()
    for i in range(ns):
        r = slice(i * slot, (i + 1) * slot)
        t = xs[i].astype(F32) + mm(ctx[:, r].T, wos[...])
        hid[r] = t
        t = t * rms_scale(t) * eg
        mixed[r] = t.astype(BF)
        mt[:, r] = t.T.astype(BF)
    save(hid, hidden)
    save(mt, mixed_t)
    load[9].wait()

    @pl.loop(0, ff // 512)
    def _(j):
        cols = pl.ds(pl.multiple_of(j * 512, 512), 512)
        a, b = gelu_parts(mm(mixed[...], wes[:, cols]))
        act[:, cols] = a.astype(BF)
        slo[:, cols] = b.astype(BF)

    save(act, active)
    save(slo, slope)
    load[10].wait()
    for i in range(2):
        r = slice(i * (n // 2), (i + 1) * (n // 2))
        alive = (lax.broadcasted_iota(jnp.int32, (n // 2, 1), 0) + i * (n // 2) < length).astype(F32)
        b = alive * (hid[r] + mm(act[r], wrs[...]))
        blk[r] = b
        lws[r] = b.astype(BF)
        rws[r] = (b * rms_scale(b) * fg).astype(BF)
    save(blk, block)
    save(lws, low)

    score = mm_t(q_rows, rws[...])
    score = jnp.where(lax.broadcasted_iota(jnp.int32, score.shape, 1) < length, score, -1e30)
    e = jnp.exp(score - jnp.max(score, axis=-1, keepdims=True))
    cross_probs = e / jnp.sum(e, axis=-1, keepdims=True)
    cross_low = cross_probs.astype(BF)
    mean_rows = mm(cross_low, rws[...]).astype(BF)
    for copy in load[11:]:
        copy.wait()
    cross_context = collect(mm(mean_rows, cvs[...])).astype(BF)
    middle = after + mm(cross_context, cos[...])
    middle_r = rms_scale(middle)
    feed_normed = (middle * middle_r * dg).astype(BF)
    dec_active, dec_slope = gelu_parts(mm(feed_normed, fes[...]))
    dec_active = dec_active.astype(BF)
    upper_grad = (dec_slope * active_back).astype(BF)
    middle_down, feed_gain = norm_down(middle, middle_r, dg, mm_t(upper_grad, fes[...]))
    middle_grad = cot.astype(F32) + middle_down
    cross_branch = middle_grad.astype(BF)
    context_grad = mm_t(cross_branch, cos[...]).astype(BF)
    g_rows = mm_t(spread(context_grad), cvs[...]).astype(BF)
    prob_grad = mm_t(g_rows, rws[...])
    score_grad = (cross_probs * (prob_grad - jnp.sum(cross_probs * prob_grad, axis=-1, keepdims=True))).astype(BF)
    pad = jnp.zeros((16 - heads % 16, n), BF)
    padw = jnp.zeros((16 - heads % 16, width), BF)
    rgs[...] = t_mm(jnp.concatenate([score_grad, pad, cross_low, pad], axis=0),
                    jnp.concatenate([q_rows, padw, g_rows, padw], axis=0)).astype(BF)
    save(rgs, rows_grad)
    score_rows = mm(score_grad, rws[...]).astype(BF)
    cross_q_grad = collect(mm(score_rows, cks[...])).astype(BF)
    after_down, cross_gain = norm_down(after, after_r, cg, mm_t(cross_q_grad, cqs[...]))
    after_grad = middle_grad + after_down
    self_branch = after_grad.astype(BF)
    self_values_grad = mm_t(self_branch, sos[...]).astype(BF)
    x_down, self_gain = norm_down(x, x_r, sg, mm_t(self_values_grad, svs[...]))
    dec_in_grad[...] = (after_grad + x_down).astype(BF)
    dec_out[...] = (middle + mm(dec_active, frs[...])).astype(BF)
    gains = dec_gains
    gains[0:1, :] = self_gain
    gains[1:2, :] = cross_gain
    gains[2:3, :] = feed_gain
    for i, r in enumerate((self_normed, self_values, cross_normed, cross_context, feed_normed)):
        left[i:i + 1, :] = r.astype(F32)
    for i, r in enumerate((self_values_grad, self_branch, cross_q_grad, cross_branch, cross_q, context_grad, cot)):
        right[i:i + 1, :] = r.astype(F32)
    wide[0:1, :] = dec_active.astype(F32)
    wide[1:2, :] = upper_grad.astype(F32)
    mids[0] = score_rows.astype(F32)
    mids[1] = mean_rows.astype(F32)
    if cut:
        rows, cols, step = width // np_, width // ns, heads // ns
        both[...] = jnp.zeros_like(both)
        cuts[...] = jnp.zeros_like(cuts)
        for j in range(ns):
            for i in range(7):
                t = right[i:i + 1, j * cols:(j + 1) * cols]
                both[j, 2 * i:2 * i + 1, :] = t[:, :128]
                both[j, 2 * i + 1:2 * i + 2, 0:cols - 128] = t[:, 128:]
            for i in range(6):
                lo = j * width + i * 128
                both[j, 14 + i:15 + i, :] = wide[1:2, lo:lo + 128]
        for i in range(np_):
            cuts[0:5, 0:rows] = left[0:5, i * rows:(i + 1) * rows]
            for a in range(3):
                lo = i * (ff // np_) + a * 128
                cuts[5 + a:6 + a, :] = wide[0:1, lo:lo + 128]
            for j in range(ns):
                for w in range(2):
                    cuts[8 + w * step:8 + (w + 1) * step, 0:rows] = (
                        mids[w, j * step:(j + 1) * step, i * rows:(i + 1) * rows])
                dec[i * ns + j, 0:16, :] = cuts[...].astype(BF)
                dec[i * ns + j, 16:48, :] = both[j].astype(BF)
    for a in range(2):
        keep(heads - 2 + a, a).wait()
    keep_cot.wait()
    for copy in cot_copies:
        copy.wait()
    for copy in saved:
        copy.wait()


def forward(np_, ns, cut, lengths, table, gains, dec_in, dec_cot, enc_in, enc_cot, weights):
    group, slot, width = enc_in.shape
    n = slot * ns
    ff = weights[4].shape[1]
    heads = table.shape[0]
    smem = pl.BlockSpec(memory_space=pltpu.SMEM)
    vm = pl.BlockSpec(memory_space=pltpu.VMEM)
    hb = pl.BlockSpec(memory_space=pl.ANY)
    S = jax.ShapeDtypeStruct
    V = pltpu.VMEM
    full, tall, floats, broad = ((n, width), BF), ((width, n), BF), ((n, width), F32), ((n, ff), BF)
    slots = ((ns, slot, width), BF)
    raw = [((5, width), F32), ((7, width), F32), ((2, ff), F32), ((2, heads, width), F32)]
    outs = [tall, full, full, full, ((heads, n, n), BF), tall, floats, tall, broad, broad, floats, full, slots, slots,
            full, ((1, width), BF), ((1, width), BF), ((3, width), F32)]
    outs += [((np_ * ns, 48, 128), BF)] if cut else raw
    scratch = [slots, full, tall, full, full, full, tall, floats, full, tall, broad, broad, floats, full, full, full,
               ((heads, 384, 128), F32), ((heads, 8, 128), F32), ((128, n), BF), ((2, n, n), F32), ((2, n, n), BF)]
    scratch += raw + [((16, 128), F32), ((ns, 32, 128), F32)] if cut else []
    dma = pltpu.SemaphoreType.DMA
    return pl.pallas_call(
        functools.partial(forward_kernel, np_, ns, cut),
        out_shape=tuple(S(*t) for t in outs),
        in_specs=[smem] + [vm] * 9 + [hb] * 16,
        out_specs=(hb,) * 15 + (vm,) * (len(outs) - 15),
        scratch_shapes=[V(w.shape, BF) for w in weights] + [V(*t) for t in scratch] + [
            dma((14,)), dma((2,)), dma((16,)), dma((ns,)), dma((ns,)), dma((ns,)), dma((ns,)), dma((2,))],
        compiler_params=pltpu.CompilerParams(
            collective_id=1, has_side_effects=True, vmem_limit_bytes=62 * 1024 * 1024),
        name="forward",
    )(lengths, table, *gains, dec_in, dec_cot, enc_in, enc_cot, *weights)


def finish_kernel(heads, red, small, dec, dec_row, dec_grad, enc, grad, *outs):
    (enc_out, grad_out, row_out, row_grad_out, qo, ko, vo, oo, expand, reduce, bias, g0, g1, g2, g3, g4, g5,
     sv, so, cq, ck, cv, co, fe, fr, wide) = outs
    enc_out[...] = enc[...]
    grad_out[...] = grad[...]
    row_out[...] = dec_row[...]
    row_grad_out[...] = dec_grad[...]
    wide[...] = dec[...].astype(F32)
    rows, cols = qo.shape
    lanes = red.shape[2]
    for i, out in ((4, (qo, ko)), (5, (vo, oo))):
        t = red[i]
        out[0][...] = t[:, :cols]
        out[1][...] = t[:, cols:]
    for i in range(2):
        expand[:, i * lanes:(i + 1) * lanes] = red[i]
        reduce[i * rows:(i + 1) * rows, :] = red[2 + i]
    bias[...] = small[40:40 + heads, 0:bias.shape[1]]
    for i, out in enumerate((g0, g1, g2, g3, g4, g5)):
        for j in range(6):
            out[pl.ds(j * 128, 128)] = small[i * 6 + j, :]

    def row(i):
        return wide[:, i, :]

    def pair(i):
        return jnp.concatenate([row(16 + 2 * i), row(17 + 2 * i)], axis=1)[:, :cols].astype(BF)

    for i, out in enumerate((sv, so, cq, co)):
        out[...] = t_mm(row(i)[:, :rows].astype(BF), pair(i))
    upper = jnp.concatenate([row(30 + i) for i in range(6)], axis=1).astype(BF)
    fe[...] = t_mm(row(4)[:, :rows].astype(BF), upper)
    active = jnp.concatenate([row(5 + i) for i in range(3)], axis=1).astype(BF)
    fr[...] = t_mm(pair(6), active)
    step = cols // 64
    for w, out in enumerate((ck, cv)):
        g = pair(4 + w)
        out[...] = jnp.concatenate(
            [t_mm(row(8 + w * step + h)[:, :rows].astype(BF), g[:, h * 64:(h + 1) * 64]) for h in range(step)], axis=1)


def finish(heads, buckets, red, small, dec, dec_row, dec_grad, enc, grad):
    rows, lanes = red.shape[1:]
    cols, width = lanes // 2, 2 * lanes
    vm = pl.BlockSpec(memory_space=pltpu.VMEM)
    S = jax.ShapeDtypeStruct
    block, broad, tall = S((rows, cols), F32), S((rows, width), F32), S((cols, lanes), F32)
    return pl.pallas_call(
        functools.partial(finish_kernel, heads),
        out_shape=(S(enc.shape, BF), S(grad.shape, BF), S(dec_row.shape, BF), S(dec_grad.shape, BF), block, block, block, block, broad, tall,
                   S((heads, buckets), F32)) + (S((width,), F32),) * 6 + (block,) * 6 + (broad, tall),
        in_specs=[vm] * 7,
        out_specs=(vm,) * 25,
        scratch_shapes=[pltpu.VMEM(dec.shape, F32)],
        compiler_params=pltpu.CompilerParams(vmem_limit_bytes=62 * 1024 * 1024),
        name="finish",
    )(red, small, dec, dec_row, dec_grad, enc, grad)


PARTS = 2
ORDERS = {
    "t00": "xfny",
    "t10": "fnyx",
    "t01": "nyfx",
    "t11": "yxfn",
    "w00": "nyfx",
    "w10": "yxfn",
    "w01": "xyfn",
    "w11": "ynxf",
    "a0": "xyfn",
    "a1": "xnyf",
}
SCHEDULE = {
    "wide": (
        ("t00", 0), ("t10", 0), ("t01", 0), ("t11", 0),
    ),
    "rows": (
        ("w00", 0),
    ),
    "dout": (
        ("w10", 0), ("w01", 0),
    ),
    "p00": (
        ("w11", 0), ("t00", 1),
    ),
    "p01": (
        ("t11", 1),
    ),
    "q0": (
        ("t01", 1), ("t10", 1), ("w01", 1), ("w10", 1),
    ),
    "p10": (
        ("t11", 2), ("h00", 0),
    ),
    "p11": (
        ("h01", 0), ("w00", 1), ("w10", 2), ("w11", 1),
    ),
    "p12": (
        ("t01", 2),
    ),
    "v1": (
        ("t00", 2), ("t10", 2), ("w01", 2), ("h00", 1),
    ),
    "ng1": (
        ("h10", 0), ("t11", 3),
    ),
    "end": (
        ("w00", 2), ("h11", 0), ("t10", 3), ("w10", 3), ("w11", 2), ("h01", 1),
        ("t00", 3), ("t01", 3), ("t11", 4), ("w01", 3), ("h10", 1), ("w10", 4),
        ("w00", 3), ("h01", 2), ("w01", 4), ("h11", 1), ("t00", 4), ("t10", 4),
        ("w11", 3), ("t01", 4), ("w00", 4), ("h10", 2), ("h11", 2), ("w11", 4),
        ("h10", 3), ("h11", 3),
    ),
}
HOPS = (1, 3, 5)


def ff_pieces():
    names = [kind + str(unit) + str(i) for kind in "tw" for i in range(PARTS) for unit in range(2)]
    return names + ["h" + str(half) + str(w) for half in range(2) for w in range(2)]


def fused_kernel(np_, ns, length, fg, eg, ag, gains_dec,
                 rows_grad, block, cot, wr, active, wide_w, hidden, slope, mixed_t_in, wo, wq, wk, wv, q_in, k_in,
                 v_in, x_in, normed_t_in, context_t_in, probs, dec, encoded,
                 red, small_out, dec_out, enc_out, grad_out,
                 acts, grads, w1, wes, bg, hid, dm, rg, ct, rb, rb_t, mixed_t, normed_t, context_t,
                 dp, ds, pbuf, k_t, band, diag, fu, r0, r0a, r1, r2, r3, r4, a1, a2, a3, over0, over1,
                 sm, smr, smz,
                 psem, isem, loc, f_s, f_r, t_s, t_r, o_s, o_r,
                 m_s, m_r, mz_s, mz_r, d_s, d_r, e_s, e_r, g_s, g_r):
    n, width = hid.shape
    ff = acts.shape[1]
    fg, eg, ag = (g[...].reshape(1, -1) for g in (fg, eg, ag))
    heads = probs.shape[0]
    nz = np_ // 2
    pieces = ff_pieces()
    rows, lanes = fu.shape[6:]
    step_rows = rows // PARTS
    count = np_ * ns
    p = lax.axis_index("pairs")
    s = lax.axis_index("seq")
    c = lax.rem(s, 2)
    y = s // 2
    xx = lax.rem(p, 2)
    z = p // 2
    me = p * ns + s
    core_peer = (p, s + 1 - 2 * c)
    y_peer = (p, lax.rem(s + 2, 4))
    x_peer = (p + 1 - 2 * xx, s)
    first_half, last_half = 1 - y, y
    own_at = {"x": xx, "y": y, "n": lax.rem(z, 2), "f": z // 2}
    peers = {"x": x_peer, "y": y_peer, "n": ((z + 1 - 2 * own_at["n"]) * 2 + xx, s),
             "f": (lax.rem(z + 2, 4) * 2 + xx, s)}

    def place(d):
        lin = lax.rem(me + d, count)
        return (lin // ns, lax.rem(lin, ns))

    barrier = pltpu.get_barrier_semaphore()

    @pl.loop(1, count)
    def _(d):
        pl.semaphore_signal(barrier, inc=1, device_id=place(d), device_id_type=MESH)

    def remote(src, dst, send, recv, peer):
        return pltpu.make_async_remote_copy(
            src_ref=src, dst_ref=dst, send_sem=send, recv_sem=recv,
            device_id=peer, device_id_type=MESH)

    def load(i, src, dst):
        return pltpu.make_async_copy(src, dst, isem.at[i])

    def part_of(ref, i):
        return ref.at[:, pl.ds(i * width, width)]

    loads = [load(i, a, b) for i, (a, b) in enumerate((
        (rows_grad, rg), (block, bg), (cot, ct), (active, acts), (wr, w1), (slope, grads), (mixed_t_in, mixed_t),
        (wide_w, wes), (hidden, hid), (normed_t_in, normed_t), (context_t_in, context_t)))]
    weights = [load(11 + i, a, w1.at[pl.ds(i * width, width)]) for i, a in enumerate((wo, wq, wk, wv))]
    heads_in = [load(15 + i, a, part_of(grads, i)) for i, a in enumerate((q_in, k_in, v_in, x_in))]
    d_out, dq, dk, dv = (part_of(acts, i) for i in range(4))
    q, k, v, x = (part_of(grads, i) for i in range(4))
    branch, dq_t, ng, in_grad, hidden_grad = ct, rb_t, dm, rg, bg
    wos, wqs, wks, wvs = (w1.at[pl.ds(i * width, width)] for i in range(4))

    def fetch(h, slot):
        return pltpu.make_async_copy(probs.at[h], pbuf.at[slot], psem.at[slot])

    def view(ref, dims, fixed):
        return ref.at[tuple(fixed.get(dim, slice(None)) for dim in dims)]

    def accumulate(dst, src, depth):
        for at in itertools.product(range(2), repeat=depth):
            dst[at] = dst[at] + src[at]

    def au(w, core, half):
        return fu.at[1 - c, 2 * w + core, half]

    def region(name, core):
        if name[0] == "h":
            return au(int(name[2]), core, first_half if name[1] == "0" else last_half), "fnx"
        unit = (2 if name[0] == "t" else 0) + int(name[1])
        return fu.at[core, unit, :, :, :, :, pl.ds(int(name[2]) * step_rows, step_rows)], "yfnx"

    def order_of(name):
        if name[0] != "h":
            return ORDERS[name]
        order = ORDERS["a" + name[2]]
        return order[:order.index("y")] if name[1] == "0" else order.replace("y", "")

    def core_copy(name):
        i = pieces.index(name)
        src, _ = region(name, 1 - c)
        dst = r0a.at[i - len(pieces) + 4] if name[0] == "h" else r0.at[i]
        return remote(src, dst, f_s.at[i], f_r.at[i], core_peer)

    def landing(name, j):
        i = pieces.index(name)
        if name[0] == "h":
            return (a1, a2, a3)[j].at[i - len(pieces) + 4]
        return (r1, r2, r3, r4)[j].at[i]

    def remaining(name, j):
        ref, dims = region(name, c)
        return ref, dims, {letter: own_at[letter] for letter in order_of(name)[:j]}

    def stage_copy(name, j):
        ref, dims, fixed = remaining(name, j)
        letter = order_of(name)[j]
        i = pieces.index(name)
        src = view(ref, dims, {**fixed, letter: 1 - own_at[letter]})
        return remote(src, landing(name, j), t_s.at[i, j], t_r.at[i, j], peers[letter])

    def hand_over(w):
        name = "h0" + str(w)
        ref, dims, fixed = remaining(name, len(order_of(name)))
        return remote(view(ref, dims, fixed), (over0, over1)[w], o_s.at[w], o_r.at[w], y_peer)

    def total_of(name):
        unit = 4 + int(name[2]) if name[0] == "h" else (2 if name[0] == "t" else 0) + int(name[1])
        if name[0] == "h":
            return red.at[unit]
        return red.at[unit, pl.ds(int(name[2]) * step_rows, step_rows)]

    def step(name, j):
        order = order_of(name)
        ref, dims, fixed = remaining(name, j)
        mine = view(ref, dims, fixed)
        depth = len(dims) - j
        closing = j == len(order) and name[:2] != "h0"
        joins = name[:2] == "h1" and ORDERS["a" + name[2]].index("y") == j
        if j == 0:
            core_copy(name).wait()
            landed = r0a.at[pieces.index(name) - len(pieces) + 4] if name[0] == "h" else r0.at[pieces.index(name)]
        else:
            stage_copy(name, j - 1).wait()
            landed = landing(name, j - 1)
        if joins:
            hand_over(int(name[2])).wait()
            extra = (over0, over1)[int(name[2])]
        if closing:
            total = mine[...].astype(F32) + landed[...].astype(F32)
            if joins:
                total = total + extra[...].astype(F32)
            total_of(name)[...] = total
            return
        accumulate(mine, landed, depth)
        if joins:
            accumulate(mine, extra, depth)
        if j < len(order):
            stage_copy(name, j).start()
        else:
            hand_over(int(name[2])).start()

    def run_slot(slot):
        for name, j in SCHEDULE.get(slot, ()):
            step(name, j)

    def dec_copy(d):
        to = place(d)
        return remote(dec.at[to[0] * ns + to[1]], dec_out.at[me], d_s.at[d], d_r.at[d], to)

    def enc_copy(d):
        t = lax.rem(s + d, ns)
        return remote(encoded.at[t], enc_out.at[s], e_s.at[d], e_r.at[d], (p, t))

    def grad_copy(d):
        t = lax.rem(s + d, ns)
        return remote(in_grad.at[t], grad_out.at[s], g_s.at[d], g_r.at[d], (p, t))

    keep_dec = pltpu.make_async_copy(dec.at[me], dec_out.at[me], loc.at[4])
    keep_enc = pltpu.make_async_copy(encoded.at[s], enc_out.at[s], loc.at[5])
    keep_grad = pltpu.make_async_copy(in_grad.at[s], grad_out.at[s], loc.at[6])

    for copy in loads:
        copy.start()
    fetch(first_half * (heads // 2), 0).start()
    fetch(first_half * (heads // 2) + 1, 1).start()
    keep_dec.start()
    keep_enc.start()
    diag[...] = jnp.zeros_like(diag)
    slot_rows = n // ns
    sm[...] = jnp.zeros_like(sm)

    def put_gain(i, gain):
        for j in range(width // 128):
            sm[0, i * 6 + j:i * 6 + j + 1, :] = gain[:, j * 128:(j + 1) * 128]

    for i in range(3):
        put_gain(i, gains_dec[i:i + 1, :])
    for i in range(3):
        loads[i].wait()
    final_gain = jnp.zeros((1, width), F32)
    for i in range(ns):
        r = slice(i * slot_rows, (i + 1) * slot_rows)
        alive = (lax.broadcasted_iota(jnp.int32, (slot_rows, 1), 0) + i * slot_rows < length[s]).astype(F32)
        b = bg[r]
        down, gain = norm_down(b, rms_scale(b), fg, rg[i].astype(F32))
        b = alive * (ct[r].astype(F32) + down)
        bg[r] = b
        low = b.astype(BF)
        rb[r] = low
        rb_t[:, r] = low.T
        final_gain = final_gain + jnp.sum(gain, axis=0, keepdims=True)
    put_gain(3, final_gain)
    pl.semaphore_wait(barrier, count - 1)
    for d in range(1, ns):
        enc_copy(d).start()

    @pl.loop(1, count)
    def _(d):
        dec_copy(d).start()

    part = width // 4
    loads[3].wait()

    @pl.loop(0, nz)
    def _(b):
        cols = pl.ds(pl.multiple_of(b * 2 * lanes, 128), 2 * lanes)
        g = mm(rb_t[...], acts[:, cols]).astype(BF)
        for j in range(4):
            for half in range(2):
                lo = j * part + half * rows
                for e in range(2):
                    fu[j % 2, 2 + half, j // 2, b // 2, lax.rem(b, 2), e] = g[lo:lo + rows, e * lanes:(e + 1) * lanes]

    for name in pieces:
        if name[0] == "t":
            core_copy(name).start()
    loads[4].wait()
    loads[5].wait()

    for j in range(ff // width):
        cols = slice(j * width, (j + 1) * width)
        grads[:, cols] = (grads[:, cols].astype(F32) * mm_t(rb[...], w1[cols, :])).astype(BF)
        run_slot("ug" + str(j))

    for copy in weights:
        copy.start()
    loads[6].wait()

    @pl.loop(0, 4)
    def _(j):
        cols = pl.ds(pl.multiple_of(j * 2 * lanes, 128), 2 * lanes)
        g = mm(mixed_t[...], grads[:, cols]).astype(BF)
        for half in range(2):
            fu[lax.rem(j, 2), half, j // 2] = g[:, half * lanes:(half + 1) * lanes].reshape(2, 2, 2, rows, lanes)

    for name in pieces:
        if name[0] == "w":
            core_copy(name).start()
    run_slot("wide")
    loads[7].wait()
    dm[...] = mm_t(grads[...], wes[...])
    for copy in heads_in:
        copy.start()
    run_slot("dm")
    loads[8].wait()
    expand_gain = jnp.zeros((1, width), F32)
    for i in range(ns):
        r = slice(i * slot_rows, (i + 1) * slot_rows)
        t = hid[r]
        down, gain = norm_down(t, rms_scale(t), eg, dm[r])
        t = bg[r] + down
        bg[r] = t
        branch[r] = t.astype(BF)
        expand_gain = expand_gain + jnp.sum(gain, axis=0, keepdims=True)
    put_gain(4, expand_gain)
    run_slot("rows")
    weights[0].wait()

    @pl.loop(0, width // 384)
    def _(j):
        cols = pl.ds(pl.multiple_of(j * 384, 128), 384)
        d_out[:, cols] = mm_t(branch[...], w1[cols, :]).astype(BF)

    for copy in heads_in:
        copy.wait()
    for copy in loads[9:]:
        copy.wait()

    run_slot("dout")

    lane = lax.broadcasted_iota(jnp.int32, (n, 128), 1)
    lane_s = lax.broadcasted_iota(jnp.int32, (128, 128), 1)
    row_s = lax.broadcasted_iota(jnp.int32, (128, 128), 0)

    def pair(half, g):
        cols = pl.ds(pl.multiple_of(half * (width // 2) + g * 128, 128), 128)
        k_t[...] = k[:, cols].T
        dop = d_out[:, cols]
        qp = q[:, cols]
        vp = v[:, cols]
        zero = jnp.zeros_like(qp)
        for a in range(2):
            h = half * (heads // 2) + 2 * g + a
            mine = (lane < 64) if a == 0 else (lane >= 64)
            dp[...] = mm_t(jnp.where(mine, vp, zero), dop)
            fetch(h, a).wait()
            for j in range(n // 128):
                pj = pbuf[a, :, j * 128:(j + 1) * 128].astype(F32)
                pd = pj * dp[:, j * 128:(j + 1) * 128]
                total = jnp.sum(pd, axis=0, keepdims=True)
                sg = pd - pj * total
                ds[:, j * 128:(j + 1) * 128] = sg.astype(BF)
                for i in range(n // 128):
                    t = sg[i * 128:(i + 1) * 128]
                    if abs(i - j) <= 1:
                        b = (i - j + 1) * 128
                        if j == 0 or (j == 1 and i == 0):
                            band[b:b + 128, :] = t
                        else:
                            band[b:b + 128, :] += t
                    else:
                        f = 5 if i > j else 4
                        diag[h, f:f + 1, :] += jnp.sum(t, axis=0, keepdims=True)
            dvp = mm(pbuf[a], jnp.where(mine, dop, zero))
            dkp = mm(ds[...], jnp.where(mine, qp, zero))
            dq_t[pl.ds(pl.multiple_of(h * 64, 64), 64), :] = mm(k_t[a * 64:(a + 1) * 64, :], ds[...]).astype(BF)
            if a == 0:
                dk_sum, dv_sum = dkp, dvp
            else:
                dk[:, cols] = (dk_sum + dkp).astype(BF)
                dv[:, cols] = (dv_sum + dvp).astype(BF)
            for b in range(3):
                t = band[b * 128:(b + 1) * 128, :]
                for bit in range(7):
                    t = jnp.where((row_s >> bit) % 2 == 1, pltpu.roll(t, 128 - (1 << bit), 1), t)
                straight = jnp.sum(jnp.where(lane_s + row_s < 128, t, 0.0), axis=0, keepdims=True)
                whole = jnp.sum(t, axis=0, keepdims=True)
                diag[h, b:b + 1, :] += straight
                diag[h, b + 1:b + 2, :] += whole - straight

    def units_of(half, tag):
        cols = pl.ds(pl.multiple_of(half * (width // 2), 128), width // 2)
        dq_h = dq_t[cols, :].T
        dq[:, cols] = dq_h
        dk_h = dk[:, cols]
        for cc in range(2):
            e = slice(cc * part, (cc + 1) * part)
            g = mm(normed_t[...], jnp.concatenate([dq_h[:, e], dk_h[:, e]], axis=1))
            au(0, cc, half)[...] = g.astype(BF).reshape(2, 2, 2, rows, lanes)
        core_copy("h" + tag + "0").start()
        run_slot("q" + tag)
        dv_h = dv[:, cols]
        br_h = branch[:, cols]
        zero = jnp.zeros((n, part), BF)
        for cc in range(2):
            e = slice(cc * part, (cc + 1) * part)
            g = (mm(normed_t[...], jnp.concatenate([dv_h[:, e], zero], axis=1))
                 + mm(context_t[...], jnp.concatenate([zero, br_h[:, e]], axis=1)))
            au(1, cc, half)[...] = g.astype(BF).reshape(2, 2, 2, rows, lanes)
        core_copy("h" + tag + "1").start()
        run_slot("v" + tag)

    quarter = heads // 4

    @pl.loop(0, quarter)
    def _(g):
        pair(first_half, g)
        nxt = jnp.where(g == quarter - 1, last_half * (heads // 2), first_half * (heads // 2) + 2 * (g + 1))
        fetch(nxt, 0).start()
        fetch(nxt + 1, 1).start()

        for i in range(quarter):
            if SCHEDULE.get("p0" + str(i)):
                @pl.when(g == i)
                def _():
                    run_slot("p0" + str(i))

    units_of(first_half, "0")

    @pl.loop(0, quarter)
    def _(g):
        pair(last_half, g)

        @pl.when(g < quarter - 1)
        def _():
            nxt = last_half * (heads // 2) + 2 * (g + 1)
            fetch(nxt, 0).start()
            fetch(nxt + 1, 1).start()

        for i in range(quarter):
            if SCHEDULE.get("p1" + str(i)):
                @pl.when(g == i)
                def _():
                    run_slot("p1" + str(i))

    units_of(last_half, "1")
    for copy in weights[1:]:
        copy.wait()

    for i in range(2):
        r = slice(i * (n // 2), (i + 1) * (n // 2))
        ng[r] = mm_t(dq[r], wqs[...]) + mm_t(dk[r], wks[...]) + mm_t(dv[r], wvs[...])
        run_slot("ng" + str(i))

    gain_sum = jnp.zeros((1, width), F32)
    for i in range(ns):
        r = slice(i * slot_rows, (i + 1) * slot_rows)
        t = x[r].astype(F32)
        down, gain = norm_down(t, rms_scale(t), ag, ng[r])
        in_grad[i] = (hidden_grad[r] + down).astype(BF)
        gain_sum = gain_sum + jnp.sum(gain, axis=0, keepdims=True)
    keep_grad.start()
    for d in range(1, ns):
        grad_copy(d).start()

    pick = diagonal_buckets((128, width), width)
    bias = jnp.zeros((16, 128), F32)
    for i in range(width // 128):
        bias = bias + lax.dot_general(diag[:, i, :], pick[:, i * 128:(i + 1) * 128], (((1,), (1,)), ((), ())),
                                      precision=HIGHEST, preferred_element_type=F32)
    sm[0, 40:56, :] = bias
    put_gain(5, gain_sum)

    def small_copy(i):
        return remote(sm.at[i], smr.at[i], m_s.at[i], m_r.at[i], (core_peer, y_peer, x_peer)[i])

    def z_small(d):
        return remote(smz.at[z], smz.at[z], mz_s.at[d], mz_r.at[d], (lax.rem(z + d, nz) * 2 + xx, s))

    def small_hop(i):
        small_copy(i).wait()
        if i < 2:
            sm[i + 1] = sm[i] + smr[i]
            small_copy(i + 1).start()
        else:
            smz[z] = sm[i] + smr[i]

            @pl.loop(1, nz)
            def _(d):
                z_small(d).start()

    small_copy(0).start()
    tail = SCHEDULE["end"]
    for i, (name, j) in enumerate(tail):
        step(name, j)
        if i in HOPS:
            small_hop(HOPS.index(i))

    @pl.loop(1, nz)
    def _(d):
        z_small(d).wait()

    small_out[...] = smz[0]

    @pl.loop(1, nz)
    def _(d):
        small_out[...] = small_out[...] + smz[d]

    keep_dec.wait()
    keep_enc.wait()
    keep_grad.wait()
    for d in range(1, ns):
        enc_copy(d).wait()
        grad_copy(d).wait()

    @pl.loop(1, count)
    def _(d):
        dec_copy(d).wait()


def fused(np_, ns, length, fg, eg, ag, gains_dec, rows_grad, block, cot, wr, active, we, hidden, slope, mixed_t,
          wo, wq, wk, wv, q, k, v, x, normed_t, context_t, probs, dec, encoded):
    n, width = hidden.shape
    ff = active.shape[1]
    heads = probs.shape[0]
    nz = np_ // 2
    rows, lanes = width // np_, ff // np_
    count = np_ * ns
    smem = pl.BlockSpec(memory_space=pltpu.SMEM)
    vm = pl.BlockSpec(memory_space=pltpu.VMEM)
    hb = pl.BlockSpec(memory_space=pl.ANY)
    S = jax.ShapeDtypeStruct
    V = pltpu.VMEM
    dma = pltpu.SemaphoreType.DMA
    nar, tall = V((n, width), BF), V((width, n), BF)
    floats = V((n, width), F32)
    slots = (ns, n // ns, width)
    small = (64, 128)
    ffs = 4 * PARTS
    sub = rows // PARTS

    def joint(w):
        return V((2,) * (3 - ORDERS["a" + str(w)].index("y")) + (rows, lanes), BF)

    return pl.pallas_call(
        functools.partial(fused_kernel, np_, ns),
        out_shape=(S((6, rows, lanes), F32), S(small, F32), S(dec.shape, BF), S(slots, BF), S(slots, BF)),
        in_specs=[smem] + [vm] * 4 + [hb] * 22,
        out_specs=(vm, vm, hb, hb, hb),
        scratch_shapes=[
            V((n, ff), BF), V((n, ff), BF), V((ff, width), BF), V((width, ff), BF), floats, floats, floats,
            V(slots, BF), nar, nar, tall, tall, tall, tall,
            V((n, n), F32), V((n, n), BF), V((2, n, n), BF), V((128, n), BF), V((384, 128), F32), V((16, 8, 128), F32),
            V((2, 4, 2, 2, 2, 2, rows, lanes), BF), V((ffs, 2, 2, 2, 2, sub, lanes), BF), V((4, 2, 2, 2, rows, lanes), BF),
            V((ffs, 2, 2, 2, sub, lanes), BF), V((ffs, 2, 2, sub, lanes), BF), V((ffs, 2, sub, lanes), BF),
            V((ffs, sub, lanes), BF), V((4, 2, 2, rows, lanes), BF), V((4, 2, rows, lanes), BF),
            V((4, rows, lanes), BF), joint(0), joint(1),
            V((3,) + small, F32), V((3,) + small, F32), V((nz,) + small, F32),
            dma((2,)), dma((19,)), dma((7,)), dma((ffs + 4,)), dma((ffs + 4,)), dma((ffs + 4, 4)), dma((ffs + 4, 4)),
            dma((2,)), dma((2,)),
            dma((3,)), dma((3,)), dma((nz,)), dma((nz,)), dma((count,)), dma((count,)),
            dma((ns,)), dma((ns,)), dma((ns,)), dma((ns,)),
        ],
        compiler_params=pltpu.CompilerParams(
            collective_id=0, has_side_effects=True, vmem_limit_bytes=62 * 1024 * 1024),
        name="fused_backward",
    )(length, fg, eg, ag, gains_dec, rows_grad.reshape(slots), block, cot, wr,
      active, we, hidden, slope, mixed_t, wo, wq, wk, wv, q, k, v, x, normed_t, context_t, probs, dec,
      encoded.reshape(slots))


def feed_back_kernel(length, rows_grad, block, cot, fg, hidden, eg, mixed, active, slope, wr, we,
                     wide, tall, hidden_grad, branch, gains, wrs, wes, bg, rb, rb_t, ug, mixed_t, dmixed, sems):
    n, width = block.shape
    ff = active.shape[1]
    groups, lanes = tall.shape[3], tall.shape[5]
    cols_dev = width // 4
    copies = [pltpu.make_async_copy(a, b, sems.at[i]) for i, (a, b) in enumerate(((wr, wrs), (we, wes)))]
    for c in copies:
        c.start()
    gains[...] = jnp.zeros_like(gains)

    @pl.loop(0, n // 128)
    def _(i):
        r = pl.ds(i * 128, 128)
        alive = (lax.broadcasted_iota(jnp.int32, (128, 1), 0) + i * 128 < length[0]).astype(F32)
        v = block[r]
        down, gain = norm_down(v, rms_scale(v), fg[...], rows_grad[r].astype(F32))
        b = alive * (cot[r].astype(F32) + down)
        bg[r] = b
        rb[r] = b.astype(BF)
        rb_t[:, pl.ds(pl.multiple_of(i * 128, 128), 128)] = b.T.astype(BF)
        mixed_t[:, pl.ds(pl.multiple_of(i * 128, 128), 128)] = mixed[r].T
        gains[0:1, :] += jnp.sum(gain, axis=0, keepdims=True)

    copies[0].wait()

    @pl.loop(0, ff // 256)
    def _(j):
        cols = pl.ds(pl.multiple_of(j * 256, 256), 256)
        ug[:, cols] = (slope[:, cols].astype(F32) * mm_t(rb[...], wrs[cols, :])).astype(BF)

    copies[1].wait()

    @pl.loop(0, width // 256)
    def _(j):
        cols = pl.ds(pl.multiple_of(j * 256, 256), 256)
        dmixed[:, cols] = mm_t(ug[...], wes[cols, :])

    @pl.loop(0, n // 128)
    def _(i):
        r = pl.ds(i * 128, 128)
        v = hidden[r]
        down, gain = norm_down(v, rms_scale(v), eg[...], dmixed[r])
        h = bg[r] + down
        hidden_grad[r] = h
        branch[r] = h.astype(BF)
        gains[1:2, :] += jnp.sum(gain, axis=0, keepdims=True)

    @pl.loop(0, 4)
    def _(j):
        for half in range(2):
            cols = pl.ds(pl.multiple_of(j * (ff // 4) + half * (ff // 8), 128), ff // 8)
            wide[half, lax.rem(j, 2), j // 2] = mm(mixed_t[...], ug[:, cols]).astype(BF)

    chunk = ff // 8
    per_group = lanes // chunk

    @pl.loop(0, 8)
    def _(i):
        cols = pl.ds(pl.multiple_of(i * chunk, 128), chunk)
        g = mm(rb_t[...], active[:, cols]).astype(BF)
        for j in range(4):
            for half in range(2):
                r = j * cols_dev + half * (cols_dev // 2)
                part = g[r:r + cols_dev // 2]
                if per_group == 1:
                    tall[half, j % 2, j // 2, i] = part
                else:
                    tall[half, j % 2, j // 2, 0, :, cols] = part


def feed_back(groups, length, rows_grad, block, cot, fg, hidden, eg, mixed, active, slope, wr, we):
    n, width = block.shape
    ff = active.shape[1]
    sm = pl.BlockSpec(memory_space=pltpu.SMEM)
    vm = pl.BlockSpec(memory_space=pltpu.VMEM)
    hb = pl.BlockSpec(memory_space=pl.ANY)
    S = jax.ShapeDtypeStruct
    V = pltpu.VMEM
    return pl.pallas_call(
        feed_back_kernel,
        out_shape=(S((2, 2, 2, width, ff // 8), BF),
                   S((2, 2, 2, groups, width // 8, ff // groups), BF), S((n, width), F32), S((n, width), BF), S((2, width), F32)),
        in_specs=[sm] + [vm] * 9 + [hb] * 2,
        out_specs=(vm,) * 5,
        scratch_shapes=[V(wr.shape, BF), V(we.shape, BF), V((n, width), F32), V((n, width), BF), V((width, n), BF),
                        V((n, ff), BF), V((width, n), BF), V((n, width), F32), pltpu.SemaphoreType.DMA((2,))],
        compiler_params=pltpu.CompilerParams(vmem_limit_bytes=60 * 1024 * 1024),
        name="feed_back",
    )(length, rows_grad, block, cot, fg.reshape(1, -1), hidden, eg.reshape(1, -1), mixed, active, slope, wr, we)


def backward_kernel(np_, ns, x, ag, q, k, v, context_t, branch, hidden_grad, normed, gains_dec, gains_feed,
                    probs, wo, wq, wk, wv, wide, tall, dec, encoded,
                    red, small_out, dec_out, enc_out, grad_out,
                    wos, wqs, wks, wvs, d_out, dp, ds, dq_t, dq, dk, dv, k_t, normed_t, ng, in_grad,
                    pbuf, band, diag, own, au, r0, r1y, r1x, r1a, r2, r3, sm, smr, smz,
                    psem, wsem, loc, c_s, c_r, a_s, a_r, b_s, b_r, ac_s, ac_r, ax_s, ax_r, z_s, z_r,
                    m_s, m_r, mz_s, mz_r, d_s, d_r, e_s, e_r, g_s, g_r):
    n, width = x.shape
    heads = probs.shape[0]
    nz = np_ // 2
    rows, lanes = r0.shape[4:]
    count = np_ * ns
    p = lax.axis_index("pairs")
    s = lax.axis_index("seq")
    c = lax.rem(s, 2)
    y = s // 2
    xx = lax.rem(p, 2)
    z = p // 2
    me = p * ns + s
    core_peer = (p, s + 1 - 2 * c)
    y_peer = (p, lax.rem(s + 2, 4))
    x_peer = (p + 1 - 2 * xx, s)

    def place(d):
        lin = lax.rem(me + d, count)
        return (lin // ns, lax.rem(lin, ns))

    barrier = pltpu.get_barrier_semaphore()

    @pl.loop(1, count)
    def _(d):
        pl.semaphore_signal(barrier, inc=1, device_id=place(d), device_id_type=MESH)

    def remote(src, dst, send, recv, peer):
        return pltpu.make_async_remote_copy(
            src_ref=src, dst_ref=dst, send_sem=send, recv_sem=recv,
            device_id=peer, device_id_type=MESH)

    weights = [pltpu.make_async_copy(a, b, wsem.at[i])
               for i, (a, b) in enumerate(((wo, wos), (wq, wqs), (wk, wks), (wv, wvs)))]

    def fetch(h, slot):
        return pltpu.make_async_copy(probs.at[h], pbuf.at[slot], psem.at[slot])

    def unit(i, core):
        return (wide, tall)[i // 2].at[i % 2, core]

    def core_copy(i):
        return remote(unit(i, 1 - c), r0.at[i], c_s.at[i], c_r.at[i], core_peer)

    def own_copy(i):
        return pltpu.make_async_copy(unit(i, c), own.at[i], loc.at[i])

    def first(i):
        if i % 2 == 0:
            return remote(own.at[i, 1 - y], r1y.at[i // 2], a_s.at[i], a_r.at[i], y_peer)
        return remote(own.at[i, :, :, 1 - xx], r1x.at[i // 2], a_s.at[i], a_r.at[i], x_peer)

    def second(i):
        if i % 2 == 0:
            return remote(own.at[i, y, :, 1 - xx], r2.at[i], b_s.at[i], b_r.at[i], x_peer)
        return remote(own.at[i, 1 - y, :, xx], r2.at[i], b_s.at[i], b_r.at[i], y_peer)

    def final(i):
        return own.at[i, y] if i < 4 else au.at[i - 4, c, y]

    def last(i, d):
        t = lax.rem(z + d, nz)
        return remote(final(i).at[t, xx], r3.at[i, d], z_s.at[i, d], z_r.at[i, d], (t * 2 + xx, s))

    def attn_core(w, half):
        return remote(au.at[w, 1 - c, half], r0.at[4 + w, half], ac_s.at[w, half], ac_r.at[w, half], core_peer)

    def attn_x(w, half):
        return remote(au.at[w, c, half, :, 1 - xx], r1a.at[w, half], ax_s.at[w, half], ax_r.at[w, half], x_peer)

    def attn_y(w):
        return remote(au.at[w, c, 1 - y, :, xx], r2.at[4 + w], b_s.at[4 + w], b_r.at[4 + w], y_peer)

    def dec_copy(d):
        to = place(d)
        return remote(dec.at[to[0] * ns + to[1]], dec_out.at[me], d_s.at[d], d_r.at[d], to)

    def enc_copy(d):
        t = lax.rem(s + d, ns)
        return remote(encoded.at[t], enc_out.at[s], e_s.at[d], e_r.at[d], (p, t))

    def grad_copy(d):
        t = lax.rem(s + d, ns)
        return remote(in_grad.at[t], grad_out.at[s], g_s.at[d], g_r.at[d], (p, t))

    keep_dec = pltpu.make_async_copy(dec.at[me], dec_out.at[me], loc.at[4])
    keep_enc = pltpu.make_async_copy(encoded.at[s], enc_out.at[s], loc.at[5])
    keep_grad = pltpu.make_async_copy(in_grad.at[s], grad_out.at[s], loc.at[6])

    def step_a(i):
        core_copy(i).wait()
        own_copy(i).wait()

        @pl.loop(0, nz)
        def _(b):
            for a in range(2):
                for e in range(2):
                    own[i, a, b, e] = own[i, a, b, e] + r0[i, a, b, e]

        first(i).start()

    def step_b(i):
        first(i).wait()

        @pl.loop(0, nz)
        def _(b):
            for e in range(2):
                if i % 2 == 0:
                    own[i, y, b, e] = own[i, y, b, e] + r1y[i // 2, b, e]
                else:
                    own[i, e, b, xx] = own[i, e, b, xx] + r1x[i // 2, e, b]

        second(i).start()

    def step_c(i):
        if i < 4:
            second(i).wait()
        else:
            attn_y(i - 4).wait()

        @pl.loop(0, nz)
        def _(b):
            f = final(i)
            f[b, xx] = f[b, xx] + r2[i, b]

        @pl.loop(1, nz)
        def _(d):
            last(i, d).start()

    def step_d(i):
        red[i] = final(i)[z, xx].astype(F32)

        @pl.loop(1, nz)
        def _(d):
            last(i, d).wait()
            red[i] = red[i] + r3[i, d].astype(F32)

    def attn_a(w, half):
        attn_core(w, half).wait()

        @pl.loop(0, nz)
        def _(b):
            for e in range(2):
                au[w, c, half, b, e] = au[w, c, half, b, e] + r0[4 + w, half, b, e]

        attn_x(w, half).start()

    def attn_b(w, half):
        attn_x(w, half).wait()

        @pl.loop(0, nz)
        def _(b):
            au[w, c, half, b, xx] = au[w, c, half, b, xx] + r1a[w, half, b]

    for copy in weights:
        copy.start()
    first_half, last_half = 1 - y, y
    fetch(first_half * (heads // 2), 0).start()
    fetch(first_half * (heads // 2) + 1, 1).start()
    for i in range(4):
        own_copy(i).start()
    keep_dec.start()
    keep_enc.start()
    diag[...] = jnp.zeros_like(diag)
    weights[0].wait()

    @pl.loop(0, width // 384)
    def _(j):
        cols = pl.ds(pl.multiple_of(j * 384, 128), 384)
        d_out[:, cols] = mm_t(branch[...], wos[cols, :]).astype(BF)

    pl.semaphore_wait(barrier, count - 1)
    for i in range(4):
        core_copy(i).start()
    for d in range(1, ns):
        enc_copy(d).start()

    @pl.loop(1, count)
    def _(d):
        dec_copy(d).start()

    @pl.loop(0, n // 128)
    def _(i):
        r = pl.ds(pl.multiple_of(i * 128, 128), 128)
        normed_t[:, r] = normed[r].T

    lane = lax.broadcasted_iota(jnp.int32, (n, 128), 1)
    lane_s = lax.broadcasted_iota(jnp.int32, (128, 128), 1)
    row_s = lax.broadcasted_iota(jnp.int32, (128, 128), 0)

    def pair(half, g):
        cols = pl.ds(pl.multiple_of(half * (width // 2) + g * 128, 128), 128)
        k_t[...] = k[:, cols].T
        dop = d_out[:, cols]
        qp = q[:, cols]
        vp = v[:, cols]
        zero = jnp.zeros_like(qp)
        for a in range(2):
            h = half * (heads // 2) + 2 * g + a
            mine = (lane < 64) if a == 0 else (lane >= 64)
            dp[...] = mm_t(jnp.where(mine, vp, zero), dop)
            fetch(h, a).wait()
            for j in range(n // 128):
                pj = pbuf[a, :, j * 128:(j + 1) * 128].astype(F32)
                pd = pj * dp[:, j * 128:(j + 1) * 128]
                total = jnp.sum(pd, axis=0, keepdims=True)
                sg = pd - pj * total
                ds[:, j * 128:(j + 1) * 128] = sg.astype(BF)
                for i in range(n // 128):
                    t = sg[i * 128:(i + 1) * 128]
                    if abs(i - j) <= 1:
                        b = (i - j + 1) * 128
                        if j == 0 or (j == 1 and i == 0):
                            band[b:b + 128, :] = t
                        else:
                            band[b:b + 128, :] += t
                    else:
                        f = 5 if i > j else 4
                        diag[h, f:f + 1, :] += jnp.sum(t, axis=0, keepdims=True)
            dvp = mm(pbuf[a], jnp.where(mine, dop, zero))
            dkp = mm(ds[...], jnp.where(mine, qp, zero))
            dq_t[pl.ds(pl.multiple_of(h * 64, 64), 64), :] = mm(k_t[a * 64:(a + 1) * 64, :], ds[...]).astype(BF)
            if a == 0:
                dk_sum, dv_sum = dkp, dvp
            else:
                dk[:, cols] = (dk_sum + dkp).astype(BF)
                dv[:, cols] = (dv_sum + dvp).astype(BF)
            for b in range(3):
                t = band[b * 128:(b + 1) * 128, :]
                for bit in range(7):
                    t = jnp.where((row_s >> bit) % 2 == 1, pltpu.roll(t, 128 - (1 << bit), 1), t)
                straight = jnp.sum(jnp.where(lane_s + row_s < 128, t, 0.0), axis=0, keepdims=True)
                whole = jnp.sum(t, axis=0, keepdims=True)
                diag[h, b:b + 1, :] += straight
                diag[h, b + 1:b + 2, :] += whole - straight

    part = width // 4

    def units_of(half):
        cols = pl.ds(pl.multiple_of(half * (width // 2), 128), width // 2)
        lower = pl.ds(pl.multiple_of(half * (width // 2), 128), width // 2)
        dq_h = dq_t[lower, :].T
        dq[:, cols] = dq_h
        dk_h = dk[:, cols]
        dv_h = dv[:, cols]
        br_h = branch[:, cols]
        zero = jnp.zeros((n, part), BF)
        for cc in range(2):
            e = slice(cc * part, (cc + 1) * part)
            g = mm(normed_t[...], jnp.concatenate([dq_h[:, e], dk_h[:, e]], axis=1))
            au[0, cc, half] = g.astype(BF).reshape(nz, 2, rows, lanes)
            g = (mm(normed_t[...], jnp.concatenate([dv_h[:, e], zero], axis=1))
                 + mm(context_t[...], jnp.concatenate([zero, br_h[:, e]], axis=1)))
            au[1, cc, half] = g.astype(BF).reshape(nz, 2, rows, lanes)
        for w in range(2):
            attn_core(w, half).start()

    quarter = heads // 4

    @pl.loop(0, quarter)
    def _(g):
        pair(first_half, g)
        nxt = jnp.where(g == quarter - 1, last_half * (heads // 2), first_half * (heads // 2) + 2 * (g + 1))
        fetch(nxt, 0).start()
        fetch(nxt + 1, 1).start()

        @pl.when(g == 0)
        def _():
            step_a(0)
            step_a(1)

        @pl.when(g == 1)
        def _():
            step_a(2)
            step_a(3)

    units_of(first_half)

    @pl.loop(0, quarter)
    def _(g):
        pair(last_half, g)

        @pl.when(g < quarter - 1)
        def _():
            nxt = last_half * (heads // 2) + 2 * (g + 1)
            fetch(nxt, 0).start()
            fetch(nxt + 1, 1).start()

        @pl.when(g == 0)
        def _():
            attn_a(0, first_half)
            attn_a(1, first_half)

        @pl.when(g == 1)
        def _():
            step_b(0)
            step_b(1)

    units_of(last_half)
    for copy in weights[1:]:
        copy.wait()

    @pl.loop(0, 2)
    def _(i):
        r = pl.ds(pl.multiple_of(i * (n // 2), 128), n // 2)
        ng[r] = mm_t(dq[r], wqs[...]) + mm_t(dk[r], wks[...]) + mm_t(dv[r], wvs[...])

    attn_a(0, last_half)
    attn_a(1, last_half)
    sm[...] = jnp.zeros_like(sm)
    slot_rows = n // ns
    gain_sum = jnp.zeros((1, width), F32)
    for i in range(ns):
        r = slice(i * slot_rows, (i + 1) * slot_rows)
        t = x[r].astype(F32)
        down, gain = norm_down(t, rms_scale(t), ag[...], ng[r])
        in_grad[i] = (hidden_grad[r] + down).astype(BF)
        gain_sum = gain_sum + jnp.sum(gain, axis=0, keepdims=True)
    keep_grad.start()
    for d in range(1, ns):
        grad_copy(d).start()

    col = lax.broadcasted_iota(jnp.int32, (128, width), 1)
    offset = (col // 128 - 1) * 128 - lax.rem(col, 128)
    offset = jnp.where(col >= width - 128, 256, jnp.where(col >= width - 256, -256, offset))
    dist = jnp.abs(offset)
    bucket = jnp.full_like(dist, 8)
    for edge in EDGES:
        bucket = bucket + (dist >= edge).astype(jnp.int32)
    bucket = jnp.where(dist < 8, dist, bucket) + jnp.where(offset > 0, 16, 0)
    pick = jnp.where(bucket == lax.broadcasted_iota(jnp.int32, (128, width), 0), 1.0, 0.0)
    bias = jnp.zeros((16, 128), F32)
    for i in range(width // 128):
        bias = bias + lax.dot_general(diag[:, i, :], pick[:, i * 128:(i + 1) * 128], (((1,), (1,)), ((), ())),
                                      precision=HIGHEST, preferred_element_type=F32)
    sm[0, 40:56, :] = bias
    gains = [gains_dec[i:i + 1, :] for i in range(3)] + [gains_feed[i:i + 1, :] for i in range(2)] + [gain_sum]
    for i, gain in enumerate(gains):
        for j in range(width // 128):
            sm[0, i * 6 + j:i * 6 + j + 1, :] = gain[:, j * 128:(j + 1) * 128]

    def small_copy(i):
        return remote(sm.at[i], smr.at[i], m_s.at[i], m_r.at[i], (core_peer, y_peer, x_peer)[i])

    def z_small(d):
        return remote(smz.at[z], smz.at[z], mz_s.at[d], mz_r.at[d], (lax.rem(z + d, nz) * 2 + xx, s))

    small_copy(0).start()
    step_b(2)
    step_b(3)
    small_copy(0).wait()
    sm[1] = sm[0] + smr[0]
    small_copy(1).start()
    attn_b(0, first_half)
    attn_y(0).start()
    attn_b(1, first_half)
    attn_y(1).start()
    step_c(0)
    step_c(1)
    small_copy(1).wait()
    sm[2] = sm[1] + smr[1]
    small_copy(2).start()
    step_c(2)
    step_c(3)
    attn_b(0, last_half)
    small_copy(2).wait()
    smz[z] = sm[2] + smr[2]

    @pl.loop(1, nz)
    def _(d):
        z_small(d).start()

    step_c(4)
    attn_b(1, last_half)
    step_c(5)
    for i in range(6):
        step_d(i)

    @pl.loop(1, nz)
    def _(d):
        z_small(d).wait()

    small_out[...] = smz[0]

    @pl.loop(1, nz)
    def _(d):
        small_out[...] = small_out[...] + smz[d]

    keep_dec.wait()
    keep_enc.wait()
    keep_grad.wait()
    for d in range(1, ns):
        enc_copy(d).wait()
        grad_copy(d).wait()

    @pl.loop(1, count)
    def _(d):
        dec_copy(d).wait()


def backward(np_, ns, x, ag, q, k, v, context_t, branch, hidden_grad, normed, gains_dec, gains_feed,
             probs, wo, wq, wk, wv, wide, tall, dec, encoded):
    n, width = x.shape
    heads = probs.shape[0]
    nz = np_ // 2
    rows, lanes = wide.shape[5:]
    count = np_ * ns
    padded = normed.shape[1]
    vm = pl.BlockSpec(memory_space=pltpu.VMEM)
    hb = pl.BlockSpec(memory_space=pl.ANY)
    S = jax.ShapeDtypeStruct
    V = pltpu.VMEM
    dma = pltpu.SemaphoreType.DMA
    nar = V((n, width), BF)
    square = V((width, width), BF)
    slots = (ns, n // ns, width)
    small = (64, 128)
    return pl.pallas_call(
        functools.partial(backward_kernel, np_, ns),
        out_shape=(S((6, rows, lanes), F32), S(small, F32), S(dec.shape, BF), S(slots, BF), S(slots, BF)),
        in_specs=[vm] * 11 + [hb] * 9,
        out_specs=(vm, vm, hb, hb, hb),
        scratch_shapes=[
            square, square, square, square, nar, V((n, n), F32), V((n, n), BF), V((width, n), BF), nar, nar, nar,
            V((128, n), BF), V((padded, n), BF), V((n, width), F32), V(slots, BF),
            V((2, n, n), BF), V((384, 128), F32), V((16, 8, 128), F32),
            V((4, 2, nz, 2, rows, lanes), BF), V((2, 2, 2, nz, 2, rows, lanes), BF), V((6, 2, nz, 2, rows, lanes), BF),
            V((2, nz, 2, rows, lanes), BF), V((2, 2, nz, rows, lanes), BF), V((2, 2, nz, rows, lanes), BF),
            V((6, nz, rows, lanes), BF), V((6, nz, rows, lanes), BF),
            V((3,) + small, F32), V((3,) + small, F32), V((nz,) + small, F32),
            dma((2,)), dma((4,)), dma((7,)), dma((4,)), dma((4,)), dma((4,)), dma((4,)), dma((6,)), dma((6,)),
            dma((2, 2)), dma((2, 2)), dma((2, 2)), dma((2, 2)), dma((6, nz)), dma((6, nz)),
            dma((3,)), dma((3,)), dma((nz,)), dma((nz,)), dma((count,)), dma((count,)),
            dma((ns,)), dma((ns,)), dma((ns,)), dma((ns,)),
        ],
        compiler_params=pltpu.CompilerParams(
            collective_id=0, has_side_effects=True, vmem_limit_bytes=62 * 1024 * 1024),
        name="backward",
    )(x, ag.reshape(1, -1), q, k, v, context_t, branch, hidden_grad, normed, gains_dec, gains_feed,
      probs, wo, wq, wk, wv, wide, tall, dec, encoded.reshape(slots))


def two_kernels(
    np_, ns, r, rp, lanes, side, length, final_gain, expand_gain, attend_gain, dec_gains,
    rows_grad, block, cot, reduce_weight, active, expand_weight, hidden, slope, mixed_t,
    output_weight, query_weight, key_weight, value_weight, query, key, value, x, normed_t,
    context_t, probs, dec_all, encoded,
):
    seq_len, ff = active.shape
    nz = np_ // 2
    wide, tall, hidden_grad, branch, feed_gains = feed_back(
        1, length, rows_grad, block, cot, final_gain, hidden, expand_gain, mixed_t.T, active,
        slope, reduce_weight, expand_weight)

    def pad(unit):
        return jnp.pad(unit, ((0, 0),) * 5 + ((0, rp - r), (0, 0)))

    tall = tall.reshape(2, 2, 2, r, side, nz, 2, ff // np_).transpose(0, 1, 2, 5, 6, 3, 4, 7)
    tall = pad(tall.reshape(2, 2, 2, nz, 2, r, lanes))
    wide = pad(wide.reshape(2, 2, 2, nz, 2, r, lanes))
    gap = ((0, 0), (0, rp - r), (0, 0))
    normed_t = jnp.pad(normed_t.reshape(np_, r, seq_len), gap).reshape(np_ * rp, seq_len)
    context_t = jnp.pad(context_t.reshape(np_, r, seq_len), gap).reshape(np_ * rp, seq_len)
    return backward(
        np_, ns, x, attend_gain, query, key, value, context_t, branch, hidden_grad, normed_t.T,
        dec_gains, feed_gains, probs, output_weight, query_weight, key_weight, value_weight,
        wide, tall, dec_all, encoded)


def per_device(
    enc_input, dec_input, lengths, attend_gain, query_weight, key_weight, value_weight,
    output_weight, bias_table, expand_gain, expand_weight, reduce_weight, final_gain,
    self_gain, self_value, self_output, cross_gain, cross_query, cross_key, cross_value,
    cross_output, feed_gain, feed_expand, feed_reduce, enc_cotangent, dec_cotangent,
):
    group, local_rows, width = enc_input.shape
    buckets, heads = bias_table.shape
    size = width // heads
    ff = expand_weight.shape[1]
    ns = lax.axis_size("seq")
    np_ = lax.axis_size("pairs")
    r = width // np_
    aligned = np_ == 8 and r % 32 == 0 and (ff // np_) % 128 == 0 and ff == 4 * width
    seq_len = local_rows * ns
    weights = (query_weight, key_weight, value_weight, output_weight, expand_weight, reduce_weight,
               self_value, self_output, cross_query, cross_key, cross_value, cross_output,
               feed_expand, feed_reduce)
    (normed_t, query, key, value, probs, context_t, hidden, mixed_t, active, slope, block, encoded,
     x, cot, rows_grad, dec_block, dec_input_grad, dec_gains, *dec_rows) = forward(
        np_, ns, aligned, lengths, bias_table.T,
        (attend_gain, expand_gain, final_gain, self_gain, cross_gain, feed_gain),
        dec_input, dec_cotangent, enc_input, enc_cotangent, weights)
    x = x.reshape(seq_len, width)
    cot = cot.reshape(seq_len, width)
    if aligned:
        dec_all, = dec_rows
        red, small_sum, dec_got, enc_out, grad_out = fused(
            np_, ns, lengths, final_gain, expand_gain, attend_gain, dec_gains, rows_grad, block, cot,
            reduce_weight, active, expand_weight, hidden, slope, mixed_t, output_weight,
            query_weight, key_weight, value_weight, query, key, value, x, normed_t, context_t,
            probs, dec_all, encoded)
        (enc_out, grad_out, dec_block, dec_input_grad, grad_query, grad_key, grad_value, grad_output, grad_expand, grad_reduce,
         bias, *rest) = finish(
            heads, buckets, red, small_sum, dec_got, dec_block, dec_input_grad, enc_out, grad_out)
        gains = rest[:6]
        grad_sv, grad_so, grad_cq, grad_ck, grad_cv, grad_co, feed_in, feed_out = rest[6:]
        return (
            enc_out, dec_block, grad_out, dec_input_grad, gains[5], grad_query, grad_key,
            grad_value, grad_output, bias.T, gains[4], grad_expand, grad_reduce.T, gains[3],
            gains[0], grad_sv, grad_so, gains[1], grad_cq, grad_ck, grad_cv, grad_co, gains[2],
            feed_in, feed_out.T,
        )
    left, right, wide_rows, mids = dec_rows
    length = lax.dynamic_slice_in_dim(lengths, lax.axis_index("seq"), 1)
    rp = -(-r // 16) * 16
    lanes = ff // 8
    side = width // 8 // r
    cols = width // ns

    left_cut = jnp.concatenate([
        left.reshape(5, np_, r).transpose(1, 0, 2).reshape(np_, 5 * r),
        wide_rows[0].reshape(np_, 4 * r),
    ], axis=1)
    mid_cut = mids.reshape(2, ns, heads // ns, np_, r).transpose(3, 1, 0, 2, 4)
    mid_cut = mid_cut.reshape(np_, ns, 6 * r)
    right_cut = jnp.concatenate([
        right.reshape(7, ns, cols).transpose(1, 0, 2).reshape(ns, 7 * cols),
        wide_rows[1].reshape(ns, 4 * cols)], axis=1)
    dec_all = jnp.concatenate([
        jnp.broadcast_to(left_cut[:, None], (np_, ns, 9 * r)), mid_cut,
        jnp.broadcast_to(right_cut[None], (np_, ns, 11 * cols))], axis=-1)
    dec_all = dec_all.astype(BF).reshape(np_ * ns, -1)
    used = dec_all.shape[1]
    dec_rows = -(-used // 2048) * 16
    dec_all = jnp.pad(dec_all, ((0, 0), (0, dec_rows * 128 - used)))
    dec_all = dec_all.reshape(np_ * ns, dec_rows, 128)

    red, small_sum, dec_got, enc_out, grad_out = two_kernels(
        np_, ns, r, rp, lanes, side, length, final_gain, expand_gain, attend_gain, dec_gains,
        rows_grad, block, cot, reduce_weight, active, expand_weight, hidden, slope, mixed_t,
        output_weight, query_weight, key_weight, value_weight, query, key, value, x, normed_t,
        context_t, probs, dec_all, encoded)

    got = dec_got.reshape(np_ * ns, -1)
    lefts = got[:, :9 * r].reshape(-1, 9, r)
    mid_got = got[:, 9 * r:15 * r].reshape(-1, 2, 3, r)
    rights = got[:, 15 * r:15 * r + 11 * cols].reshape(-1, 11, cols)
    plain = jnp.einsum("nkr,nkc->krc", lefts[:, :4], rights[:, :4], preferred_element_type=F32)
    crossed = jnp.einsum("nkhr,nkhd->krhd", mid_got, rights[:, 4:6].reshape(-1, 2, 3, size),
                         preferred_element_type=F32).reshape(2, r, cols)
    feed_in = jnp.einsum("nr,nc->rc", lefts[:, 4], rights[:, 7:11].reshape(-1, 4 * cols),
                         preferred_element_type=F32)
    feed_out = jnp.einsum("nr,nc->rc", lefts[:, 5:9].reshape(-1, 4 * r), rights[:, 6],
                          preferred_element_type=F32)
    red = red[:, :r]
    grad_reduce = red[2:4].reshape(2, r, side, ff // np_).reshape(cols, ff // np_).T
    gains = small_sum[:36].reshape(6, width)
    bias = small_sum[40:40 + heads, :buckets].T
    return (
        enc_out, dec_block, grad_out, dec_input_grad,
        gains[5],
        red[4][:, :cols], red[4][:, cols:], red[5][:, :cols], red[5][:, cols:],
        bias,
        gains[4],
        jnp.concatenate([red[0], red[1]], axis=1), grad_reduce,
        gains[3],
        gains[0], plain[0], plain[1],
        gains[1], plain[2], crossed[0], crossed[1], plain[3],
        gains[2], feed_in, feed_out,
    )


def solution(mesh):
    rows = P("pairs", "seq", None)
    single = P(("pairs", "seq"), None)
    block = P("pairs", "seq")
    return jax.shard_map(
        per_device,
        mesh=mesh,
        in_specs=(rows, single, P("pairs")) + (P(),) * 21 + (rows, single),
        out_specs=(
            rows, single, rows, single,
            P(), block, block, block, block, P(), P(), block, block, P(),
            P(), block, block, P(), block, block, block, block, P(), block, block,
        ),
        check_vma=False,
    )
```

```python
import functools
import itertools

import jax
import jax.numpy as jnp
from jax import lax
from jax.experimental import pallas as pl
from jax.experimental.pallas import tpu as pltpu
from jax.sharding import PartitionSpec as P

EPSILON = 1e-06
EDGES = (12, 16, 23, 32, 46, 64, 91)
HIGHEST = lax.Precision.HIGHEST
MESH = pl.DeviceIdType.MESH
BF = jnp.bfloat16
F32 = jnp.float32


def mm(a, b):
    return jnp.dot(a, b, preferred_element_type=F32)
def mm_t(a, b):
    return lax.dot_general(a, b, (((1,), (1,)), ((), ())), preferred_element_type=F32)
def t_mm(a, b):
    return lax.dot_general(a, b, (((0,), (0,)), ((), ())), preferred_element_type=F32)

def rms_scale(v):
    return lax.rsqrt(jnp.mean(v * v, axis=-1, keepdims=True) + EPSILON)

def gelu_parts(u):
    u2 = u * u
    t = jnp.tanh(u * (0.7978845608 + (0.7978845608 * 0.044715) * u2))
    half = 0.5 + 0.5 * t
    return u * half, half + half * (1.0 - t) * u * (0.7978845608 + (3 * 0.7978845608 * 0.044715) * u2)

def norm_down(v, r, g, dy):
    vr = v * r
    gd = g * dy
    return r * (gd - vr * jnp.mean(vr * gd, axis=-1, keepdims=True)), vr * dy

def diagonal_buckets(shape, width):
    col = lax.broadcasted_iota(jnp.int32, shape, 1)
    offset = (col // 128 - 1) * 128 - lax.rem(col, 128)
    offset = jnp.where(col >= width - 128, 256, jnp.where(col >= width - 256, -256, offset))
    dist = jnp.abs(offset)
    bucket = jnp.full_like(dist, 8)
    for edge in EDGES:
        bucket = bucket + (dist >= edge).astype(jnp.int32)
    bucket = jnp.where(dist < 8, dist, bucket) + jnp.where(offset > 0, 16, 0)
    return jnp.where(bucket == lax.rem(lax.broadcasted_iota(jnp.int32, shape, 0), 32), 1.0, 0.0)


def forward_kernel(np_, ns, cut, lengths, table, ag, eg, fg, sg, cg, dg, dec_in, dec_cot, enc_in, enc_cot,
                   wq, wk, wv, wo, we, wr, sv, so, cq, ck, cv, co, fe, fr,
                   normed_t, q, k, v, probs, context_t, hidden, mixed_t, active, slope, block, low, x_out, cot_out,
                   rows_grad, dec_out, dec_in_grad, dec_gains, *rest):
    if cut:
        dec, *rest = rest
    else:
        left, right, wide, mids, *rest = rest
    (wqs, wks, wvs, wos, wes, wrs, svs, sos, cqs, cks, cvs, cos, fes, frs, xs, normed, nt, qs, ks, vs, ctx, hid,
     mixed, mt, act, slo, blk, rws, lws, rgs, band, vecs, v_t, s_t, pbuf, *rest) = rest
    if cut:
        left, right, wide, mids, cuts, both, *rest = rest
    sems, psem, osem, x_s, x_r, c_s, c_r, loc = rest
    ag, eg, fg, sg, cg, dg = (g[...].reshape(1, -1) for g in (ag, eg, fg, sg, cg, dg))
    n, width = normed.shape
    heads = probs.shape[0]
    size = width // heads
    ff = act.shape[1]
    slot = n // ns
    p = lax.axis_index("pairs")
    s = lax.axis_index("seq")
    length = lengths[s]

    barrier = pltpu.get_barrier_semaphore()
    for d in range(1, ns):
        pl.semaphore_signal(barrier, inc=1, device_id=(p, lax.rem(s + d, ns)), device_id_type=MESH)

    def rows_copy(src, dst, send, recv, d):
        t = lax.rem(s + d, ns)
        return pltpu.make_async_remote_copy(
            src_ref=src.at[t], dst_ref=dst.at[s], send_sem=send.at[d], recv_sem=recv.at[d],
            device_id=(p, t), device_id_type=MESH)

    x_copies = [rows_copy(enc_in, xs, x_s, x_r, d) for d in range(1, ns)]
    cot_copies = [rows_copy(enc_cot, cot_out, c_s, c_r, d) for d in range(1, ns)]
    keep_x = pltpu.make_async_copy(enc_in.at[s], xs.at[s], loc.at[0])
    keep_cot = pltpu.make_async_copy(enc_cot.at[s], cot_out.at[s], loc.at[1])
    keep_x.start()
    load = []
    for src, dst in ((sv, svs), (so, sos), (cq, cqs), (ck, cks), (fr, frs), (wq, wqs), (wk, wks), (wv, wvs),
                     (wo, wos), (we, wes), (wr, wrs), (cv, cvs), (co, cos), (fe, fes)):
        load.append(pltpu.make_async_copy(src, dst, sems.at[len(load)]))
        load[-1].start()
    pl.semaphore_wait(barrier, ns - 1)
    for copy in x_copies + cot_copies:
        copy.start()
    keep_cot.start()
    saved = []

    def save(src, dst):
        copy = pltpu.make_async_copy(src, dst, osem.at[len(saved)])
        saved.append(copy)
        copy.start()

    vec = lax.dot_general(table[...], diagonal_buckets((table.shape[1], width), width), (((1,), (0,)), ((), ())),
                          precision=HIGHEST, preferred_element_type=F32)
    for i in range(width // 128):
        vecs[:, i, :] = vec[:, i * 128:(i + 1) * 128]
    lane_s = lax.broadcasted_iota(jnp.int32, (128, 128), 1)
    row_s = lax.broadcasted_iota(jnp.int32, (128, 128), 0)

    @pl.loop(0, heads)
    def _(h):
        for b in range(3):
            t = jnp.where(lane_s + row_s < 128, vecs[h, b:b + 1, :], vecs[h, b + 1:b + 2, :])
            for bit in range(7):
                t = jnp.where((row_s >> bit) % 2 == 1, pltpu.roll(t, 1 << bit, 1), t)
            band[h, b * 128:(b + 1) * 128, :] = t

    x = dec_in[...].astype(F32)
    cot = dec_cot[...]
    own = (lax.broadcasted_iota(jnp.int32, (heads, width), 1) // size
           == lax.broadcasted_iota(jnp.int32, (heads, width), 0))

    def spread(r):
        return jnp.where(own, r.astype(F32), 0.0).astype(BF)

    def collect(r):
        return jnp.sum(jnp.where(own, r, 0.0), axis=0, keepdims=True)

    x_r = rms_scale(x)
    self_normed = (x * x_r * sg).astype(BF)
    load[0].wait()
    self_values = mm(self_normed, svs[...]).astype(BF)
    load[1].wait()
    after = x + mm(self_values, sos[...])
    after_r = rms_scale(after)
    cross_normed = (after * after_r * cg).astype(BF)
    load[2].wait()
    cross_q = mm(cross_normed, cqs[...]).astype(BF)
    load[3].wait()
    q_rows = mm_t(spread(cross_q), cks[...]).astype(BF)
    load[4].wait()
    active_back = mm_t(cot, frs[...])

    keep_x.wait()
    for copy in x_copies:
        copy.wait()
    save(xs, x_out)
    for i in range(ns):
        r = slice(i * slot, (i + 1) * slot)
        t = xs[i].astype(F32)
        t = t * rms_scale(t) * ag
        normed[r] = t.astype(BF)
        nt[:, r] = t.T.astype(BF)
    save(nt, normed_t)
    for j, (w, out, dst) in enumerate(((wqs, qs, q), (wks, ks, k), (wvs, vs, v))):
        load[5 + j].wait()
        for i in range(2):
            r = slice(i * (n // 2), (i + 1) * (n // 2))
            out[r] = mm(normed[r], w[...]).astype(BF)
        save(out, dst)

    lane = lax.broadcasted_iota(jnp.int32, (n, 128), 1)
    row = lax.broadcasted_iota(jnp.int32, (n, 128), 0)
    q_mark = jnp.where(lane == 0, 1.0, 0.0).astype(BF)
    k_mark = jnp.where((lane == 0) & (row >= length), -1e30, 0.0).astype(BF)

    def keep(h, a):
        return pltpu.make_async_copy(pbuf.at[a], probs.at[h], psem.at[a])

    @pl.loop(0, heads // 2)
    def _(g):
        cols = pl.ds(pl.multiple_of(g * 128, 128), 128)
        v_t[...] = vs[:, cols].T
        qq = jnp.concatenate([qs[:, cols], q_mark], axis=1)
        kp = ks[:, cols]
        for a in range(2):
            h = 2 * g + a
            mine = (lane < 64) if a == 0 else (lane >= 64)
            kk = jnp.concatenate([jnp.where(mine, kp, jnp.zeros_like(kp)), k_mark], axis=1)
            s_t[a] = mm_t(kk, qq)

            @pl.when(g > 0)
            def _():
                keep(h - 2, a).wait()

            for j in range(n // 128):
                tile = []
                for i in range(n // 128):
                    t = s_t[a, i * 128:(i + 1) * 128, j * 128:(j + 1) * 128]
                    if abs(i - j) <= 1:
                        t = t + band[h, (i - j + 1) * 128:(i - j + 2) * 128, :]
                    else:
                        f = 5 if i > j else 4
                        t = t + vecs[h, f:f + 1, :]
                    tile.append(t)
                t = jnp.concatenate(tile, axis=0)
                m = jnp.max(t, axis=0, keepdims=True)
                e = jnp.exp(t - m)
                total = jnp.sum(e, axis=0, keepdims=True)
                pbuf[a, :, j * 128:(j + 1) * 128] = (e * (1.0 / total)).astype(BF)
            ctx[pl.ds(pl.multiple_of(h * 64, 64), 64), :] = mm(v_t[a * 64:(a + 1) * 64, :], pbuf[a]).astype(BF)
            keep(h, a).start()

    save(ctx, context_t)
    load[8].wait()
    for i in range(ns):
        r = slice(i * slot, (i + 1) * slot)
        t = xs[i].astype(F32) + mm(ctx[:, r].T, wos[...])
        hid[r] = t
        t = t * rms_scale(t) * eg
        mixed[r] = t.astype(BF)
        mt[:, r] = t.T.astype(BF)
    save(hid, hidden)
    save(mt, mixed_t)
    load[9].wait()

    @pl.loop(0, ff // 512)
    def _(j):
        cols = pl.ds(pl.multiple_of(j * 512, 512), 512)
        a, b = gelu_parts(mm(mixed[...], wes[:, cols]))
        act[:, cols] = a.astype(BF)
        slo[:, cols] = b.astype(BF)

    save(act, active)
    save(slo, slope)
    load[10].wait()
    for i in range(2):
        r = slice(i * (n // 2), (i + 1) * (n // 2))
        alive = (lax.broadcasted_iota(jnp.int32, (n // 2, 1), 0) + i * (n // 2) < length).astype(F32)
        b = alive * (hid[r] + mm(act[r], wrs[...]))
        blk[r] = b
        lws[r] = b.astype(BF)
        rws[r] = (b * rms_scale(b) * fg).astype(BF)
    save(blk, block)
    save(lws, low)

    score = mm_t(q_rows, rws[...])
    score = jnp.where(lax.broadcasted_iota(jnp.int32, score.shape, 1) < length, score, -1e30)
    e = jnp.exp(score - jnp.max(score, axis=-1, keepdims=True))
    cross_probs = e / jnp.sum(e, axis=-1, keepdims=True)
    cross_low = cross_probs.astype(BF)
    mean_rows = mm(cross_low, rws[...]).astype(BF)
    for copy in load[11:]:
        copy.wait()
    cross_context = collect(mm(mean_rows, cvs[...])).astype(BF)
    middle = after + mm(cross_context, cos[...])
    middle_r = rms_scale(middle)
    feed_normed = (middle * middle_r * dg).astype(BF)
    dec_active, dec_slope = gelu_parts(mm(feed_normed, fes[...]))
    dec_active = dec_active.astype(BF)
    upper_grad = (dec_slope * active_back).astype(BF)
    middle_down, feed_gain = norm_down(middle, middle_r, dg, mm_t(upper_grad, fes[...]))
    middle_grad = cot.astype(F32) + middle_down
    cross_branch = middle_grad.astype(BF)
    context_grad = mm_t(cross_branch, cos[...]).astype(BF)
    g_rows = mm_t(spread(context_grad), cvs[...]).astype(BF)
    prob_grad = mm_t(g_rows, rws[...])
    score_grad = (cross_probs * (prob_grad - jnp.sum(cross_probs * prob_grad, axis=-1, keepdims=True))).astype(BF)
    pad = jnp.zeros((16 - heads % 16, n), BF)
    padw = jnp.zeros((16 - heads % 16, width), BF)
    rgs[...] = t_mm(jnp.concatenate([score_grad, pad, cross_low, pad], axis=0),
                    jnp.concatenate([q_rows, padw, g_rows, padw], axis=0)).astype(BF)
    save(rgs, rows_grad)
    score_rows = mm(score_grad, rws[...]).astype(BF)
    cross_q_grad = collect(mm(score_rows, cks[...])).astype(BF)
    after_down, cross_gain = norm_down(after, after_r, cg, mm_t(cross_q_grad, cqs[...]))
    after_grad = middle_grad + after_down
    self_branch = after_grad.astype(BF)
    self_values_grad = mm_t(self_branch, sos[...]).astype(BF)
    x_down, self_gain = norm_down(x, x_r, sg, mm_t(self_values_grad, svs[...]))
    dec_in_grad[...] = (after_grad + x_down).astype(BF)
    dec_out[...] = (middle + mm(dec_active, frs[...])).astype(BF)
    gains = dec_gains
    gains[0:1, :] = self_gain
    gains[1:2, :] = cross_gain
    gains[2:3, :] = feed_gain
    for i, r in enumerate((self_normed, self_values, cross_normed, cross_context, feed_normed)):
        left[i:i + 1, :] = r.astype(F32)
    for i, r in enumerate((self_values_grad, self_branch, cross_q_grad, cross_branch, cross_q, context_grad, cot)):
        right[i:i + 1, :] = r.astype(F32)
    wide[0:1, :] = dec_active.astype(F32)
    wide[1:2, :] = upper_grad.astype(F32)
    mids[0] = score_rows.astype(F32)
    mids[1] = mean_rows.astype(F32)
    if cut:
        rows, cols, step = width // np_, width // ns, heads // ns
        both[...] = jnp.zeros_like(both)
        cuts[...] = jnp.zeros_like(cuts)
        for j in range(ns):
            for i in range(7):
                t = right[i:i + 1, j * cols:(j + 1) * cols]
                both[j, 2 * i:2 * i + 1, :] = t[:, :128]
                both[j, 2 * i + 1:2 * i + 2, 0:cols - 128] = t[:, 128:]
            for i in range(6):
                lo = j * width + i * 128
                both[j, 14 + i:15 + i, :] = wide[1:2, lo:lo + 128]
        for i in range(np_):
            cuts[0:5, 0:rows] = left[0:5, i * rows:(i + 1) * rows]
            for a in range(3):
                lo = i * (ff // np_) + a * 128
                cuts[5 + a:6 + a, :] = wide[0:1, lo:lo + 128]
            for j in range(ns):
                for w in range(2):
                    cuts[8 + w * step:8 + (w + 1) * step, 0:rows] = (
                        mids[w, j * step:(j + 1) * step, i * rows:(i + 1) * rows])
                dec[i * ns + j, 0:16, :] = cuts[...].astype(BF)
                dec[i * ns + j, 16:48, :] = both[j].astype(BF)
    for a in range(2):
        keep(heads - 2 + a, a).wait()
    keep_cot.wait()
    for copy in cot_copies:
        copy.wait()
    for copy in saved:
        copy.wait()


def forward(np_, ns, cut, lengths, table, gains, dec_in, dec_cot, enc_in, enc_cot, weights):
    group, slot, width = enc_in.shape
    n = slot * ns
    ff = weights[4].shape[1]
    heads = table.shape[0]
    smem = pl.BlockSpec(memory_space=pltpu.SMEM)
    vm = pl.BlockSpec(memory_space=pltpu.VMEM)
    hb = pl.BlockSpec(memory_space=pl.ANY)
    S = jax.ShapeDtypeStruct
    V = pltpu.VMEM
    full, tall, floats, broad = ((n, width), BF), ((width, n), BF), ((n, width), F32), ((n, ff), BF)
    slots = ((ns, slot, width), BF)
    raw = [((5, width), F32), ((7, width), F32), ((2, ff), F32), ((2, heads, width), F32)]
    outs = [tall, full, full, full, ((heads, n, n), BF), tall, floats, tall, broad, broad, floats, full, slots, slots,
            full, ((1, width), BF), ((1, width), BF), ((3, width), F32)]
    outs += [((np_ * ns, 48, 128), BF)] if cut else raw
    scratch = [slots, full, tall, full, full, full, tall, floats, full, tall, broad, broad, floats, full, full, full,
               ((heads, 384, 128), F32), ((heads, 8, 128), F32), ((128, n), BF), ((2, n, n), F32), ((2, n, n), BF)]
    scratch += raw + [((16, 128), F32), ((ns, 32, 128), F32)] if cut else []
    dma = pltpu.SemaphoreType.DMA
    return pl.pallas_call(
        functools.partial(forward_kernel, np_, ns, cut),
        out_shape=tuple(S(*t) for t in outs),
        in_specs=[smem] + [vm] * 9 + [hb] * 16,
        out_specs=(hb,) * 15 + (vm,) * (len(outs) - 15),
        scratch_shapes=[V(w.shape, BF) for w in weights] + [V(*t) for t in scratch] + [
            dma((14,)), dma((2,)), dma((16,)), dma((ns,)), dma((ns,)), dma((ns,)), dma((ns,)), dma((2,))],
        compiler_params=pltpu.CompilerParams(
            collective_id=1, has_side_effects=True, vmem_limit_bytes=62 * 1024 * 1024),
        name="forward",
    )(lengths, table, *gains, dec_in, dec_cot, enc_in, enc_cot, *weights)


def finish_kernel(heads, red, small, dec, dec_row, dec_grad, enc, grad, *outs):
    (enc_out, grad_out, row_out, row_grad_out, qo, ko, vo, oo, expand, reduce, bias, g0, g1, g2, g3, g4, g5,
     sv, so, cq, ck, cv, co, fe, fr, wide) = outs
    enc_out[...] = enc[...]
    grad_out[...] = grad[...]
    row_out[...] = dec_row[...]
    row_grad_out[...] = dec_grad[...]
    wide[...] = dec[...].astype(F32)
    rows, cols = qo.shape
    lanes = red.shape[2]
    for i, out in ((4, (qo, ko)), (5, (vo, oo))):
        t = red[i]
        out[0][...] = t[:, :cols]
        out[1][...] = t[:, cols:]
    for i in range(2):
        expand[:, i * lanes:(i + 1) * lanes] = red[i]
        reduce[i * rows:(i + 1) * rows, :] = red[2 + i]
    for h in range(heads):
        at = 36 + h // 4
        bias[h:h + 1, :] = small[at // 24, at % 24:at % 24 + 1, h % 4 * 32:h % 4 * 32 + 32]
    for i, out in enumerate((g0, g1, g2, g3, g4, g5)):
        for j in range(6):
            at = i * 6 + j
            out[pl.ds(j * 128, 128)] = small[at // 24, at % 24, :]

    def row(i):
        return wide[:, i, :]

    def pair(i):
        return jnp.concatenate([row(16 + 2 * i), row(17 + 2 * i)], axis=1)[:, :cols].astype(BF)

    for i, out in enumerate((sv, so, cq, co)):
        out[...] = t_mm(row(i)[:, :rows].astype(BF), pair(i))
    upper = jnp.concatenate([row(30 + i) for i in range(6)], axis=1).astype(BF)
    fe[...] = t_mm(row(4)[:, :rows].astype(BF), upper)
    active = jnp.concatenate([row(5 + i) for i in range(3)], axis=1).astype(BF)
    fr[...] = t_mm(pair(6), active)
    step = cols // 64
    for w, out in enumerate((ck, cv)):
        g = pair(4 + w)
        out[...] = jnp.concatenate(
            [t_mm(row(8 + w * step + h)[:, :rows].astype(BF), g[:, h * 64:(h + 1) * 64]) for h in range(step)], axis=1)


def finish(heads, buckets, red, small, dec, dec_row, dec_grad, enc, grad):
    rows, lanes = red.shape[1:]
    cols, width = lanes // 2, 2 * lanes
    vm = pl.BlockSpec(memory_space=pltpu.VMEM)
    S = jax.ShapeDtypeStruct
    block, broad, tall = S((rows, cols), F32), S((rows, width), F32), S((cols, lanes), F32)
    return pl.pallas_call(
        functools.partial(finish_kernel, heads),
        out_shape=(S(enc.shape, BF), S(grad.shape, BF), S(dec_row.shape, BF), S(dec_grad.shape, BF), block, block, block, block, broad, tall,
                   S((heads, buckets), F32)) + (S((width,), F32),) * 6 + (block,) * 6 + (broad, tall),
        in_specs=[vm] * 7,
        out_specs=(vm,) * 25,
        scratch_shapes=[pltpu.VMEM(dec.shape, F32)],
        compiler_params=pltpu.CompilerParams(vmem_limit_bytes=62 * 1024 * 1024),
        name="finish",
    )(red, small, dec, dec_row, dec_grad, enc, grad)


PARTS = 2
ORDERS = {
    "t00": "xfny",
    "t10": "fnyx",
    "t01": "nyfx",
    "t11": "yxfn",
    "w00": "nyfx",
    "w10": "yxfn",
    "w01": "xyfn",
    "w11": "ynxf",
    "a0": "xyfn",
    "a1": "xnyf",
}
SCHEDULE = {
    "wide": (
        ("t00", 0), ("t10", 0), ("t01", 0), ("t11", 0),
    ),
    "rows": (
        ("w00", 0),
    ),
    "dout": (
        ("w10", 0), ("w01", 0),
    ),
    "p00": (
        ("w11", 0), ("t00", 1),
    ),
    "p01": (
        ("t11", 1),
    ),
    "q0": (
        ("t01", 1), ("t10", 1), ("w01", 1), ("w10", 1),
    ),
    "p10": (
        ("t11", 2), ("h00", 0),
    ),
    "p11": (
        ("h01", 0), ("w00", 1), ("w10", 2), ("w11", 1),
    ),
    "p12": (
        ("t01", 2),
    ),
    "v1": (
        ("t00", 2), ("t10", 2), ("w01", 2), ("h00", 1),
    ),
    "ng1": (
        ("h10", 0), ("t11", 3),
    ),
    "end": (
        ("w00", 2), ("h11", 0), ("t10", 3), ("w10", 3), ("w11", 2), ("h01", 1),
        ("t00", 3), ("t01", 3), ("t11", 4), ("w01", 3), ("h10", 1), ("w10", 4),
        ("w00", 3), ("h01", 2), ("w01", 4), ("h11", 1), ("t00", 4), ("t10", 4),
        ("w11", 3), ("t01", 4), ("w00", 4), ("h10", 2), ("h11", 2), ("w11", 4),
        ("h10", 3), ("h11", 3),
    ),
}
HOPS = (0, 5)


def ff_pieces():
    names = [kind + str(unit) + str(i) for kind in "tw" for i in range(PARTS) for unit in range(2)]
    return names + ["h" + str(half) + str(w) for half in range(2) for w in range(2)]


def fused_kernel(np_, ns, length, fg, eg, ag, gains_dec,
                 rows_grad, block, cot, wr, active, wide_w, hidden, slope, mixed_t_in, wo, wq, wk, wv, q_in, k_in,
                 v_in, x_in, normed_t_in, context_t_in, probs, dec, encoded,
                 red, small_out, dec_out, enc_out, grad_out,
                 acts, grads, w1, wes, bg, hid, dm, rg, ct, rb, rb_t, mixed_t, normed_t, context_t,
                 dp, ds, pbuf, k_t, band, diag, fu, r0, r0a, r1, r2, r3, r4, a1, a2, a3, over0, over1,
                 sm, smr, smz, smf,
                 psem, isem, loc, f_s, f_r, t_s, t_r, o_s, o_r,
                 m_s, m_r, mz_s, mz_r, d_s, d_r, e_s, e_r, g_s, g_r):
    n, width = hid.shape
    ff = acts.shape[1]
    fg, eg, ag = (g[...].reshape(1, -1) for g in (fg, eg, ag))
    heads = probs.shape[0]
    nz = np_ // 2
    pieces = ff_pieces()
    rows, lanes = fu.shape[6:]
    step_rows = rows // PARTS
    count = np_ * ns
    p = lax.axis_index("pairs")
    s = lax.axis_index("seq")
    c = lax.rem(s, 2)
    y = s // 2
    xx = lax.rem(p, 2)
    z = p // 2
    me = p * ns + s
    core_peer = (p, s + 1 - 2 * c)
    y_peer = (p, lax.rem(s + 2, 4))
    x_peer = (p + 1 - 2 * xx, s)
    first_half, last_half = 1 - y, y
    own_at = {"x": xx, "y": y, "n": lax.rem(z, 2), "f": z // 2}
    peers = {"x": x_peer, "y": y_peer, "n": ((z + 1 - 2 * own_at["n"]) * 2 + xx, s),
             "f": (lax.rem(z + 2, 4) * 2 + xx, s)}

    def place(d):
        lin = lax.rem(me + d, count)
        return (lin // ns, lax.rem(lin, ns))

    barrier = pltpu.get_barrier_semaphore()

    @pl.loop(1, count)
    def _(d):
        pl.semaphore_signal(barrier, inc=1, device_id=place(d), device_id_type=MESH)

    def remote(src, dst, send, recv, peer):
        return pltpu.make_async_remote_copy(
            src_ref=src, dst_ref=dst, send_sem=send, recv_sem=recv,
            device_id=peer, device_id_type=MESH)

    def load(i, src, dst):
        return pltpu.make_async_copy(src, dst, isem.at[i])

    def part_of(ref, i):
        return ref.at[:, pl.ds(i * width, width)]

    loads = [load(i, a, b) for i, (a, b) in enumerate((
        (rows_grad, rg), (block, bg), (cot, ct), (active, acts), (wr, w1), (slope, grads), (mixed_t_in, mixed_t),
        (wide_w, wes), (hidden, hid), (normed_t_in, normed_t), (context_t_in, context_t)))]
    weights = [load(11 + i, a, w1.at[pl.ds(i * width, width)]) for i, a in enumerate((wo, wq, wk, wv))]
    heads_in = [load(15 + i, a, part_of(grads, i)) for i, a in enumerate((q_in, k_in, v_in, x_in))]
    d_out, dq, dk, dv = (part_of(acts, i) for i in range(4))
    q, k, v, x = (part_of(grads, i) for i in range(4))
    branch, dq_t, ng, in_grad, hidden_grad = ct, rb_t, dm, rg, bg
    wos, wqs, wks, wvs = (w1.at[pl.ds(i * width, width)] for i in range(4))

    def fetch(h, slot):
        return pltpu.make_async_copy(probs.at[h], pbuf.at[slot], psem.at[slot])

    def view(ref, dims, fixed):
        return ref.at[tuple(fixed.get(dim, slice(None)) for dim in dims)]

    def accumulate(dst, src, depth):
        for at in itertools.product(range(2), repeat=depth):
            dst[at] = dst[at] + src[at]

    def au(w, core, half):
        return fu.at[1 - c, 2 * w + core, half]

    def region(name, core):
        if name[0] == "h":
            return au(int(name[2]), core, first_half if name[1] == "0" else last_half), "fnx"
        unit = (2 if name[0] == "t" else 0) + int(name[1])
        return fu.at[core, unit, :, :, :, :, pl.ds(int(name[2]) * step_rows, step_rows)], "yfnx"

    def order_of(name):
        if name[0] != "h":
            return ORDERS[name]
        order = ORDERS["a" + name[2]]
        return order[:order.index("y")] if name[1] == "0" else order.replace("y", "")

    def core_copy(name):
        i = pieces.index(name)
        src, _ = region(name, 1 - c)
        dst = r0a.at[i - len(pieces) + 4] if name[0] == "h" else r0.at[i]
        return remote(src, dst, f_s.at[i], f_r.at[i], core_peer)

    def landing(name, j):
        i = pieces.index(name)
        if name[0] == "h":
            return (a1, a2, a3)[j].at[i - len(pieces) + 4]
        return (r1, r2, r3, r4)[j].at[i]

    def remaining(name, j):
        ref, dims = region(name, c)
        return ref, dims, {letter: own_at[letter] for letter in order_of(name)[:j]}

    def stage_copy(name, j):
        ref, dims, fixed = remaining(name, j)
        letter = order_of(name)[j]
        i = pieces.index(name)
        src = view(ref, dims, {**fixed, letter: 1 - own_at[letter]})
        return remote(src, landing(name, j), t_s.at[i, j], t_r.at[i, j], peers[letter])

    def hand_over(w):
        name = "h0" + str(w)
        ref, dims, fixed = remaining(name, len(order_of(name)))
        return remote(view(ref, dims, fixed), (over0, over1)[w], o_s.at[w], o_r.at[w], y_peer)

    def total_of(name):
        unit = 4 + int(name[2]) if name[0] == "h" else (2 if name[0] == "t" else 0) + int(name[1])
        if name[0] == "h":
            return red.at[unit]
        return red.at[unit, pl.ds(int(name[2]) * step_rows, step_rows)]

    def step(name, j):
        order = order_of(name)
        ref, dims, fixed = remaining(name, j)
        mine = view(ref, dims, fixed)
        depth = len(dims) - j
        closing = j == len(order) and name[:2] != "h0"
        joins = name[:2] == "h1" and ORDERS["a" + name[2]].index("y") == j
        if j == 0:
            core_copy(name).wait()
            landed = r0a.at[pieces.index(name) - len(pieces) + 4] if name[0] == "h" else r0.at[pieces.index(name)]
        else:
            stage_copy(name, j - 1).wait()
            landed = landing(name, j - 1)
        if joins:
            hand_over(int(name[2])).wait()
            extra = (over0, over1)[int(name[2])]
        if closing:
            total = mine[...].astype(F32) + landed[...].astype(F32)
            if joins:
                total = total + extra[...].astype(F32)
            total_of(name)[...] = total
            return
        accumulate(mine, landed, depth)
        if joins:
            accumulate(mine, extra, depth)
        if j < len(order):
            stage_copy(name, j).start()
        else:
            hand_over(int(name[2])).start()

    def run_slot(slot):
        for name, j in SCHEDULE.get(slot, ()):
            step(name, j)

    def dec_copy(d):
        to = place(d)
        return remote(dec.at[to[0] * ns + to[1]], dec_out.at[me], d_s.at[d], d_r.at[d], to)

    def enc_copy(d):
        t = lax.rem(s + d, ns)
        return remote(encoded.at[t], enc_out.at[s], e_s.at[d], e_r.at[d], (p, t))

    def grad_copy(d):
        t = lax.rem(s + d, ns)
        return remote(in_grad.at[t], grad_out.at[s], g_s.at[d], g_r.at[d], (p, t))

    keep_dec = pltpu.make_async_copy(dec.at[me], dec_out.at[me], loc.at[4])
    keep_enc = pltpu.make_async_copy(encoded.at[s], enc_out.at[s], loc.at[5])
    keep_grad = pltpu.make_async_copy(in_grad.at[s], grad_out.at[s], loc.at[6])

    for copy in loads:
        copy.start()
    fetch(first_half * (heads // 2), 0).start()
    fetch(first_half * (heads // 2) + 1, 1).start()
    keep_dec.start()
    keep_enc.start()
    diag[...] = jnp.zeros_like(diag)
    slot_rows = n // ns
    sm[...] = jnp.zeros_like(sm)

    def put_gain(i, gain):
        for j in range(width // 128):
            at = i * 6 + j
            sm[at // 24, at % 24:at % 24 + 1, :] = gain[:, j * 128:(j + 1) * 128]

    for i in range(3):
        put_gain(i, gains_dec[i:i + 1, :])
    for i in range(3):
        loads[i].wait()
    final_gain = jnp.zeros((1, width), F32)
    for i in range(ns):
        r = slice(i * slot_rows, (i + 1) * slot_rows)
        alive = (lax.broadcasted_iota(jnp.int32, (slot_rows, 1), 0) + i * slot_rows < length[s]).astype(F32)
        b = bg[r]
        down, gain = norm_down(b, rms_scale(b), fg, rg[i].astype(F32))
        b = alive * (ct[r].astype(F32) + down)
        bg[r] = b
        low = b.astype(BF)
        rb[r] = low
        rb_t[:, r] = low.T
        final_gain = final_gain + jnp.sum(gain, axis=0, keepdims=True)
    put_gain(3, final_gain)
    pl.semaphore_wait(barrier, count - 1)
    for d in range(1, ns):
        enc_copy(d).start()

    @pl.loop(1, count)
    def _(d):
        dec_copy(d).start()

    part = width // 4
    loads[3].wait()

    @pl.loop(0, nz)
    def _(b):
        cols = pl.ds(pl.multiple_of(b * 2 * lanes, 128), 2 * lanes)
        g = mm(rb_t[...], acts[:, cols]).astype(BF)
        for j in range(4):
            for half in range(2):
                lo = j * part + half * rows
                for e in range(2):
                    fu[j % 2, 2 + half, j // 2, b // 2, lax.rem(b, 2), e] = g[lo:lo + rows, e * lanes:(e + 1) * lanes]

    for name in pieces:
        if name[0] == "t":
            core_copy(name).start()
    loads[4].wait()
    loads[5].wait()

    for j in range(ff // width):
        cols = slice(j * width, (j + 1) * width)
        grads[:, cols] = (grads[:, cols].astype(F32) * mm_t(rb[...], w1[cols, :])).astype(BF)
        run_slot("ug" + str(j))

    for copy in weights:
        copy.start()
    loads[6].wait()

    @pl.loop(0, 4)
    def _(j):
        cols = pl.ds(pl.multiple_of(j * 2 * lanes, 128), 2 * lanes)
        g = mm(mixed_t[...], grads[:, cols]).astype(BF)
        for half in range(2):
            fu[lax.rem(j, 2), half, j // 2] = g[:, half * lanes:(half + 1) * lanes].reshape(2, 2, 2, rows, lanes)

    for name in pieces:
        if name[0] == "w":
            core_copy(name).start()
    run_slot("wide")
    loads[7].wait()
    dm[...] = mm_t(grads[...], wes[...])
    for copy in heads_in:
        copy.start()
    run_slot("dm")
    loads[8].wait()
    expand_gain = jnp.zeros((1, width), F32)
    for i in range(ns):
        r = slice(i * slot_rows, (i + 1) * slot_rows)
        t = hid[r]
        down, gain = norm_down(t, rms_scale(t), eg, dm[r])
        t = bg[r] + down
        bg[r] = t
        branch[r] = t.astype(BF)
        expand_gain = expand_gain + jnp.sum(gain, axis=0, keepdims=True)
    put_gain(4, expand_gain)
    run_slot("rows")
    weights[0].wait()

    @pl.loop(0, width // 384)
    def _(j):
        cols = pl.ds(pl.multiple_of(j * 384, 128), 384)
        d_out[:, cols] = mm_t(branch[...], w1[cols, :]).astype(BF)

    for copy in heads_in:
        copy.wait()
    for copy in loads[9:]:
        copy.wait()

    run_slot("dout")

    lane = lax.broadcasted_iota(jnp.int32, (n, 128), 1)
    lane_s = lax.broadcasted_iota(jnp.int32, (128, 128), 1)
    row_s = lax.broadcasted_iota(jnp.int32, (128, 128), 0)

    def pair(half, g):
        cols = pl.ds(pl.multiple_of(half * (width // 2) + g * 128, 128), 128)
        k_t[...] = k[:, cols].T
        dop = d_out[:, cols]
        qp = q[:, cols]
        vp = v[:, cols]
        zero = jnp.zeros_like(qp)
        for a in range(2):
            h = half * (heads // 2) + 2 * g + a
            mine = (lane < 64) if a == 0 else (lane >= 64)
            dp[...] = mm_t(jnp.where(mine, vp, zero), dop)
            fetch(h, a).wait()
            for j in range(n // 128):
                pj = pbuf[a, :, j * 128:(j + 1) * 128].astype(F32)
                pd = pj * dp[:, j * 128:(j + 1) * 128]
                total = jnp.sum(pd, axis=0, keepdims=True)
                sg = pd - pj * total
                ds[:, j * 128:(j + 1) * 128] = sg.astype(BF)
                for i in range(n // 128):
                    t = sg[i * 128:(i + 1) * 128]
                    if abs(i - j) <= 1:
                        b = (i - j + 1) * 128
                        if j == 0 or (j == 1 and i == 0):
                            band[b:b + 128, :] = t
                        else:
                            band[b:b + 128, :] += t
                    else:
                        f = 5 if i > j else 4
                        diag[h, f:f + 1, :] += jnp.sum(t, axis=0, keepdims=True)
            dvp = mm(pbuf[a], jnp.where(mine, dop, zero))
            dkp = mm(ds[...], jnp.where(mine, qp, zero))
            dq_t[pl.ds(pl.multiple_of(h * 64, 64), 64), :] = mm(k_t[a * 64:(a + 1) * 64, :], ds[...]).astype(BF)
            if a == 0:
                dk_sum, dv_sum = dkp, dvp
            else:
                dk[:, cols] = (dk_sum + dkp).astype(BF)
                dv[:, cols] = (dv_sum + dvp).astype(BF)
            for b in range(3):
                t = band[b * 128:(b + 1) * 128, :]
                for bit in range(7):
                    t = jnp.where((row_s >> bit) % 2 == 1, pltpu.roll(t, 128 - (1 << bit), 1), t)
                straight = jnp.sum(jnp.where(lane_s + row_s < 128, t, 0.0), axis=0, keepdims=True)
                whole = jnp.sum(t, axis=0, keepdims=True)
                diag[h, b:b + 1, :] += straight
                diag[h, b + 1:b + 2, :] += whole - straight

    def units_of(half, tag):
        cols = pl.ds(pl.multiple_of(half * (width // 2), 128), width // 2)
        dq_h = dq_t[cols, :].T
        dq[:, cols] = dq_h
        dk_h = dk[:, cols]
        for cc in range(2):
            e = slice(cc * part, (cc + 1) * part)
            g = mm(normed_t[...], jnp.concatenate([dq_h[:, e], dk_h[:, e]], axis=1))
            au(0, cc, half)[...] = g.astype(BF).reshape(2, 2, 2, rows, lanes)
        core_copy("h" + tag + "0").start()
        run_slot("q" + tag)
        dv_h = dv[:, cols]
        br_h = branch[:, cols]
        zero = jnp.zeros((n, part), BF)
        for cc in range(2):
            e = slice(cc * part, (cc + 1) * part)
            g = (mm(normed_t[...], jnp.concatenate([dv_h[:, e], zero], axis=1))
                 + mm(context_t[...], jnp.concatenate([zero, br_h[:, e]], axis=1)))
            au(1, cc, half)[...] = g.astype(BF).reshape(2, 2, 2, rows, lanes)
        core_copy("h" + tag + "1").start()
        run_slot("v" + tag)

    quarter = heads // 4

    @pl.loop(0, quarter)
    def _(g):
        pair(first_half, g)
        nxt = jnp.where(g == quarter - 1, last_half * (heads // 2), first_half * (heads // 2) + 2 * (g + 1))
        fetch(nxt, 0).start()
        fetch(nxt + 1, 1).start()

        for i in range(quarter):
            if SCHEDULE.get("p0" + str(i)):
                @pl.when(g == i)
                def _():
                    run_slot("p0" + str(i))

    units_of(first_half, "0")

    @pl.loop(0, quarter)
    def _(g):
        pair(last_half, g)

        @pl.when(g < quarter - 1)
        def _():
            nxt = last_half * (heads // 2) + 2 * (g + 1)
            fetch(nxt, 0).start()
            fetch(nxt + 1, 1).start()

        for i in range(quarter):
            if SCHEDULE.get("p1" + str(i)):
                @pl.when(g == i)
                def _():
                    run_slot("p1" + str(i))

    units_of(last_half, "1")
    for copy in weights[1:]:
        copy.wait()

    for i in range(2):
        r = slice(i * (n // 2), (i + 1) * (n // 2))
        ng[r] = mm_t(dq[r], wqs[...]) + mm_t(dk[r], wks[...]) + mm_t(dv[r], wvs[...])
        run_slot("ng" + str(i))

    gain_sum = jnp.zeros((1, width), F32)
    for i in range(ns):
        r = slice(i * slot_rows, (i + 1) * slot_rows)
        t = x[r].astype(F32)
        down, gain = norm_down(t, rms_scale(t), ag, ng[r])
        in_grad[i] = (hidden_grad[r] + down).astype(BF)
        gain_sum = gain_sum + jnp.sum(gain, axis=0, keepdims=True)
    keep_grad.start()
    for d in range(1, ns):
        grad_copy(d).start()

    pick = diagonal_buckets((128, width), width)
    bias = jnp.zeros((16, 128), F32)
    for i in range(width // 128):
        bias = bias + lax.dot_general(diag[:, i, :], pick[:, i * 128:(i + 1) * 128], (((1,), (1,)), ((), ())),
                                      precision=HIGHEST, preferred_element_type=F32)
    place_of = lax.broadcasted_iota(jnp.int32, (1, 128), 1) // 32
    for h in range(heads):
        at = 36 + h // 4
        sm[at // 24, at % 24:at % 24 + 1, :] += jnp.where(place_of == h % 4, bias[h:h + 1, :], 0.0)
    put_gain(5, gain_sum)

    chips = 2 * np_
    chip = 2 * p + y
    small_first = remote(sm.at[1 - c], smr, m_s.at[0], m_r.at[0], core_peer)
    small_last = remote(smf.at[c], smf.at[c], m_s.at[1], m_r.at[1], core_peer)

    def small_copy(d):
        to = lax.rem(chip + d, chips)
        return remote(smz.at[chip], smz.at[chip], mz_s.at[d], mz_r.at[d], (to // 2, lax.rem(to, 2) * 2 + c))

    small_first.start()
    tail = SCHEDULE["end"]
    for i, (name, j) in enumerate(tail):
        step(name, j)
        if i == HOPS[0]:
            small_first.wait()
            smz[chip] = sm[c] + smr[...]

            @pl.loop(1, chips)
            def _(d):
                small_copy(d).start()
        if i == len(tail) - HOPS[1]:
            @pl.loop(1, chips)
            def _(d):
                small_copy(d).wait()

            total = smz[0]
            for other in range(1, chips):
                total = total + smz[other]
            smf[c] = total
            small_last.start()

    small_last.wait()
    small_out[...] = smf[...]
    keep_dec.wait()
    keep_enc.wait()
    keep_grad.wait()
    for d in range(1, ns):
        enc_copy(d).wait()
        grad_copy(d).wait()

    @pl.loop(1, count)
    def _(d):
        dec_copy(d).wait()


def fused(np_, ns, length, fg, eg, ag, gains_dec, rows_grad, block, cot, wr, active, we, hidden, slope, mixed_t,
          wo, wq, wk, wv, q, k, v, x, normed_t, context_t, probs, dec, encoded):
    n, width = hidden.shape
    ff = active.shape[1]
    heads = probs.shape[0]
    nz = np_ // 2
    rows, lanes = width // np_, ff // np_
    count = np_ * ns
    smem = pl.BlockSpec(memory_space=pltpu.SMEM)
    vm = pl.BlockSpec(memory_space=pltpu.VMEM)
    hb = pl.BlockSpec(memory_space=pl.ANY)
    S = jax.ShapeDtypeStruct
    V = pltpu.VMEM
    dma = pltpu.SemaphoreType.DMA
    nar, tall = V((n, width), BF), V((width, n), BF)
    floats = V((n, width), F32)
    slots = (ns, n // ns, width)
    small = (2, 24, 128)
    ffs = 4 * PARTS
    sub = rows // PARTS

    def joint(w):
        return V((2,) * (3 - ORDERS["a" + str(w)].index("y")) + (rows, lanes), BF)

    return pl.pallas_call(
        functools.partial(fused_kernel, np_, ns),
        out_shape=(S((6, rows, lanes), F32), S(small, F32), S(dec.shape, BF), S(slots, BF), S(slots, BF)),
        in_specs=[smem] + [vm] * 4 + [hb] * 22,
        out_specs=(vm, vm, hb, hb, hb),
        scratch_shapes=[
            V((n, ff), BF), V((n, ff), BF), V((ff, width), BF), V((width, ff), BF), floats, floats, floats,
            V(slots, BF), nar, nar, tall, tall, tall, tall,
            V((n, n), F32), V((n, n), BF), V((2, n, n), BF), V((128, n), BF), V((384, 128), F32), V((16, 8, 128), F32),
            V((2, 4, 2, 2, 2, 2, rows, lanes), BF), V((ffs, 2, 2, 2, 2, sub, lanes), BF), V((4, 2, 2, 2, rows, lanes), BF),
            V((ffs, 2, 2, 2, sub, lanes), BF), V((ffs, 2, 2, sub, lanes), BF), V((ffs, 2, sub, lanes), BF),
            V((ffs, sub, lanes), BF), V((4, 2, 2, rows, lanes), BF), V((4, 2, rows, lanes), BF),
            V((4, rows, lanes), BF), joint(0), joint(1),
            V(small, F32), V(small[1:], F32), V((2 * np_,) + small[1:], F32), V(small, F32),
            dma((2,)), dma((19,)), dma((7,)), dma((ffs + 4,)), dma((ffs + 4,)), dma((ffs + 4, 4)), dma((ffs + 4, 4)),
            dma((2,)), dma((2,)),
            dma((2,)), dma((2,)), dma((2 * np_,)), dma((2 * np_,)), dma((count,)), dma((count,)),
            dma((ns,)), dma((ns,)), dma((ns,)), dma((ns,)),
        ],
        compiler_params=pltpu.CompilerParams(
            collective_id=0, has_side_effects=True, vmem_limit_bytes=62 * 1024 * 1024),
        name="fused_backward",
    )(length, fg, eg, ag, gains_dec, rows_grad.reshape(slots), block, cot, wr,
      active, we, hidden, slope, mixed_t, wo, wq, wk, wv, q, k, v, x, normed_t, context_t, probs, dec,
      encoded.reshape(slots))


def feed_back_kernel(length, rows_grad, block, cot, fg, hidden, eg, mixed, active, slope, wr, we,
                     wide, tall, hidden_grad, branch, gains, wrs, wes, bg, rb, rb_t, ug, mixed_t, dmixed, sems):
    n, width = block.shape
    ff = active.shape[1]
    groups, lanes = tall.shape[3], tall.shape[5]
    cols_dev = width // 4
    copies = [pltpu.make_async_copy(a, b, sems.at[i]) for i, (a, b) in enumerate(((wr, wrs), (we, wes)))]
    for c in copies:
        c.start()
    gains[...] = jnp.zeros_like(gains)

    @pl.loop(0, n // 128)
    def _(i):
        r = pl.ds(i * 128, 128)
        alive = (lax.broadcasted_iota(jnp.int32, (128, 1), 0) + i * 128 < length[0]).astype(F32)
        v = block[r]
        down, gain = norm_down(v, rms_scale(v), fg[...], rows_grad[r].astype(F32))
        b = alive * (cot[r].astype(F32) + down)
        bg[r] = b
        rb[r] = b.astype(BF)
        rb_t[:, pl.ds(pl.multiple_of(i * 128, 128), 128)] = b.T.astype(BF)
        mixed_t[:, pl.ds(pl.multiple_of(i * 128, 128), 128)] = mixed[r].T
        gains[0:1, :] += jnp.sum(gain, axis=0, keepdims=True)

    copies[0].wait()

    @pl.loop(0, ff // 256)
    def _(j):
        cols = pl.ds(pl.multiple_of(j * 256, 256), 256)
        ug[:, cols] = (slope[:, cols].astype(F32) * mm_t(rb[...], wrs[cols, :])).astype(BF)

    copies[1].wait()

    @pl.loop(0, width // 256)
    def _(j):
        cols = pl.ds(pl.multiple_of(j * 256, 256), 256)
        dmixed[:, cols] = mm_t(ug[...], wes[cols, :])

    @pl.loop(0, n // 128)
    def _(i):
        r = pl.ds(i * 128, 128)
        v = hidden[r]
        down, gain = norm_down(v, rms_scale(v), eg[...], dmixed[r])
        h = bg[r] + down
        hidden_grad[r] = h
        branch[r] = h.astype(BF)
        gains[1:2, :] += jnp.sum(gain, axis=0, keepdims=True)

    @pl.loop(0, 4)
    def _(j):
        for half in range(2):
            cols = pl.ds(pl.multiple_of(j * (ff // 4) + half * (ff // 8), 128), ff // 8)
            wide[half, lax.rem(j, 2), j // 2] = mm(mixed_t[...], ug[:, cols]).astype(BF)

    chunk = ff // 8
    per_group = lanes // chunk

    @pl.loop(0, 8)
    def _(i):
        cols = pl.ds(pl.multiple_of(i * chunk, 128), chunk)
        g = mm(rb_t[...], active[:, cols]).astype(BF)
        for j in range(4):
            for half in range(2):
                r = j * cols_dev + half * (cols_dev // 2)
                part = g[r:r + cols_dev // 2]
                if per_group == 1:
                    tall[half, j % 2, j // 2, i] = part
                else:
                    tall[half, j % 2, j // 2, 0, :, cols] = part


def feed_back(groups, length, rows_grad, block, cot, fg, hidden, eg, mixed, active, slope, wr, we):
    n, width = block.shape
    ff = active.shape[1]
    sm = pl.BlockSpec(memory_space=pltpu.SMEM)
    vm = pl.BlockSpec(memory_space=pltpu.VMEM)
    hb = pl.BlockSpec(memory_space=pl.ANY)
    S = jax.ShapeDtypeStruct
    V = pltpu.VMEM
    return pl.pallas_call(
        feed_back_kernel,
        out_shape=(S((2, 2, 2, width, ff // 8), BF),
                   S((2, 2, 2, groups, width // 8, ff // groups), BF), S((n, width), F32), S((n, width), BF), S((2, width), F32)),
        in_specs=[sm] + [vm] * 9 + [hb] * 2,
        out_specs=(vm,) * 5,
        scratch_shapes=[V(wr.shape, BF), V(we.shape, BF), V((n, width), F32), V((n, width), BF), V((width, n), BF),
                        V((n, ff), BF), V((width, n), BF), V((n, width), F32), pltpu.SemaphoreType.DMA((2,))],
        compiler_params=pltpu.CompilerParams(vmem_limit_bytes=60 * 1024 * 1024),
        name="feed_back",
    )(length, rows_grad, block, cot, fg.reshape(1, -1), hidden, eg.reshape(1, -1), mixed, active, slope, wr, we)


def backward_kernel(np_, ns, x, ag, q, k, v, context_t, branch, hidden_grad, normed, gains_dec, gains_feed,
                    probs, wo, wq, wk, wv, wide, tall, dec, encoded,
                    red, small_out, dec_out, enc_out, grad_out,
                    wos, wqs, wks, wvs, d_out, dp, ds, dq_t, dq, dk, dv, k_t, normed_t, ng, in_grad,
                    pbuf, band, diag, own, au, r0, r1y, r1x, r1a, r2, r3, sm, smr, smz,
                    psem, wsem, loc, c_s, c_r, a_s, a_r, b_s, b_r, ac_s, ac_r, ax_s, ax_r, z_s, z_r,
                    m_s, m_r, mz_s, mz_r, d_s, d_r, e_s, e_r, g_s, g_r):
    n, width = x.shape
    heads = probs.shape[0]
    nz = np_ // 2
    rows, lanes = r0.shape[4:]
    count = np_ * ns
    p = lax.axis_index("pairs")
    s = lax.axis_index("seq")
    c = lax.rem(s, 2)
    y = s // 2
    xx = lax.rem(p, 2)
    z = p // 2
    me = p * ns + s
    core_peer = (p, s + 1 - 2 * c)
    y_peer = (p, lax.rem(s + 2, 4))
    x_peer = (p + 1 - 2 * xx, s)

    def place(d):
        lin = lax.rem(me + d, count)
        return (lin // ns, lax.rem(lin, ns))

    barrier = pltpu.get_barrier_semaphore()

    @pl.loop(1, count)
    def _(d):
        pl.semaphore_signal(barrier, inc=1, device_id=place(d), device_id_type=MESH)

    def remote(src, dst, send, recv, peer):
        return pltpu.make_async_remote_copy(
            src_ref=src, dst_ref=dst, send_sem=send, recv_sem=recv,
            device_id=peer, device_id_type=MESH)

    weights = [pltpu.make_async_copy(a, b, wsem.at[i])
               for i, (a, b) in enumerate(((wo, wos), (wq, wqs), (wk, wks), (wv, wvs)))]

    def fetch(h, slot):
        return pltpu.make_async_copy(probs.at[h], pbuf.at[slot], psem.at[slot])

    def unit(i, core):
        return (wide, tall)[i // 2].at[i % 2, core]

    def core_copy(i):
        return remote(unit(i, 1 - c), r0.at[i], c_s.at[i], c_r.at[i], core_peer)

    def own_copy(i):
        return pltpu.make_async_copy(unit(i, c), own.at[i], loc.at[i])

    def first(i):
        if i % 2 == 0:
            return remote(own.at[i, 1 - y], r1y.at[i // 2], a_s.at[i], a_r.at[i], y_peer)
        return remote(own.at[i, :, :, 1 - xx], r1x.at[i // 2], a_s.at[i], a_r.at[i], x_peer)

    def second(i):
        if i % 2 == 0:
            return remote(own.at[i, y, :, 1 - xx], r2.at[i], b_s.at[i], b_r.at[i], x_peer)
        return remote(own.at[i, 1 - y, :, xx], r2.at[i], b_s.at[i], b_r.at[i], y_peer)

    def final(i):
        return own.at[i, y] if i < 4 else au.at[i - 4, c, y]

    def last(i, d):
        t = lax.rem(z + d, nz)
        return remote(final(i).at[t, xx], r3.at[i, d], z_s.at[i, d], z_r.at[i, d], (t * 2 + xx, s))

    def attn_core(w, half):
        return remote(au.at[w, 1 - c, half], r0.at[4 + w, half], ac_s.at[w, half], ac_r.at[w, half], core_peer)

    def attn_x(w, half):
        return remote(au.at[w, c, half, :, 1 - xx], r1a.at[w, half], ax_s.at[w, half], ax_r.at[w, half], x_peer)

    def attn_y(w):
        return remote(au.at[w, c, 1 - y, :, xx], r2.at[4 + w], b_s.at[4 + w], b_r.at[4 + w], y_peer)

    def dec_copy(d):
        to = place(d)
        return remote(dec.at[to[0] * ns + to[1]], dec_out.at[me], d_s.at[d], d_r.at[d], to)

    def enc_copy(d):
        t = lax.rem(s + d, ns)
        return remote(encoded.at[t], enc_out.at[s], e_s.at[d], e_r.at[d], (p, t))

    def grad_copy(d):
        t = lax.rem(s + d, ns)
        return remote(in_grad.at[t], grad_out.at[s], g_s.at[d], g_r.at[d], (p, t))

    keep_dec = pltpu.make_async_copy(dec.at[me], dec_out.at[me], loc.at[4])
    keep_enc = pltpu.make_async_copy(encoded.at[s], enc_out.at[s], loc.at[5])
    keep_grad = pltpu.make_async_copy(in_grad.at[s], grad_out.at[s], loc.at[6])

    def step_a(i):
        core_copy(i).wait()
        own_copy(i).wait()

        @pl.loop(0, nz)
        def _(b):
            for a in range(2):
                for e in range(2):
                    own[i, a, b, e] = own[i, a, b, e] + r0[i, a, b, e]

        first(i).start()

    def step_b(i):
        first(i).wait()

        @pl.loop(0, nz)
        def _(b):
            for e in range(2):
                if i % 2 == 0:
                    own[i, y, b, e] = own[i, y, b, e] + r1y[i // 2, b, e]
                else:
                    own[i, e, b, xx] = own[i, e, b, xx] + r1x[i // 2, e, b]

        second(i).start()

    def step_c(i):
        if i < 4:
            second(i).wait()
        else:
            attn_y(i - 4).wait()

        @pl.loop(0, nz)
        def _(b):
            f = final(i)
            f[b, xx] = f[b, xx] + r2[i, b]

        @pl.loop(1, nz)
        def _(d):
            last(i, d).start()

    def step_d(i):
        red[i] = final(i)[z, xx].astype(F32)

        @pl.loop(1, nz)
        def _(d):
            last(i, d).wait()
            red[i] = red[i] + r3[i, d].astype(F32)

    def attn_a(w, half):
        attn_core(w, half).wait()

        @pl.loop(0, nz)
        def _(b):
            for e in range(2):
                au[w, c, half, b, e] = au[w, c, half, b, e] + r0[4 + w, half, b, e]

        attn_x(w, half).start()

    def attn_b(w, half):
        attn_x(w, half).wait()

        @pl.loop(0, nz)
        def _(b):
            au[w, c, half, b, xx] = au[w, c, half, b, xx] + r1a[w, half, b]

    for copy in weights:
        copy.start()
    first_half, last_half = 1 - y, y
    fetch(first_half * (heads // 2), 0).start()
    fetch(first_half * (heads // 2) + 1, 1).start()
    for i in range(4):
        own_copy(i).start()
    keep_dec.start()
    keep_enc.start()
    diag[...] = jnp.zeros_like(diag)
    weights[0].wait()

    @pl.loop(0, width // 384)
    def _(j):
        cols = pl.ds(pl.multiple_of(j * 384, 128), 384)
        d_out[:, cols] = mm_t(branch[...], wos[cols, :]).astype(BF)

    pl.semaphore_wait(barrier, count - 1)
    for i in range(4):
        core_copy(i).start()
    for d in range(1, ns):
        enc_copy(d).start()

    @pl.loop(1, count)
    def _(d):
        dec_copy(d).start()

    @pl.loop(0, n // 128)
    def _(i):
        r = pl.ds(pl.multiple_of(i * 128, 128), 128)
        normed_t[:, r] = normed[r].T

    lane = lax.broadcasted_iota(jnp.int32, (n, 128), 1)
    lane_s = lax.broadcasted_iota(jnp.int32, (128, 128), 1)
    row_s = lax.broadcasted_iota(jnp.int32, (128, 128), 0)

    def pair(half, g):
        cols = pl.ds(pl.multiple_of(half * (width // 2) + g * 128, 128), 128)
        k_t[...] = k[:, cols].T
        dop = d_out[:, cols]
        qp = q[:, cols]
        vp = v[:, cols]
        zero = jnp.zeros_like(qp)
        for a in range(2):
            h = half * (heads // 2) + 2 * g + a
            mine = (lane < 64) if a == 0 else (lane >= 64)
            dp[...] = mm_t(jnp.where(mine, vp, zero), dop)
            fetch(h, a).wait()
            for j in range(n // 128):
                pj = pbuf[a, :, j * 128:(j + 1) * 128].astype(F32)
                pd = pj * dp[:, j * 128:(j + 1) * 128]
                total = jnp.sum(pd, axis=0, keepdims=True)
                sg = pd - pj * total
                ds[:, j * 128:(j + 1) * 128] = sg.astype(BF)
                for i in range(n // 128):
                    t = sg[i * 128:(i + 1) * 128]
                    if abs(i - j) <= 1:
                        b = (i - j + 1) * 128
                        if j == 0 or (j == 1 and i == 0):
                            band[b:b + 128, :] = t
                        else:
                            band[b:b + 128, :] += t
                    else:
                        f = 5 if i > j else 4
                        diag[h, f:f + 1, :] += jnp.sum(t, axis=0, keepdims=True)
            dvp = mm(pbuf[a], jnp.where(mine, dop, zero))
            dkp = mm(ds[...], jnp.where(mine, qp, zero))
            dq_t[pl.ds(pl.multiple_of(h * 64, 64), 64), :] = mm(k_t[a * 64:(a + 1) * 64, :], ds[...]).astype(BF)
            if a == 0:
                dk_sum, dv_sum = dkp, dvp
            else:
                dk[:, cols] = (dk_sum + dkp).astype(BF)
                dv[:, cols] = (dv_sum + dvp).astype(BF)
            for b in range(3):
                t = band[b * 128:(b + 1) * 128, :]
                for bit in range(7):
                    t = jnp.where((row_s >> bit) % 2 == 1, pltpu.roll(t, 128 - (1 << bit), 1), t)
                straight = jnp.sum(jnp.where(lane_s + row_s < 128, t, 0.0), axis=0, keepdims=True)
                whole = jnp.sum(t, axis=0, keepdims=True)
                diag[h, b:b + 1, :] += straight
                diag[h, b + 1:b + 2, :] += whole - straight

    part = width // 4

    def units_of(half):
        cols = pl.ds(pl.multiple_of(half * (width // 2), 128), width // 2)
        lower = pl.ds(pl.multiple_of(half * (width // 2), 128), width // 2)
        dq_h = dq_t[lower, :].T
        dq[:, cols] = dq_h
        dk_h = dk[:, cols]
        dv_h = dv[:, cols]
        br_h = branch[:, cols]
        zero = jnp.zeros((n, part), BF)
        for cc in range(2):
            e = slice(cc * part, (cc + 1) * part)
            g = mm(normed_t[...], jnp.concatenate([dq_h[:, e], dk_h[:, e]], axis=1))
            au[0, cc, half] = g.astype(BF).reshape(nz, 2, rows, lanes)
            g = (mm(normed_t[...], jnp.concatenate([dv_h[:, e], zero], axis=1))
                 + mm(context_t[...], jnp.concatenate([zero, br_h[:, e]], axis=1)))
            au[1, cc, half] = g.astype(BF).reshape(nz, 2, rows, lanes)
        for w in range(2):
            attn_core(w, half).start()

    quarter = heads // 4

    @pl.loop(0, quarter)
    def _(g):
        pair(first_half, g)
        nxt = jnp.where(g == quarter - 1, last_half * (heads // 2), first_half * (heads // 2) + 2 * (g + 1))
        fetch(nxt, 0).start()
        fetch(nxt + 1, 1).start()

        @pl.when(g == 0)
        def _():
            step_a(0)
            step_a(1)

        @pl.when(g == 1)
        def _():
            step_a(2)
            step_a(3)

    units_of(first_half)

    @pl.loop(0, quarter)
    def _(g):
        pair(last_half, g)

        @pl.when(g < quarter - 1)
        def _():
            nxt = last_half * (heads // 2) + 2 * (g + 1)
            fetch(nxt, 0).start()
            fetch(nxt + 1, 1).start()

        @pl.when(g == 0)
        def _():
            attn_a(0, first_half)
            attn_a(1, first_half)

        @pl.when(g == 1)
        def _():
            step_b(0)
            step_b(1)

    units_of(last_half)
    for copy in weights[1:]:
        copy.wait()

    @pl.loop(0, 2)
    def _(i):
        r = pl.ds(pl.multiple_of(i * (n // 2), 128), n // 2)
        ng[r] = mm_t(dq[r], wqs[...]) + mm_t(dk[r], wks[...]) + mm_t(dv[r], wvs[...])

    attn_a(0, last_half)
    attn_a(1, last_half)
    sm[...] = jnp.zeros_like(sm)
    slot_rows = n // ns
    gain_sum = jnp.zeros((1, width), F32)
    for i in range(ns):
        r = slice(i * slot_rows, (i + 1) * slot_rows)
        t = x[r].astype(F32)
        down, gain = norm_down(t, rms_scale(t), ag[...], ng[r])
        in_grad[i] = (hidden_grad[r] + down).astype(BF)
        gain_sum = gain_sum + jnp.sum(gain, axis=0, keepdims=True)
    keep_grad.start()
    for d in range(1, ns):
        grad_copy(d).start()

    col = lax.broadcasted_iota(jnp.int32, (128, width), 1)
    offset = (col // 128 - 1) * 128 - lax.rem(col, 128)
    offset = jnp.where(col >= width - 128, 256, jnp.where(col >= width - 256, -256, offset))
    dist = jnp.abs(offset)
    bucket = jnp.full_like(dist, 8)
    for edge in EDGES:
        bucket = bucket + (dist >= edge).astype(jnp.int32)
    bucket = jnp.where(dist < 8, dist, bucket) + jnp.where(offset > 0, 16, 0)
    pick = jnp.where(bucket == lax.broadcasted_iota(jnp.int32, (128, width), 0), 1.0, 0.0)
    bias = jnp.zeros((16, 128), F32)
    for i in range(width // 128):
        bias = bias + lax.dot_general(diag[:, i, :], pick[:, i * 128:(i + 1) * 128], (((1,), (1,)), ((), ())),
                                      precision=HIGHEST, preferred_element_type=F32)
    sm[0, 40:56, :] = bias
    gains = [gains_dec[i:i + 1, :] for i in range(3)] + [gains_feed[i:i + 1, :] for i in range(2)] + [gain_sum]
    for i, gain in enumerate(gains):
        for j in range(width // 128):
            sm[0, i * 6 + j:i * 6 + j + 1, :] = gain[:, j * 128:(j + 1) * 128]

    def small_copy(i):
        return remote(sm.at[i], smr.at[i], m_s.at[i], m_r.at[i], (core_peer, y_peer, x_peer)[i])

    def z_small(d):
        return remote(smz.at[z], smz.at[z], mz_s.at[d], mz_r.at[d], (lax.rem(z + d, nz) * 2 + xx, s))

    small_copy(0).start()
    step_b(2)
    step_b(3)
    small_copy(0).wait()
    sm[1] = sm[0] + smr[0]
    small_copy(1).start()
    attn_b(0, first_half)
    attn_y(0).start()
    attn_b(1, first_half)
    attn_y(1).start()
    step_c(0)
    step_c(1)
    small_copy(1).wait()
    sm[2] = sm[1] + smr[1]
    small_copy(2).start()
    step_c(2)
    step_c(3)
    attn_b(0, last_half)
    small_copy(2).wait()
    smz[z] = sm[2] + smr[2]

    @pl.loop(1, nz)
    def _(d):
        z_small(d).start()

    step_c(4)
    attn_b(1, last_half)
    step_c(5)
    for i in range(6):
        step_d(i)

    @pl.loop(1, nz)
    def _(d):
        z_small(d).wait()

    small_out[...] = smz[0]

    @pl.loop(1, nz)
    def _(d):
        small_out[...] = small_out[...] + smz[d]

    keep_dec.wait()
    keep_enc.wait()
    keep_grad.wait()
    for d in range(1, ns):
        enc_copy(d).wait()
        grad_copy(d).wait()

    @pl.loop(1, count)
    def _(d):
        dec_copy(d).wait()


def backward(np_, ns, x, ag, q, k, v, context_t, branch, hidden_grad, normed, gains_dec, gains_feed,
             probs, wo, wq, wk, wv, wide, tall, dec, encoded):
    n, width = x.shape
    heads = probs.shape[0]
    nz = np_ // 2
    rows, lanes = wide.shape[5:]
    count = np_ * ns
    padded = normed.shape[1]
    vm = pl.BlockSpec(memory_space=pltpu.VMEM)
    hb = pl.BlockSpec(memory_space=pl.ANY)
    S = jax.ShapeDtypeStruct
    V = pltpu.VMEM
    dma = pltpu.SemaphoreType.DMA
    nar = V((n, width), BF)
    square = V((width, width), BF)
    slots = (ns, n // ns, width)
    small = (64, 128)
    return pl.pallas_call(
        functools.partial(backward_kernel, np_, ns),
        out_shape=(S((6, rows, lanes), F32), S(small, F32), S(dec.shape, BF), S(slots, BF), S(slots, BF)),
        in_specs=[vm] * 11 + [hb] * 9,
        out_specs=(vm, vm, hb, hb, hb),
        scratch_shapes=[
            square, square, square, square, nar, V((n, n), F32), V((n, n), BF), V((width, n), BF), nar, nar, nar,
            V((128, n), BF), V((padded, n), BF), V((n, width), F32), V(slots, BF),
            V((2, n, n), BF), V((384, 128), F32), V((16, 8, 128), F32),
            V((4, 2, nz, 2, rows, lanes), BF), V((2, 2, 2, nz, 2, rows, lanes), BF), V((6, 2, nz, 2, rows, lanes), BF),
            V((2, nz, 2, rows, lanes), BF), V((2, 2, nz, rows, lanes), BF), V((2, 2, nz, rows, lanes), BF),
            V((6, nz, rows, lanes), BF), V((6, nz, rows, lanes), BF),
            V((3,) + small, F32), V((3,) + small, F32), V((nz,) + small, F32),
            dma((2,)), dma((4,)), dma((7,)), dma((4,)), dma((4,)), dma((4,)), dma((4,)), dma((6,)), dma((6,)),
            dma((2, 2)), dma((2, 2)), dma((2, 2)), dma((2, 2)), dma((6, nz)), dma((6, nz)),
            dma((3,)), dma((3,)), dma((nz,)), dma((nz,)), dma((count,)), dma((count,)),
            dma((ns,)), dma((ns,)), dma((ns,)), dma((ns,)),
        ],
        compiler_params=pltpu.CompilerParams(
            collective_id=0, has_side_effects=True, vmem_limit_bytes=62 * 1024 * 1024),
        name="backward",
    )(x, ag.reshape(1, -1), q, k, v, context_t, branch, hidden_grad, normed, gains_dec, gains_feed,
      probs, wo, wq, wk, wv, wide, tall, dec, encoded.reshape(slots))


def two_kernels(
    np_, ns, r, rp, lanes, side, length, final_gain, expand_gain, attend_gain, dec_gains,
    rows_grad, block, cot, reduce_weight, active, expand_weight, hidden, slope, mixed_t,
    output_weight, query_weight, key_weight, value_weight, query, key, value, x, normed_t,
    context_t, probs, dec_all, encoded,
):
    seq_len, ff = active.shape
    nz = np_ // 2
    wide, tall, hidden_grad, branch, feed_gains = feed_back(
        1, length, rows_grad, block, cot, final_gain, hidden, expand_gain, mixed_t.T, active,
        slope, reduce_weight, expand_weight)

    def pad(unit):
        return jnp.pad(unit, ((0, 0),) * 5 + ((0, rp - r), (0, 0)))

    tall = tall.reshape(2, 2, 2, r, side, nz, 2, ff // np_).transpose(0, 1, 2, 5, 6, 3, 4, 7)
    tall = pad(tall.reshape(2, 2, 2, nz, 2, r, lanes))
    wide = pad(wide.reshape(2, 2, 2, nz, 2, r, lanes))
    gap = ((0, 0), (0, rp - r), (0, 0))
    normed_t = jnp.pad(normed_t.reshape(np_, r, seq_len), gap).reshape(np_ * rp, seq_len)
    context_t = jnp.pad(context_t.reshape(np_, r, seq_len), gap).reshape(np_ * rp, seq_len)
    return backward(
        np_, ns, x, attend_gain, query, key, value, context_t, branch, hidden_grad, normed_t.T,
        dec_gains, feed_gains, probs, output_weight, query_weight, key_weight, value_weight,
        wide, tall, dec_all, encoded)


def per_device(
    enc_input, dec_input, lengths, attend_gain, query_weight, key_weight, value_weight,
    output_weight, bias_table, expand_gain, expand_weight, reduce_weight, final_gain,
    self_gain, self_value, self_output, cross_gain, cross_query, cross_key, cross_value,
    cross_output, feed_gain, feed_expand, feed_reduce, enc_cotangent, dec_cotangent,
):
    group, local_rows, width = enc_input.shape
    buckets, heads = bias_table.shape
    size = width // heads
    ff = expand_weight.shape[1]
    ns = lax.axis_size("seq")
    np_ = lax.axis_size("pairs")
    r = width // np_
    aligned = np_ == 8 and r % 32 == 0 and (ff // np_) % 128 == 0 and ff == 4 * width
    seq_len = local_rows * ns
    weights = (query_weight, key_weight, value_weight, output_weight, expand_weight, reduce_weight,
               self_value, self_output, cross_query, cross_key, cross_value, cross_output,
               feed_expand, feed_reduce)
    (normed_t, query, key, value, probs, context_t, hidden, mixed_t, active, slope, block, encoded,
     x, cot, rows_grad, dec_block, dec_input_grad, dec_gains, *dec_rows) = forward(
        np_, ns, aligned, lengths, bias_table.T,
        (attend_gain, expand_gain, final_gain, self_gain, cross_gain, feed_gain),
        dec_input, dec_cotangent, enc_input, enc_cotangent, weights)
    x = x.reshape(seq_len, width)
    cot = cot.reshape(seq_len, width)
    if aligned:
        dec_all, = dec_rows
        red, small_sum, dec_got, enc_out, grad_out = fused(
            np_, ns, lengths, final_gain, expand_gain, attend_gain, dec_gains, rows_grad, block, cot,
            reduce_weight, active, expand_weight, hidden, slope, mixed_t, output_weight,
            query_weight, key_weight, value_weight, query, key, value, x, normed_t, context_t,
            probs, dec_all, encoded)
        (enc_out, grad_out, dec_block, dec_input_grad, grad_query, grad_key, grad_value, grad_output, grad_expand, grad_reduce,
         bias, *rest) = finish(
            heads, buckets, red, small_sum, dec_got, dec_block, dec_input_grad, enc_out, grad_out)
        gains = rest[:6]
        grad_sv, grad_so, grad_cq, grad_ck, grad_cv, grad_co, feed_in, feed_out = rest[6:]
        return (
            enc_out, dec_block, grad_out, dec_input_grad, gains[5], grad_query, grad_key,
            grad_value, grad_output, bias.T, gains[4], grad_expand, grad_reduce.T, gains[3],
            gains[0], grad_sv, grad_so, gains[1], grad_cq, grad_ck, grad_cv, grad_co, gains[2],
            feed_in, feed_out.T,
        )
    left, right, wide_rows, mids = dec_rows
    length = lax.dynamic_slice_in_dim(lengths, lax.axis_index("seq"), 1)
    rp = -(-r // 16) * 16
    lanes = ff // 8
    side = width // 8 // r
    cols = width // ns

    left_cut = jnp.concatenate([
        left.reshape(5, np_, r).transpose(1, 0, 2).reshape(np_, 5 * r),
        wide_rows[0].reshape(np_, 4 * r),
    ], axis=1)
    mid_cut = mids.reshape(2, ns, heads // ns, np_, r).transpose(3, 1, 0, 2, 4)
    mid_cut = mid_cut.reshape(np_, ns, 6 * r)
    right_cut = jnp.concatenate([
        right.reshape(7, ns, cols).transpose(1, 0, 2).reshape(ns, 7 * cols),
        wide_rows[1].reshape(ns, 4 * cols)], axis=1)
    dec_all = jnp.concatenate([
        jnp.broadcast_to(left_cut[:, None], (np_, ns, 9 * r)), mid_cut,
        jnp.broadcast_to(right_cut[None], (np_, ns, 11 * cols))], axis=-1)
    dec_all = dec_all.astype(BF).reshape(np_ * ns, -1)
    used = dec_all.shape[1]
    dec_rows = -(-used // 2048) * 16
    dec_all = jnp.pad(dec_all, ((0, 0), (0, dec_rows * 128 - used)))
    dec_all = dec_all.reshape(np_ * ns, dec_rows, 128)

    red, small_sum, dec_got, enc_out, grad_out = two_kernels(
        np_, ns, r, rp, lanes, side, length, final_gain, expand_gain, attend_gain, dec_gains,
        rows_grad, block, cot, reduce_weight, active, expand_weight, hidden, slope, mixed_t,
        output_weight, query_weight, key_weight, value_weight, query, key, value, x, normed_t,
        context_t, probs, dec_all, encoded)

    got = dec_got.reshape(np_ * ns, -1)
    lefts = got[:, :9 * r].reshape(-1, 9, r)
    mid_got = got[:, 9 * r:15 * r].reshape(-1, 2, 3, r)
    rights = got[:, 15 * r:15 * r + 11 * cols].reshape(-1, 11, cols)
    plain = jnp.einsum("nkr,nkc->krc", lefts[:, :4], rights[:, :4], preferred_element_type=F32)
    crossed = jnp.einsum("nkhr,nkhd->krhd", mid_got, rights[:, 4:6].reshape(-1, 2, 3, size),
                         preferred_element_type=F32).reshape(2, r, cols)
    feed_in = jnp.einsum("nr,nc->rc", lefts[:, 4], rights[:, 7:11].reshape(-1, 4 * cols),
                         preferred_element_type=F32)
    feed_out = jnp.einsum("nr,nc->rc", lefts[:, 5:9].reshape(-1, 4 * r), rights[:, 6],
                          preferred_element_type=F32)
    red = red[:, :r]
    grad_reduce = red[2:4].reshape(2, r, side, ff // np_).reshape(cols, ff // np_).T
    gains = small_sum[:36].reshape(6, width)
    bias = small_sum[40:40 + heads, :buckets].T
    return (
        enc_out, dec_block, grad_out, dec_input_grad,
        gains[5],
        red[4][:, :cols], red[4][:, cols:], red[5][:, :cols], red[5][:, cols:],
        bias,
        gains[4],
        jnp.concatenate([red[0], red[1]], axis=1), grad_reduce,
        gains[3],
        gains[0], plain[0], plain[1],
        gains[1], plain[2], crossed[0], crossed[1], plain[3],
        gains[2], feed_in, feed_out,
    )


def solution(mesh):
    rows = P("pairs", "seq", None)
    single = P(("pairs", "seq"), None)
    block = P("pairs", "seq")
    return jax.shard_map(
        per_device,
        mesh=mesh,
        in_specs=(rows, single, P("pairs")) + (P(),) * 21 + (rows, single),
        out_specs=(
            rows, single, rows, single,
            P(), block, block, block, block, P(), P(), block, block, P(),
            P(), block, block, P(), block, block, block, block, P(), block, block,
        ),
        check_vma=False,
    )
```

```python
import functools
import itertools

import jax
import jax.numpy as jnp
from jax import lax
from jax.experimental import pallas as pl
from jax.experimental.pallas import tpu as pltpu
from jax.sharding import PartitionSpec as P

EPSILON = 1e-06
EDGES = (12, 16, 23, 32, 46, 64, 91)
HIGHEST = lax.Precision.HIGHEST
MESH = pl.DeviceIdType.MESH
BF = jnp.bfloat16
F32 = jnp.float32


def mm(a, b):
    return jnp.dot(a, b, preferred_element_type=F32)
def mm_t(a, b):
    return lax.dot_general(a, b, (((1,), (1,)), ((), ())), preferred_element_type=F32)
def t_mm(a, b):
    return lax.dot_general(a, b, (((0,), (0,)), ((), ())), preferred_element_type=F32)

def rms_scale(v):
    return lax.rsqrt(jnp.mean(v * v, axis=-1, keepdims=True) + EPSILON)

def gelu_parts(u):
    u2 = u * u
    t = jnp.tanh(u * (0.7978845608 + (0.7978845608 * 0.044715) * u2))
    half = 0.5 + 0.5 * t
    lower = u * half
    return lower, half + lower * (1.0 - t) * (0.7978845608 + (3 * 0.7978845608 * 0.044715) * u2)

def norm_down(v, r, g, dy):
    vr = v * r
    gd = g * dy
    return r * (gd - vr * jnp.mean(vr * gd, axis=-1, keepdims=True)), vr * dy

def diagonal_buckets(shape, width):
    col = lax.broadcasted_iota(jnp.int32, shape, 1)
    offset = (col // 128 - 1) * 128 - lax.rem(col, 128)
    offset = jnp.where(col >= width - 128, 256, jnp.where(col >= width - 256, -256, offset))
    dist = jnp.abs(offset)
    bucket = jnp.full_like(dist, 8)
    for edge in EDGES:
        bucket = bucket + (dist >= edge).astype(jnp.int32)
    bucket = jnp.where(dist < 8, dist, bucket) + jnp.where(offset > 0, 16, 0)
    return jnp.where(bucket == lax.rem(lax.broadcasted_iota(jnp.int32, shape, 0), 32), 1.0, 0.0)


def own_heads(heads, width):
    return (lax.broadcasted_iota(jnp.int32, (heads, width), 1) // (width // heads)
            == lax.broadcasted_iota(jnp.int32, (heads, width), 0))


def decoder_start_back(x, sg, after, cg, middle_grad, score_rows, ck, cq, so, sv):
    own = own_heads(*score_rows.shape)
    cross_q_grad = jnp.sum(jnp.where(own, mm(score_rows, ck[...]), 0.0), axis=0, keepdims=True).astype(BF)
    after_down, cross_gain = norm_down(after, rms_scale(after), cg, mm_t(cross_q_grad, cq[...]))
    after_grad = middle_grad + after_down
    self_branch = after_grad.astype(BF)
    self_values_grad = mm_t(self_branch, so[...]).astype(BF)
    x_down, self_gain = norm_down(x, rms_scale(x), sg, mm_t(self_values_grad, sv[...]))
    return cross_q_grad, self_branch, self_values_grad, (after_grad + x_down).astype(BF), self_gain, cross_gain


def cut_rows(np_, ns, left, right, at, wide, mids, dec, cuts, both):
    heads, width = mids.shape[1:]
    ff = wide.shape[1]
    rows, cols, step = width // np_, width // ns, heads // ns
    both[...] = jnp.zeros_like(both)
    cuts[...] = jnp.zeros_like(cuts)
    for j in range(ns):
        for i in range(7):
            t = right[at + i:at + i + 1, j * cols:(j + 1) * cols]
            both[j, 2 * i:2 * i + 1, :] = t[:, :128]
            both[j, 2 * i + 1:2 * i + 2, 0:cols - 128] = t[:, 128:]
        for i in range(6):
            lo = j * width + i * 128
            both[j, 14 + i:15 + i, :] = wide[1:2, lo:lo + 128]
    for i in range(np_):
        cuts[0:5, 0:rows] = left[0:5, i * rows:(i + 1) * rows]
        for a in range(3):
            lo = i * (ff // np_) + a * 128
            cuts[5 + a:6 + a, :] = wide[0:1, lo:lo + 128]
        for j in range(ns):
            for w in range(2):
                cuts[8 + w * step:8 + (w + 1) * step, 0:rows] = (
                    mids[w, j * step:(j + 1) * step, i * rows:(i + 1) * rows])
            dec[i * ns + j, 0:16, :] = cuts[...].astype(BF)
            dec[i * ns + j, 16:48, :] = both[j].astype(BF)


def forward_kernel(np_, ns, cut, lengths, table, ag, eg, fg, sg, cg, dg, dec_in, dec_cot, enc_in, enc_cot,
                   wq, wk, wv, wo, we, wr, sv, so, cq, ck, cv, co, fe, fr,
                   normed_t, q, k, v, probs, context_t, hidden, mixed_t, active, slope, block, low, x_out, cot_out,
                   rows_grad, wide, mids, dec_in_grad, *rest):
    if cut:
        state, dec, *rest = rest
    else:
        dec_out, dec_gains, left, right, *rest = rest
    (wqs, wks, wvs, wos, wes, wrs, svs, sos, cqs, cks, cvs, cos, fes, frs, xs, normed, nt, qs, ks, vs, ctx, hid,
     mixed, mt, act, slo, blk, rws, lws, rgs, band, vecs, v_t, s_t, pbuf, *rest) = rest
    if cut:
        cuts, both, *rest = rest
    sems, psem, osem, x_s, x_r, c_s, c_r, loc = rest
    ag, eg, fg, sg, cg, dg = (g[...].reshape(1, -1) for g in (ag, eg, fg, sg, cg, dg))
    n, width = normed.shape
    heads = probs.shape[0]
    size = width // heads
    ff = act.shape[1]
    slot = n // ns
    p = lax.axis_index("pairs")
    s = lax.axis_index("seq")
    length = lengths[s]

    barrier = pltpu.get_barrier_semaphore()
    for d in range(1, ns):
        pl.semaphore_signal(barrier, inc=1, device_id=(p, lax.rem(s + d, ns)), device_id_type=MESH)

    def rows_copy(src, dst, send, recv, d):
        t = lax.rem(s + d, ns)
        return pltpu.make_async_remote_copy(
            src_ref=src.at[t], dst_ref=dst.at[s], send_sem=send.at[d], recv_sem=recv.at[d],
            device_id=(p, t), device_id_type=MESH)

    x_copies = [rows_copy(enc_in, xs, x_s, x_r, d) for d in range(1, ns)]
    cot_copies = [rows_copy(enc_cot, cot_out, c_s, c_r, d) for d in range(1, ns)]
    keep_x = pltpu.make_async_copy(enc_in.at[s], xs.at[s], loc.at[0])
    keep_cot = pltpu.make_async_copy(enc_cot.at[s], cot_out.at[s], loc.at[1])
    keep_x.start()
    load = []
    for src, dst in ((sv, svs), (so, sos), (cq, cqs), (ck, cks), (fr, frs), (wq, wqs), (wk, wks), (wv, wvs),
                     (wo, wos), (we, wes), (wr, wrs), (cv, cvs), (co, cos), (fe, fes)):
        load.append(pltpu.make_async_copy(src, dst, sems.at[len(load)]))
        load[-1].start()
    pl.semaphore_wait(barrier, ns - 1)
    for copy in x_copies + cot_copies:
        copy.start()
    keep_cot.start()
    saved = []

    def save(src, dst):
        copy = pltpu.make_async_copy(src, dst, osem.at[len(saved)])
        saved.append(copy)
        copy.start()

    vec = lax.dot_general(table[...], diagonal_buckets((table.shape[1], width), width), (((1,), (0,)), ((), ())),
                          precision=HIGHEST, preferred_element_type=F32)
    for i in range(width // 128):
        vecs[:, i, :] = vec[:, i * 128:(i + 1) * 128]
    lane_s = lax.broadcasted_iota(jnp.int32, (128, 128), 1)
    row_s = lax.broadcasted_iota(jnp.int32, (128, 128), 0)

    @pl.loop(0, heads)
    def _(h):
        for b in range(3):
            t = jnp.where(lane_s + row_s < 128, vecs[h, b:b + 1, :], vecs[h, b + 1:b + 2, :])
            for bit in range(7):
                t = jnp.where((row_s >> bit) % 2 == 1, pltpu.roll(t, 1 << bit, 1), t)
            band[h, b * 128:(b + 1) * 128, :] = t

    x = dec_in[...].astype(F32)
    cot = dec_cot[...]
    own = own_heads(heads, width)

    def spread(r):
        return jnp.where(own, r.astype(F32), 0.0).astype(BF)

    def collect(r):
        return jnp.sum(jnp.where(own, r, 0.0), axis=0, keepdims=True)

    x_r = rms_scale(x)
    self_normed = (x * x_r * sg).astype(BF)
    load[0].wait()
    self_values = mm(self_normed, svs[...]).astype(BF)
    load[1].wait()
    after = x + mm(self_values, sos[...])
    after_r = rms_scale(after)
    cross_normed = (after * after_r * cg).astype(BF)
    load[2].wait()
    cross_q = mm(cross_normed, cqs[...]).astype(BF)
    load[3].wait()
    q_rows = mm_t(spread(cross_q), cks[...]).astype(BF)
    load[4].wait()
    active_back = mm_t(cot, frs[...])

    keep_x.wait()
    for copy in x_copies:
        copy.wait()
    save(xs, x_out)
    for i in range(ns):
        r = slice(i * slot, (i + 1) * slot)
        t = xs[i].astype(F32)
        t = t * rms_scale(t) * ag
        normed[r] = t.astype(BF)
        nt[:, r] = t.T.astype(BF)
    save(nt, normed_t)
    for j, (w, out, dst) in enumerate(((wqs, qs, q), (wks, ks, k), (wvs, vs, v))):
        load[5 + j].wait()
        for i in range(2):
            r = slice(i * (n // 2), (i + 1) * (n // 2))
            out[r] = mm(normed[r], w[...]).astype(BF)
        save(out, dst)

    lane = lax.broadcasted_iota(jnp.int32, (n, 128), 1)
    row = lax.broadcasted_iota(jnp.int32, (n, 128), 0)
    q_mark = jnp.where(lane == 0, 1.0, 0.0).astype(BF)
    k_mark = jnp.where((lane == 0) & (row >= length), -1e30, 0.0).astype(BF)

    def keep(g, a):
        at = 2 * lax.rem(g, 2) + a
        return pltpu.make_async_copy(pbuf.at[at], probs.at[2 * g + a], psem.at[at])

    @pl.loop(0, heads // 2)
    def _(g):
        @pl.when(g > 1)
        def _():
            for a in range(2):
                keep(g - 2, a).wait()

        cols = pl.ds(pl.multiple_of(g * 128, 128), 128)
        v_t[...] = vs[:, cols].T
        qq = jnp.concatenate([qs[:, cols], q_mark], axis=1)
        kp = ks[:, cols]
        for a in range(2):
            mine = (lane < 64) if a == 0 else (lane >= 64)
            kk = jnp.concatenate([jnp.where(mine, kp, jnp.zeros_like(kp)), k_mark], axis=1)
            s_t[a] = mm_t(kk, qq)
        for a in range(2):
            h = 2 * g + a
            at = 2 * lax.rem(g, 2) + a
            for j in range(n // 128):
                tile = []
                for i in range(n // 128):
                    t = s_t[a, i * 128:(i + 1) * 128, j * 128:(j + 1) * 128]
                    if abs(i - j) <= 1:
                        t = t + band[h, (i - j + 1) * 128:(i - j + 2) * 128, :]
                    else:
                        f = 5 if i > j else 4
                        t = t + vecs[h, f:f + 1, :]
                    tile.append(t)
                t = jnp.concatenate(tile, axis=0)
                m = jnp.max(t, axis=0, keepdims=True)
                e = jnp.exp(t - m)
                total = jnp.sum(e, axis=0, keepdims=True)
                pbuf[at, :, j * 128:(j + 1) * 128] = (e * (1.0 / total)).astype(BF)
            ctx[pl.ds(pl.multiple_of(h * 64, 64), 64), :] = mm(v_t[a * 64:(a + 1) * 64, :], pbuf[at]).astype(BF)
            keep(g, a).start()

    save(ctx, context_t)
    load[8].wait()
    for i in range(ns):
        r = slice(i * slot, (i + 1) * slot)
        t = xs[i].astype(F32) + mm(ctx[:, r].T, wos[...])
        hid[r] = t
        t = t * rms_scale(t) * eg
        mixed[r] = t.astype(BF)
        mt[:, r] = t.T.astype(BF)
    save(hid, hidden)
    save(mt, mixed_t)
    load[9].wait()

    chunk = s_t.shape[2]

    def rise(j):
        s_t[j % 2] = mm(mixed[...], wes[:, j * chunk:(j + 1) * chunk])

    rise(0)
    for j in range(ff // chunk):
        if j + 1 < ff // chunk:
            rise(j + 1)
        a, b = gelu_parts(s_t[j % 2])
        act[:, j * chunk:(j + 1) * chunk] = a.astype(BF)
        slo[:, j * chunk:(j + 1) * chunk] = b.astype(BF)

    save(act, active)
    save(slo, slope)
    load[10].wait()
    for i in range(2):
        r = slice(i * (n // 2), (i + 1) * (n // 2))
        alive = (lax.broadcasted_iota(jnp.int32, (n // 2, 1), 0) + i * (n // 2) < length).astype(F32)
        b = alive * (hid[r] + mm(act[r], wrs[...]))
        blk[r] = b
        lws[r] = b.astype(BF)
        rws[r] = (b * rms_scale(b) * fg).astype(BF)
    save(blk, block)
    save(lws, low)

    score = mm_t(q_rows, rws[...])
    score = jnp.where(lax.broadcasted_iota(jnp.int32, score.shape, 1) < length, score, -1e30)
    e = jnp.exp(score - jnp.max(score, axis=-1, keepdims=True))
    cross_probs = e / jnp.sum(e, axis=-1, keepdims=True)
    cross_low = cross_probs.astype(BF)
    mean_rows = mm(cross_low, rws[...]).astype(BF)
    for copy in load[11:]:
        copy.wait()
    cross_context = collect(mm(mean_rows, cvs[...])).astype(BF)
    middle = after + mm(cross_context, cos[...])
    middle_r = rms_scale(middle)
    feed_normed = (middle * middle_r * dg).astype(BF)
    dec_active, dec_slope = gelu_parts(mm(feed_normed, fes[...]))
    dec_active = dec_active.astype(BF)
    upper_grad = (dec_slope * active_back).astype(BF)
    middle_down, feed_gain = norm_down(middle, middle_r, dg, mm_t(upper_grad, fes[...]))
    middle_grad = cot.astype(F32) + middle_down
    cross_branch = middle_grad.astype(BF)
    context_grad = mm_t(cross_branch, cos[...]).astype(BF)
    g_rows = mm_t(spread(context_grad), cvs[...]).astype(BF)
    prob_grad = mm_t(g_rows, rws[...])
    score_grad = (cross_probs * (prob_grad - jnp.sum(cross_probs * prob_grad, axis=-1, keepdims=True))).astype(BF)
    pad = jnp.zeros((16 - heads % 16, n), BF)
    padw = jnp.zeros((16 - heads % 16, width), BF)
    rgs[...] = t_mm(jnp.concatenate([score_grad, pad, cross_low, pad], axis=0),
                    jnp.concatenate([q_rows, padw, g_rows, padw], axis=0)).astype(BF)
    save(rgs, rows_grad)
    score_rows = mm(score_grad, rws[...]).astype(BF)
    left_rows = (self_normed, self_values, cross_normed, cross_context, feed_normed)
    cross_q_grad, self_branch, self_values_grad, in_grad, self_gain, cross_gain = decoder_start_back(
        x, sg, after, cg, middle_grad, score_rows, cks, cqs, sos, svs)
    dec_in_grad[...] = in_grad
    right_rows = (self_values_grad, self_branch, cross_q_grad, cross_branch, cross_q, context_grad, cot)
    if cut:
        for i, r in enumerate(left_rows + (middle,) + right_rows + (self_gain, cross_gain, feed_gain)):
            state[i:i + 1, :] = r.astype(F32)
    else:
        dec_out[...] = (middle + mm(dec_active, frs[...])).astype(BF)
        for i, r in enumerate((self_gain, cross_gain, feed_gain)):
            dec_gains[i:i + 1, :] = r
        for i, r in enumerate(left_rows):
            left[i:i + 1, :] = r.astype(F32)
        for i, r in enumerate(right_rows):
            right[i:i + 1, :] = r.astype(F32)
    wide[0:1, :] = dec_active.astype(F32)
    wide[1:2, :] = upper_grad.astype(F32)
    mids[0] = score_rows.astype(F32)
    mids[1] = mean_rows.astype(F32)
    if cut:
        cut_rows(np_, ns, state, state, 6, wide, mids, dec, cuts, both)
    for g in range(heads // 2 - 2, heads // 2):
        for a in range(2):
            keep(g, a).wait()
    keep_cot.wait()
    for copy in cot_copies:
        copy.wait()
    for copy in saved:
        copy.wait()


def forward(np_, ns, cut, lengths, table, gains, dec_in, dec_cot, enc_in, enc_cot, weights):
    group, slot, width = enc_in.shape
    n = slot * ns
    ff = weights[4].shape[1]
    heads = table.shape[0]
    smem = pl.BlockSpec(memory_space=pltpu.SMEM)
    vm = pl.BlockSpec(memory_space=pltpu.VMEM)
    hb = pl.BlockSpec(memory_space=pl.ANY)
    S = jax.ShapeDtypeStruct
    V = pltpu.VMEM
    full, tall, floats, broad = ((n, width), BF), ((width, n), BF), ((n, width), F32), ((n, ff), BF)
    slots = ((ns, slot, width), BF)
    outs = [tall, full, full, full, ((heads, n, n), BF), tall, floats, tall, broad, broad, floats, full, slots, slots,
            full, ((2, ff), F32), ((2, heads, width), F32), ((1, width), BF)]
    outs += [((16, width), F32), ((np_ * ns, 48, 128), BF)] if cut else [
        ((1, width), BF), ((3, width), F32), ((5, width), F32), ((7, width), F32)]
    scratch = [slots, full, tall, full, full, full, tall, floats, full, tall, broad, broad, floats, full, full, full,
               ((heads, 384, 128), F32), ((heads, 8, 128), F32), ((128, n), BF), ((2, n, n), F32), ((4, n, n), BF)]
    scratch += [((16, 128), F32), ((ns, 32, 128), F32)] if cut else []
    dma = pltpu.SemaphoreType.DMA
    return pl.pallas_call(
        functools.partial(forward_kernel, np_, ns, cut),
        out_shape=tuple(S(*t) for t in outs),
        in_specs=[smem] + [vm] * 9 + [hb] * 16,
        out_specs=(hb,) * 15 + (vm,) * (len(outs) - 15),
        scratch_shapes=[V(w.shape, BF) for w in weights] + [V(*t) for t in scratch] + [
            dma((14,)), dma((4,)), dma((16,)), dma((ns,)), dma((ns,)), dma((ns,)), dma((ns,)), dma((2,))],
        compiler_params=pltpu.CompilerParams(
            collective_id=1, has_side_effects=True, vmem_limit_bytes=62 * 1024 * 1024),
        name="forward",
    )(lengths, table, *gains, dec_in, dec_cot, enc_in, enc_cot, *weights)


def finish_kernel(heads, red, small, dec, dec_row, dec_grad, enc, grad, *outs):
    (enc_out, grad_out, row_out, row_grad_out, qo, ko, vo, oo, expand, reduce, bias, g0, g1, g2, g3, g4, g5,
     sv, so, cq, ck, cv, co, fe, fr, wide) = outs
    enc_out[...] = enc[...]
    grad_out[...] = grad[...]
    row_out[...] = dec_row[...]
    row_grad_out[...] = dec_grad[...]
    wide[...] = dec[...].astype(F32)
    rows, cols = qo.shape
    lanes = red.shape[2]
    for i, out in ((4, (qo, ko)), (5, (vo, oo))):
        t = red[i]
        out[0][...] = t[:, :cols]
        out[1][...] = t[:, cols:]
    for i in range(2):
        expand[:, i * lanes:(i + 1) * lanes] = red[i]
        reduce[i * rows:(i + 1) * rows, :] = red[2 + i]
    for h in range(heads):
        at = 36 + h // 4
        bias[h:h + 1, :] = small[at // 24, at % 24:at % 24 + 1, h % 4 * 32:h % 4 * 32 + 32]
    for i, out in enumerate((g0, g1, g2, g3, g4, g5)):
        for j in range(6):
            at = i * 6 + j
            out[pl.ds(j * 128, 128)] = small[at // 24, at % 24, :]

    def row(i):
        return wide[:, i, :]

    def pair(i):
        return jnp.concatenate([row(16 + 2 * i), row(17 + 2 * i)], axis=1)[:, :cols].astype(BF)

    for i, out in enumerate((sv, so, cq, co)):
        out[...] = t_mm(row(i)[:, :rows].astype(BF), pair(i))
    upper = jnp.concatenate([row(30 + i) for i in range(6)], axis=1).astype(BF)
    fe[...] = t_mm(row(4)[:, :rows].astype(BF), upper)
    active = jnp.concatenate([row(5 + i) for i in range(3)], axis=1).astype(BF)
    fr[...] = t_mm(pair(6), active)
    step = cols // 64
    for w, out in enumerate((ck, cv)):
        g = pair(4 + w)
        out[...] = jnp.concatenate(
            [t_mm(row(8 + w * step + h)[:, :rows].astype(BF), g[:, h * 64:(h + 1) * 64]) for h in range(step)], axis=1)


def finish(heads, buckets, red, small, dec, dec_row, dec_grad, enc, grad):
    rows, lanes = red.shape[1:]
    cols, width = lanes // 2, 2 * lanes
    vm = pl.BlockSpec(memory_space=pltpu.VMEM)
    S = jax.ShapeDtypeStruct
    block, broad, tall = S((rows, cols), F32), S((rows, width), F32), S((cols, lanes), F32)
    return pl.pallas_call(
        functools.partial(finish_kernel, heads),
        out_shape=(S(enc.shape, BF), S(grad.shape, BF), S(dec_row.shape, BF), S(dec_grad.shape, BF), block, block, block, block, broad, tall,
                   S((heads, buckets), F32)) + (S((width,), F32),) * 6 + (block,) * 6 + (broad, tall),
        in_specs=[vm] * 7,
        out_specs=(vm,) * 25,
        scratch_shapes=[pltpu.VMEM(dec.shape, F32)],
        compiler_params=pltpu.CompilerParams(vmem_limit_bytes=62 * 1024 * 1024),
        name="finish",
    )(red, small, dec, dec_row, dec_grad, enc, grad)


PARTS = 2
ORDERS = {
    "t00": "xfny",
    "t10": "fnyx",
    "t01": "nyfx",
    "t11": "yxfn",
    "w00": "nyfx",
    "w10": "yxfn",
    "w01": "xyfn",
    "w11": "ynxf",
    "a0": "xyfn",
    "a1": "xnyf",
}
SCHEDULE = {
    "wide": (
        ("t00", 0), ("t10", 0), ("t01", 0), ("t11", 0),
    ),
    "rows": (
        ("w00", 0),
    ),
    "dout": (
        ("w10", 0), ("w01", 0),
    ),
    "p00": (
        ("w11", 0), ("t00", 1),
    ),
    "p01": (
        ("t11", 1),
    ),
    "q0": (
        ("t01", 1), ("t10", 1), ("w01", 1), ("w10", 1),
    ),
    "p10": (
        ("t11", 2), ("h00", 0),
    ),
    "p11": (
        ("h01", 0), ("w00", 1), ("w10", 2), ("w11", 1),
    ),
    "p12": (
        ("t01", 2),
    ),
    "v1": (
        ("t00", 2), ("t10", 2), ("w01", 2), ("h00", 1),
    ),
    "ng1": (
        ("h10", 0), ("t11", 3),
    ),
    "end": (
        ("w00", 2), ("h11", 0), ("t10", 3), ("w10", 3), ("w11", 2), ("h01", 1),
        ("t00", 3), ("t01", 3), ("t11", 4), ("w01", 3), ("h10", 1), ("w10", 4),
        ("w00", 3), ("h01", 2), ("w01", 4), ("h11", 1), ("t00", 4), ("t10", 4),
        ("w11", 3), ("t01", 4), ("w00", 4), ("h10", 2), ("h11", 2), ("w11", 4),
        ("h10", 3), ("h11", 3),
    ),
}
HOPS = (0, 5)
DECODER = 4


def ff_pieces():
    names = [kind + str(unit) + str(i) for kind in "tw" for i in range(PARTS) for unit in range(2)]
    return names + ["h" + str(half) + str(w) for half in range(2) for w in range(2)]


def fused_kernel(np_, ns, length, fg_in, eg_in, ag_in, state_in, wide_in,
                 rows_grad, block, cot, wr, active, wide_w, hidden, slope, mixed_t_in, wo, wq, wk, wv, q_in, k_in,
                 v_in, x_in, normed_t_in, context_t_in, probs, dec, encoded, fr,
                 red, small_out, dec_got, enc_out, grad_out, dec_out,
                 acts, grads, w1, wes, bg, hid, dm, rg, ct, rb, rb_t, mixed_t, normed_t, context_t,
                 dp, ds, pbuf, k_t, band, diag, fu, r0, r0a, r1, r2, r3, r4, a1, a2, a3, over0, over1,
                 sm, smr, smz, smf,
                 fg, eg, ag, state, wide,
                 psem, isem, loc, f_s, f_r, t_s, t_r, o_s, o_r,
                 m_s, m_r, mz_s, mz_r, d_s, d_r, e_s, e_r, g_s, g_r):
    n, width = hid.shape
    ff = acts.shape[1]
    heads = probs.shape[0]
    nz = np_ // 2
    pieces = ff_pieces()
    rows, lanes = fu.shape[6:]
    step_rows = rows // PARTS
    count = np_ * ns
    p = lax.axis_index("pairs")
    s = lax.axis_index("seq")
    c = lax.rem(s, 2)
    y = s // 2
    xx = lax.rem(p, 2)
    z = p // 2
    me = p * ns + s
    core_peer = (p, s + 1 - 2 * c)
    y_peer = (p, lax.rem(s + 2, 4))
    x_peer = (p + 1 - 2 * xx, s)
    first_half, last_half = 1 - y, y
    own_at = {"x": xx, "y": y, "n": lax.rem(z, 2), "f": z // 2}
    peers = {"x": x_peer, "y": y_peer, "n": ((z + 1 - 2 * own_at["n"]) * 2 + xx, s),
             "f": (lax.rem(z + 2, 4) * 2 + xx, s)}

    def place(d):
        lin = lax.rem(me + d, count)
        return (lin // ns, lax.rem(lin, ns))

    barrier = pltpu.get_barrier_semaphore()

    @pl.loop(1, count)
    def _(d):
        pl.semaphore_signal(barrier, inc=1, device_id=place(d), device_id_type=MESH)

    def remote(src, dst, send, recv, peer):
        return pltpu.make_async_remote_copy(
            src_ref=src, dst_ref=dst, send_sem=send, recv_sem=recv,
            device_id=peer, device_id_type=MESH)

    def load(i, src, dst):
        return pltpu.make_async_copy(src, dst, isem.at[i])

    def part_of(ref, i):
        return ref.at[:, pl.ds(i * width, width)]

    loads = [load(i, a, b) for i, (a, b) in enumerate((
        (rows_grad, rg), (block, bg), (cot, ct), (active, acts), (wr, w1), (slope, grads), (mixed_t_in, mixed_t),
        (wide_w, wes), (hidden, hid), (normed_t_in, normed_t), (context_t_in, context_t)))]
    weights = [load(11 + i, a, w1.at[pl.ds(i * width, width)]) for i, a in enumerate((wo, wq, wk, wv))]
    heads_in = [load(15 + i, a, part_of(grads, i)) for i, a in enumerate((q_in, k_in, v_in, x_in))]
    d_out, dq, dk, dv = (part_of(acts, i) for i in range(4))
    q, k, v, x = (part_of(grads, i) for i in range(4))
    branch, dq_t, ng, in_grad, hidden_grad = ct, rb_t, dm, rg, bg
    smalls = [load(20 + i, a, b) for i, (a, b) in enumerate((
        (fg_in, fg), (eg_in, eg), (ag_in, ag), (state_in, state), (wide_in, wide)))]
    late = load(19, fr, w1)
    wos, wqs, wks, wvs = (w1.at[pl.ds(i * width, width)] for i in range(4))

    def fetch(h, slot):
        return pltpu.make_async_copy(probs.at[h], pbuf.at[slot], psem.at[slot])

    def view(ref, dims, fixed):
        return ref.at[tuple(fixed.get(dim, slice(None)) for dim in dims)]

    def accumulate(dst, src, depth):
        for at in itertools.product(range(2), repeat=depth):
            dst[at] = dst[at] + src[at]

    def au(w, core, half):
        return fu.at[1 - c, 2 * w + core, half]

    def region(name, core):
        if name[0] == "h":
            return au(int(name[2]), core, first_half if name[1] == "0" else last_half), "fnx"
        unit = (2 if name[0] == "t" else 0) + int(name[1])
        return fu.at[core, unit, :, :, :, :, pl.ds(int(name[2]) * step_rows, step_rows)], "yfnx"

    def order_of(name):
        if name[0] != "h":
            return ORDERS[name]
        order = ORDERS["a" + name[2]]
        return order[:order.index("y")] if name[1] == "0" else order.replace("y", "")

    def core_copy(name):
        i = pieces.index(name)
        src, _ = region(name, 1 - c)
        dst = r0a.at[i - len(pieces) + 4] if name[0] == "h" else r0.at[i]
        return remote(src, dst, f_s.at[i], f_r.at[i], core_peer)

    def landing(name, j):
        i = pieces.index(name)
        if name[0] == "h":
            return (a1, a2, a3)[j].at[i - len(pieces) + 4]
        return (r1, r2, r3, r4)[j].at[i]

    def remaining(name, j):
        ref, dims = region(name, c)
        return ref, dims, {letter: own_at[letter] for letter in order_of(name)[:j]}

    def stage_copy(name, j):
        ref, dims, fixed = remaining(name, j)
        letter = order_of(name)[j]
        i = pieces.index(name)
        src = view(ref, dims, {**fixed, letter: 1 - own_at[letter]})
        return remote(src, landing(name, j), t_s.at[i, j], t_r.at[i, j], peers[letter])

    def hand_over(w):
        name = "h0" + str(w)
        ref, dims, fixed = remaining(name, len(order_of(name)))
        return remote(view(ref, dims, fixed), (over0, over1)[w], o_s.at[w], o_r.at[w], y_peer)

    def total_of(name):
        unit = 4 + int(name[2]) if name[0] == "h" else (2 if name[0] == "t" else 0) + int(name[1])
        if name[0] == "h":
            return red.at[unit]
        return red.at[unit, pl.ds(int(name[2]) * step_rows, step_rows)]

    def step(name, j):
        order = order_of(name)
        ref, dims, fixed = remaining(name, j)
        mine = view(ref, dims, fixed)
        depth = len(dims) - j
        closing = j == len(order) and name[:2] != "h0"
        joins = name[:2] == "h1" and ORDERS["a" + name[2]].index("y") == j
        if j == 0:
            core_copy(name).wait()
            landed = r0a.at[pieces.index(name) - len(pieces) + 4] if name[0] == "h" else r0.at[pieces.index(name)]
        else:
            stage_copy(name, j - 1).wait()
            landed = landing(name, j - 1)
        if joins:
            hand_over(int(name[2])).wait()
            extra = (over0, over1)[int(name[2])]
        if closing:
            total = mine[...].astype(F32) + landed[...].astype(F32)
            if joins:
                total = total + extra[...].astype(F32)
            total_of(name)[...] = total
            return
        accumulate(mine, landed, depth)
        if joins:
            accumulate(mine, extra, depth)
        if j < len(order):
            stage_copy(name, j).start()
        else:
            hand_over(int(name[2])).start()

    def run_slot(slot):
        for name, j in SCHEDULE.get(slot, ()):
            step(name, j)

    def dec_copy(d):
        to = place(d)
        return remote(dec.at[to[0] * ns + to[1]], dec_got.at[me], d_s.at[d], d_r.at[d], to)

    def enc_copy(d):
        t = lax.rem(s + d, ns)
        return remote(encoded.at[t], enc_out.at[s], e_s.at[d], e_r.at[d], (p, t))

    def grad_copy(d):
        t = lax.rem(s + d, ns)
        return remote(in_grad.at[t], grad_out.at[s], g_s.at[d], g_r.at[d], (p, t))

    keep_dec = pltpu.make_async_copy(dec.at[me], dec_got.at[me], loc.at[4])
    keep_enc = pltpu.make_async_copy(encoded.at[s], enc_out.at[s], loc.at[5])
    keep_grad = pltpu.make_async_copy(in_grad.at[s], grad_out.at[s], loc.at[6])

    for copy in smalls[:1] + loads + smalls[1:]:
        copy.start()
    fetch(first_half * (heads // 2), 0).start()
    fetch(first_half * (heads // 2) + 1, 1).start()
    keep_dec.start()
    keep_enc.start()
    diag[...] = jnp.zeros_like(diag)
    slot_rows = n // ns
    sm[...] = jnp.zeros_like(sm)

    def put_gain(i, gain):
        for j in range(width // 128):
            at = i * 6 + j
            sm[at // 24, at % 24:at % 24 + 1, :] = gain[:, j * 128:(j + 1) * 128]

    smalls[0].wait()
    for i in range(3):
        loads[i].wait()
    final_gain = jnp.zeros((1, width), F32)
    for i in range(ns):
        r = slice(i * slot_rows, (i + 1) * slot_rows)
        alive = (lax.broadcasted_iota(jnp.int32, (slot_rows, 1), 0) + i * slot_rows < length[s]).astype(F32)
        b = bg[r]
        down, gain = norm_down(b, rms_scale(b), fg[...].reshape(1, -1), rg[i].astype(F32))
        b = alive * (ct[r].astype(F32) + down)
        bg[r] = b
        low = b.astype(BF)
        rb[r] = low
        rb_t[:, r] = low.T
        final_gain = final_gain + jnp.sum(gain, axis=0, keepdims=True)
    put_gain(3, final_gain)
    pl.semaphore_wait(barrier, count - 1)
    for d in range(1, ns):
        enc_copy(d).start()

    @pl.loop(1, count)
    def _(d):
        dec_copy(d).start()

    part = width // 4
    loads[3].wait()

    @pl.loop(0, nz)
    def _(b):
        cols = pl.ds(pl.multiple_of(b * 2 * lanes, 128), 2 * lanes)
        g = mm(rb_t[...], acts[:, cols]).astype(BF)
        for j in range(4):
            for half in range(2):
                lo = j * part + half * rows
                for e in range(2):
                    fu[j % 2, 2 + half, j // 2, b // 2, lax.rem(b, 2), e] = g[lo:lo + rows, e * lanes:(e + 1) * lanes]

    for name in pieces:
        if name[0] == "t":
            core_copy(name).start()
    loads[4].wait()
    loads[5].wait()

    for j in range(ff // width):
        cols = slice(j * width, (j + 1) * width)
        grads[:, cols] = (grads[:, cols].astype(F32) * mm_t(rb[...], w1[cols, :])).astype(BF)
        if j == 0:
            for copy in smalls[3:]:
                copy.wait()
            for i in range(3):
                put_gain(i, state[13 + i:14 + i, :])
        run_slot("ug" + str(j))

    for copy in weights:
        copy.start()
    loads[6].wait()

    @pl.loop(0, 4)
    def _(j):
        cols = pl.ds(pl.multiple_of(j * 2 * lanes, 128), 2 * lanes)
        g = mm(mixed_t[...], grads[:, cols]).astype(BF)
        for half in range(2):
            fu[lax.rem(j, 2), half, j // 2] = g[:, half * lanes:(half + 1) * lanes].reshape(2, 2, 2, rows, lanes)

    for name in pieces:
        if name[0] == "w":
            core_copy(name).start()
    run_slot("wide")
    loads[7].wait()
    dm[...] = mm_t(grads[...], wes[...])
    for copy in heads_in:
        copy.start()
    run_slot("dm")
    loads[8].wait()
    smalls[1].wait()
    expand_gain = jnp.zeros((1, width), F32)
    for i in range(ns):
        r = slice(i * slot_rows, (i + 1) * slot_rows)
        t = hid[r]
        down, gain = norm_down(t, rms_scale(t), eg[...].reshape(1, -1), dm[r])
        t = bg[r] + down
        bg[r] = t
        branch[r] = t.astype(BF)
        expand_gain = expand_gain + jnp.sum(gain, axis=0, keepdims=True)
    put_gain(4, expand_gain)
    run_slot("rows")
    weights[0].wait()

    @pl.loop(0, width // 384)
    def _(j):
        cols = pl.ds(pl.multiple_of(j * 384, 128), 384)
        d_out[:, cols] = mm_t(branch[...], w1[cols, :]).astype(BF)

    for copy in heads_in:
        copy.wait()
    for copy in loads[9:]:
        copy.wait()

    run_slot("dout")

    lane = lax.broadcasted_iota(jnp.int32, (n, 128), 1)
    lane_s = lax.broadcasted_iota(jnp.int32, (128, 128), 1)
    row_s = lax.broadcasted_iota(jnp.int32, (128, 128), 0)

    def pair(half, g):
        cols = pl.ds(pl.multiple_of(half * (width // 2) + g * 128, 128), 128)
        k_t[...] = k[:, cols].T
        dop = d_out[:, cols]
        qp = q[:, cols]
        vp = v[:, cols]
        zero = jnp.zeros_like(qp)
        for a in range(2):
            h = half * (heads // 2) + 2 * g + a
            mine = (lane < 64) if a == 0 else (lane >= 64)
            dp[...] = mm_t(jnp.where(mine, vp, zero), dop)
            fetch(h, a).wait()
            for j in range(n // 128):
                pj = pbuf[a, :, j * 128:(j + 1) * 128].astype(F32)
                pd = pj * dp[:, j * 128:(j + 1) * 128]
                total = jnp.sum(pd, axis=0, keepdims=True)
                sg = pd - pj * total
                ds[:, j * 128:(j + 1) * 128] = sg.astype(BF)
                for i in range(n // 128):
                    t = sg[i * 128:(i + 1) * 128]
                    if abs(i - j) <= 1:
                        b = (i - j + 1) * 128
                        if j == 0 or (j == 1 and i == 0):
                            band[b:b + 128, :] = t
                        else:
                            band[b:b + 128, :] += t
                    else:
                        f = 5 if i > j else 4
                        diag[h, f:f + 1, :] += jnp.sum(t, axis=0, keepdims=True)
            dvp = mm(pbuf[a], jnp.where(mine, dop, zero))
            dkp = mm(ds[...], jnp.where(mine, qp, zero))
            dq_t[pl.ds(pl.multiple_of(h * 64, 64), 64), :] = mm(k_t[a * 64:(a + 1) * 64, :], ds[...]).astype(BF)
            if a == 0:
                dk_sum, dv_sum = dkp, dvp
            else:
                dk[:, cols] = (dk_sum + dkp).astype(BF)
                dv[:, cols] = (dv_sum + dvp).astype(BF)
            for b in range(3):
                t = band[b * 128:(b + 1) * 128, :]
                for bit in range(7):
                    t = jnp.where((row_s >> bit) % 2 == 1, pltpu.roll(t, 128 - (1 << bit), 1), t)
                straight = jnp.sum(jnp.where(lane_s + row_s < 128, t, 0.0), axis=0, keepdims=True)
                whole = jnp.sum(t, axis=0, keepdims=True)
                diag[h, b:b + 1, :] += straight
                diag[h, b + 1:b + 2, :] += whole - straight

    def units_of(half, tag):
        cols = pl.ds(pl.multiple_of(half * (width // 2), 128), width // 2)
        dq_h = dq_t[cols, :].T
        dq[:, cols] = dq_h
        dk_h = dk[:, cols]
        for cc in range(2):
            e = slice(cc * part, (cc + 1) * part)
            g = mm(normed_t[...], jnp.concatenate([dq_h[:, e], dk_h[:, e]], axis=1))
            au(0, cc, half)[...] = g.astype(BF).reshape(2, 2, 2, rows, lanes)
        core_copy("h" + tag + "0").start()
        run_slot("q" + tag)
        dv_h = dv[:, cols]
        br_h = branch[:, cols]
        zero = jnp.zeros((n, part), BF)
        for cc in range(2):
            e = slice(cc * part, (cc + 1) * part)
            g = (mm(normed_t[...], jnp.concatenate([dv_h[:, e], zero], axis=1))
                 + mm(context_t[...], jnp.concatenate([zero, br_h[:, e]], axis=1)))
            au(1, cc, half)[...] = g.astype(BF).reshape(2, 2, 2, rows, lanes)
        core_copy("h" + tag + "1").start()
        run_slot("v" + tag)

    quarter = heads // 4

    @pl.loop(0, quarter)
    def _(g):
        pair(first_half, g)
        nxt = jnp.where(g == quarter - 1, last_half * (heads // 2), first_half * (heads // 2) + 2 * (g + 1))
        fetch(nxt, 0).start()
        fetch(nxt + 1, 1).start()

        for i in range(quarter):
            if SCHEDULE.get("p0" + str(i)):
                @pl.when(g == i)
                def _():
                    run_slot("p0" + str(i))

    units_of(first_half, "0")

    @pl.loop(0, quarter)
    def _(g):
        pair(last_half, g)

        @pl.when(g < quarter - 1)
        def _():
            nxt = last_half * (heads // 2) + 2 * (g + 1)
            fetch(nxt, 0).start()
            fetch(nxt + 1, 1).start()

        for i in range(quarter):
            if SCHEDULE.get("p1" + str(i)):
                @pl.when(g == i)
                def _():
                    run_slot("p1" + str(i))

    units_of(last_half, "1")
    for copy in weights[1:]:
        copy.wait()

    for i in range(2):
        r = slice(i * (n // 2), (i + 1) * (n // 2))
        ng[r] = mm_t(dq[r], wqs[...]) + mm_t(dk[r], wks[...]) + mm_t(dv[r], wvs[...])
        run_slot("ng" + str(i))

    late.start()
    smalls[2].wait()
    gain_sum = jnp.zeros((1, width), F32)
    for i in range(ns):
        r = slice(i * slot_rows, (i + 1) * slot_rows)
        t = x[r].astype(F32)
        down, gain = norm_down(t, rms_scale(t), ag[...].reshape(1, -1), ng[r])
        in_grad[i] = (hidden_grad[r] + down).astype(BF)
        gain_sum = gain_sum + jnp.sum(gain, axis=0, keepdims=True)
    keep_grad.start()
    for d in range(1, ns):
        grad_copy(d).start()

    pick = diagonal_buckets((128, width), width)
    bias = jnp.zeros((16, 128), F32)
    for i in range(width // 128):
        bias = bias + lax.dot_general(diag[:, i, :], pick[:, i * 128:(i + 1) * 128], (((1,), (1,)), ((), ())),
                                      precision=HIGHEST, preferred_element_type=F32)
    place_of = lax.broadcasted_iota(jnp.int32, (1, 128), 1) // 32
    for h in range(heads):
        at = 36 + h // 4
        sm[at // 24, at % 24:at % 24 + 1, :] += jnp.where(place_of == h % 4, bias[h:h + 1, :], 0.0)
    put_gain(5, gain_sum)

    chips = 2 * np_
    chip = 2 * p + y
    small_first = remote(sm.at[1 - c], smr, m_s.at[0], m_r.at[0], core_peer)
    small_last = remote(smf.at[c], smf.at[c], m_s.at[1], m_r.at[1], core_peer)

    def small_copy(d):
        to = lax.rem(chip + d, chips)
        return remote(smz.at[chip], smz.at[chip], mz_s.at[d], mz_r.at[d], (to // 2, lax.rem(to, 2) * 2 + c))

    small_first.start()
    tail = SCHEDULE["end"]
    for i, (name, j) in enumerate(tail):
        step(name, j)
        if i == DECODER:
            late.wait()
            dec_out[...] = (state[5:6, :] + mm(wide[0:1, :].astype(BF), w1[...])).astype(BF)
        if i == HOPS[0]:
            small_first.wait()
            smz[chip] = sm[c] + smr[...]

            @pl.loop(1, chips)
            def _(d):
                small_copy(d).start()
        if i == len(tail) - HOPS[1]:
            @pl.loop(1, chips)
            def _(d):
                small_copy(d).wait()

            total = smz[0]
            for other in range(1, chips):
                total = total + smz[other]
            smf[c] = total
            small_last.start()

    small_last.wait()
    small_out[...] = smf[...]
    keep_dec.wait()
    keep_enc.wait()
    keep_grad.wait()
    for d in range(1, ns):
        enc_copy(d).wait()
        grad_copy(d).wait()

    @pl.loop(1, count)
    def _(d):
        dec_copy(d).wait()


def fused(np_, ns, length, fg, eg, ag, state, wide, rows_grad, block, cot, wr, active, we, hidden, slope, mixed_t,
          wo, wq, wk, wv, q, k, v, x, normed_t, context_t, probs, dec, encoded, fr):
    n, width = hidden.shape
    ff = active.shape[1]
    heads = probs.shape[0]
    nz = np_ // 2
    rows, lanes = width // np_, ff // np_
    count = np_ * ns
    smem = pl.BlockSpec(memory_space=pltpu.SMEM)
    vm = pl.BlockSpec(memory_space=pltpu.VMEM)
    hb = pl.BlockSpec(memory_space=pl.ANY)
    S = jax.ShapeDtypeStruct
    V = pltpu.VMEM
    dma = pltpu.SemaphoreType.DMA
    nar, tall = V((n, width), BF), V((width, n), BF)
    floats = V((n, width), F32)
    slots = (ns, n // ns, width)
    small = (2, 24, 128)
    ffs = 4 * PARTS
    sub = rows // PARTS

    def joint(w):
        return V((2,) * (3 - ORDERS["a" + str(w)].index("y")) + (rows, lanes), BF)

    return pl.pallas_call(
        functools.partial(fused_kernel, np_, ns),
        out_shape=(S((6, rows, lanes), F32), S(small, F32), S((count, 48, 128), BF), S(slots, BF), S(slots, BF),
                   S((1, width), BF)),
        in_specs=[smem] + [hb] * 28,
        out_specs=(vm, vm, hb, hb, hb, vm),
        scratch_shapes=[
            V((n, ff), BF), V((n, ff), BF), V((ff, width), BF), V((width, ff), BF), floats, floats, floats,
            V(slots, BF), nar, nar, tall, tall, tall, tall,
            V((n, n), F32), V((n, n), BF), V((2, n, n), BF), V((128, n), BF), V((384, 128), F32), V((16, 8, 128), F32),
            V((2, 4, 2, 2, 2, 2, rows, lanes), BF), V((ffs, 2, 2, 2, 2, sub, lanes), BF), V((4, 2, 2, 2, rows, lanes), BF),
            V((ffs, 2, 2, 2, sub, lanes), BF), V((ffs, 2, 2, sub, lanes), BF), V((ffs, 2, sub, lanes), BF),
            V((ffs, sub, lanes), BF), V((4, 2, 2, rows, lanes), BF), V((4, 2, rows, lanes), BF),
            V((4, rows, lanes), BF), joint(0), joint(1),
            V(small, F32), V(small[1:], F32), V((2 * np_,) + small[1:], F32), V(small, F32),
            V((width,), F32), V((width,), F32), V((width,), F32), V((16, width), F32), V((2, ff), F32),
            dma((2,)), dma((26,)), dma((7,)), dma((ffs + 4,)), dma((ffs + 4,)), dma((ffs + 4, 4)), dma((ffs + 4, 4)),
            dma((2,)), dma((2,)),
            dma((2,)), dma((2,)), dma((2 * np_,)), dma((2 * np_,)), dma((count,)), dma((count,)),
            dma((ns,)), dma((ns,)), dma((ns,)), dma((ns,)),
        ],
        compiler_params=pltpu.CompilerParams(
            collective_id=0, has_side_effects=True, vmem_limit_bytes=62 * 1024 * 1024),
        name="fused_backward",
    )(length, fg, eg, ag, state, wide, rows_grad.reshape(slots), block, cot, wr,
      active, we, hidden, slope, mixed_t, wo, wq, wk, wv, q, k, v, x, normed_t, context_t, probs, dec,
      encoded.reshape(slots), fr)


def feed_back_kernel(length, rows_grad, block, cot, fg, hidden, eg, mixed, active, slope, wr, we,
                     wide, tall, hidden_grad, branch, gains, wrs, wes, bg, rb, rb_t, ug, mixed_t, dmixed, sems):
    n, width = block.shape
    ff = active.shape[1]
    groups, lanes = tall.shape[3], tall.shape[5]
    cols_dev = width // 4
    copies = [pltpu.make_async_copy(a, b, sems.at[i]) for i, (a, b) in enumerate(((wr, wrs), (we, wes)))]
    for c in copies:
        c.start()
    gains[...] = jnp.zeros_like(gains)

    @pl.loop(0, n // 128)
    def _(i):
        r = pl.ds(i * 128, 128)
        alive = (lax.broadcasted_iota(jnp.int32, (128, 1), 0) + i * 128 < length[0]).astype(F32)
        v = block[r]
        down, gain = norm_down(v, rms_scale(v), fg[...], rows_grad[r].astype(F32))
        b = alive * (cot[r].astype(F32) + down)
        bg[r] = b
        rb[r] = b.astype(BF)
        rb_t[:, pl.ds(pl.multiple_of(i * 128, 128), 128)] = b.T.astype(BF)
        mixed_t[:, pl.ds(pl.multiple_of(i * 128, 128), 128)] = mixed[r].T
        gains[0:1, :] += jnp.sum(gain, axis=0, keepdims=True)

    copies[0].wait()

    @pl.loop(0, ff // 256)
    def _(j):
        cols = pl.ds(pl.multiple_of(j * 256, 256), 256)
        ug[:, cols] = (slope[:, cols].astype(F32) * mm_t(rb[...], wrs[cols, :])).astype(BF)

    copies[1].wait()

    @pl.loop(0, width // 256)
    def _(j):
        cols = pl.ds(pl.multiple_of(j * 256, 256), 256)
        dmixed[:, cols] = mm_t(ug[...], wes[cols, :])

    @pl.loop(0, n // 128)
    def _(i):
        r = pl.ds(i * 128, 128)
        v = hidden[r]
        down, gain = norm_down(v, rms_scale(v), eg[...], dmixed[r])
        h = bg[r] + down
        hidden_grad[r] = h
        branch[r] = h.astype(BF)
        gains[1:2, :] += jnp.sum(gain, axis=0, keepdims=True)

    @pl.loop(0, 4)
    def _(j):
        for half in range(2):
            cols = pl.ds(pl.multiple_of(j * (ff // 4) + half * (ff // 8), 128), ff // 8)
            wide[half, lax.rem(j, 2), j // 2] = mm(mixed_t[...], ug[:, cols]).astype(BF)

    chunk = ff // 8
    per_group = lanes // chunk

    @pl.loop(0, 8)
    def _(i):
        cols = pl.ds(pl.multiple_of(i * chunk, 128), chunk)
        g = mm(rb_t[...], active[:, cols]).astype(BF)
        for j in range(4):
            for half in range(2):
                r = j * cols_dev + half * (cols_dev // 2)
                part = g[r:r + cols_dev // 2]
                if per_group == 1:
                    tall[half, j % 2, j // 2, i] = part
                else:
                    tall[half, j % 2, j // 2, 0, :, cols] = part


def feed_back(groups, length, rows_grad, block, cot, fg, hidden, eg, mixed, active, slope, wr, we):
    n, width = block.shape
    ff = active.shape[1]
    sm = pl.BlockSpec(memory_space=pltpu.SMEM)
    vm = pl.BlockSpec(memory_space=pltpu.VMEM)
    hb = pl.BlockSpec(memory_space=pl.ANY)
    S = jax.ShapeDtypeStruct
    V = pltpu.VMEM
    return pl.pallas_call(
        feed_back_kernel,
        out_shape=(S((2, 2, 2, width, ff // 8), BF),
                   S((2, 2, 2, groups, width // 8, ff // groups), BF), S((n, width), F32), S((n, width), BF), S((2, width), F32)),
        in_specs=[sm] + [vm] * 9 + [hb] * 2,
        out_specs=(vm,) * 5,
        scratch_shapes=[V(wr.shape, BF), V(we.shape, BF), V((n, width), F32), V((n, width), BF), V((width, n), BF),
                        V((n, ff), BF), V((width, n), BF), V((n, width), F32), pltpu.SemaphoreType.DMA((2,))],
        compiler_params=pltpu.CompilerParams(vmem_limit_bytes=60 * 1024 * 1024),
        name="feed_back",
    )(length, rows_grad, block, cot, fg.reshape(1, -1), hidden, eg.reshape(1, -1), mixed, active, slope, wr, we)


def backward_kernel(np_, ns, x, ag, q, k, v, context_t, branch, hidden_grad, normed, gains_dec, gains_feed,
                    probs, wo, wq, wk, wv, wide, tall, dec, encoded,
                    red, small_out, dec_out, enc_out, grad_out,
                    wos, wqs, wks, wvs, d_out, dp, ds, dq_t, dq, dk, dv, k_t, normed_t, ng, in_grad,
                    pbuf, band, diag, own, au, r0, r1y, r1x, r1a, r2, r3, sm, smr, smz,
                    psem, wsem, loc, c_s, c_r, a_s, a_r, b_s, b_r, ac_s, ac_r, ax_s, ax_r, z_s, z_r,
                    m_s, m_r, mz_s, mz_r, d_s, d_r, e_s, e_r, g_s, g_r):
    n, width = x.shape
    heads = probs.shape[0]
    nz = np_ // 2
    rows, lanes = r0.shape[4:]
    count = np_ * ns
    p = lax.axis_index("pairs")
    s = lax.axis_index("seq")
    c = lax.rem(s, 2)
    y = s // 2
    xx = lax.rem(p, 2)
    z = p // 2
    me = p * ns + s
    core_peer = (p, s + 1 - 2 * c)
    y_peer = (p, lax.rem(s + 2, 4))
    x_peer = (p + 1 - 2 * xx, s)

    def place(d):
        lin = lax.rem(me + d, count)
        return (lin // ns, lax.rem(lin, ns))

    barrier = pltpu.get_barrier_semaphore()

    @pl.loop(1, count)
    def _(d):
        pl.semaphore_signal(barrier, inc=1, device_id=place(d), device_id_type=MESH)

    def remote(src, dst, send, recv, peer):
        return pltpu.make_async_remote_copy(
            src_ref=src, dst_ref=dst, send_sem=send, recv_sem=recv,
            device_id=peer, device_id_type=MESH)

    weights = [pltpu.make_async_copy(a, b, wsem.at[i])
               for i, (a, b) in enumerate(((wo, wos), (wq, wqs), (wk, wks), (wv, wvs)))]

    def fetch(h, slot):
        return pltpu.make_async_copy(probs.at[h], pbuf.at[slot], psem.at[slot])

    def unit(i, core):
        return (wide, tall)[i // 2].at[i % 2, core]

    def core_copy(i):
        return remote(unit(i, 1 - c), r0.at[i], c_s.at[i], c_r.at[i], core_peer)

    def own_copy(i):
        return pltpu.make_async_copy(unit(i, c), own.at[i], loc.at[i])

    def first(i):
        if i % 2 == 0:
            return remote(own.at[i, 1 - y], r1y.at[i // 2], a_s.at[i], a_r.at[i], y_peer)
        return remote(own.at[i, :, :, 1 - xx], r1x.at[i // 2], a_s.at[i], a_r.at[i], x_peer)

    def second(i):
        if i % 2 == 0:
            return remote(own.at[i, y, :, 1 - xx], r2.at[i], b_s.at[i], b_r.at[i], x_peer)
        return remote(own.at[i, 1 - y, :, xx], r2.at[i], b_s.at[i], b_r.at[i], y_peer)

    def final(i):
        return own.at[i, y] if i < 4 else au.at[i - 4, c, y]

    def last(i, d):
        t = lax.rem(z + d, nz)
        return remote(final(i).at[t, xx], r3.at[i, d], z_s.at[i, d], z_r.at[i, d], (t * 2 + xx, s))

    def attn_core(w, half):
        return remote(au.at[w, 1 - c, half], r0.at[4 + w, half], ac_s.at[w, half], ac_r.at[w, half], core_peer)

    def attn_x(w, half):
        return remote(au.at[w, c, half, :, 1 - xx], r1a.at[w, half], ax_s.at[w, half], ax_r.at[w, half], x_peer)

    def attn_y(w):
        return remote(au.at[w, c, 1 - y, :, xx], r2.at[4 + w], b_s.at[4 + w], b_r.at[4 + w], y_peer)

    def dec_copy(d):
        to = place(d)
        return remote(dec.at[to[0] * ns + to[1]], dec_out.at[me], d_s.at[d], d_r.at[d], to)

    def enc_copy(d):
        t = lax.rem(s + d, ns)
        return remote(encoded.at[t], enc_out.at[s], e_s.at[d], e_r.at[d], (p, t))

    def grad_copy(d):
        t = lax.rem(s + d, ns)
        return remote(in_grad.at[t], grad_out.at[s], g_s.at[d], g_r.at[d], (p, t))

    keep_dec = pltpu.make_async_copy(dec.at[me], dec_out.at[me], loc.at[4])
    keep_enc = pltpu.make_async_copy(encoded.at[s], enc_out.at[s], loc.at[5])
    keep_grad = pltpu.make_async_copy(in_grad.at[s], grad_out.at[s], loc.at[6])

    def step_a(i):
        core_copy(i).wait()
        own_copy(i).wait()

        @pl.loop(0, nz)
        def _(b):
            for a in range(2):
                for e in range(2):
                    own[i, a, b, e] = own[i, a, b, e] + r0[i, a, b, e]

        first(i).start()

    def step_b(i):
        first(i).wait()

        @pl.loop(0, nz)
        def _(b):
            for e in range(2):
                if i % 2 == 0:
                    own[i, y, b, e] = own[i, y, b, e] + r1y[i // 2, b, e]
                else:
                    own[i, e, b, xx] = own[i, e, b, xx] + r1x[i // 2, e, b]

        second(i).start()

    def step_c(i):
        if i < 4:
            second(i).wait()
        else:
            attn_y(i - 4).wait()

        @pl.loop(0, nz)
        def _(b):
            f = final(i)
            f[b, xx] = f[b, xx] + r2[i, b]

        @pl.loop(1, nz)
        def _(d):
            last(i, d).start()

    def step_d(i):
        red[i] = final(i)[z, xx].astype(F32)

        @pl.loop(1, nz)
        def _(d):
            last(i, d).wait()
            red[i] = red[i] + r3[i, d].astype(F32)

    def attn_a(w, half):
        attn_core(w, half).wait()

        @pl.loop(0, nz)
        def _(b):
            for e in range(2):
                au[w, c, half, b, e] = au[w, c, half, b, e] + r0[4 + w, half, b, e]

        attn_x(w, half).start()

    def attn_b(w, half):
        attn_x(w, half).wait()

        @pl.loop(0, nz)
        def _(b):
            au[w, c, half, b, xx] = au[w, c, half, b, xx] + r1a[w, half, b]

    for copy in weights:
        copy.start()
    first_half, last_half = 1 - y, y
    fetch(first_half * (heads // 2), 0).start()
    fetch(first_half * (heads // 2) + 1, 1).start()
    for i in range(4):
        own_copy(i).start()
    keep_dec.start()
    keep_enc.start()
    diag[...] = jnp.zeros_like(diag)
    weights[0].wait()

    @pl.loop(0, width // 384)
    def _(j):
        cols = pl.ds(pl.multiple_of(j * 384, 128), 384)
        d_out[:, cols] = mm_t(branch[...], wos[cols, :]).astype(BF)

    pl.semaphore_wait(barrier, count - 1)
    for i in range(4):
        core_copy(i).start()
    for d in range(1, ns):
        enc_copy(d).start()

    @pl.loop(1, count)
    def _(d):
        dec_copy(d).start()

    @pl.loop(0, n // 128)
    def _(i):
        r = pl.ds(pl.multiple_of(i * 128, 128), 128)
        normed_t[:, r] = normed[r].T

    lane = lax.broadcasted_iota(jnp.int32, (n, 128), 1)
    lane_s = lax.broadcasted_iota(jnp.int32, (128, 128), 1)
    row_s = lax.broadcasted_iota(jnp.int32, (128, 128), 0)

    def pair(half, g):
        cols = pl.ds(pl.multiple_of(half * (width // 2) + g * 128, 128), 128)
        k_t[...] = k[:, cols].T
        dop = d_out[:, cols]
        qp = q[:, cols]
        vp = v[:, cols]
        zero = jnp.zeros_like(qp)
        for a in range(2):
            h = half * (heads // 2) + 2 * g + a
            mine = (lane < 64) if a == 0 else (lane >= 64)
            dp[...] = mm_t(jnp.where(mine, vp, zero), dop)
            fetch(h, a).wait()
            for j in range(n // 128):
                pj = pbuf[a, :, j * 128:(j + 1) * 128].astype(F32)
                pd = pj * dp[:, j * 128:(j + 1) * 128]
                total = jnp.sum(pd, axis=0, keepdims=True)
                sg = pd - pj * total
                ds[:, j * 128:(j + 1) * 128] = sg.astype(BF)
                for i in range(n // 128):
                    t = sg[i * 128:(i + 1) * 128]
                    if abs(i - j) <= 1:
                        b = (i - j + 1) * 128
                        if j == 0 or (j == 1 and i == 0):
                            band[b:b + 128, :] = t
                        else:
                            band[b:b + 128, :] += t
                    else:
                        f = 5 if i > j else 4
                        diag[h, f:f + 1, :] += jnp.sum(t, axis=0, keepdims=True)
            dvp = mm(pbuf[a], jnp.where(mine, dop, zero))
            dkp = mm(ds[...], jnp.where(mine, qp, zero))
            dq_t[pl.ds(pl.multiple_of(h * 64, 64), 64), :] = mm(k_t[a * 64:(a + 1) * 64, :], ds[...]).astype(BF)
            if a == 0:
                dk_sum, dv_sum = dkp, dvp
            else:
                dk[:, cols] = (dk_sum + dkp).astype(BF)
                dv[:, cols] = (dv_sum + dvp).astype(BF)
            for b in range(3):
                t = band[b * 128:(b + 1) * 128, :]
                for bit in range(7):
                    t = jnp.where((row_s >> bit) % 2 == 1, pltpu.roll(t, 128 - (1 << bit), 1), t)
                straight = jnp.sum(jnp.where(lane_s + row_s < 128, t, 0.0), axis=0, keepdims=True)
                whole = jnp.sum(t, axis=0, keepdims=True)
                diag[h, b:b + 1, :] += straight
                diag[h, b + 1:b + 2, :] += whole - straight

    part = width // 4

    def units_of(half):
        cols = pl.ds(pl.multiple_of(half * (width // 2), 128), width // 2)
        lower = pl.ds(pl.multiple_of(half * (width // 2), 128), width // 2)
        dq_h = dq_t[lower, :].T
        dq[:, cols] = dq_h
        dk_h = dk[:, cols]
        dv_h = dv[:, cols]
        br_h = branch[:, cols]
        zero = jnp.zeros((n, part), BF)
        for cc in range(2):
            e = slice(cc * part, (cc + 1) * part)
            g = mm(normed_t[...], jnp.concatenate([dq_h[:, e], dk_h[:, e]], axis=1))
            au[0, cc, half] = g.astype(BF).reshape(nz, 2, rows, lanes)
            g = (mm(normed_t[...], jnp.concatenate([dv_h[:, e], zero], axis=1))
                 + mm(context_t[...], jnp.concatenate([zero, br_h[:, e]], axis=1)))
            au[1, cc, half] = g.astype(BF).reshape(nz, 2, rows, lanes)
        for w in range(2):
            attn_core(w, half).start()

    quarter = heads // 4

    @pl.loop(0, quarter)
    def _(g):
        pair(first_half, g)
        nxt = jnp.where(g == quarter - 1, last_half * (heads // 2), first_half * (heads // 2) + 2 * (g + 1))
        fetch(nxt, 0).start()
        fetch(nxt + 1, 1).start()

        @pl.when(g == 0)
        def _():
            step_a(0)
            step_a(1)

        @pl.when(g == 1)
        def _():
            step_a(2)
            step_a(3)

    units_of(first_half)

    @pl.loop(0, quarter)
    def _(g):
        pair(last_half, g)

        @pl.when(g < quarter - 1)
        def _():
            nxt = last_half * (heads // 2) + 2 * (g + 1)
            fetch(nxt, 0).start()
            fetch(nxt + 1, 1).start()

        @pl.when(g == 0)
        def _():
            attn_a(0, first_half)
            attn_a(1, first_half)

        @pl.when(g == 1)
        def _():
            step_b(0)
            step_b(1)

    units_of(last_half)
    for copy in weights[1:]:
        copy.wait()

    @pl.loop(0, 2)
    def _(i):
        r = pl.ds(pl.multiple_of(i * (n // 2), 128), n // 2)
        ng[r] = mm_t(dq[r], wqs[...]) + mm_t(dk[r], wks[...]) + mm_t(dv[r], wvs[...])

    attn_a(0, last_half)
    attn_a(1, last_half)
    sm[...] = jnp.zeros_like(sm)
    slot_rows = n // ns
    gain_sum = jnp.zeros((1, width), F32)
    for i in range(ns):
        r = slice(i * slot_rows, (i + 1) * slot_rows)
        t = x[r].astype(F32)
        down, gain = norm_down(t, rms_scale(t), ag[...], ng[r])
        in_grad[i] = (hidden_grad[r] + down).astype(BF)
        gain_sum = gain_sum + jnp.sum(gain, axis=0, keepdims=True)
    keep_grad.start()
    for d in range(1, ns):
        grad_copy(d).start()

    col = lax.broadcasted_iota(jnp.int32, (128, width), 1)
    offset = (col // 128 - 1) * 128 - lax.rem(col, 128)
    offset = jnp.where(col >= width - 128, 256, jnp.where(col >= width - 256, -256, offset))
    dist = jnp.abs(offset)
    bucket = jnp.full_like(dist, 8)
    for edge in EDGES:
        bucket = bucket + (dist >= edge).astype(jnp.int32)
    bucket = jnp.where(dist < 8, dist, bucket) + jnp.where(offset > 0, 16, 0)
    pick = jnp.where(bucket == lax.broadcasted_iota(jnp.int32, (128, width), 0), 1.0, 0.0)
    bias = jnp.zeros((16, 128), F32)
    for i in range(width // 128):
        bias = bias + lax.dot_general(diag[:, i, :], pick[:, i * 128:(i + 1) * 128], (((1,), (1,)), ((), ())),
                                      precision=HIGHEST, preferred_element_type=F32)
    sm[0, 40:56, :] = bias
    gains = [gains_dec[i:i + 1, :] for i in range(3)] + [gains_feed[i:i + 1, :] for i in range(2)] + [gain_sum]
    for i, gain in enumerate(gains):
        for j in range(width // 128):
            sm[0, i * 6 + j:i * 6 + j + 1, :] = gain[:, j * 128:(j + 1) * 128]

    def small_copy(i):
        return remote(sm.at[i], smr.at[i], m_s.at[i], m_r.at[i], (core_peer, y_peer, x_peer)[i])

    def z_small(d):
        return remote(smz.at[z], smz.at[z], mz_s.at[d], mz_r.at[d], (lax.rem(z + d, nz) * 2 + xx, s))

    small_copy(0).start()
    step_b(2)
    step_b(3)
    small_copy(0).wait()
    sm[1] = sm[0] + smr[0]
    small_copy(1).start()
    attn_b(0, first_half)
    attn_y(0).start()
    attn_b(1, first_half)
    attn_y(1).start()
    step_c(0)
    step_c(1)
    small_copy(1).wait()
    sm[2] = sm[1] + smr[1]
    small_copy(2).start()
    step_c(2)
    step_c(3)
    attn_b(0, last_half)
    small_copy(2).wait()
    smz[z] = sm[2] + smr[2]

    @pl.loop(1, nz)
    def _(d):
        z_small(d).start()

    step_c(4)
    attn_b(1, last_half)
    step_c(5)
    for i in range(6):
        step_d(i)

    @pl.loop(1, nz)
    def _(d):
        z_small(d).wait()

    small_out[...] = smz[0]

    @pl.loop(1, nz)
    def _(d):
        small_out[...] = small_out[...] + smz[d]

    keep_dec.wait()
    keep_enc.wait()
    keep_grad.wait()
    for d in range(1, ns):
        enc_copy(d).wait()
        grad_copy(d).wait()

    @pl.loop(1, count)
    def _(d):
        dec_copy(d).wait()


def backward(np_, ns, x, ag, q, k, v, context_t, branch, hidden_grad, normed, gains_dec, gains_feed,
             probs, wo, wq, wk, wv, wide, tall, dec, encoded):
    n, width = x.shape
    heads = probs.shape[0]
    nz = np_ // 2
    rows, lanes = wide.shape[5:]
    count = np_ * ns
    padded = normed.shape[1]
    vm = pl.BlockSpec(memory_space=pltpu.VMEM)
    hb = pl.BlockSpec(memory_space=pl.ANY)
    S = jax.ShapeDtypeStruct
    V = pltpu.VMEM
    dma = pltpu.SemaphoreType.DMA
    nar = V((n, width), BF)
    square = V((width, width), BF)
    slots = (ns, n // ns, width)
    small = (64, 128)
    return pl.pallas_call(
        functools.partial(backward_kernel, np_, ns),
        out_shape=(S((6, rows, lanes), F32), S(small, F32), S(dec.shape, BF), S(slots, BF), S(slots, BF)),
        in_specs=[vm] * 11 + [hb] * 9,
        out_specs=(vm, vm, hb, hb, hb),
        scratch_shapes=[
            square, square, square, square, nar, V((n, n), F32), V((n, n), BF), V((width, n), BF), nar, nar, nar,
            V((128, n), BF), V((padded, n), BF), V((n, width), F32), V(slots, BF),
            V((2, n, n), BF), V((384, 128), F32), V((16, 8, 128), F32),
            V((4, 2, nz, 2, rows, lanes), BF), V((2, 2, 2, nz, 2, rows, lanes), BF), V((6, 2, nz, 2, rows, lanes), BF),
            V((2, nz, 2, rows, lanes), BF), V((2, 2, nz, rows, lanes), BF), V((2, 2, nz, rows, lanes), BF),
            V((6, nz, rows, lanes), BF), V((6, nz, rows, lanes), BF),
            V((3,) + small, F32), V((3,) + small, F32), V((nz,) + small, F32),
            dma((2,)), dma((4,)), dma((7,)), dma((4,)), dma((4,)), dma((4,)), dma((4,)), dma((6,)), dma((6,)),
            dma((2, 2)), dma((2, 2)), dma((2, 2)), dma((2, 2)), dma((6, nz)), dma((6, nz)),
            dma((3,)), dma((3,)), dma((nz,)), dma((nz,)), dma((count,)), dma((count,)),
            dma((ns,)), dma((ns,)), dma((ns,)), dma((ns,)),
        ],
        compiler_params=pltpu.CompilerParams(
            collective_id=0, has_side_effects=True, vmem_limit_bytes=62 * 1024 * 1024),
        name="backward",
    )(x, ag.reshape(1, -1), q, k, v, context_t, branch, hidden_grad, normed, gains_dec, gains_feed,
      probs, wo, wq, wk, wv, wide, tall, dec, encoded.reshape(slots))


def two_kernels(
    np_, ns, r, rp, lanes, side, length, final_gain, expand_gain, attend_gain, dec_gains,
    rows_grad, block, cot, reduce_weight, active, expand_weight, hidden, slope, mixed_t,
    output_weight, query_weight, key_weight, value_weight, query, key, value, x, normed_t,
    context_t, probs, dec_all, encoded,
):
    seq_len, ff = active.shape
    nz = np_ // 2
    wide, tall, hidden_grad, branch, feed_gains = feed_back(
        1, length, rows_grad, block, cot, final_gain, hidden, expand_gain, mixed_t.T, active,
        slope, reduce_weight, expand_weight)

    def pad(unit):
        return jnp.pad(unit, ((0, 0),) * 5 + ((0, rp - r), (0, 0)))

    tall = tall.reshape(2, 2, 2, r, side, nz, 2, ff // np_).transpose(0, 1, 2, 5, 6, 3, 4, 7)
    tall = pad(tall.reshape(2, 2, 2, nz, 2, r, lanes))
    wide = pad(wide.reshape(2, 2, 2, nz, 2, r, lanes))
    gap = ((0, 0), (0, rp - r), (0, 0))
    normed_t = jnp.pad(normed_t.reshape(np_, r, seq_len), gap).reshape(np_ * rp, seq_len)
    context_t = jnp.pad(context_t.reshape(np_, r, seq_len), gap).reshape(np_ * rp, seq_len)
    return backward(
        np_, ns, x, attend_gain, query, key, value, context_t, branch, hidden_grad, normed_t.T,
        dec_gains, feed_gains, probs, output_weight, query_weight, key_weight, value_weight,
        wide, tall, dec_all, encoded)


def per_device(
    enc_input, dec_input, lengths, attend_gain, query_weight, key_weight, value_weight,
    output_weight, bias_table, expand_gain, expand_weight, reduce_weight, final_gain,
    self_gain, self_value, self_output, cross_gain, cross_query, cross_key, cross_value,
    cross_output, feed_gain, feed_expand, feed_reduce, enc_cotangent, dec_cotangent,
):
    group, local_rows, width = enc_input.shape
    buckets, heads = bias_table.shape
    size = width // heads
    ff = expand_weight.shape[1]
    ns = lax.axis_size("seq")
    np_ = lax.axis_size("pairs")
    r = width // np_
    aligned = np_ == 8 and r % 32 == 0 and (ff // np_) % 128 == 0 and ff == 4 * width
    seq_len = local_rows * ns
    weights = (query_weight, key_weight, value_weight, output_weight, expand_weight, reduce_weight,
               self_value, self_output, cross_query, cross_key, cross_value, cross_output,
               feed_expand, feed_reduce)
    (normed_t, query, key, value, probs, context_t, hidden, mixed_t, active, slope, block, encoded,
     x, cot, rows_grad, wide_rows, mids, dec_input_grad, *dec_rows) = forward(
        np_, ns, aligned, lengths, bias_table.T,
        (attend_gain, expand_gain, final_gain, self_gain, cross_gain, feed_gain),
        dec_input, dec_cotangent, enc_input, enc_cotangent, weights)
    x = x.reshape(seq_len, width)
    cot = cot.reshape(seq_len, width)
    if aligned:
        state, dec_all = dec_rows
        red, small_sum, dec_got, enc_out, grad_out, dec_block = fused(
            np_, ns, lengths, final_gain, expand_gain, attend_gain, state, wide_rows,
            rows_grad, block, cot,
            reduce_weight, active, expand_weight, hidden, slope, mixed_t, output_weight,
            query_weight, key_weight, value_weight, query, key, value, x, normed_t, context_t,
            probs, dec_all, encoded, feed_reduce)
        (enc_out, grad_out, dec_block, dec_input_grad, grad_query, grad_key, grad_value, grad_output, grad_expand, grad_reduce,
         bias, *rest) = finish(
            heads, buckets, red, small_sum, dec_got, dec_block, dec_input_grad, enc_out, grad_out)
        gains = rest[:6]
        grad_sv, grad_so, grad_cq, grad_ck, grad_cv, grad_co, feed_in, feed_out = rest[6:]
        return (
            enc_out, dec_block, grad_out, dec_input_grad, gains[5], grad_query, grad_key,
            grad_value, grad_output, bias.T, gains[4], grad_expand, grad_reduce.T, gains[3],
            gains[0], grad_sv, grad_so, gains[1], grad_cq, grad_ck, grad_cv, grad_co, gains[2],
            feed_in, feed_out.T,
        )
    dec_block, dec_gains, left, right = dec_rows
    length = lax.dynamic_slice_in_dim(lengths, lax.axis_index("seq"), 1)
    rp = -(-r // 16) * 16
    lanes = ff // 8
    side = width // 8 // r
    cols = width // ns

    left_cut = jnp.concatenate([
        left.reshape(5, np_, r).transpose(1, 0, 2).reshape(np_, 5 * r),
        wide_rows[0].reshape(np_, 4 * r),
    ], axis=1)
    mid_cut = mids.reshape(2, ns, heads // ns, np_, r).transpose(3, 1, 0, 2, 4)
    mid_cut = mid_cut.reshape(np_, ns, 6 * r)
    right_cut = jnp.concatenate([
        right.reshape(7, ns, cols).transpose(1, 0, 2).reshape(ns, 7 * cols),
        wide_rows[1].reshape(ns, 4 * cols)], axis=1)
    dec_all = jnp.concatenate([
        jnp.broadcast_to(left_cut[:, None], (np_, ns, 9 * r)), mid_cut,
        jnp.broadcast_to(right_cut[None], (np_, ns, 11 * cols))], axis=-1)
    dec_all = dec_all.astype(BF).reshape(np_ * ns, -1)
    used = dec_all.shape[1]
    dec_rows = -(-used // 2048) * 16
    dec_all = jnp.pad(dec_all, ((0, 0), (0, dec_rows * 128 - used)))
    dec_all = dec_all.reshape(np_ * ns, dec_rows, 128)

    red, small_sum, dec_got, enc_out, grad_out = two_kernels(
        np_, ns, r, rp, lanes, side, length, final_gain, expand_gain, attend_gain, dec_gains,
        rows_grad, block, cot, reduce_weight, active, expand_weight, hidden, slope, mixed_t,
        output_weight, query_weight, key_weight, value_weight, query, key, value, x, normed_t,
        context_t, probs, dec_all, encoded)

    got = dec_got.reshape(np_ * ns, -1)
    lefts = got[:, :9 * r].reshape(-1, 9, r)
    mid_got = got[:, 9 * r:15 * r].reshape(-1, 2, 3, r)
    rights = got[:, 15 * r:15 * r + 11 * cols].reshape(-1, 11, cols)
    plain = jnp.einsum("nkr,nkc->krc", lefts[:, :4], rights[:, :4], preferred_element_type=F32)
    crossed = jnp.einsum("nkhr,nkhd->krhd", mid_got, rights[:, 4:6].reshape(-1, 2, 3, size),
                         preferred_element_type=F32).reshape(2, r, cols)
    feed_in = jnp.einsum("nr,nc->rc", lefts[:, 4], rights[:, 7:11].reshape(-1, 4 * cols),
                         preferred_element_type=F32)
    feed_out = jnp.einsum("nr,nc->rc", lefts[:, 5:9].reshape(-1, 4 * r), rights[:, 6],
                          preferred_element_type=F32)
    red = red[:, :r]
    grad_reduce = red[2:4].reshape(2, r, side, ff // np_).reshape(cols, ff // np_).T
    gains = small_sum[:36].reshape(6, width)
    bias = small_sum[40:40 + heads, :buckets].T
    return (
        enc_out, dec_block, grad_out, dec_input_grad,
        gains[5],
        red[4][:, :cols], red[4][:, cols:], red[5][:, :cols], red[5][:, cols:],
        bias,
        gains[4],
        jnp.concatenate([red[0], red[1]], axis=1), grad_reduce,
        gains[3],
        gains[0], plain[0], plain[1],
        gains[1], plain[2], crossed[0], crossed[1], plain[3],
        gains[2], feed_in, feed_out,
    )


def solution(mesh):
    rows = P("pairs", "seq", None)
    single = P(("pairs", "seq"), None)
    block = P("pairs", "seq")
    return jax.shard_map(
        per_device,
        mesh=mesh,
        in_specs=(rows, single, P("pairs")) + (P(),) * 21 + (rows, single),
        out_specs=(
            rows, single, rows, single,
            P(), block, block, block, block, P(), P(), block, block, P(),
            P(), block, block, P(), block, block, block, block, P(), block, block,
        ),
        check_vma=False,
    )
```

```python
import functools
import itertools

import jax
import jax.numpy as jnp
from jax import lax
from jax.experimental import pallas as pl
from jax.experimental.pallas import tpu as pltpu
from jax.sharding import PartitionSpec as P

EPSILON = 1e-06
EDGES = (12, 16, 23, 32, 46, 64, 91)
HIGHEST = lax.Precision.HIGHEST
MESH = pl.DeviceIdType.MESH
BF = jnp.bfloat16
F32 = jnp.float32


def mm(a, b):
    return jnp.dot(a, b, preferred_element_type=F32)
def mm_t(a, b):
    return lax.dot_general(a, b, (((1,), (1,)), ((), ())), preferred_element_type=F32)
def t_mm(a, b):
    return lax.dot_general(a, b, (((0,), (0,)), ((), ())), preferred_element_type=F32)

def rms_scale(v):
    return lax.rsqrt(jnp.mean(v * v, axis=-1, keepdims=True) + EPSILON)

def gelu_parts(u):
    u2 = u * u
    t = jnp.tanh(u * (0.7978845608 + (0.7978845608 * 0.044715) * u2))
    half = 0.5 + 0.5 * t
    lower = u * half
    return lower, half + lower * (1.0 - t) * (0.7978845608 + (3 * 0.7978845608 * 0.044715) * u2)

def norm_down(v, r, g, dy):
    vr = v * r
    gd = g * dy
    return r * (gd - vr * jnp.mean(vr * gd, axis=-1, keepdims=True)), vr * dy

def diagonal_buckets(shape, width):
    col = lax.broadcasted_iota(jnp.int32, shape, 1)
    offset = (col // 128 - 1) * 128 - lax.rem(col, 128)
    offset = jnp.where(col >= width - 128, 256, jnp.where(col >= width - 256, -256, offset))
    dist = jnp.abs(offset)
    bucket = jnp.full_like(dist, 8)
    for edge in EDGES:
        bucket = bucket + (dist >= edge).astype(jnp.int32)
    bucket = jnp.where(dist < 8, dist, bucket) + jnp.where(offset > 0, 16, 0)
    return jnp.where(bucket == lax.rem(lax.broadcasted_iota(jnp.int32, shape, 0), 32), 1.0, 0.0)


def own_heads(heads, width):
    return (lax.broadcasted_iota(jnp.int32, (heads, width), 1) // (width // heads)
            == lax.broadcasted_iota(jnp.int32, (heads, width), 0))


def decoder_start_back(x, sg, after, cg, middle_grad, score_rows, ck, cq, so, sv):
    own = own_heads(*score_rows.shape)
    cross_q_grad = jnp.sum(jnp.where(own, mm(score_rows, ck[...]), 0.0), axis=0, keepdims=True).astype(BF)
    after_down, cross_gain = norm_down(after, rms_scale(after), cg, mm_t(cross_q_grad, cq[...]))
    after_grad = middle_grad + after_down
    self_branch = after_grad.astype(BF)
    self_values_grad = mm_t(self_branch, so[...]).astype(BF)
    x_down, self_gain = norm_down(x, rms_scale(x), sg, mm_t(self_values_grad, sv[...]))
    return cross_q_grad, self_branch, self_values_grad, (after_grad + x_down).astype(BF), self_gain, cross_gain


def cut_rows(np_, ns, left, right, at, wide, mids, dec, cuts, both):
    heads, width = mids.shape[1:]
    ff = wide.shape[1]
    rows, cols, step = width // np_, width // ns, heads // ns
    both[...] = jnp.zeros_like(both)
    cuts[...] = jnp.zeros_like(cuts)
    for j in range(ns):
        for i in range(7):
            t = right[at + i:at + i + 1, j * cols:(j + 1) * cols]
            both[j, 2 * i:2 * i + 1, :] = t[:, :128]
            both[j, 2 * i + 1:2 * i + 2, 0:cols - 128] = t[:, 128:]
        for i in range(6):
            lo = j * width + i * 128
            both[j, 14 + i:15 + i, :] = wide[1:2, lo:lo + 128]
    for i in range(np_):
        cuts[0:5, 0:rows] = left[0:5, i * rows:(i + 1) * rows]
        for a in range(3):
            lo = i * (ff // np_) + a * 128
            cuts[5 + a:6 + a, :] = wide[0:1, lo:lo + 128]
        for j in range(ns):
            for w in range(2):
                cuts[8 + w * step:8 + (w + 1) * step, 0:rows] = (
                    mids[w, j * step:(j + 1) * step, i * rows:(i + 1) * rows])
            dec[i * ns + j, 0:16, :] = cuts[...].astype(BF)
            dec[i * ns + j, 16:48, :] = both[j].astype(BF)


def forward_kernel(np_, ns, cut, lengths, table, ag, eg, fg, sg, cg, dg, dec_in, dec_cot, enc_in, enc_cot,
                   wq, wk, wv, wo, we, wr, sv, so, cq, ck, cv, co, fe, fr,
                   normed_t, q, k, v, probs, context_t, hidden, mixed_t, active, slope, block, low, x_out, cot_out,
                   rows_grad, wide, mids, dec_in_grad, *rest):
    if cut:
        state, dec, *rest = rest
    else:
        dec_out, dec_gains, left, right, *rest = rest
    (wqs, wks, wvs, wos, wes, wrs, svs, sos, cqs, cks, cvs, cos, fes, frs, xs, normed, nt, qs, ks, vs, ctx, hid,
     mixed, mt, act, slo, blk, rws, lws, rgs, band, vecs, v_t, s_t, pbuf, *rest) = rest
    if cut:
        cuts, both, *rest = rest
    sems, psem, osem, x_s, x_r, c_s, c_r, loc = rest
    ag, eg, fg, sg, cg, dg = (g[...].reshape(1, -1) for g in (ag, eg, fg, sg, cg, dg))
    n, width = normed.shape
    heads = probs.shape[0]
    size = width // heads
    ff = act.shape[1]
    slot = n // ns
    p = lax.axis_index("pairs")
    s = lax.axis_index("seq")
    length = lengths[s]

    barrier = pltpu.get_barrier_semaphore()
    for d in range(1, ns):
        pl.semaphore_signal(barrier, inc=1, device_id=(p, lax.rem(s + d, ns)), device_id_type=MESH)

    def rows_copy(src, dst, send, recv, d):
        t = lax.rem(s + d, ns)
        return pltpu.make_async_remote_copy(
            src_ref=src.at[t], dst_ref=dst.at[s], send_sem=send.at[d], recv_sem=recv.at[d],
            device_id=(p, t), device_id_type=MESH)

    x_copies = [rows_copy(enc_in, xs, x_s, x_r, d) for d in range(1, ns)]
    cot_copies = [rows_copy(enc_cot, cot_out, c_s, c_r, d) for d in range(1, ns)]
    keep_x = pltpu.make_async_copy(enc_in.at[s], xs.at[s], loc.at[0])
    keep_cot = pltpu.make_async_copy(enc_cot.at[s], cot_out.at[s], loc.at[1])
    keep_x.start()
    load = []
    for src, dst in ((sv, svs), (so, sos), (cq, cqs), (ck, cks), (fr, frs), (wq, wqs), (wk, wks), (wv, wvs),
                     (wo, wos), (we, wes), (wr, wrs), (cv, cvs), (co, cos), (fe, fes)):
        load.append(pltpu.make_async_copy(src, dst, sems.at[len(load)]))
        load[-1].start()
    pl.semaphore_wait(barrier, ns - 1)
    for copy in x_copies + cot_copies:
        copy.start()
    keep_cot.start()
    saved = []

    def save(src, dst):
        copy = pltpu.make_async_copy(src, dst, osem.at[len(saved)])
        saved.append(copy)
        copy.start()

    vec = lax.dot_general(table[...], diagonal_buckets((table.shape[1], width), width), (((1,), (0,)), ((), ())),
                          precision=HIGHEST, preferred_element_type=F32)
    for i in range(width // 128):
        vecs[:, i, :] = vec[:, i * 128:(i + 1) * 128]
    lane_s = lax.broadcasted_iota(jnp.int32, (128, 128), 1)
    row_s = lax.broadcasted_iota(jnp.int32, (128, 128), 0)

    @pl.loop(0, heads)
    def _(h):
        for b in range(3):
            t = jnp.where(lane_s + row_s < 128, vecs[h, b:b + 1, :], vecs[h, b + 1:b + 2, :])
            for bit in range(7):
                t = jnp.where((row_s >> bit) % 2 == 1, pltpu.roll(t, 1 << bit, 1), t)
            band[h, b * 128:(b + 1) * 128, :] = t

    x = dec_in[...].astype(F32)
    cot = dec_cot[...]
    own = own_heads(heads, width)

    def spread(r):
        return jnp.where(own, r.astype(F32), 0.0).astype(BF)

    def collect(r):
        return jnp.sum(jnp.where(own, r, 0.0), axis=0, keepdims=True)

    x_r = rms_scale(x)
    self_normed = (x * x_r * sg).astype(BF)
    load[0].wait()
    self_values = mm(self_normed, svs[...]).astype(BF)
    load[1].wait()
    after = x + mm(self_values, sos[...])
    after_r = rms_scale(after)
    cross_normed = (after * after_r * cg).astype(BF)
    load[2].wait()
    cross_q = mm(cross_normed, cqs[...]).astype(BF)
    load[3].wait()
    q_rows = mm_t(spread(cross_q), cks[...]).astype(BF)
    load[4].wait()
    active_back = mm_t(cot, frs[...])

    keep_x.wait()
    for copy in x_copies:
        copy.wait()
    save(xs, x_out)
    for i in range(ns):
        r = slice(i * slot, (i + 1) * slot)
        t = xs[i].astype(F32)
        t = t * rms_scale(t) * ag
        normed[r] = t.astype(BF)
        nt[:, r] = t.T.astype(BF)
    save(nt, normed_t)
    for j, (w, out, dst) in enumerate(((wqs, qs, q), (wks, ks, k), (wvs, vs, v))):
        load[5 + j].wait()
        for i in range(2):
            r = slice(i * (n // 2), (i + 1) * (n // 2))
            out[r] = mm(normed[r], w[...]).astype(BF)
        save(out, dst)

    lane = lax.broadcasted_iota(jnp.int32, (n, 128), 1)
    row = lax.broadcasted_iota(jnp.int32, (n, 128), 0)
    q_mark = jnp.where(lane == 0, 1.0, 0.0).astype(BF)
    k_mark = jnp.where((lane == 0) & (row >= length), -1e30, 0.0).astype(BF)

    def keep(g, a):
        at = 2 * lax.rem(g, 2) + a
        return pltpu.make_async_copy(pbuf.at[at], probs.at[2 * g + a], psem.at[at])

    @pl.loop(0, heads // 2)
    def _(g):
        @pl.when(g > 1)
        def _():
            for a in range(2):
                keep(g - 2, a).wait()

        cols = pl.ds(pl.multiple_of(g * 128, 128), 128)
        v_t[...] = vs[:, cols].T
        qq = jnp.concatenate([qs[:, cols], q_mark], axis=1)
        kp = ks[:, cols]
        for a in range(2):
            mine = (lane < 64) if a == 0 else (lane >= 64)
            kk = jnp.concatenate([jnp.where(mine, kp, jnp.zeros_like(kp)), k_mark], axis=1)
            s_t[a] = mm_t(kk, qq)
        for a in range(2):
            h = 2 * g + a
            at = 2 * lax.rem(g, 2) + a
            for j in range(n // 128):
                tile = []
                for i in range(n // 128):
                    t = s_t[a, i * 128:(i + 1) * 128, j * 128:(j + 1) * 128]
                    if abs(i - j) <= 1:
                        t = t + band[h, (i - j + 1) * 128:(i - j + 2) * 128, :]
                    else:
                        f = 5 if i > j else 4
                        t = t + vecs[h, f:f + 1, :]
                    tile.append(t)
                t = jnp.concatenate(tile, axis=0)
                m = jnp.max(t, axis=0, keepdims=True)
                e = jnp.exp(t - m)
                total = jnp.sum(e, axis=0, keepdims=True)
                pbuf[at, :, j * 128:(j + 1) * 128] = (e * (1.0 / total)).astype(BF)
            ctx[pl.ds(pl.multiple_of(h * 64, 64), 64), :] = mm(v_t[a * 64:(a + 1) * 64, :], pbuf[at]).astype(BF)
            keep(g, a).start()

    save(ctx, context_t)
    load[8].wait()
    for i in range(ns):
        r = slice(i * slot, (i + 1) * slot)
        t = xs[i].astype(F32) + mm(ctx[:, r].T, wos[...])
        hid[r] = t
        t = t * rms_scale(t) * eg
        mixed[r] = t.astype(BF)
        mt[:, r] = t.T.astype(BF)
    save(hid, hidden)
    save(mt, mixed_t)
    load[9].wait()

    chunk = s_t.shape[2]

    def rise(j):
        s_t[j % 2] = mm(mixed[...], wes[:, j * chunk:(j + 1) * chunk])

    rise(0)
    for j in range(ff // chunk):
        if j + 1 < ff // chunk:
            rise(j + 1)
        a, b = gelu_parts(s_t[j % 2])
        act[:, j * chunk:(j + 1) * chunk] = a.astype(BF)
        slo[:, j * chunk:(j + 1) * chunk] = b.astype(BF)

    save(act, active)
    save(slo, slope)
    load[10].wait()
    for i in range(2):
        r = slice(i * (n // 2), (i + 1) * (n // 2))
        alive = (lax.broadcasted_iota(jnp.int32, (n // 2, 1), 0) + i * (n // 2) < length).astype(F32)
        b = alive * (hid[r] + mm(act[r], wrs[...]))
        blk[r] = b
        lws[r] = b.astype(BF)
        rws[r] = (b * rms_scale(b) * fg).astype(BF)
    save(blk, block)
    save(lws, low)

    score = mm_t(q_rows, rws[...])
    score = jnp.where(lax.broadcasted_iota(jnp.int32, score.shape, 1) < length, score, -1e30)
    e = jnp.exp(score - jnp.max(score, axis=-1, keepdims=True))
    cross_probs = e / jnp.sum(e, axis=-1, keepdims=True)
    cross_low = cross_probs.astype(BF)
    mean_rows = mm(cross_low, rws[...]).astype(BF)
    for copy in load[11:]:
        copy.wait()
    cross_context = collect(mm(mean_rows, cvs[...])).astype(BF)
    middle = after + mm(cross_context, cos[...])
    middle_r = rms_scale(middle)
    feed_normed = (middle * middle_r * dg).astype(BF)
    dec_active, dec_slope = gelu_parts(mm(feed_normed, fes[...]))
    dec_active = dec_active.astype(BF)
    upper_grad = (dec_slope * active_back).astype(BF)
    middle_down, feed_gain = norm_down(middle, middle_r, dg, mm_t(upper_grad, fes[...]))
    middle_grad = cot.astype(F32) + middle_down
    cross_branch = middle_grad.astype(BF)
    context_grad = mm_t(cross_branch, cos[...]).astype(BF)
    g_rows = mm_t(spread(context_grad), cvs[...]).astype(BF)
    prob_grad = mm_t(g_rows, rws[...])
    score_grad = (cross_probs * (prob_grad - jnp.sum(cross_probs * prob_grad, axis=-1, keepdims=True))).astype(BF)
    pad = jnp.zeros((16 - heads % 16, n), BF)
    padw = jnp.zeros((16 - heads % 16, width), BF)
    rgs[...] = t_mm(jnp.concatenate([score_grad, pad, cross_low, pad], axis=0),
                    jnp.concatenate([q_rows, padw, g_rows, padw], axis=0)).astype(BF)
    save(rgs, rows_grad)
    score_rows = mm(score_grad, rws[...]).astype(BF)
    left_rows = (self_normed, self_values, cross_normed, cross_context, feed_normed)
    cross_q_grad, self_branch, self_values_grad, in_grad, self_gain, cross_gain = decoder_start_back(
        x, sg, after, cg, middle_grad, score_rows, cks, cqs, sos, svs)
    dec_in_grad[...] = in_grad
    right_rows = (self_values_grad, self_branch, cross_q_grad, cross_branch, cross_q, context_grad, cot)
    if cut:
        for i, r in enumerate(left_rows + (middle,) + right_rows + (self_gain, cross_gain, feed_gain)):
            state[i:i + 1, :] = r.astype(F32)
    else:
        dec_out[...] = (middle + mm(dec_active, frs[...])).astype(BF)
        for i, r in enumerate((self_gain, cross_gain, feed_gain)):
            dec_gains[i:i + 1, :] = r
        for i, r in enumerate(left_rows):
            left[i:i + 1, :] = r.astype(F32)
        for i, r in enumerate(right_rows):
            right[i:i + 1, :] = r.astype(F32)
    wide[0:1, :] = dec_active.astype(F32)
    wide[1:2, :] = upper_grad.astype(F32)
    mids[0] = score_rows.astype(F32)
    mids[1] = mean_rows.astype(F32)
    if cut:
        cut_rows(np_, ns, state, state, 6, wide, mids, dec, cuts, both)
    for g in range(heads // 2 - 2, heads // 2):
        for a in range(2):
            keep(g, a).wait()
    keep_cot.wait()
    for copy in cot_copies:
        copy.wait()
    for copy in saved:
        copy.wait()


def forward(np_, ns, cut, lengths, table, gains, dec_in, dec_cot, enc_in, enc_cot, weights):
    group, slot, width = enc_in.shape
    n = slot * ns
    ff = weights[4].shape[1]
    heads = table.shape[0]
    smem = pl.BlockSpec(memory_space=pltpu.SMEM)
    vm = pl.BlockSpec(memory_space=pltpu.VMEM)
    hb = pl.BlockSpec(memory_space=pl.ANY)
    S = jax.ShapeDtypeStruct
    V = pltpu.VMEM
    full, tall, floats, broad = ((n, width), BF), ((width, n), BF), ((n, width), F32), ((n, ff), BF)
    slots = ((ns, slot, width), BF)
    outs = [tall, full, full, full, ((heads, n, n), BF), tall, floats, tall, broad, broad, floats, full, slots, slots,
            full, ((2, ff), F32), ((2, heads, width), F32), ((1, width), BF)]
    outs += [((16, width), F32), ((np_ * ns, 48, 128), BF)] if cut else [
        ((1, width), BF), ((3, width), F32), ((5, width), F32), ((7, width), F32)]
    scratch = [slots, full, tall, full, full, full, tall, floats, full, tall, broad, broad, floats, full, full, full,
               ((heads, 384, 128), F32), ((heads, 8, 128), F32), ((128, n), BF), ((2, n, n), F32), ((4, n, n), BF)]
    scratch += [((16, 128), F32), ((ns, 32, 128), F32)] if cut else []
    dma = pltpu.SemaphoreType.DMA
    return pl.pallas_call(
        functools.partial(forward_kernel, np_, ns, cut),
        out_shape=tuple(S(*t) for t in outs),
        in_specs=[smem] + [vm] * 9 + [hb] * 16,
        out_specs=(hb,) * 15 + (vm,) * (len(outs) - 15),
        scratch_shapes=[V(w.shape, BF) for w in weights] + [V(*t) for t in scratch] + [
            dma((14,)), dma((4,)), dma((16,)), dma((ns,)), dma((ns,)), dma((ns,)), dma((ns,)), dma((2,))],
        compiler_params=pltpu.CompilerParams(
            collective_id=1, has_side_effects=True, vmem_limit_bytes=62 * 1024 * 1024),
        name="forward",
    )(lengths, table, *gains, dec_in, dec_cot, enc_in, enc_cot, *weights)


def finish_kernel(heads, red, small, dec, dec_row, dec_grad, enc, grad, *outs):
    (enc_out, grad_out, row_out, row_grad_out, qo, ko, vo, oo, expand, reduce, bias, g0, g1, g2, g3, g4, g5,
     sv, so, cq, ck, cv, co, fe, fr, wide) = outs
    enc_out[...] = enc[...]
    grad_out[...] = grad[...]
    row_out[...] = dec_row[...]
    row_grad_out[...] = dec_grad[...]
    wide[...] = dec[...].astype(F32)
    rows, cols = qo.shape
    lanes = red.shape[2]
    for i, out in ((4, (qo, ko)), (5, (vo, oo))):
        t = red[i]
        out[0][...] = t[:, :cols]
        out[1][...] = t[:, cols:]
    for i in range(2):
        expand[:, i * lanes:(i + 1) * lanes] = red[i]
        reduce[i * rows:(i + 1) * rows, :] = red[2 + i]
    for h in range(heads):
        at = 36 + h // 4
        bias[h:h + 1, :] = small[at // 24, at % 24:at % 24 + 1, h % 4 * 32:h % 4 * 32 + 32]
    for i, out in enumerate((g0, g1, g2, g3, g4, g5)):
        for j in range(6):
            at = i * 6 + j
            out[pl.ds(j * 128, 128)] = small[at // 24, at % 24, :]

    def row(i):
        return wide[:, i, :]

    def pair(i):
        return jnp.concatenate([row(16 + 2 * i), row(17 + 2 * i)], axis=1)[:, :cols].astype(BF)

    for i, out in enumerate((sv, so, cq, co)):
        out[...] = t_mm(row(i)[:, :rows].astype(BF), pair(i))
    upper = jnp.concatenate([row(30 + i) for i in range(6)], axis=1).astype(BF)
    fe[...] = t_mm(row(4)[:, :rows].astype(BF), upper)
    active = jnp.concatenate([row(5 + i) for i in range(3)], axis=1).astype(BF)
    fr[...] = t_mm(pair(6), active)
    step = cols // 64
    for w, out in enumerate((ck, cv)):
        g = pair(4 + w)
        out[...] = jnp.concatenate(
            [t_mm(row(8 + w * step + h)[:, :rows].astype(BF), g[:, h * 64:(h + 1) * 64]) for h in range(step)], axis=1)


def finish(heads, buckets, red, small, dec, dec_row, dec_grad, enc, grad):
    rows, lanes = red.shape[1:]
    cols, width = lanes // 2, 2 * lanes
    vm = pl.BlockSpec(memory_space=pltpu.VMEM)
    S = jax.ShapeDtypeStruct
    block, broad, tall = S((rows, cols), F32), S((rows, width), F32), S((cols, lanes), F32)
    return pl.pallas_call(
        functools.partial(finish_kernel, heads),
        out_shape=(S(enc.shape, BF), S(grad.shape, BF), S(dec_row.shape, BF), S(dec_grad.shape, BF), block, block, block, block, broad, tall,
                   S((heads, buckets), F32)) + (S((width,), F32),) * 6 + (block,) * 6 + (broad, tall),
        in_specs=[vm] * 7,
        out_specs=(vm,) * 25,
        scratch_shapes=[pltpu.VMEM(dec.shape, F32)],
        compiler_params=pltpu.CompilerParams(vmem_limit_bytes=62 * 1024 * 1024),
        name="finish",
    )(red, small, dec, dec_row, dec_grad, enc, grad)


PARTS = 2
ORDERS = {
    "t00": "yxfn",
    "t10": "xnfy",
    "t01": "yxnf",
    "t11": "xynf",
    "w00": "yfnx",
    "w10": "fnxy",
    "w01": "nyxf",
    "w11": "xnyf",
    "a0": "ynxf",
    "a1": "xynf",
}
SCHEDULE = {
    "wide": (
        ("t11", 0), ("t01", 0),
    ),
    "dm": (
        ("t10", 0), ("t00", 0),
    ),
    "rows": (
        ("w11", 0), ("w01", 0), ("w00", 0), ("w10", 0),
    ),
    "p02": (
        ("t10", 1), ("t11", 1),
    ),
    "q0": (
        ("w00", 1), ("w11", 1), ("t00", 1), ("w01", 1),
    ),
    "v0": (
        ("t01", 1), ("t11", 2), ("t10", 2), ("h00", 0),
    ),
    "p10": (
        ("w01", 2), ("t00", 2), ("h01", 0),
    ),
    "p11": (
        ("w10", 1), ("t01", 2),
    ),
    "p12": (
        ("w01", 3), ("w00", 2),
    ),
    "q1": (
        ("t11", 3), ("t01", 3),
    ),
    "v1": (
        ("h01", 1), ("t00", 3), ("w10", 2), ("h10", 0),
    ),
    "ng0": (
        ("w11", 2), ("w00", 3), ("t10", 3),
    ),
    "ng1": (
        ("h11", 0),
    ),
    "end": (
        ("h10", 1), ("w11", 3), ("h11", 1), ("h10", 2), ("w10", 3), ("h11", 2),
        ("t10", 4), ("h10", 3), ("t11", 4), ("w01", 4), ("w00", 4), ("t00", 4),
        ("w11", 4), ("w10", 4), ("t01", 4), ("h11", 3),
    ),
}
HOPS = (0, 5)
DECODER = 4


def ff_pieces():
    names = [kind + str(unit) + str(i) for kind in "tw" for i in range(PARTS) for unit in range(2)]
    return names + ["h" + str(half) + str(w) for half in range(2) for w in range(2)]


def fused_kernel(np_, ns, length, fg_in, eg_in, ag_in, state_in, wide_in,
                 rows_grad, block, cot, wr, active, wide_w, hidden, slope, mixed_t_in, wo, wq, wk, wv, q_in, k_in,
                 v_in, x_in, normed_t_in, context_t_in, probs, dec, encoded, fr,
                 red, small_out, dec_got, enc_out, grad_out, dec_out,
                 acts, grads, w1, wes, bg, hid, dm, rg, ct, rb, rb_t, mixed_t, normed_t, context_t,
                 dp, ds, pbuf, k_t, band, diag, fu, r0, r0a, r1, r2, r3, r4, a1, a2, a3, over0, over1,
                 sm, smr, smz, smf,
                 fg, eg, ag, state, wide,
                 psem, isem, loc, f_s, f_r, t_s, t_r, o_s, o_r,
                 m_s, m_r, mz_s, mz_r, d_s, d_r, e_s, e_r, g_s, g_r):
    n, width = hid.shape
    ff = acts.shape[1]
    heads = probs.shape[0]
    nz = np_ // 2
    pieces = ff_pieces()
    rows, lanes = fu.shape[6:]
    step_rows = rows // PARTS
    count = np_ * ns
    p = lax.axis_index("pairs")
    s = lax.axis_index("seq")
    c = lax.rem(s, 2)
    y = s // 2
    xx = lax.rem(p, 2)
    z = p // 2
    me = p * ns + s
    core_peer = (p, s + 1 - 2 * c)
    y_peer = (p, lax.rem(s + 2, 4))
    x_peer = (p + 1 - 2 * xx, s)
    first_half, last_half = 1 - y, y
    own_at = {"x": xx, "y": y, "n": lax.rem(z, 2), "f": z // 2}
    peers = {"x": x_peer, "y": y_peer, "n": ((z + 1 - 2 * own_at["n"]) * 2 + xx, s),
             "f": (lax.rem(z + 2, 4) * 2 + xx, s)}

    def place(d):
        lin = lax.rem(me + d, count)
        return (lin // ns, lax.rem(lin, ns))

    barrier = pltpu.get_barrier_semaphore()

    @pl.loop(1, count)
    def _(d):
        pl.semaphore_signal(barrier, inc=1, device_id=place(d), device_id_type=MESH)

    def remote(src, dst, send, recv, peer):
        return pltpu.make_async_remote_copy(
            src_ref=src, dst_ref=dst, send_sem=send, recv_sem=recv,
            device_id=peer, device_id_type=MESH)

    def load(i, src, dst):
        return pltpu.make_async_copy(src, dst, isem.at[i])

    def part_of(ref, i):
        return ref.at[:, pl.ds(i * width, width)]

    loads = [load(i, a, b) for i, (a, b) in enumerate((
        (rows_grad, rg), (block, bg), (cot, ct), (active, acts), (wr, w1), (slope, grads), (mixed_t_in, mixed_t),
        (wide_w, wes), (hidden, hid), (normed_t_in, normed_t), (context_t_in, context_t)))]
    weights = [load(11 + i, a, w1.at[pl.ds(i * width, width)]) for i, a in enumerate((wo, wq, wk, wv))]
    heads_in = [load(15 + i, a, part_of(grads, i)) for i, a in enumerate((q_in, k_in, v_in, x_in))]
    d_out, dq, dk, dv = (part_of(acts, i) for i in range(4))
    q, k, v, x = (part_of(grads, i) for i in range(4))
    branch, dq_t, ng, in_grad, hidden_grad = ct, rb_t, dm, rg, bg
    smalls = [load(20 + i, a, b) for i, (a, b) in enumerate((
        (fg_in, fg), (eg_in, eg), (ag_in, ag), (state_in, state), (wide_in, wide)))]
    late = load(19, fr, w1)
    wos, wqs, wks, wvs = (w1.at[pl.ds(i * width, width)] for i in range(4))

    def fetch(h, slot):
        return pltpu.make_async_copy(probs.at[h], pbuf.at[slot], psem.at[slot])

    def view(ref, dims, fixed):
        return ref.at[tuple(fixed.get(dim, slice(None)) for dim in dims)]

    def accumulate(dst, src, depth):
        for at in itertools.product(range(2), repeat=depth):
            dst[at] = dst[at] + src[at]

    def au(w, core, half):
        return fu.at[1 - c, 2 * w + core, half]

    def region(name, core):
        if name[0] == "h":
            return au(int(name[2]), core, first_half if name[1] == "0" else last_half), "fnx"
        unit = (2 if name[0] == "t" else 0) + int(name[1])
        return fu.at[core, unit, :, :, :, :, pl.ds(int(name[2]) * step_rows, step_rows)], "yfnx"

    def order_of(name):
        if name[0] != "h":
            return ORDERS[name]
        order = ORDERS["a" + name[2]]
        return order[:order.index("y")] if name[1] == "0" else order.replace("y", "")

    def core_copy(name):
        i = pieces.index(name)
        src, _ = region(name, 1 - c)
        dst = r0a.at[i - len(pieces) + 4] if name[0] == "h" else r0.at[i]
        return remote(src, dst, f_s.at[i], f_r.at[i], core_peer)

    def landing(name, j):
        i = pieces.index(name)
        if name[0] == "h":
            return (a1, a2, a3)[j].at[i - len(pieces) + 4]
        return (r1, r2, r3, r4)[j].at[i]

    def remaining(name, j):
        ref, dims = region(name, c)
        return ref, dims, {letter: own_at[letter] for letter in order_of(name)[:j]}

    def stage_copy(name, j):
        ref, dims, fixed = remaining(name, j)
        letter = order_of(name)[j]
        i = pieces.index(name)
        src = view(ref, dims, {**fixed, letter: 1 - own_at[letter]})
        return remote(src, landing(name, j), t_s.at[i, j], t_r.at[i, j], peers[letter])

    def hand_over(w):
        name = "h0" + str(w)
        ref, dims, fixed = remaining(name, len(order_of(name)))
        return remote(view(ref, dims, fixed), (over0, over1)[w], o_s.at[w], o_r.at[w], y_peer)

    def total_of(name):
        unit = 4 + int(name[2]) if name[0] == "h" else (2 if name[0] == "t" else 0) + int(name[1])
        if name[0] == "h":
            return red.at[unit]
        return red.at[unit, pl.ds(int(name[2]) * step_rows, step_rows)]

    def step(name, j):
        order = order_of(name)
        ref, dims, fixed = remaining(name, j)
        mine = view(ref, dims, fixed)
        depth = len(dims) - j
        closing = j == len(order) and name[:2] != "h0"
        joins = name[:2] == "h1" and ORDERS["a" + name[2]].index("y") == j
        if j == 0:
            core_copy(name).wait()
            landed = r0a.at[pieces.index(name) - len(pieces) + 4] if name[0] == "h" else r0.at[pieces.index(name)]
        else:
            stage_copy(name, j - 1).wait()
            landed = landing(name, j - 1)
        if joins:
            hand_over(int(name[2])).wait()
            extra = (over0, over1)[int(name[2])]
        if closing:
            total = mine[...].astype(F32) + landed[...].astype(F32)
            if joins:
                total = total + extra[...].astype(F32)
            total_of(name)[...] = total
            return
        accumulate(mine, landed, depth)
        if joins:
            accumulate(mine, extra, depth)
        if j < len(order):
            stage_copy(name, j).start()
        else:
            hand_over(int(name[2])).start()

    def run_slot(slot):
        for name, j in SCHEDULE.get(slot, ()):
            step(name, j)

    def dec_copy(d):
        to = place(d)
        return remote(dec.at[to[0] * ns + to[1]], dec_got.at[me], d_s.at[d], d_r.at[d], to)

    def enc_copy(d):
        t = lax.rem(s + d, ns)
        return remote(encoded.at[t], enc_out.at[s], e_s.at[d], e_r.at[d], (p, t))

    def grad_copy(d):
        t = lax.rem(s + d, ns)
        return remote(in_grad.at[t], grad_out.at[s], g_s.at[d], g_r.at[d], (p, t))

    keep_dec = pltpu.make_async_copy(dec.at[me], dec_got.at[me], loc.at[4])
    keep_enc = pltpu.make_async_copy(encoded.at[s], enc_out.at[s], loc.at[5])
    keep_grad = pltpu.make_async_copy(in_grad.at[s], grad_out.at[s], loc.at[6])

    for copy in smalls[:1] + loads + smalls[1:]:
        copy.start()
    fetch(first_half * (heads // 2), 0).start()
    fetch(first_half * (heads // 2) + 1, 1).start()
    keep_dec.start()
    keep_enc.start()
    diag[...] = jnp.zeros_like(diag)
    slot_rows = n // ns
    sm[...] = jnp.zeros_like(sm)

    def put_gain(i, gain):
        for j in range(width // 128):
            at = i * 6 + j
            sm[at // 24, at % 24:at % 24 + 1, :] = gain[:, j * 128:(j + 1) * 128]

    smalls[0].wait()
    for i in range(3):
        loads[i].wait()
    final_gain = jnp.zeros((1, width), F32)
    for i in range(ns):
        r = slice(i * slot_rows, (i + 1) * slot_rows)
        alive = (lax.broadcasted_iota(jnp.int32, (slot_rows, 1), 0) + i * slot_rows < length[s]).astype(F32)
        b = bg[r]
        down, gain = norm_down(b, rms_scale(b), fg[...].reshape(1, -1), rg[i].astype(F32))
        b = alive * (ct[r].astype(F32) + down)
        bg[r] = b
        low = b.astype(BF)
        rb[r] = low
        rb_t[:, r] = low.T
        final_gain = final_gain + jnp.sum(gain, axis=0, keepdims=True)
    put_gain(3, final_gain)
    pl.semaphore_wait(barrier, count - 1)
    for d in range(1, ns):
        enc_copy(d).start()

    @pl.loop(1, count)
    def _(d):
        dec_copy(d).start()

    part = width // 4
    loads[3].wait()

    @pl.loop(0, nz)
    def _(b):
        cols = pl.ds(pl.multiple_of(b * 2 * lanes, 128), 2 * lanes)
        g = mm(rb_t[...], acts[:, cols]).astype(BF)
        for j in range(4):
            for half in range(2):
                lo = j * part + half * rows
                for e in range(2):
                    fu[j % 2, 2 + half, j // 2, b // 2, lax.rem(b, 2), e] = g[lo:lo + rows, e * lanes:(e + 1) * lanes]

    for name in pieces:
        if name[0] == "t":
            core_copy(name).start()
    loads[4].wait()
    loads[5].wait()

    for j in range(ff // width):
        cols = slice(j * width, (j + 1) * width)
        grads[:, cols] = (grads[:, cols].astype(F32) * mm_t(rb[...], w1[cols, :])).astype(BF)
        if j == 0:
            for copy in smalls[3:]:
                copy.wait()
            for i in range(3):
                put_gain(i, state[13 + i:14 + i, :])
        run_slot("ug" + str(j))

    for copy in weights:
        copy.start()
    loads[6].wait()

    @pl.loop(0, 4)
    def _(j):
        cols = pl.ds(pl.multiple_of(j * 2 * lanes, 128), 2 * lanes)
        g = mm(mixed_t[...], grads[:, cols]).astype(BF)
        for half in range(2):
            fu[lax.rem(j, 2), half, j // 2] = g[:, half * lanes:(half + 1) * lanes].reshape(2, 2, 2, rows, lanes)

    for name in pieces:
        if name[0] == "w":
            core_copy(name).start()
    run_slot("wide")
    loads[7].wait()
    dm[...] = mm_t(grads[...], wes[...])
    for copy in heads_in:
        copy.start()
    run_slot("dm")
    loads[8].wait()
    smalls[1].wait()
    expand_gain = jnp.zeros((1, width), F32)
    for i in range(ns):
        r = slice(i * slot_rows, (i + 1) * slot_rows)
        t = hid[r]
        down, gain = norm_down(t, rms_scale(t), eg[...].reshape(1, -1), dm[r])
        t = bg[r] + down
        bg[r] = t
        branch[r] = t.astype(BF)
        expand_gain = expand_gain + jnp.sum(gain, axis=0, keepdims=True)
    put_gain(4, expand_gain)
    run_slot("rows")
    weights[0].wait()

    @pl.loop(0, width // 384)
    def _(j):
        cols = pl.ds(pl.multiple_of(j * 384, 128), 384)
        d_out[:, cols] = mm_t(branch[...], w1[cols, :]).astype(BF)

    for copy in heads_in:
        copy.wait()
    for copy in loads[9:]:
        copy.wait()

    run_slot("dout")

    lane = lax.broadcasted_iota(jnp.int32, (n, 128), 1)
    lane_s = lax.broadcasted_iota(jnp.int32, (128, 128), 1)
    row_s = lax.broadcasted_iota(jnp.int32, (128, 128), 0)

    def pair(half, g):
        cols = pl.ds(pl.multiple_of(half * (width // 2) + g * 128, 128), 128)
        k_t[...] = k[:, cols].T
        dop = d_out[:, cols]
        qp = q[:, cols]
        vp = v[:, cols]
        zero = jnp.zeros_like(qp)
        for a in range(2):
            h = half * (heads // 2) + 2 * g + a
            mine = (lane < 64) if a == 0 else (lane >= 64)
            dp[...] = mm_t(jnp.where(mine, vp, zero), dop)
            fetch(h, a).wait()
            for j in range(n // 128):
                pj = pbuf[a, :, j * 128:(j + 1) * 128].astype(F32)
                pd = pj * dp[:, j * 128:(j + 1) * 128]
                total = jnp.sum(pd, axis=0, keepdims=True)
                sg = pd - pj * total
                ds[:, j * 128:(j + 1) * 128] = sg.astype(BF)
                for i in range(n // 128):
                    t = sg[i * 128:(i + 1) * 128]
                    if abs(i - j) <= 1:
                        b = (i - j + 1) * 128
                        if j == 0 or (j == 1 and i == 0):
                            band[b:b + 128, :] = t
                        else:
                            band[b:b + 128, :] += t
                    else:
                        f = 5 if i > j else 4
                        diag[h, f:f + 1, :] += jnp.sum(t, axis=0, keepdims=True)
            dvp = mm(pbuf[a], jnp.where(mine, dop, zero))
            dkp = mm(ds[...], jnp.where(mine, qp, zero))
            dq_t[pl.ds(pl.multiple_of(h * 64, 64), 64), :] = mm(k_t[a * 64:(a + 1) * 64, :], ds[...]).astype(BF)
            if a == 0:
                dk_sum, dv_sum = dkp, dvp
            else:
                dk[:, cols] = (dk_sum + dkp).astype(BF)
                dv[:, cols] = (dv_sum + dvp).astype(BF)
            for b in range(3):
                t = band[b * 128:(b + 1) * 128, :]
                for bit in range(7):
                    t = jnp.where((row_s >> bit) % 2 == 1, pltpu.roll(t, 128 - (1 << bit), 1), t)
                straight = jnp.sum(jnp.where(lane_s + row_s < 128, t, 0.0), axis=0, keepdims=True)
                whole = jnp.sum(t, axis=0, keepdims=True)
                diag[h, b:b + 1, :] += straight
                diag[h, b + 1:b + 2, :] += whole - straight

    def units_of(half, tag):
        cols = pl.ds(pl.multiple_of(half * (width // 2), 128), width // 2)
        dq_h = dq_t[cols, :].T
        dq[:, cols] = dq_h
        dk_h = dk[:, cols]
        for cc in range(2):
            e = slice(cc * part, (cc + 1) * part)
            g = mm(normed_t[...], jnp.concatenate([dq_h[:, e], dk_h[:, e]], axis=1))
            au(0, cc, half)[...] = g.astype(BF).reshape(2, 2, 2, rows, lanes)
        core_copy("h" + tag + "0").start()
        run_slot("q" + tag)
        dv_h = dv[:, cols]
        br_h = branch[:, cols]
        zero = jnp.zeros((n, part), BF)
        for cc in range(2):
            e = slice(cc * part, (cc + 1) * part)
            g = (mm(normed_t[...], jnp.concatenate([dv_h[:, e], zero], axis=1))
                 + mm(context_t[...], jnp.concatenate([zero, br_h[:, e]], axis=1)))
            au(1, cc, half)[...] = g.astype(BF).reshape(2, 2, 2, rows, lanes)
        core_copy("h" + tag + "1").start()
        run_slot("v" + tag)

    quarter = heads // 4

    @pl.loop(0, quarter)
    def _(g):
        pair(first_half, g)
        nxt = jnp.where(g == quarter - 1, last_half * (heads // 2), first_half * (heads // 2) + 2 * (g + 1))
        fetch(nxt, 0).start()
        fetch(nxt + 1, 1).start()

        for i in range(quarter):
            if SCHEDULE.get("p0" + str(i)):
                @pl.when(g == i)
                def _():
                    run_slot("p0" + str(i))

    units_of(first_half, "0")

    @pl.loop(0, quarter)
    def _(g):
        pair(last_half, g)

        @pl.when(g < quarter - 1)
        def _():
            nxt = last_half * (heads // 2) + 2 * (g + 1)
            fetch(nxt, 0).start()
            fetch(nxt + 1, 1).start()

        for i in range(quarter):
            if SCHEDULE.get("p1" + str(i)):
                @pl.when(g == i)
                def _():
                    run_slot("p1" + str(i))

    units_of(last_half, "1")
    for copy in weights[1:]:
        copy.wait()

    for i in range(2):
        r = slice(i * (n // 2), (i + 1) * (n // 2))
        ng[r] = mm_t(dq[r], wqs[...]) + mm_t(dk[r], wks[...]) + mm_t(dv[r], wvs[...])
        run_slot("ng" + str(i))

    late.start()
    smalls[2].wait()
    gain_sum = jnp.zeros((1, width), F32)
    for i in range(ns):
        r = slice(i * slot_rows, (i + 1) * slot_rows)
        t = x[r].astype(F32)
        down, gain = norm_down(t, rms_scale(t), ag[...].reshape(1, -1), ng[r])
        in_grad[i] = (hidden_grad[r] + down).astype(BF)
        gain_sum = gain_sum + jnp.sum(gain, axis=0, keepdims=True)
    keep_grad.start()
    for d in range(1, ns):
        grad_copy(d).start()

    pick = diagonal_buckets((128, width), width)
    bias = jnp.zeros((16, 128), F32)
    for i in range(width // 128):
        bias = bias + lax.dot_general(diag[:, i, :], pick[:, i * 128:(i + 1) * 128], (((1,), (1,)), ((), ())),
                                      precision=HIGHEST, preferred_element_type=F32)
    place_of = lax.broadcasted_iota(jnp.int32, (1, 128), 1) // 32
    for h in range(heads):
        at = 36 + h // 4
        sm[at // 24, at % 24:at % 24 + 1, :] += jnp.where(place_of == h % 4, bias[h:h + 1, :], 0.0)
    put_gain(5, gain_sum)

    chips = 2 * np_
    chip = 2 * p + y
    small_first = remote(sm.at[1 - c], smr, m_s.at[0], m_r.at[0], core_peer)
    small_last = remote(smf.at[c], smf.at[c], m_s.at[1], m_r.at[1], core_peer)

    def small_copy(d):
        to = lax.rem(chip + d, chips)
        return remote(smz.at[chip], smz.at[chip], mz_s.at[d], mz_r.at[d], (to // 2, lax.rem(to, 2) * 2 + c))

    small_first.start()
    tail = SCHEDULE["end"]
    for i, (name, j) in enumerate(tail):
        step(name, j)
        if i == DECODER:
            late.wait()
            dec_out[...] = (state[5:6, :] + mm(wide[0:1, :].astype(BF), w1[...])).astype(BF)
        if i == HOPS[0]:
            small_first.wait()
            smz[chip] = sm[c] + smr[...]

            @pl.loop(1, chips)
            def _(d):
                small_copy(d).start()
        if i == len(tail) - HOPS[1]:
            @pl.loop(1, chips)
            def _(d):
                small_copy(d).wait()

            total = smz[0]
            for other in range(1, chips):
                total = total + smz[other]
            smf[c] = total
            small_last.start()

    small_last.wait()
    small_out[...] = smf[...]
    keep_dec.wait()
    keep_enc.wait()
    keep_grad.wait()
    for d in range(1, ns):
        enc_copy(d).wait()
        grad_copy(d).wait()

    @pl.loop(1, count)
    def _(d):
        dec_copy(d).wait()


def fused(np_, ns, length, fg, eg, ag, state, wide, rows_grad, block, cot, wr, active, we, hidden, slope, mixed_t,
          wo, wq, wk, wv, q, k, v, x, normed_t, context_t, probs, dec, encoded, fr):
    n, width = hidden.shape
    ff = active.shape[1]
    heads = probs.shape[0]
    nz = np_ // 2
    rows, lanes = width // np_, ff // np_
    count = np_ * ns
    smem = pl.BlockSpec(memory_space=pltpu.SMEM)
    vm = pl.BlockSpec(memory_space=pltpu.VMEM)
    hb = pl.BlockSpec(memory_space=pl.ANY)
    S = jax.ShapeDtypeStruct
    V = pltpu.VMEM
    dma = pltpu.SemaphoreType.DMA
    nar, tall = V((n, width), BF), V((width, n), BF)
    floats = V((n, width), F32)
    slots = (ns, n // ns, width)
    small = (2, 24, 128)
    ffs = 4 * PARTS
    sub = rows // PARTS

    def joint(w):
        return V((2,) * (3 - ORDERS["a" + str(w)].index("y")) + (rows, lanes), BF)

    return pl.pallas_call(
        functools.partial(fused_kernel, np_, ns),
        out_shape=(S((6, rows, lanes), F32), S(small, F32), S((count, 48, 128), BF), S(slots, BF), S(slots, BF),
                   S((1, width), BF)),
        in_specs=[smem] + [hb] * 28,
        out_specs=(vm, vm, hb, hb, hb, vm),
        scratch_shapes=[
            V((n, ff), BF), V((n, ff), BF), V((ff, width), BF), V((width, ff), BF), floats, floats, floats,
            V(slots, BF), nar, nar, tall, tall, tall, tall,
            V((n, n), F32), V((n, n), BF), V((2, n, n), BF), V((128, n), BF), V((384, 128), F32), V((16, 8, 128), F32),
            V((2, 4, 2, 2, 2, 2, rows, lanes), BF), V((ffs, 2, 2, 2, 2, sub, lanes), BF), V((4, 2, 2, 2, rows, lanes), BF),
            V((ffs, 2, 2, 2, sub, lanes), BF), V((ffs, 2, 2, sub, lanes), BF), V((ffs, 2, sub, lanes), BF),
            V((ffs, sub, lanes), BF), V((4, 2, 2, rows, lanes), BF), V((4, 2, rows, lanes), BF),
            V((4, rows, lanes), BF), joint(0), joint(1),
            V(small, F32), V(small[1:], F32), V((2 * np_,) + small[1:], F32), V(small, F32),
            V((width,), F32), V((width,), F32), V((width,), F32), V((16, width), F32), V((2, ff), F32),
            dma((2,)), dma((26,)), dma((7,)), dma((ffs + 4,)), dma((ffs + 4,)), dma((ffs + 4, 4)), dma((ffs + 4, 4)),
            dma((2,)), dma((2,)),
            dma((2,)), dma((2,)), dma((2 * np_,)), dma((2 * np_,)), dma((count,)), dma((count,)),
            dma((ns,)), dma((ns,)), dma((ns,)), dma((ns,)),
        ],
        compiler_params=pltpu.CompilerParams(
            collective_id=0, has_side_effects=True, vmem_limit_bytes=62 * 1024 * 1024),
        name="fused_backward",
    )(length, fg, eg, ag, state, wide, rows_grad.reshape(slots), block, cot, wr,
      active, we, hidden, slope, mixed_t, wo, wq, wk, wv, q, k, v, x, normed_t, context_t, probs, dec,
      encoded.reshape(slots), fr)


def feed_back_kernel(length, rows_grad, block, cot, fg, hidden, eg, mixed, active, slope, wr, we,
                     wide, tall, hidden_grad, branch, gains, wrs, wes, bg, rb, rb_t, ug, mixed_t, dmixed, sems):
    n, width = block.shape
    ff = active.shape[1]
    groups, lanes = tall.shape[3], tall.shape[5]
    cols_dev = width // 4
    copies = [pltpu.make_async_copy(a, b, sems.at[i]) for i, (a, b) in enumerate(((wr, wrs), (we, wes)))]
    for c in copies:
        c.start()
    gains[...] = jnp.zeros_like(gains)

    @pl.loop(0, n // 128)
    def _(i):
        r = pl.ds(i * 128, 128)
        alive = (lax.broadcasted_iota(jnp.int32, (128, 1), 0) + i * 128 < length[0]).astype(F32)
        v = block[r]
        down, gain = norm_down(v, rms_scale(v), fg[...], rows_grad[r].astype(F32))
        b = alive * (cot[r].astype(F32) + down)
        bg[r] = b
        rb[r] = b.astype(BF)
        rb_t[:, pl.ds(pl.multiple_of(i * 128, 128), 128)] = b.T.astype(BF)
        mixed_t[:, pl.ds(pl.multiple_of(i * 128, 128), 128)] = mixed[r].T
        gains[0:1, :] += jnp.sum(gain, axis=0, keepdims=True)

    copies[0].wait()

    @pl.loop(0, ff // 256)
    def _(j):
        cols = pl.ds(pl.multiple_of(j * 256, 256), 256)
        ug[:, cols] = (slope[:, cols].astype(F32) * mm_t(rb[...], wrs[cols, :])).astype(BF)

    copies[1].wait()

    @pl.loop(0, width // 256)
    def _(j):
        cols = pl.ds(pl.multiple_of(j * 256, 256), 256)
        dmixed[:, cols] = mm_t(ug[...], wes[cols, :])

    @pl.loop(0, n // 128)
    def _(i):
        r = pl.ds(i * 128, 128)
        v = hidden[r]
        down, gain = norm_down(v, rms_scale(v), eg[...], dmixed[r])
        h = bg[r] + down
        hidden_grad[r] = h
        branch[r] = h.astype(BF)
        gains[1:2, :] += jnp.sum(gain, axis=0, keepdims=True)

    @pl.loop(0, 4)
    def _(j):
        for half in range(2):
            cols = pl.ds(pl.multiple_of(j * (ff // 4) + half * (ff // 8), 128), ff // 8)
            wide[half, lax.rem(j, 2), j // 2] = mm(mixed_t[...], ug[:, cols]).astype(BF)

    chunk = ff // 8
    per_group = lanes // chunk

    @pl.loop(0, 8)
    def _(i):
        cols = pl.ds(pl.multiple_of(i * chunk, 128), chunk)
        g = mm(rb_t[...], active[:, cols]).astype(BF)
        for j in range(4):
            for half in range(2):
                r = j * cols_dev + half * (cols_dev // 2)
                part = g[r:r + cols_dev // 2]
                if per_group == 1:
                    tall[half, j % 2, j // 2, i] = part
                else:
                    tall[half, j % 2, j // 2, 0, :, cols] = part


def feed_back(groups, length, rows_grad, block, cot, fg, hidden, eg, mixed, active, slope, wr, we):
    n, width = block.shape
    ff = active.shape[1]
    sm = pl.BlockSpec(memory_space=pltpu.SMEM)
    vm = pl.BlockSpec(memory_space=pltpu.VMEM)
    hb = pl.BlockSpec(memory_space=pl.ANY)
    S = jax.ShapeDtypeStruct
    V = pltpu.VMEM
    return pl.pallas_call(
        feed_back_kernel,
        out_shape=(S((2, 2, 2, width, ff // 8), BF),
                   S((2, 2, 2, groups, width // 8, ff // groups), BF), S((n, width), F32), S((n, width), BF), S((2, width), F32)),
        in_specs=[sm] + [vm] * 9 + [hb] * 2,
        out_specs=(vm,) * 5,
        scratch_shapes=[V(wr.shape, BF), V(we.shape, BF), V((n, width), F32), V((n, width), BF), V((width, n), BF),
                        V((n, ff), BF), V((width, n), BF), V((n, width), F32), pltpu.SemaphoreType.DMA((2,))],
        compiler_params=pltpu.CompilerParams(vmem_limit_bytes=60 * 1024 * 1024),
        name="feed_back",
    )(length, rows_grad, block, cot, fg.reshape(1, -1), hidden, eg.reshape(1, -1), mixed, active, slope, wr, we)


def backward_kernel(np_, ns, x, ag, q, k, v, context_t, branch, hidden_grad, normed, gains_dec, gains_feed,
                    probs, wo, wq, wk, wv, wide, tall, dec, encoded,
                    red, small_out, dec_out, enc_out, grad_out,
                    wos, wqs, wks, wvs, d_out, dp, ds, dq_t, dq, dk, dv, k_t, normed_t, ng, in_grad,
                    pbuf, band, diag, own, au, r0, r1y, r1x, r1a, r2, r3, sm, smr, smz,
                    psem, wsem, loc, c_s, c_r, a_s, a_r, b_s, b_r, ac_s, ac_r, ax_s, ax_r, z_s, z_r,
                    m_s, m_r, mz_s, mz_r, d_s, d_r, e_s, e_r, g_s, g_r):
    n, width = x.shape
    heads = probs.shape[0]
    nz = np_ // 2
    rows, lanes = r0.shape[4:]
    count = np_ * ns
    p = lax.axis_index("pairs")
    s = lax.axis_index("seq")
    c = lax.rem(s, 2)
    y = s // 2
    xx = lax.rem(p, 2)
    z = p // 2
    me = p * ns + s
    core_peer = (p, s + 1 - 2 * c)
    y_peer = (p, lax.rem(s + 2, 4))
    x_peer = (p + 1 - 2 * xx, s)

    def place(d):
        lin = lax.rem(me + d, count)
        return (lin // ns, lax.rem(lin, ns))

    barrier = pltpu.get_barrier_semaphore()

    @pl.loop(1, count)
    def _(d):
        pl.semaphore_signal(barrier, inc=1, device_id=place(d), device_id_type=MESH)

    def remote(src, dst, send, recv, peer):
        return pltpu.make_async_remote_copy(
            src_ref=src, dst_ref=dst, send_sem=send, recv_sem=recv,
            device_id=peer, device_id_type=MESH)

    weights = [pltpu.make_async_copy(a, b, wsem.at[i])
               for i, (a, b) in enumerate(((wo, wos), (wq, wqs), (wk, wks), (wv, wvs)))]

    def fetch(h, slot):
        return pltpu.make_async_copy(probs.at[h], pbuf.at[slot], psem.at[slot])

    def unit(i, core):
        return (wide, tall)[i // 2].at[i % 2, core]

    def core_copy(i):
        return remote(unit(i, 1 - c), r0.at[i], c_s.at[i], c_r.at[i], core_peer)

    def own_copy(i):
        return pltpu.make_async_copy(unit(i, c), own.at[i], loc.at[i])

    def first(i):
        if i % 2 == 0:
            return remote(own.at[i, 1 - y], r1y.at[i // 2], a_s.at[i], a_r.at[i], y_peer)
        return remote(own.at[i, :, :, 1 - xx], r1x.at[i // 2], a_s.at[i], a_r.at[i], x_peer)

    def second(i):
        if i % 2 == 0:
            return remote(own.at[i, y, :, 1 - xx], r2.at[i], b_s.at[i], b_r.at[i], x_peer)
        return remote(own.at[i, 1 - y, :, xx], r2.at[i], b_s.at[i], b_r.at[i], y_peer)

    def final(i):
        return own.at[i, y] if i < 4 else au.at[i - 4, c, y]

    def last(i, d):
        t = lax.rem(z + d, nz)
        return remote(final(i).at[t, xx], r3.at[i, d], z_s.at[i, d], z_r.at[i, d], (t * 2 + xx, s))

    def attn_core(w, half):
        return remote(au.at[w, 1 - c, half], r0.at[4 + w, half], ac_s.at[w, half], ac_r.at[w, half], core_peer)

    def attn_x(w, half):
        return remote(au.at[w, c, half, :, 1 - xx], r1a.at[w, half], ax_s.at[w, half], ax_r.at[w, half], x_peer)

    def attn_y(w):
        return remote(au.at[w, c, 1 - y, :, xx], r2.at[4 + w], b_s.at[4 + w], b_r.at[4 + w], y_peer)

    def dec_copy(d):
        to = place(d)
        return remote(dec.at[to[0] * ns + to[1]], dec_out.at[me], d_s.at[d], d_r.at[d], to)

    def enc_copy(d):
        t = lax.rem(s + d, ns)
        return remote(encoded.at[t], enc_out.at[s], e_s.at[d], e_r.at[d], (p, t))

    def grad_copy(d):
        t = lax.rem(s + d, ns)
        return remote(in_grad.at[t], grad_out.at[s], g_s.at[d], g_r.at[d], (p, t))

    keep_dec = pltpu.make_async_copy(dec.at[me], dec_out.at[me], loc.at[4])
    keep_enc = pltpu.make_async_copy(encoded.at[s], enc_out.at[s], loc.at[5])
    keep_grad = pltpu.make_async_copy(in_grad.at[s], grad_out.at[s], loc.at[6])

    def step_a(i):
        core_copy(i).wait()
        own_copy(i).wait()

        @pl.loop(0, nz)
        def _(b):
            for a in range(2):
                for e in range(2):
                    own[i, a, b, e] = own[i, a, b, e] + r0[i, a, b, e]

        first(i).start()

    def step_b(i):
        first(i).wait()

        @pl.loop(0, nz)
        def _(b):
            for e in range(2):
                if i % 2 == 0:
                    own[i, y, b, e] = own[i, y, b, e] + r1y[i // 2, b, e]
                else:
                    own[i, e, b, xx] = own[i, e, b, xx] + r1x[i // 2, e, b]

        second(i).start()

    def step_c(i):
        if i < 4:
            second(i).wait()
        else:
            attn_y(i - 4).wait()

        @pl.loop(0, nz)
        def _(b):
            f = final(i)
            f[b, xx] = f[b, xx] + r2[i, b]

        @pl.loop(1, nz)
        def _(d):
            last(i, d).start()

    def step_d(i):
        red[i] = final(i)[z, xx].astype(F32)

        @pl.loop(1, nz)
        def _(d):
            last(i, d).wait()
            red[i] = red[i] + r3[i, d].astype(F32)

    def attn_a(w, half):
        attn_core(w, half).wait()

        @pl.loop(0, nz)
        def _(b):
            for e in range(2):
                au[w, c, half, b, e] = au[w, c, half, b, e] + r0[4 + w, half, b, e]

        attn_x(w, half).start()

    def attn_b(w, half):
        attn_x(w, half).wait()

        @pl.loop(0, nz)
        def _(b):
            au[w, c, half, b, xx] = au[w, c, half, b, xx] + r1a[w, half, b]

    for copy in weights:
        copy.start()
    first_half, last_half = 1 - y, y
    fetch(first_half * (heads // 2), 0).start()
    fetch(first_half * (heads // 2) + 1, 1).start()
    for i in range(4):
        own_copy(i).start()
    keep_dec.start()
    keep_enc.start()
    diag[...] = jnp.zeros_like(diag)
    weights[0].wait()

    @pl.loop(0, width // 384)
    def _(j):
        cols = pl.ds(pl.multiple_of(j * 384, 128), 384)
        d_out[:, cols] = mm_t(branch[...], wos[cols, :]).astype(BF)

    pl.semaphore_wait(barrier, count - 1)
    for i in range(4):
        core_copy(i).start()
    for d in range(1, ns):
        enc_copy(d).start()

    @pl.loop(1, count)
    def _(d):
        dec_copy(d).start()

    @pl.loop(0, n // 128)
    def _(i):
        r = pl.ds(pl.multiple_of(i * 128, 128), 128)
        normed_t[:, r] = normed[r].T

    lane = lax.broadcasted_iota(jnp.int32, (n, 128), 1)
    lane_s = lax.broadcasted_iota(jnp.int32, (128, 128), 1)
    row_s = lax.broadcasted_iota(jnp.int32, (128, 128), 0)

    def pair(half, g):
        cols = pl.ds(pl.multiple_of(half * (width // 2) + g * 128, 128), 128)
        k_t[...] = k[:, cols].T
        dop = d_out[:, cols]
        qp = q[:, cols]
        vp = v[:, cols]
        zero = jnp.zeros_like(qp)
        for a in range(2):
            h = half * (heads // 2) + 2 * g + a
            mine = (lane < 64) if a == 0 else (lane >= 64)
            dp[...] = mm_t(jnp.where(mine, vp, zero), dop)
            fetch(h, a).wait()
            for j in range(n // 128):
                pj = pbuf[a, :, j * 128:(j + 1) * 128].astype(F32)
                pd = pj * dp[:, j * 128:(j + 1) * 128]
                total = jnp.sum(pd, axis=0, keepdims=True)
                sg = pd - pj * total
                ds[:, j * 128:(j + 1) * 128] = sg.astype(BF)
                for i in range(n // 128):
                    t = sg[i * 128:(i + 1) * 128]
                    if abs(i - j) <= 1:
                        b = (i - j + 1) * 128
                        if j == 0 or (j == 1 and i == 0):
                            band[b:b + 128, :] = t
                        else:
                            band[b:b + 128, :] += t
                    else:
                        f = 5 if i > j else 4
                        diag[h, f:f + 1, :] += jnp.sum(t, axis=0, keepdims=True)
            dvp = mm(pbuf[a], jnp.where(mine, dop, zero))
            dkp = mm(ds[...], jnp.where(mine, qp, zero))
            dq_t[pl.ds(pl.multiple_of(h * 64, 64), 64), :] = mm(k_t[a * 64:(a + 1) * 64, :], ds[...]).astype(BF)
            if a == 0:
                dk_sum, dv_sum = dkp, dvp
            else:
                dk[:, cols] = (dk_sum + dkp).astype(BF)
                dv[:, cols] = (dv_sum + dvp).astype(BF)
            for b in range(3):
                t = band[b * 128:(b + 1) * 128, :]
                for bit in range(7):
                    t = jnp.where((row_s >> bit) % 2 == 1, pltpu.roll(t, 128 - (1 << bit), 1), t)
                straight = jnp.sum(jnp.where(lane_s + row_s < 128, t, 0.0), axis=0, keepdims=True)
                whole = jnp.sum(t, axis=0, keepdims=True)
                diag[h, b:b + 1, :] += straight
                diag[h, b + 1:b + 2, :] += whole - straight

    part = width // 4

    def units_of(half):
        cols = pl.ds(pl.multiple_of(half * (width // 2), 128), width // 2)
        lower = pl.ds(pl.multiple_of(half * (width // 2), 128), width // 2)
        dq_h = dq_t[lower, :].T
        dq[:, cols] = dq_h
        dk_h = dk[:, cols]
        dv_h = dv[:, cols]
        br_h = branch[:, cols]
        zero = jnp.zeros((n, part), BF)
        for cc in range(2):
            e = slice(cc * part, (cc + 1) * part)
            g = mm(normed_t[...], jnp.concatenate([dq_h[:, e], dk_h[:, e]], axis=1))
            au[0, cc, half] = g.astype(BF).reshape(nz, 2, rows, lanes)
            g = (mm(normed_t[...], jnp.concatenate([dv_h[:, e], zero], axis=1))
                 + mm(context_t[...], jnp.concatenate([zero, br_h[:, e]], axis=1)))
            au[1, cc, half] = g.astype(BF).reshape(nz, 2, rows, lanes)
        for w in range(2):
            attn_core(w, half).start()

    quarter = heads // 4

    @pl.loop(0, quarter)
    def _(g):
        pair(first_half, g)
        nxt = jnp.where(g == quarter - 1, last_half * (heads // 2), first_half * (heads // 2) + 2 * (g + 1))
        fetch(nxt, 0).start()
        fetch(nxt + 1, 1).start()

        @pl.when(g == 0)
        def _():
            step_a(0)
            step_a(1)

        @pl.when(g == 1)
        def _():
            step_a(2)
            step_a(3)

    units_of(first_half)

    @pl.loop(0, quarter)
    def _(g):
        pair(last_half, g)

        @pl.when(g < quarter - 1)
        def _():
            nxt = last_half * (heads // 2) + 2 * (g + 1)
            fetch(nxt, 0).start()
            fetch(nxt + 1, 1).start()

        @pl.when(g == 0)
        def _():
            attn_a(0, first_half)
            attn_a(1, first_half)

        @pl.when(g == 1)
        def _():
            step_b(0)
            step_b(1)

    units_of(last_half)
    for copy in weights[1:]:
        copy.wait()

    @pl.loop(0, 2)
    def _(i):
        r = pl.ds(pl.multiple_of(i * (n // 2), 128), n // 2)
        ng[r] = mm_t(dq[r], wqs[...]) + mm_t(dk[r], wks[...]) + mm_t(dv[r], wvs[...])

    attn_a(0, last_half)
    attn_a(1, last_half)
    sm[...] = jnp.zeros_like(sm)
    slot_rows = n // ns
    gain_sum = jnp.zeros((1, width), F32)
    for i in range(ns):
        r = slice(i * slot_rows, (i + 1) * slot_rows)
        t = x[r].astype(F32)
        down, gain = norm_down(t, rms_scale(t), ag[...], ng[r])
        in_grad[i] = (hidden_grad[r] + down).astype(BF)
        gain_sum = gain_sum + jnp.sum(gain, axis=0, keepdims=True)
    keep_grad.start()
    for d in range(1, ns):
        grad_copy(d).start()

    col = lax.broadcasted_iota(jnp.int32, (128, width), 1)
    offset = (col // 128 - 1) * 128 - lax.rem(col, 128)
    offset = jnp.where(col >= width - 128, 256, jnp.where(col >= width - 256, -256, offset))
    dist = jnp.abs(offset)
    bucket = jnp.full_like(dist, 8)
    for edge in EDGES:
        bucket = bucket + (dist >= edge).astype(jnp.int32)
    bucket = jnp.where(dist < 8, dist, bucket) + jnp.where(offset > 0, 16, 0)
    pick = jnp.where(bucket == lax.broadcasted_iota(jnp.int32, (128, width), 0), 1.0, 0.0)
    bias = jnp.zeros((16, 128), F32)
    for i in range(width // 128):
        bias = bias + lax.dot_general(diag[:, i, :], pick[:, i * 128:(i + 1) * 128], (((1,), (1,)), ((), ())),
                                      precision=HIGHEST, preferred_element_type=F32)
    sm[0, 40:56, :] = bias
    gains = [gains_dec[i:i + 1, :] for i in range(3)] + [gains_feed[i:i + 1, :] for i in range(2)] + [gain_sum]
    for i, gain in enumerate(gains):
        for j in range(width // 128):
            sm[0, i * 6 + j:i * 6 + j + 1, :] = gain[:, j * 128:(j + 1) * 128]

    def small_copy(i):
        return remote(sm.at[i], smr.at[i], m_s.at[i], m_r.at[i], (core_peer, y_peer, x_peer)[i])

    def z_small(d):
        return remote(smz.at[z], smz.at[z], mz_s.at[d], mz_r.at[d], (lax.rem(z + d, nz) * 2 + xx, s))

    small_copy(0).start()
    step_b(2)
    step_b(3)
    small_copy(0).wait()
    sm[1] = sm[0] + smr[0]
    small_copy(1).start()
    attn_b(0, first_half)
    attn_y(0).start()
    attn_b(1, first_half)
    attn_y(1).start()
    step_c(0)
    step_c(1)
    small_copy(1).wait()
    sm[2] = sm[1] + smr[1]
    small_copy(2).start()
    step_c(2)
    step_c(3)
    attn_b(0, last_half)
    small_copy(2).wait()
    smz[z] = sm[2] + smr[2]

    @pl.loop(1, nz)
    def _(d):
        z_small(d).start()

    step_c(4)
    attn_b(1, last_half)
    step_c(5)
    for i in range(6):
        step_d(i)

    @pl.loop(1, nz)
    def _(d):
        z_small(d).wait()

    small_out[...] = smz[0]

    @pl.loop(1, nz)
    def _(d):
        small_out[...] = small_out[...] + smz[d]

    keep_dec.wait()
    keep_enc.wait()
    keep_grad.wait()
    for d in range(1, ns):
        enc_copy(d).wait()
        grad_copy(d).wait()

    @pl.loop(1, count)
    def _(d):
        dec_copy(d).wait()


def backward(np_, ns, x, ag, q, k, v, context_t, branch, hidden_grad, normed, gains_dec, gains_feed,
             probs, wo, wq, wk, wv, wide, tall, dec, encoded):
    n, width = x.shape
    heads = probs.shape[0]
    nz = np_ // 2
    rows, lanes = wide.shape[5:]
    count = np_ * ns
    padded = normed.shape[1]
    vm = pl.BlockSpec(memory_space=pltpu.VMEM)
    hb = pl.BlockSpec(memory_space=pl.ANY)
    S = jax.ShapeDtypeStruct
    V = pltpu.VMEM
    dma = pltpu.SemaphoreType.DMA
    nar = V((n, width), BF)
    square = V((width, width), BF)
    slots = (ns, n // ns, width)
    small = (64, 128)
    return pl.pallas_call(
        functools.partial(backward_kernel, np_, ns),
        out_shape=(S((6, rows, lanes), F32), S(small, F32), S(dec.shape, BF), S(slots, BF), S(slots, BF)),
        in_specs=[vm] * 11 + [hb] * 9,
        out_specs=(vm, vm, hb, hb, hb),
        scratch_shapes=[
            square, square, square, square, nar, V((n, n), F32), V((n, n), BF), V((width, n), BF), nar, nar, nar,
            V((128, n), BF), V((padded, n), BF), V((n, width), F32), V(slots, BF),
            V((2, n, n), BF), V((384, 128), F32), V((16, 8, 128), F32),
            V((4, 2, nz, 2, rows, lanes), BF), V((2, 2, 2, nz, 2, rows, lanes), BF), V((6, 2, nz, 2, rows, lanes), BF),
            V((2, nz, 2, rows, lanes), BF), V((2, 2, nz, rows, lanes), BF), V((2, 2, nz, rows, lanes), BF),
            V((6, nz, rows, lanes), BF), V((6, nz, rows, lanes), BF),
            V((3,) + small, F32), V((3,) + small, F32), V((nz,) + small, F32),
            dma((2,)), dma((4,)), dma((7,)), dma((4,)), dma((4,)), dma((4,)), dma((4,)), dma((6,)), dma((6,)),
            dma((2, 2)), dma((2, 2)), dma((2, 2)), dma((2, 2)), dma((6, nz)), dma((6, nz)),
            dma((3,)), dma((3,)), dma((nz,)), dma((nz,)), dma((count,)), dma((count,)),
            dma((ns,)), dma((ns,)), dma((ns,)), dma((ns,)),
        ],
        compiler_params=pltpu.CompilerParams(
            collective_id=0, has_side_effects=True, vmem_limit_bytes=62 * 1024 * 1024),
        name="backward",
    )(x, ag.reshape(1, -1), q, k, v, context_t, branch, hidden_grad, normed, gains_dec, gains_feed,
      probs, wo, wq, wk, wv, wide, tall, dec, encoded.reshape(slots))


def two_kernels(
    np_, ns, r, rp, lanes, side, length, final_gain, expand_gain, attend_gain, dec_gains,
    rows_grad, block, cot, reduce_weight, active, expand_weight, hidden, slope, mixed_t,
    output_weight, query_weight, key_weight, value_weight, query, key, value, x, normed_t,
    context_t, probs, dec_all, encoded,
):
    seq_len, ff = active.shape
    nz = np_ // 2
    wide, tall, hidden_grad, branch, feed_gains = feed_back(
        1, length, rows_grad, block, cot, final_gain, hidden, expand_gain, mixed_t.T, active,
        slope, reduce_weight, expand_weight)

    def pad(unit):
        return jnp.pad(unit, ((0, 0),) * 5 + ((0, rp - r), (0, 0)))

    tall = tall.reshape(2, 2, 2, r, side, nz, 2, ff // np_).transpose(0, 1, 2, 5, 6, 3, 4, 7)
    tall = pad(tall.reshape(2, 2, 2, nz, 2, r, lanes))
    wide = pad(wide.reshape(2, 2, 2, nz, 2, r, lanes))
    gap = ((0, 0), (0, rp - r), (0, 0))
    normed_t = jnp.pad(normed_t.reshape(np_, r, seq_len), gap).reshape(np_ * rp, seq_len)
    context_t = jnp.pad(context_t.reshape(np_, r, seq_len), gap).reshape(np_ * rp, seq_len)
    return backward(
        np_, ns, x, attend_gain, query, key, value, context_t, branch, hidden_grad, normed_t.T,
        dec_gains, feed_gains, probs, output_weight, query_weight, key_weight, value_weight,
        wide, tall, dec_all, encoded)


def per_device(
    enc_input, dec_input, lengths, attend_gain, query_weight, key_weight, value_weight,
    output_weight, bias_table, expand_gain, expand_weight, reduce_weight, final_gain,
    self_gain, self_value, self_output, cross_gain, cross_query, cross_key, cross_value,
    cross_output, feed_gain, feed_expand, feed_reduce, enc_cotangent, dec_cotangent,
):
    group, local_rows, width = enc_input.shape
    buckets, heads = bias_table.shape
    size = width // heads
    ff = expand_weight.shape[1]
    ns = lax.axis_size("seq")
    np_ = lax.axis_size("pairs")
    r = width // np_
    aligned = np_ == 8 and r % 32 == 0 and (ff // np_) % 128 == 0 and ff == 4 * width
    seq_len = local_rows * ns
    weights = (query_weight, key_weight, value_weight, output_weight, expand_weight, reduce_weight,
               self_value, self_output, cross_query, cross_key, cross_value, cross_output,
               feed_expand, feed_reduce)
    (normed_t, query, key, value, probs, context_t, hidden, mixed_t, active, slope, block, encoded,
     x, cot, rows_grad, wide_rows, mids, dec_input_grad, *dec_rows) = forward(
        np_, ns, aligned, lengths, bias_table.T,
        (attend_gain, expand_gain, final_gain, self_gain, cross_gain, feed_gain),
        dec_input, dec_cotangent, enc_input, enc_cotangent, weights)
    x = x.reshape(seq_len, width)
    cot = cot.reshape(seq_len, width)
    if aligned:
        state, dec_all = dec_rows
        red, small_sum, dec_got, enc_out, grad_out, dec_block = fused(
            np_, ns, lengths, final_gain, expand_gain, attend_gain, state, wide_rows,
            rows_grad, block, cot,
            reduce_weight, active, expand_weight, hidden, slope, mixed_t, output_weight,
            query_weight, key_weight, value_weight, query, key, value, x, normed_t, context_t,
            probs, dec_all, encoded, feed_reduce)
        (enc_out, grad_out, dec_block, dec_input_grad, grad_query, grad_key, grad_value, grad_output, grad_expand, grad_reduce,
         bias, *rest) = finish(
            heads, buckets, red, small_sum, dec_got, dec_block, dec_input_grad, enc_out, grad_out)
        gains = rest[:6]
        grad_sv, grad_so, grad_cq, grad_ck, grad_cv, grad_co, feed_in, feed_out = rest[6:]
        return (
            enc_out, dec_block, grad_out, dec_input_grad, gains[5], grad_query, grad_key,
            grad_value, grad_output, bias.T, gains[4], grad_expand, grad_reduce.T, gains[3],
            gains[0], grad_sv, grad_so, gains[1], grad_cq, grad_ck, grad_cv, grad_co, gains[2],
            feed_in, feed_out.T,
        )
    dec_block, dec_gains, left, right = dec_rows
    length = lax.dynamic_slice_in_dim(lengths, lax.axis_index("seq"), 1)
    rp = -(-r // 16) * 16
    lanes = ff // 8
    side = width // 8 // r
    cols = width // ns

    left_cut = jnp.concatenate([
        left.reshape(5, np_, r).transpose(1, 0, 2).reshape(np_, 5 * r),
        wide_rows[0].reshape(np_, 4 * r),
    ], axis=1)
    mid_cut = mids.reshape(2, ns, heads // ns, np_, r).transpose(3, 1, 0, 2, 4)
    mid_cut = mid_cut.reshape(np_, ns, 6 * r)
    right_cut = jnp.concatenate([
        right.reshape(7, ns, cols).transpose(1, 0, 2).reshape(ns, 7 * cols),
        wide_rows[1].reshape(ns, 4 * cols)], axis=1)
    dec_all = jnp.concatenate([
        jnp.broadcast_to(left_cut[:, None], (np_, ns, 9 * r)), mid_cut,
        jnp.broadcast_to(right_cut[None], (np_, ns, 11 * cols))], axis=-1)
    dec_all = dec_all.astype(BF).reshape(np_ * ns, -1)
    used = dec_all.shape[1]
    dec_rows = -(-used // 2048) * 16
    dec_all = jnp.pad(dec_all, ((0, 0), (0, dec_rows * 128 - used)))
    dec_all = dec_all.reshape(np_ * ns, dec_rows, 128)

    red, small_sum, dec_got, enc_out, grad_out = two_kernels(
        np_, ns, r, rp, lanes, side, length, final_gain, expand_gain, attend_gain, dec_gains,
        rows_grad, block, cot, reduce_weight, active, expand_weight, hidden, slope, mixed_t,
        output_weight, query_weight, key_weight, value_weight, query, key, value, x, normed_t,
        context_t, probs, dec_all, encoded)

    got = dec_got.reshape(np_ * ns, -1)
    lefts = got[:, :9 * r].reshape(-1, 9, r)
    mid_got = got[:, 9 * r:15 * r].reshape(-1, 2, 3, r)
    rights = got[:, 15 * r:15 * r + 11 * cols].reshape(-1, 11, cols)
    plain = jnp.einsum("nkr,nkc->krc", lefts[:, :4], rights[:, :4], preferred_element_type=F32)
    crossed = jnp.einsum("nkhr,nkhd->krhd", mid_got, rights[:, 4:6].reshape(-1, 2, 3, size),
                         preferred_element_type=F32).reshape(2, r, cols)
    feed_in = jnp.einsum("nr,nc->rc", lefts[:, 4], rights[:, 7:11].reshape(-1, 4 * cols),
                         preferred_element_type=F32)
    feed_out = jnp.einsum("nr,nc->rc", lefts[:, 5:9].reshape(-1, 4 * r), rights[:, 6],
                          preferred_element_type=F32)
    red = red[:, :r]
    grad_reduce = red[2:4].reshape(2, r, side, ff // np_).reshape(cols, ff // np_).T
    gains = small_sum[:36].reshape(6, width)
    bias = small_sum[40:40 + heads, :buckets].T
    return (
        enc_out, dec_block, grad_out, dec_input_grad,
        gains[5],
        red[4][:, :cols], red[4][:, cols:], red[5][:, :cols], red[5][:, cols:],
        bias,
        gains[4],
        jnp.concatenate([red[0], red[1]], axis=1), grad_reduce,
        gains[3],
        gains[0], plain[0], plain[1],
        gains[1], plain[2], crossed[0], crossed[1], plain[3],
        gains[2], feed_in, feed_out,
    )


def solution(mesh):
    rows = P("pairs", "seq", None)
    single = P(("pairs", "seq"), None)
    block = P("pairs", "seq")
    return jax.shard_map(
        per_device,
        mesh=mesh,
        in_specs=(rows, single, P("pairs")) + (P(),) * 21 + (rows, single),
        out_specs=(
            rows, single, rows, single,
            P(), block, block, block, block, P(), P(), block, block, P(),
            P(), block, block, P(), block, block, block, block, P(), block, block,
        ),
        check_vma=False,
    )
```
